32 devices in a mesh: grp: 2 (over y), seq: 8 (over z, x), ch: 2 (over core).
Axes of the slice: x: 2, y: 2, z: 4, core: 2. Of those that a mesh axis runs over, the one named last changes fastest.
Arguments:
- tokens: bfloat16 [2048, 2048], P(('grp', 'seq'), 'ch'), parts along dimension 0, may hold values from -6 to 6
- gate_q: bfloat16 [2048, 2048], P(('grp', 'seq'), 'ch'), parts along dimension 0, may hold values from -6 to 6
- gate_k: bfloat16 [2048, 2048], P(('grp', 'seq'), 'ch'), parts along dimension 0, may hold values from -6 to 6
- w_value: bfloat16 [2048, 2048], P('seq', 'ch'), may hold values from -0.125 to 0.125
- skip: float32 [2048], P('ch'), may hold values from 0.5 to 1.5
- filter_spectrum: bfloat16 [2, 16, 128, 2048], P(None, 'seq', None, 'ch'), may hold values from -12 to 12
- w_out: bfloat16 [2048, 2048], P('seq', 'ch'), may hold values from -0.125 to 0.125
Outputs:
- mixed: bfloat16 [2048, 2048], P(('grp', 'seq'), 'ch'), parts along dimension 0
The draws below stay inside these ranges and needn't reach their ends.
There are 2 independent parts, one for each index of `grp`. The reference program is written for one: setup_inputs(seed, part) draws one part's arguments, and reference() takes and returns one part's arrays. A program takes and returns all parts, laid end to end along the dimension named above; an argument that names none is the same for every part. Nothing has to cross between parts.
All inputs are finite; a program needn't handle non-finite values.
Results may differ from the reference program's by a relative error of at most 0.009.
Values may be sent and summed in bfloat16 or wider, within the bound.
No kernel may reach another device: no remote copies, remote signals or barrier semaphores. Data moves between devices by JAX's collectives and lax.ppermute only.
A program may use at most 64 MiB of HBM per device.

```python
import math
import jax
import jax.numpy as jnp
from jax import lax

DM = 2048
HC = 2048
TOK_DEV = 128
SEQ_LEN = 1024
FREQ_ROWS = 16
N_SEQ = 8


def steps_of(key, extent, shards, smallest, high):
    def one(dim, parts):
        draws = jax.random.uniform(jax.random.fold_in(jax.random.fold_in(key, 6), dim), (parts,), jnp.float32, smallest / len(shards), high / len(shards))
        return jnp.repeat(jnp.exp(draws), extent[dim] // parts).reshape((-1,) + (1,) * (len(extent) - dim - 1))

    factor_of = one(*shards[0])
    for cut in shards[1:]:
        factor_of = factor_of * one(*cut)
    return factor_of


def bell_draw(own_key, dims, scale, limit, split=(), held_as=jnp.bfloat16):
    gain = steps_of(own_key, dims, split, -0.22, 0.18) if split else 1.0
    drawn = jax.random.normal(own_key, dims, jnp.float32) * scale * gain
    return jnp.minimum(jnp.maximum(drawn, -limit), limit).astype(held_as)


def setup_inputs(seed: int = 0, part: int = 0) -> dict:
    key_list = jax.random.split(jax.random.key(seed), 8)
    part_splits = jax.random.split(jax.random.fold_in(key_list[7], part), 8)
    return {
        "tokens": bell_draw(part_splits[0], (SEQ_LEN, DM), 1.0, 6.0, ((0, 8), (1, 2))),
        "gate_q": bell_draw(part_splits[1], (SEQ_LEN, HC), 1.0, 6.0, ((0, 8), (1, 2))),
        "gate_k": bell_draw(part_splits[2], (SEQ_LEN, HC), 1.0, 6.0, ((0, 8), (1, 2))),
        "w_value": bell_draw(key_list[3], (DM, HC), DM ** -0.5, 0.125, ((0, 8), (1, 2))),
        "skip": jnp.clip(0.5 + 1.0 * jax.random.uniform(key_list[4], (HC,), jnp.float32) ** steps_of(key_list[4], (HC,), ((0, 2),), -0.2, 0.2), 0.5, 1.5),
        "filter_spectrum": bell_draw(key_list[5], (2, FREQ_ROWS, TOK_DEV, HC), 2.0, 12.0, ((1, 8), (3, 2))),
        "w_out": bell_draw(key_list[6], (DM, HC), HC ** -0.5, 0.125, ((0, 8), (1, 2))),
    }


def angles(count, first, second):
    phase = (2.0 * math.pi / count) * ((first[:, None] * second[None, :]) % count).astype(jnp.float32)
    return jnp.cos(phase), jnp.sin(phase)


def widened(values):
    return lax.optimization_barrier(values).astype(jnp.float32)


def reference(tokens, gate_q, gate_k, w_value, skip, filter_spectrum, w_out):
    seq_count = N_SEQ
    length_b = TOK_DEV
    freq_rows = 2 * seq_count
    fft_length = freq_rows * length_b
    value = jnp.dot(tokens, w_value, preferred_element_type=jnp.float32).astype(jnp.bfloat16)
    drive = (gate_k.astype(jnp.float32) * widened(value)).astype(jnp.bfloat16)
    index_rows = jnp.arange(freq_rows, dtype=jnp.int32)
    index_seq = jnp.arange(seq_count, dtype=jnp.int32)
    index_b = jnp.arange(length_b, dtype=jnp.int32)
    cos_first, sin_first = angles(freq_rows, index_rows, index_seq)
    cos_first = widened(cos_first.astype(jnp.bfloat16))
    sin_first = widened(sin_first.astype(jnp.bfloat16))
    cos_seq, sin_seq = angles(length_b, index_b, index_b)
    cos_seq = widened(cos_seq.astype(jnp.bfloat16))
    sin_seq = widened(sin_seq.astype(jnp.bfloat16))
    twist_cos, twist_sin = angles(fft_length, index_rows, index_b)
    twist_cos = twist_cos[:, :, None]
    twist_sin = twist_sin[:, :, None]
    width = math.gcd(HC, 128)
    blocks = HC // width

    def convolve(pair):
        block, spectrum = pair
        data = widened(block)
        real_part = jnp.einsum("ka,abc->kbc", cos_first, data)
        imag_part = -jnp.einsum("ka,abc->kbc", sin_first, data)
        section_real = widened((real_part * twist_cos + imag_part * twist_sin).astype(jnp.bfloat16))
        section_imag = widened((imag_part * twist_cos - real_part * twist_sin).astype(jnp.bfloat16))
        spectrum_real = jnp.einsum("qb,kbc->kqc", cos_seq, section_real) + jnp.einsum("qb,kbc->kqc", sin_seq, section_imag)
        spectrum_imag = jnp.einsum("qb,kbc->kqc", cos_seq, section_imag) - jnp.einsum("qb,kbc->kqc", sin_seq, section_real)
        filter_real = spectrum[0].astype(jnp.float32)
        filter_imag = spectrum[1].astype(jnp.float32)
        product_real = widened((spectrum_real * filter_real - spectrum_imag * filter_imag).astype(jnp.bfloat16))
        product_imag = widened((spectrum_real * filter_imag + spectrum_imag * filter_real).astype(jnp.bfloat16))
        inverse_real = jnp.einsum("qb,kqc->kbc", cos_seq, product_real) - jnp.einsum("qb,kqc->kbc", sin_seq, product_imag)
        inverse_imag = jnp.einsum("qb,kqc->kbc", sin_seq, product_real) + jnp.einsum("qb,kqc->kbc", cos_seq, product_imag)
        back_real = widened((inverse_real * twist_cos - inverse_imag * twist_sin).astype(jnp.bfloat16))
        back_imag = widened((inverse_real * twist_sin + inverse_imag * twist_cos).astype(jnp.bfloat16))
        result = jnp.einsum("ka,kbc->abc", cos_first, back_real) - jnp.einsum("ka,kbc->abc", sin_first, back_imag)
        return (result * (1.0 / fft_length)).astype(jnp.bfloat16)

    drive_blocks = drive.reshape(seq_count, length_b, blocks, width).transpose(2, 0, 1, 3)
    filter_blocks = filter_spectrum.reshape(2, freq_rows, length_b, blocks, width).transpose(3, 0, 1, 2, 4)
    conv = lax.map(convolve, (drive_blocks, filter_blocks))
    conv = conv.transpose(1, 2, 0, 3).reshape(seq_count * length_b, HC)
    gated = (gate_q.astype(jnp.float32) * (widened(conv) + skip[None, :] * widened(drive))).astype(jnp.bfloat16)
    return jnp.dot(gated, w_out.T, preferred_element_type=jnp.float32).astype(jnp.bfloat16)
```

```python
import functools
import math

import jax
import jax.numpy as jnp
import numpy as np
from jax import lax
from jax.experimental import pallas as pl
from jax.experimental.pallas import tpu as pltpu
from jax.sharding import PartitionSpec as P

AXES = ("grp", "seq", "ch")
BF16 = jnp.bfloat16
F32 = jnp.float32


def angles(count, first, second):
    phase = 2.0 * math.pi / count * (first[:, None] * second[None, :] % count).astype(jnp.float32)
    return (jnp.cos(phase), jnp.sin(phase))


def widened(values):
    return lax.optimization_barrier(values).astype(jnp.float32)


def dot(a, b):
    return jnp.dot(a, b, preferred_element_type=F32)


def dot_t(a, b):
    return lax.dot_general(a, b, (((1,), (1,)), ((), ())), preferred_element_type=F32)


def in_vmem(kernel, out_shape, scratch=(), smem=1, flops=0, moved=0):
    def call(*operands):
        specs = [pl.BlockSpec(memory_space=pltpu.SMEM)] * smem
        specs += [pl.BlockSpec(memory_space=pltpu.VMEM)] * (len(operands) - smem)
        return pl.pallas_call(
            kernel,
            out_shape=out_shape,
            in_specs=specs,
            out_specs=jax.tree.map(lambda _: pl.BlockSpec(memory_space=pltpu.VMEM), out_shape),
            scratch_shapes=list(scratch),
            compiler_params=pltpu.CompilerParams(vmem_limit_bytes=48 * 1024 * 1024),
            cost_estimate=pl.CostEstimate(flops=flops, bytes_accessed=moved, transcendentals=0),
        )(*operands)

    return call


def low_lanes(shape):
    return lax.broadcasted_iota(jnp.int32, shape, len(shape) - 1) < 64


def half_turn(values):
    return pltpu.roll(values, 64, values.ndim - 1)


def pack_filter(where, filt, out):
    y = where[0]
    low = low_lanes((128, 128))
    for x in range(2):
        for j in range(2):
            base = pl.multiple_of(y * 512 + x * 256 + j * 128, 128)
            for part in range(2):
                even = filt[part, 0, :, pl.ds(base, 128)].astype(F32)
                odd = filt[part, 1, :, pl.ds(base, 128)].astype(F32)
                out[2 * (2 * j) + x, part] = jnp.where(low, even, half_turn(odd)).astype(BF16)
                out[2 * (2 * j + 1) + x, part] = jnp.where(low, half_turn(even), odd).astype(BF16)


def value_kernel(where, mine, other, *refs):
    pieces, gates = refs[:8], refs[8:12]
    drive, outs = refs[12], refs[13:17]
    acc, packed = refs[17], refs[18]
    x, z, c = where[1], where[2], where[3]
    acc[...] = jnp.zeros_like(acc)
    for r in range(4):
        owner = lax.rem(z - r + 4, 4)
        for k in range(2):
            row = jnp.where(k == 0, x, 1 - x)
            off = pl.multiple_of(lax.rem(owner, 2) * 512 + row * 256, 256)
            piece = pieces[2 * r + k]

            @pl.when(owner // 2 == c)
            def _():
                acc[...] += dot(mine[:, pl.ds(off, 256)], piece[...])

            @pl.when(owner // 2 != c)
            def _():
                acc[...] += dot(other[:, pl.ds(off, 256)], piece[...])

    for p in range(4):
        rows = pl.ds(p * 128, 128)
        value = acc[rows, :].astype(BF16).astype(F32)
        drive[rows, :] = (gates[p][...].astype(F32) * value).astype(BF16)
    low = low_lanes((256, 128))
    for j in range(2):
        lanes = pl.ds(j * 128, 128)
        first = drive[pl.ds(0, 256), lanes].astype(F32)
        second = drive[pl.ds(256, 256), lanes].astype(F32)
        packed[2 * j] = jnp.where(low, first, half_turn(second)).astype(BF16)
        packed[2 * j + 1] = jnp.where(low, half_turn(first), second).astype(BF16)
    for r in range(4):
        outs[r][...] = packed[lax.rem(z + r, 4)]


def add(a, b):
    return b if a is None else a if b is None else a + b


def sub(a, b):
    return a if b is None else -b if a is None else a - b


def scaled(a, s):
    if a is None or abs(s) < 1e-9:
        return None
    if abs(s - 1) < 1e-9:
        return a
    if abs(s + 1) < 1e-9:
        return -a
    return a * np.float32(s)


def cmul(a, angle):
    co, si = math.cos(angle), math.sin(angle)
    return (sub(scaled(a[0], co), scaled(a[1], si)), add(scaled(a[0], si), scaled(a[1], co)))


def cadd(a, b):
    return (add(a[0], b[0]), add(a[1], b[1]))


def conj(a):
    return (a[0], None if a[1] is None else -a[1])


def short_transform(values, count, rows):
    if len(values) == 1:
        return [(values[0], None)] * rows
    half = count // 2
    need = half // 2 + 1
    even = short_transform(values[0::2], half, need)
    odd = short_transform(values[1::2], half, need)

    def at(t, k):
        k %= half
        return t[k] if k < need else conj(t[half - k])

    return [cadd(at(even, k), cmul(at(odd, k), -2 * math.pi * k / count)) for k in range(rows)]


def conv_kernel(where, d0, d1, d2, d3, filt, table, table_t, o0, o1, o2, o3, data, first, sums):
    x, z = where[1], where[2]
    for r, block in enumerate((d0, d1, d2, d3)):
        base = 2 * lax.rem(z - r + 4, 4)
        data[base + x] = block[pl.ds(0, 128), :]
        data[base + 1 - x] = block[pl.ds(128, 128), :]
    for i in range(8):
        rows = pl.ds(16 * i, 16)
        values = [data[a, rows, :].astype(F32) for a in range(8)]
        spectrum = short_transform(values, 16, 9)
        for k in range(9):
            re, im = spectrum[k]
            first[k, rows, :] = re.astype(BF16)
            if im is None:
                im = jnp.zeros_like(re)
            first[k, pl.ds(128 + 16 * i, 16), :] = im.astype(BF16)
            if 0 < k < 8:
                first[16 - k, rows, :] = re.astype(BF16)
                first[16 - k, pl.ds(128 + 16 * i, 16), :] = (-im).astype(BF16)
    low = low_lanes((128, 128))

    def back(k):
        spectrum = dot(table[k], first[k])
        re, im = spectrum[:128], spectrum[128:]
        pair = [filt[k // 2, part].astype(F32) for part in range(2)]
        if k % 2 == 0:
            fr, fi = [jnp.where(low, f, half_turn(f)) for f in pair]
        else:
            fr, fi = [jnp.where(low, half_turn(f), f) for f in pair]
        product = jnp.concatenate([re * fr - im * fi, re * fi + im * fr], axis=0).astype(BF16)
        return dot(table_t[k], product)

    sums[0] = back(0)
    sums[8] = back(8)
    for k in range(1, 8):
        one, two = back(k), back(16 - k)
        sums[k, pl.ds(0, 128)] = one[:128] + two[:128]
        sums[k, pl.ds(128, 128)] = one[128:] - two[128:]
    for i in range(16):
        rows, below = pl.ds(8 * i, 8), pl.ds(128 + 8 * i, 8)
        scale = 1.0 / 2048
        re = [sums[k, rows, :] * scale for k in range(9)]
        im = [None] + [sums[k, below, :] * scale for k in range(1, 8)] + [None]
        for a in range(5):
            groups = [None] * 4
            for k in range(9):
                ang = 2 * math.pi * (k * a % 16) / 16
                groups[k % 2] = add(groups[k % 2], scaled(re[k], math.cos(ang)))
                groups[2 + k % 2] = sub(groups[2 + k % 2], scaled(im[k], math.sin(ang)))
            ec, oc, es, os = groups
            data[a, rows, :] = add(add(ec, oc), add(es, os)).astype(BF16)
            if 0 < a < 4:
                data[8 - a, rows, :] = sub(sub(add(ec, os), oc), es).astype(BF16)
    for r, out in enumerate((o0, o1, o2, o3)):
        base = 2 * lax.rem(z + r, 4)
        out[pl.ds(0, 128), :] = data[base + x]
        out[pl.ds(128, 128), :] = data[base + 1 - x]


def gate_kernel(where, e0, e1, e2, e3, drive, skip, g0, g1, g2, g3, gated, conv):
    z = where[2]
    for r, block in enumerate((e0, e1, e2, e3)):
        conv[lax.rem(z - r + 4, 4)] = block[...]
    low = low_lanes((256, 128))
    for j in range(2):
        lanes = pl.ds(j * 128, 128)
        even, odd = conv[2 * j].astype(F32), conv[2 * j + 1].astype(F32)
        parts = (jnp.where(low, even, half_turn(odd)), jnp.where(low, half_turn(even), odd))
        for p, gate in enumerate((g0, g1, g2, g3)):
            rows = pl.ds(p * 128, 128)
            own = parts[p // 2][(p % 2) * 128 : (p % 2) * 128 + 128]
            direct = skip[:, lanes] * drive[rows, lanes].astype(F32)
            gated[rows, lanes] = (gate[:, lanes].astype(F32) * (own + direct)).astype(BF16)


def out_kernel(where, gated, other, *refs):
    mine, theirs = refs[:4], refs[4:8]
    own, sends = refs[8], refs[9:12]
    for p in (3, 2, 1, 0):
        rows = pl.ds(p * 128, 128)
        for i in range(4):
            total = dot_t(gated[rows, :], mine[i][...]) + dot_t(other[rows, :], theirs[i][...])
            lanes = pl.ds(i * 256, 256)
            if p == 0:
                own[:, lanes] = total
            else:
                sends[p - 1][:, lanes] = total.astype(BF16)


def tables():
    k = np.arange(16)[:, None, None] + 16 * np.arange(128)[None, :, None]
    phase = 2 * np.pi / 2048 * (k * np.arange(128)[None, None, :] % 2048)
    co, si = np.cos(phase), np.sin(phase)
    table = np.concatenate([np.concatenate([co, si], 2), np.concatenate([-si, co], 2)], 1)
    table = table.astype(jnp.bfloat16)
    return table, np.ascontiguousarray(table.transpose(0, 2, 1))


def planes(tokens, gate_q, gate_k, w_value, skip, filter_spectrum, w_out):
    y, s, c = (lax.axis_index(a) for a in AXES)
    x, z = s % 2, s // 2
    seq, deep = 8, 4
    where = jnp.stack([y, x, z, c]).astype(jnp.int32)

    def permute(values, move):
        pairs = []
        for g in range(2):
            for i in range(seq):
                for k in range(2):
                    g2, z2, x2, k2 = move(g, i // 2, i % 2, k)
                    pairs.append(((g * seq + i) * 2 + k, (g2 * seq + z2 * 2 + x2) * 2 + k2))
        return lax.ppermute(values, AXES, pairs)

    def to_x(values):
        return permute(values, lambda g, z, x, k: (g, z, 1 - x, k))

    def to_core(values):
        return permute(values, lambda g, z, x, k: (g, z, x, 1 - k))

    def to_z(values, r):
        return permute(values, lambda g, z, x, k: (g, (z + r) % deep, x, k))

    def to_peer(values, p):
        return permute(values, lambda g, z, x, k: (g ^ (p // 2), z, x ^ (p % 2), k))

    def quarter(values, p=0):
        q = (y ^ (p // 2)) * 2 + (x ^ (p % 2))
        return lax.dynamic_slice_in_dim(values, q * 256, 256, axis=values.ndim - 1)

    def around(weight):
        pieces = [quarter(weight), to_x(quarter(weight, 1))]
        for _ in range(3):
            pieces += [to_z(pieces[-2], 1), to_z(pieces[-1], 1)]
        return pieces

    value_pieces = around(w_value)
    received = [
        to_peer(jnp.concatenate([tokens, quarter(gate_k, p), quarter(gate_q, p)], axis=1), p)
        for p in (1, 2, 3)
    ]
    keys = [quarter(gate_k)] + [m[:, 1024:1280] for m in received]
    queries = [quarter(gate_q)] + [m[:, 1280:] for m in received]
    mine = jnp.concatenate([tokens] + [m[:, :1024] for m in received], axis=0)
    other = to_core(mine)
    shape = jax.ShapeDtypeStruct
    packed = in_vmem(pack_filter, shape((8, 2, 128, 128), BF16), moved=1 << 20)(where, filter_spectrum)
    filters = lax.all_to_all(packed, "seq", split_axis=0, concat_axis=0, tiled=True)
    block = shape((256, 128), BF16)
    drive, *sends = in_vmem(
        value_kernel,
        [shape((512, 256), BF16)] + [block] * 4,
        [pltpu.VMEM((512, 256), F32), pltpu.VMEM((4, 256, 128), BF16)],
        flops=1 << 29,
        moved=4 << 20,
    )(where, mine, other, *value_pieces, *keys)
    columns = [sends[0]] + [to_z(sends[r], r) for r in (1, 2, 3)]
    table, table_t = tables()
    sends = in_vmem(
        conv_kernel,
        [block] * 4,
        [
            pltpu.VMEM((8, 128, 128), BF16),
            pltpu.VMEM((16, 256, 128), BF16),
            pltpu.VMEM((9, 256, 128), F32),
        ],
        flops=1 << 30,
        moved=5 << 20,
    )(where, *columns, filters, table, table_t)
    rows = [sends[0]] + [to_z(sends[r], r) for r in (1, 2, 3)]

    out_pieces = around(w_out)
    order = []
    for i in range(deep):
        r = (z - i) % deep
        for k in range(2):
            which = (x + k) % 2
            order.append(2 * r + which)
    stacked = jnp.stack(out_pieces)
    ordered = [lax.dynamic_index_in_dim(stacked, o, 0, keepdims=False) for o in order]
    halves = jnp.stack(ordered).reshape(2, 4, 256, 256)
    keep = lax.dynamic_index_in_dim(halves, c, 0, keepdims=False)
    give = lax.dynamic_index_in_dim(halves, 1 - c, 0, keepdims=False)
    theirs = to_core(give)
    gated = in_vmem(
        gate_kernel, shape((512, 256), BF16), [pltpu.VMEM((4, 256, 128), BF16)], moved=1 << 20
    )(where, *rows, drive, quarter(skip)[None, :], *queries)
    gated_other = to_core(gated)
    own, *sends = in_vmem(
        out_kernel,
        [shape((128, 1024), F32)] + [shape((128, 1024), BF16)] * 3,
        flops=1 << 30,
        moved=4 << 20,
    )(where, gated, gated_other, *[keep[i] for i in range(4)], *[theirs[i] for i in range(4)])
    parts = [to_peer(sends[p - 1], p) for p in (3, 2, 1)]
    total = own
    for part in parts:
        total = total + part.astype(F32)
    return total.astype(BF16)


def shards(tokens, gate_q, gate_k, w_value, skip, filter_spectrum, w_out):
    seq_count = lax.axis_size("seq")
    position = lax.axis_index("seq")
    length_b = tokens.shape[0]
    columns_each = length_b // seq_count
    freq_rows = 2 * seq_count
    freqs_each = freq_rows // seq_count
    fft_length = freq_rows * length_b
    features = lax.all_gather(tokens, "ch", axis=1, tiled=True)
    value_weight, out_weight = (
        lax.all_gather(w_value, "seq", axis=0, tiled=True),
        lax.all_gather(w_out, "seq", axis=0, tiled=True),
    )
    value = jnp.dot(features, value_weight, preferred_element_type=jnp.float32)
    value = value.astype(jnp.bfloat16)
    drive = (gate_k.astype(jnp.float32) * widened(value)).astype(jnp.bfloat16)
    channels = drive.shape[1]
    columns = lax.all_to_all(drive[None], "seq", split_axis=1, concat_axis=0, tiled=True)
    index_rows = jnp.arange(freq_rows, dtype=jnp.int32)
    index_seq = jnp.arange(seq_count, dtype=jnp.int32)
    index_b = jnp.arange(length_b, dtype=jnp.int32)
    cos_first, sin_first = angles(freq_rows, index_rows, index_seq)
    cos_first = cos_first.astype(jnp.bfloat16)
    sin_first = sin_first.astype(jnp.bfloat16)
    flattened = columns.reshape(seq_count, columns_each * channels)
    real_part = jnp.dot(cos_first, flattened, preferred_element_type=jnp.float32)
    imag_part = jnp.dot(-sin_first, flattened, preferred_element_type=jnp.float32)
    real_part = real_part.reshape(freq_rows, columns_each, channels)
    imag_part = imag_part.reshape(freq_rows, columns_each, channels)
    mine_b = position * columns_each + jnp.arange(columns_each, dtype=jnp.int32)
    twist_cos, twist_sin = angles(fft_length, index_rows, mine_b)
    twist_cos = twist_cos[:, :, None]
    twist_sin = twist_sin[:, :, None]
    section = jnp.stack(
        [
            real_part * twist_cos + imag_part * twist_sin,
            imag_part * twist_cos - real_part * twist_sin,
        ]
    ).astype(jnp.bfloat16)
    spectral = lax.all_to_all(section, "seq", split_axis=1, concat_axis=2, tiled=True)
    cos_seq, sin_seq = angles(length_b, index_b, index_b)
    cos_seq = cos_seq.astype(jnp.bfloat16)
    sin_seq = sin_seq.astype(jnp.bfloat16)
    spectrum_real = jnp.einsum(
        "qb,kbc->kqc", cos_seq, spectral[0], preferred_element_type=jnp.float32
    ) + jnp.einsum("qb,kbc->kqc", sin_seq, spectral[1], preferred_element_type=jnp.float32)
    spectrum_imag = jnp.einsum(
        "qb,kbc->kqc", cos_seq, spectral[1], preferred_element_type=jnp.float32
    ) - jnp.einsum("qb,kbc->kqc", sin_seq, spectral[0], preferred_element_type=jnp.float32)
    filter_real = filter_spectrum[0].astype(jnp.float32)
    filter_imag = filter_spectrum[1].astype(jnp.float32)
    product = jnp.stack(
        [
            spectrum_real * filter_real - spectrum_imag * filter_imag,
            spectrum_real * filter_imag + spectrum_imag * filter_real,
        ]
    ).astype(jnp.bfloat16)
    inverse_real = jnp.einsum(
        "qb,kqc->kbc", cos_seq, product[0], preferred_element_type=jnp.float32
    ) - jnp.einsum("qb,kqc->kbc", sin_seq, product[1], preferred_element_type=jnp.float32)
    inverse_imag = jnp.einsum(
        "qb,kqc->kbc", sin_seq, product[0], preferred_element_type=jnp.float32
    ) + jnp.einsum("qb,kqc->kbc", cos_seq, product[1], preferred_element_type=jnp.float32)
    mine_k = position * freqs_each + jnp.arange(freqs_each, dtype=jnp.int32)
    back_cos, back_sin = angles(fft_length, mine_k, index_b)
    back_cos = back_cos[:, :, None]
    back_sin = back_sin[:, :, None]
    back = jnp.stack(
        [
            inverse_real * back_cos - inverse_imag * back_sin,
            inverse_real * back_sin + inverse_imag * back_cos,
        ]
    ).astype(jnp.bfloat16)
    returned = lax.all_to_all(back, "seq", split_axis=2, concat_axis=1, tiled=True)
    flat_real = returned[0].reshape(freq_rows, columns_each * channels)
    flat_imag = returned[1].reshape(freq_rows, columns_each * channels)
    conv = jnp.dot(cos_first.T, flat_real, preferred_element_type=jnp.float32) - jnp.dot(
        sin_first.T, flat_imag, preferred_element_type=jnp.float32
    )
    conv = (
        (conv * (1.0 / fft_length)).reshape(seq_count, columns_each, channels).astype(jnp.bfloat16)
    )
    conv_rows = lax.all_to_all(conv, "seq", split_axis=0, concat_axis=1, tiled=True)[0]
    gated = (
        gate_q.astype(jnp.float32) * (widened(conv_rows) + skip[None, :] * widened(drive))
    ).astype(jnp.bfloat16)
    partial_value = lax.dot_general(
        gated, out_weight, (((1,), (1,)), ((), ())), preferred_element_type=jnp.float32
    )
    return lax.psum_scatter(
        partial_value.astype(jnp.bfloat16), "ch", scatter_dimension=1, tiled=True
    )


def solution(mesh):
    placed = (
        P(("grp", "seq"), "ch"),
        P(("grp", "seq"), "ch"),
        P(("grp", "seq"), "ch"),
        P("seq", "ch"),
        P("ch"),
        P(None, "seq", None, "ch"),
        P("seq", "ch"),
    )
    sizes = mesh.shape
    body = planes if (sizes["grp"], sizes["seq"], sizes["ch"]) == (2, 8, 2) else shards
    return jax.shard_map(
        body, mesh=mesh, in_specs=placed, out_specs=P(("grp", "seq"), "ch"), check_vma=False
    )
```

```python
import functools
import math

import jax
import jax.numpy as jnp
import numpy as np
from jax import lax
from jax.experimental import pallas as pl
from jax.experimental.pallas import tpu as pltpu
from jax.sharding import PartitionSpec as P

AXES = ("grp", "seq", "ch")
BF16 = jnp.bfloat16
F32 = jnp.float32


def angles(count, first, second):
    phase = 2.0 * math.pi / count * (first[:, None] * second[None, :] % count).astype(jnp.float32)
    return (jnp.cos(phase), jnp.sin(phase))


def widened(values):
    return lax.optimization_barrier(values).astype(jnp.float32)


def dot(a, b):
    return jnp.dot(a, b, preferred_element_type=F32)


def dot_t(a, b):
    return lax.dot_general(a, b, (((1,), (1,)), ((), ())), preferred_element_type=F32)


def in_vmem(kernel, out_shape, scratch=(), smem=1, flops=0, moved=0):
    def call(*operands):
        specs = [pl.BlockSpec(memory_space=pltpu.SMEM)] * smem
        specs += [pl.BlockSpec(memory_space=pltpu.VMEM)] * (len(operands) - smem)
        return pl.pallas_call(
            kernel,
            out_shape=out_shape,
            in_specs=specs,
            out_specs=jax.tree.map(lambda _: pl.BlockSpec(memory_space=pltpu.VMEM), out_shape),
            scratch_shapes=list(scratch),
            compiler_params=pltpu.CompilerParams(vmem_limit_bytes=48 * 1024 * 1024),
            cost_estimate=pl.CostEstimate(flops=flops, bytes_accessed=moved, transcendentals=0),
        )(*operands)

    return call


def low_lanes(shape):
    return lax.broadcasted_iota(jnp.int32, shape, len(shape) - 1) < 64


def half_turn(values):
    return pltpu.roll(values, 64, values.ndim - 1)


def both(first, second, low):
    return (
        jnp.where(low, first, half_turn(second)).astype(BF16),
        jnp.where(low, half_turn(first), second).astype(BF16),
    )


def pack_weight(where, weight, own, away):
    y, x = where[0], where[1]
    own[...] = weight[:, pl.ds(pl.multiple_of(y * 512 + x * 256, 256), 256)]
    away[...] = weight[:, pl.ds(pl.multiple_of(y * 512 + 256 - x * 256, 256), 256)]


def pack_messages(where, tokens, key, query, after, m1, m2, m3, own):
    y, x = where[0], where[1]
    for p, out in enumerate((own, m1, m2, m3)):
        row = 1 - y if p // 2 else y
        column = 1 - x if p % 2 else x
        lanes = pl.ds(pl.multiple_of(row * 512 + column * 256, 256), 256)
        if p:
            out[:, pl.ds(0, 1024)] = tokens[...]
        base = 1024 if p else 0
        out[:, pl.ds(base, 256)] = key[:, lanes]
        out[:, pl.ds(base + 256, 256)] = query[:, lanes]


def pack_filter(where, filt, after, own, away):
    y, x, z = where[0], where[1], where[2]
    low = low_lanes((128, 128))
    for k, out in enumerate((own, away)):
        column = 1 - x if k else x
        for j in range(2):
            base = pl.multiple_of(y * 512 + column * 256 + j * 128, 128)
            for part in range(2):
                even = filt[part, 0, :, pl.ds(base, 128)].astype(F32)
                odd = filt[part, 1, :, pl.ds(base, 128)].astype(F32)
                one, two = both(even, odd, low)
                out[lax.rem(2 * j - z + 4, 4), part] = one
                out[lax.rem(2 * j + 1 - z + 4, 4), part] = two


def value_kernel(where, *refs):
    mine, other, gates, pieces = refs[:4], refs[4:8], refs[8], refs[9:17]
    drive, outs = refs[17], refs[18:22]
    acc, packed = refs[22], refs[23]
    x, z, c = where[1], where[2], where[3]
    acc[...] = jnp.zeros_like(acc)

    def gather(blocks, lanes):
        return jnp.concatenate([b[:, lanes] for b in blocks], axis=0)

    for r in range(4):
        owner = lax.rem(z - r + 4, 4)
        for k in range(2):
            row = 1 - x if k else x
            lanes = pl.ds(pl.multiple_of(lax.rem(owner, 2) * 512 + row * 256, 256), 256)
            piece = pieces[2 * r + k]

            @pl.when(owner // 2 == c)
            def _():
                acc[...] += dot(gather(mine, lanes), piece[...])

            @pl.when(owner // 2 != c)
            def _():
                acc[...] += dot(gather(other, lanes), piece[...])

    for p in range(4):
        rows = pl.ds(p * 128, 128)
        gate = mine[p][:, 1024:1280] if p else gates[:, 0:256]
        value = acc[rows, :].astype(BF16).astype(F32)
        drive[rows, :] = (gate.astype(F32) * value).astype(BF16)
    low = low_lanes((256, 128))
    for j in range(2):
        lanes = pl.ds(j * 128, 128)
        first = drive[pl.ds(0, 256), lanes].astype(F32)
        second = drive[pl.ds(256, 256), lanes].astype(F32)
        packed[2 * j], packed[2 * j + 1] = both(first, second, low)
    for r in range(4):
        outs[r][...] = packed[lax.rem(z + r, 4)]


def add(a, b):
    return b if a is None else a if b is None else a + b


def sub(a, b):
    return a if b is None else -b if a is None else a - b


def scaled(a, s):
    if a is None or abs(s) < 1e-9:
        return None
    if abs(s - 1) < 1e-9:
        return a
    if abs(s + 1) < 1e-9:
        return -a
    return a * np.float32(s)


def cmul(a, angle):
    co, si = math.cos(angle), math.sin(angle)
    return (sub(scaled(a[0], co), scaled(a[1], si)), add(scaled(a[0], si), scaled(a[1], co)))


def cadd(a, b):
    return (add(a[0], b[0]), add(a[1], b[1]))


def conj(a):
    return (a[0], None if a[1] is None else -a[1])


def short_transform(values, count, rows):
    if len(values) == 1:
        return [(values[0], None)] * rows
    half = count // 2
    need = half // 2 + 1
    even = short_transform(values[0::2], half, need)
    odd = short_transform(values[1::2], half, need)

    def at(t, k):
        k %= half
        return t[k] if k < need else conj(t[half - k])

    return [cadd(at(even, k), cmul(at(odd, k), -2 * math.pi * k / count)) for k in range(rows)]


def conv_kernel(where, *refs):
    drives, filters, (table, table_t) = refs[:4], refs[4:8], refs[8:10]
    outs, (data, filt, first, sums) = refs[10:14], refs[14:]
    x, z = where[1], where[2]
    for r, block in enumerate(drives):
        base = 2 * lax.rem(z - r + 4, 4)
        filt[base + x] = filters[r][0]
        filt[base + 1 - x] = filters[r][1]
        data[base + x] = block[pl.ds(0, 128), :]
        data[base + 1 - x] = block[pl.ds(128, 128), :]
    for i in range(8):
        rows = pl.ds(16 * i, 16)
        values = [data[a, rows, :].astype(F32) for a in range(8)]
        spectrum = short_transform(values, 16, 9)
        for k in range(9):
            re, im = spectrum[k]
            if im is None:
                im = jnp.zeros_like(re)
            first[k, rows, 0:128] = re.astype(BF16)
            first[k, rows, 128:256] = im.astype(BF16)
            if 0 < k < 8:
                first[16 - k, rows, 0:128] = re.astype(BF16)
                first[16 - k, rows, 128:256] = (-im).astype(BF16)
    low = low_lanes((128, 128))

    def back(k):
        four = dot(table[k], first[k])
        re = four[:128, :128] + four[128:, 128:]
        im = four[:128, 128:] - four[128:, :128]
        pair = [filt[k // 2, part].astype(F32) for part in range(2)]
        if k % 2 == 0:
            fr, fi = [jnp.where(low, f, half_turn(f)) for f in pair]
        else:
            fr, fi = [jnp.where(low, half_turn(f), f) for f in pair]
        product = jnp.concatenate([re * fr - im * fi, re * fi + im * fr], axis=1).astype(BF16)
        four = dot(table_t[k], product)
        return four[:128, :128] - four[128:, 128:], four[128:, :128] + four[:128, 128:]

    sums[0, pl.ds(0, 128)] = back(0)[0]
    sums[8, pl.ds(0, 128)] = back(8)[0]
    for k in range(1, 8):
        one, two = back(k), back(16 - k)
        sums[k, pl.ds(0, 128)] = one[0] + two[0]
        sums[k, pl.ds(128, 128)] = one[1] - two[1]
    for i in range(16):
        rows, below = pl.ds(8 * i, 8), pl.ds(128 + 8 * i, 8)
        scale = 1.0 / 2048
        re = [sums[k, rows, :] * scale for k in range(9)]
        im = [None] + [sums[k, below, :] * scale for k in range(1, 8)] + [None]
        for a in range(5):
            groups = [None] * 4
            for k in range(9):
                ang = 2 * math.pi * (k * a % 16) / 16
                groups[k % 2] = add(groups[k % 2], scaled(re[k], math.cos(ang)))
                groups[2 + k % 2] = sub(groups[2 + k % 2], scaled(im[k], math.sin(ang)))
            ec, oc, es, os = groups
            data[a, rows, :] = add(add(ec, oc), add(es, os)).astype(BF16)
            if 0 < a < 4:
                data[8 - a, rows, :] = sub(sub(add(ec, os), oc), es).astype(BF16)
    for r, out in enumerate(outs):
        base = 2 * lax.rem(z + r, 4)
        out[pl.ds(0, 128), :] = data[base + x]
        out[pl.ds(128, 128), :] = data[base + 1 - x]


def gate_kernel(where, e0, e1, e2, e3, drive, skip, gates, g1, g2, g3, gated, conv):
    z = where[2]
    for r, block in enumerate((e0, e1, e2, e3)):
        conv[lax.rem(z - r + 4, 4)] = block[...]
    low = low_lanes((256, 128))
    for j in range(2):
        lanes = pl.ds(j * 128, 128)
        even, odd = conv[2 * j].astype(F32), conv[2 * j + 1].astype(F32)
        parts = (jnp.where(low, even, half_turn(odd)), jnp.where(low, half_turn(even), odd))
        for p, gate in enumerate((gates, g1, g2, g3)):
            rows = pl.ds(p * 128, 128)
            own = parts[p // 2][(p % 2) * 128 : (p % 2) * 128 + 128]
            direct = skip[:, lanes] * drive[rows, lanes].astype(F32)
            query = gate[:, pl.ds((1280 if p else 256) + j * 128, 128)].astype(F32)
            gated[rows, lanes] = (query * (own + direct)).astype(BF16)


def sort_weight(where, *refs):
    pieces, keep, give = refs[:4], refs[4], refs[5]
    x, z, c = where[1], where[2], where[3]
    for r in range(4):
        owner = lax.rem(z - r + 4, 4)
        for k in range(2):
            to = 2 * lax.rem(owner, 2) + (1 - x if k else x)

            @pl.when(owner // 2 == c)
            def _():
                keep[to] = pieces[r][k]

            @pl.when(owner // 2 != c)
            def _():
                give[to] = pieces[r][k]


def out_kernel(gated, other, keep, theirs, own, *sends):
    for p in (3, 2, 1, 0):
        rows = pl.ds(p * 128, 128)
        for i in range(4):
            total = dot_t(gated[rows, :], keep[i]) + dot_t(other[rows, :], theirs[i])
            lanes = pl.ds(i * 256, 256)
            if p == 0:
                own[:, lanes] = total
            else:
                sends[p - 1][:, lanes] = total.astype(BF16)


def tables():
    k = np.arange(16)[:, None, None] + 16 * np.arange(128)[None, :, None]
    phase = 2 * np.pi / 2048 * (k * np.arange(128)[None, None, :] % 2048)
    co, si = np.cos(phase), np.sin(phase)
    back = np.concatenate([co.transpose(0, 2, 1), si.transpose(0, 2, 1)], 1)
    return np.concatenate([co, si], 1).astype(jnp.bfloat16), back.astype(jnp.bfloat16)


def planes(tokens, gate_q, gate_k, w_value, skip, filter_spectrum, w_out):
    y, s, c = (lax.axis_index(a) for a in AXES)
    x, z = s % 2, s // 2
    seq, deep = 8, 4
    where = jnp.stack([y, x, z, c]).astype(jnp.int32)

    def permute(values, move):
        pairs = []
        for g in range(2):
            for i in range(seq):
                for k in range(2):
                    g2, z2, x2, k2 = move(g, i // 2, i % 2, k)
                    pairs.append(((g * seq + i) * 2 + k, (g2 * seq + z2 * 2 + x2) * 2 + k2))
        return lax.ppermute(values, AXES, pairs)

    def to_x(values):
        return permute(values, lambda g, z, x, k: (g, z, 1 - x, k))

    def to_core(values):
        return permute(values, lambda g, z, x, k: (g, z, x, 1 - k))

    def to_z(values, r):
        return permute(values, lambda g, z, x, k: (g, (z + r) % deep, x, k))

    def to_peer(values, p):
        return permute(values, lambda g, z, x, k: (g ^ (p // 2), z, x ^ (p % 2), k))

    def after(values, *done):
        return lax.optimization_barrier((values,) + done)[0]

    shape = jax.ShapeDtypeStruct
    block, square = shape((256, 128), BF16), shape((256, 256), BF16)
    message = shape((128, 1536), BF16)
    split = in_vmem(pack_weight, [square] * 2, moved=1 << 20)
    own_first, away = split(where, w_value)
    ring = [own_first, to_x(away)]
    *messages, gates = in_vmem(
        pack_messages, [message] * 3 + [shape((128, 512), BF16)], moved=2 << 20
    )(where, tokens, gate_k, gate_q, own_first[:16, :128])
    received = [to_peer(messages[p - 1], p) for p in (1, 2, 3)]
    by_plane = shape((4, 2, 128, 128), BF16)
    packed, away = in_vmem(pack_filter, [by_plane] * 2, moved=1 << 20)(
        where, filter_spectrum, messages[0][:16, :128]
    )
    got = to_x(away)
    filters = [jnp.stack([packed[r], got[r]]) for r in range(4)]
    filters = filters[:1] + [to_z(filters[r], r) for r in (1, 2, 3)]
    mine = [tokens] + received
    other = [to_core(m) for m in mine]
    ring += [to_z(ring[0], 1), to_z(ring[1], 1)]
    ring += [to_z(ring[2], 1), to_z(ring[3], 1)]
    ring += [to_z(after(ring[4], *received), 1), to_z(ring[5], 1)]
    own_out, away = split(where, after(w_out, messages[0]))
    pair = jnp.stack([own_out, to_x(after(away, got))])
    gates = after(gates, *filters)
    drive, *sends = in_vmem(
        value_kernel,
        [shape((512, 256), BF16)] + [block] * 4,
        [pltpu.VMEM((512, 256), F32), pltpu.VMEM((4, 256, 128), BF16)],
        flops=1 << 29,
        moved=4 << 20,
    )(where, *mine, *other, gates, *ring)
    columns = [sends[0]] + [to_z(sends[r], r) for r in (1, 2, 3)]
    table, table_t = tables()
    sends = in_vmem(
        conv_kernel,
        [block] * 4,
        [
            pltpu.VMEM((8, 128, 128), BF16),
            pltpu.VMEM((8, 2, 128, 128), BF16),
            pltpu.VMEM((16, 128, 256), BF16),
            pltpu.VMEM((9, 256, 128), F32),
        ],
        flops=1 << 30,
        moved=5 << 20,
    )(where, *columns, *filters, table, table_t)
    rows = [sends[0]] + [to_z(sends[r], r) for r in (1, 2, 3)]

    hops = [after(pair, ring[6], ring[7])]
    hops.append(to_z(hops[0], 1))
    hops.append(to_z(after(hops[1], drive), 1))
    hops.append(to_z(after(hops[2], sends[0]), 1))
    quad = shape((4, 256, 256), BF16)
    keep, give = in_vmem(sort_weight, [quad] * 2, moved=2 << 20)(where, *hops)
    theirs = to_core(give)
    channels = lax.dynamic_slice_in_dim(skip, (y * 2 + x) * 256, 256)[None, :]
    gated = in_vmem(
        gate_kernel, shape((512, 256), BF16), [pltpu.VMEM((4, 256, 128), BF16)], moved=1 << 20
    )(where, *rows, drive, channels, gates, *received)
    gated_other = to_core(gated)
    own, *sends = in_vmem(
        out_kernel,
        [shape((128, 1024), F32)] + [shape((128, 1024), BF16)] * 3,
        smem=0,
        flops=1 << 30,
        moved=4 << 20,
    )(gated, gated_other, keep, theirs)
    total = own
    for p in (3, 2, 1):
        total = total + to_peer(sends[p - 1], p).astype(F32)
    return total.astype(BF16)


def shards(tokens, gate_q, gate_k, w_value, skip, filter_spectrum, w_out):
    seq_count = lax.axis_size("seq")
    position = lax.axis_index("seq")
    length_b = tokens.shape[0]
    columns_each = length_b // seq_count
    freq_rows = 2 * seq_count
    freqs_each = freq_rows // seq_count
    fft_length = freq_rows * length_b
    features = lax.all_gather(tokens, "ch", axis=1, tiled=True)
    value_weight, out_weight = (
        lax.all_gather(w_value, "seq", axis=0, tiled=True),
        lax.all_gather(w_out, "seq", axis=0, tiled=True),
    )
    value = jnp.dot(features, value_weight, preferred_element_type=jnp.float32)
    value = value.astype(jnp.bfloat16)
    drive = (gate_k.astype(jnp.float32) * widened(value)).astype(jnp.bfloat16)
    channels = drive.shape[1]
    columns = lax.all_to_all(drive[None], "seq", split_axis=1, concat_axis=0, tiled=True)
    index_rows = jnp.arange(freq_rows, dtype=jnp.int32)
    index_seq = jnp.arange(seq_count, dtype=jnp.int32)
    index_b = jnp.arange(length_b, dtype=jnp.int32)
    cos_first, sin_first = angles(freq_rows, index_rows, index_seq)
    cos_first = cos_first.astype(jnp.bfloat16)
    sin_first = sin_first.astype(jnp.bfloat16)
    flattened = columns.reshape(seq_count, columns_each * channels)
    real_part = jnp.dot(cos_first, flattened, preferred_element_type=jnp.float32)
    imag_part = jnp.dot(-sin_first, flattened, preferred_element_type=jnp.float32)
    real_part = real_part.reshape(freq_rows, columns_each, channels)
    imag_part = imag_part.reshape(freq_rows, columns_each, channels)
    mine_b = position * columns_each + jnp.arange(columns_each, dtype=jnp.int32)
    twist_cos, twist_sin = angles(fft_length, index_rows, mine_b)
    twist_cos = twist_cos[:, :, None]
    twist_sin = twist_sin[:, :, None]
    section = jnp.stack(
        [
            real_part * twist_cos + imag_part * twist_sin,
            imag_part * twist_cos - real_part * twist_sin,
        ]
    ).astype(jnp.bfloat16)
    spectral = lax.all_to_all(section, "seq", split_axis=1, concat_axis=2, tiled=True)
    cos_seq, sin_seq = angles(length_b, index_b, index_b)
    cos_seq = cos_seq.astype(jnp.bfloat16)
    sin_seq = sin_seq.astype(jnp.bfloat16)
    spectrum_real = jnp.einsum(
        "qb,kbc->kqc", cos_seq, spectral[0], preferred_element_type=jnp.float32
    ) + jnp.einsum("qb,kbc->kqc", sin_seq, spectral[1], preferred_element_type=jnp.float32)
    spectrum_imag = jnp.einsum(
        "qb,kbc->kqc", cos_seq, spectral[1], preferred_element_type=jnp.float32
    ) - jnp.einsum("qb,kbc->kqc", sin_seq, spectral[0], preferred_element_type=jnp.float32)
    filter_real = filter_spectrum[0].astype(jnp.float32)
    filter_imag = filter_spectrum[1].astype(jnp.float32)
    product = jnp.stack(
        [
            spectrum_real * filter_real - spectrum_imag * filter_imag,
            spectrum_real * filter_imag + spectrum_imag * filter_real,
        ]
    ).astype(jnp.bfloat16)
    inverse_real = jnp.einsum(
        "qb,kqc->kbc", cos_seq, product[0], preferred_element_type=jnp.float32
    ) - jnp.einsum("qb,kqc->kbc", sin_seq, product[1], preferred_element_type=jnp.float32)
    inverse_imag = jnp.einsum(
        "qb,kqc->kbc", sin_seq, product[0], preferred_element_type=jnp.float32
    ) + jnp.einsum("qb,kqc->kbc", cos_seq, product[1], preferred_element_type=jnp.float32)
    mine_k = position * freqs_each + jnp.arange(freqs_each, dtype=jnp.int32)
    back_cos, back_sin = angles(fft_length, mine_k, index_b)
    back_cos = back_cos[:, :, None]
    back_sin = back_sin[:, :, None]
    back = jnp.stack(
        [
            inverse_real * back_cos - inverse_imag * back_sin,
            inverse_real * back_sin + inverse_imag * back_cos,
        ]
    ).astype(jnp.bfloat16)
    returned = lax.all_to_all(back, "seq", split_axis=2, concat_axis=1, tiled=True)
    flat_real = returned[0].reshape(freq_rows, columns_each * channels)
    flat_imag = returned[1].reshape(freq_rows, columns_each * channels)
    conv = jnp.dot(cos_first.T, flat_real, preferred_element_type=jnp.float32) - jnp.dot(
        sin_first.T, flat_imag, preferred_element_type=jnp.float32
    )
    conv = (
        (conv * (1.0 / fft_length)).reshape(seq_count, columns_each, channels).astype(jnp.bfloat16)
    )
    conv_rows = lax.all_to_all(conv, "seq", split_axis=0, concat_axis=1, tiled=True)[0]
    gated = (
        gate_q.astype(jnp.float32) * (widened(conv_rows) + skip[None, :] * widened(drive))
    ).astype(jnp.bfloat16)
    partial_value = lax.dot_general(
        gated, out_weight, (((1,), (1,)), ((), ())), preferred_element_type=jnp.float32
    )
    return lax.psum_scatter(
        partial_value.astype(jnp.bfloat16), "ch", scatter_dimension=1, tiled=True
    )


def solution(mesh):
    placed = (
        P(("grp", "seq"), "ch"),
        P(("grp", "seq"), "ch"),
        P(("grp", "seq"), "ch"),
        P("seq", "ch"),
        P("ch"),
        P(None, "seq", None, "ch"),
        P("seq", "ch"),
    )
    sizes = mesh.shape
    body = planes if (sizes["grp"], sizes["seq"], sizes["ch"]) == (2, 8, 2) else shards
    return jax.shard_map(
        body, mesh=mesh, in_specs=placed, out_specs=P(("grp", "seq"), "ch"), check_vma=False
    )
```

```python
import functools
import math

import jax
import jax.numpy as jnp
import numpy as np
from jax import lax
from jax.experimental import pallas as pl
from jax.experimental.pallas import tpu as pltpu
from jax.sharding import PartitionSpec as P

AXES = ("grp", "seq", "ch")
BF16 = jnp.bfloat16
F32 = jnp.float32


def angles(count, first, second):
    phase = 2.0 * math.pi / count * (first[:, None] * second[None, :] % count).astype(jnp.float32)
    return (jnp.cos(phase), jnp.sin(phase))


def widened(values):
    return lax.optimization_barrier(values).astype(jnp.float32)


def dot(a, b):
    return jnp.dot(a, b, preferred_element_type=F32)


def dot_t(a, b):
    return lax.dot_general(a, b, (((1,), (1,)), ((), ())), preferred_element_type=F32)


def in_vmem(kernel, out_shape, scratch=(), smem=1, flops=0, moved=0):
    def call(*operands):
        specs = [pl.BlockSpec(memory_space=pltpu.SMEM)] * smem
        specs += [pl.BlockSpec(memory_space=pltpu.VMEM)] * (len(operands) - smem)
        return pl.pallas_call(
            kernel,
            out_shape=out_shape,
            in_specs=specs,
            out_specs=jax.tree.map(lambda _: pl.BlockSpec(memory_space=pltpu.VMEM), out_shape),
            scratch_shapes=list(scratch),
            compiler_params=pltpu.CompilerParams(vmem_limit_bytes=48 * 1024 * 1024),
            cost_estimate=pl.CostEstimate(flops=flops, bytes_accessed=moved, transcendentals=0),
        )(*operands)

    return call


def low_lanes(shape):
    return lax.broadcasted_iota(jnp.int32, shape, len(shape) - 1) < 64


def half_turn(values):
    return pltpu.roll(values, 64, values.ndim - 1)


def both(first, second, low):
    return (
        jnp.where(low, first, half_turn(second)).astype(BF16),
        jnp.where(low, half_turn(first), second).astype(BF16),
    )


def prologue(where, tokens, key, query, value, out, filt, *refs):
    own_v, away_v, own_o, away_o, to_x, to_y, own, away_f, sem = refs
    y, x = where[0], where[1]

    def lanes(p):
        row = 1 - y if p // 2 else y
        column = 1 - x if p % 2 else x
        return pl.ds(pl.multiple_of(row * 512 + column * 256, 256), 256)

    moves = [(value.at[:, lanes(0)], own_v), (value.at[:, lanes(1)], away_v)]
    moves += [(out.at[:, lanes(0)], own_o), (out.at[:, lanes(1)], away_o)]
    moves.append((filt.at[:, :, :, lanes(1)], away_f))
    moves += [(tokens, m.at[:, pl.ds(512, 1024)]) for m in (to_x, to_y)]
    for p, target, base in ((0, own, 0), (1, to_x, 0), (2, to_y, 0), (3, to_x, 1536)):
        moves.append((key.at[:, lanes(p)], target.at[:, pl.ds(base, 256)]))
        moves.append((query.at[:, lanes(p)], target.at[:, pl.ds(base + 256, 256)]))
    copies = [pltpu.make_async_copy(a, b, sem.at[i]) for i, (a, b) in enumerate(moves)]
    for copy in copies:
        copy.start()
    for copy in copies:
        copy.wait()


def pack_filter(where, filt, near, *outs):
    y, x, z = where[0], where[1], where[2]
    packed, outs = outs[4], outs[:4]
    low = low_lanes((128, 128))
    for k in range(2):
        for j in range(2):
            base = pl.multiple_of(y * 512 + x * 256 + j * 128, 128)
            for part in range(2):
                if k:
                    pair = [near[part, i, :, pl.ds(j * 128, 128)].astype(F32) for i in range(2)]
                else:
                    pair = [filt[part, i, :, pl.ds(base, 128)].astype(F32) for i in range(2)]
                one, two = both(*pair, low)
                packed[2 * j, k, part] = one
                packed[2 * j + 1, k, part] = two
    for r in range(4):
        outs[r][...] = packed[lax.rem(z + r, 4)]


def value_kernel(where, *refs):
    mine, other, gates, pieces = refs[:4], refs[4:8], refs[8], refs[9:17]
    drive, outs = refs[17], refs[18:22]
    acc, packed = refs[22], refs[23]
    x, z, c = where[1], where[2], where[3]
    acc[...] = jnp.zeros_like(acc)

    def gather(blocks, base):
        lanes = [pl.ds(pl.multiple_of(base + (512 if p else 0), 256), 256) for p in range(4)]
        return jnp.concatenate([b[:, at] for b, at in zip(blocks, lanes)], axis=0)

    for r in range(4):
        owner = lax.rem(z - r + 4, 4)
        for k in range(2):
            row = 1 - x if k else x
            base = lax.rem(owner, 2) * 512 + row * 256
            piece = pieces[2 * r + k]

            @pl.when(owner // 2 == c)
            def _():
                acc[...] += dot(gather(mine, base), piece[...])

            @pl.when(owner // 2 != c)
            def _():
                acc[...] += dot(gather(other, base), piece[...])

    for p in range(4):
        rows = pl.ds(p * 128, 128)
        gate = mine[p][:, 1536:1792] if p == 3 else (mine[p] if p else gates)[:, 0:256]
        value = acc[rows, :].astype(BF16).astype(F32)
        drive[rows, :] = (gate.astype(F32) * value).astype(BF16)
    low = low_lanes((256, 128))
    for j in range(2):
        lanes = pl.ds(j * 128, 128)
        first = drive[pl.ds(0, 256), lanes].astype(F32)
        second = drive[pl.ds(256, 256), lanes].astype(F32)
        packed[2 * j], packed[2 * j + 1] = both(first, second, low)
    for r in range(4):
        outs[r][...] = packed[lax.rem(z + r, 4)]


def add(a, b):
    return b if a is None else a if b is None else a + b


def sub(a, b):
    return a if b is None else -b if a is None else a - b


def scaled(a, s):
    if a is None or abs(s) < 1e-9:
        return None
    if abs(s - 1) < 1e-9:
        return a
    if abs(s + 1) < 1e-9:
        return -a
    return a * np.float32(s)


def cmul(a, angle):
    co, si = math.cos(angle), math.sin(angle)
    return (sub(scaled(a[0], co), scaled(a[1], si)), add(scaled(a[0], si), scaled(a[1], co)))


def cadd(a, b):
    return (add(a[0], b[0]), add(a[1], b[1]))


def conj(a):
    return (a[0], None if a[1] is None else -a[1])


def short_transform(values, count, rows):
    if len(values) == 1:
        return [(values[0], None)] * rows
    half = count // 2
    need = half // 2 + 1
    even = short_transform(values[0::2], half, need)
    odd = short_transform(values[1::2], half, need)

    def at(t, k):
        k %= half
        return t[k] if k < need else conj(t[half - k])

    return [cadd(at(even, k), cmul(at(odd, k), -2 * math.pi * k / count)) for k in range(rows)]


def conv_kernel(where, *refs):
    drives, filters, (table, table_t) = refs[:4], refs[4:8], refs[8:10]
    outs, (data, filt, first, sums) = refs[10:14], refs[14:]
    x, z = where[1], where[2]
    for r, block in enumerate(drives):
        base = 2 * lax.rem(z - r + 4, 4)
        filt[base + x] = filters[r][0]
        filt[base + 1 - x] = filters[r][1]
        data[base + x] = block[pl.ds(0, 128), :]
        data[base + 1 - x] = block[pl.ds(128, 128), :]
    for i in range(8):
        rows = pl.ds(16 * i, 16)
        values = [data[a, rows, :].astype(F32) for a in range(8)]
        spectrum = short_transform(values, 16, 9)
        for k in range(9):
            re, im = spectrum[k]
            if im is None:
                im = jnp.zeros_like(re)
            first[k, rows, 0:128] = re.astype(BF16)
            first[k, rows, 128:256] = im.astype(BF16)
            if 0 < k < 8:
                first[16 - k, rows, 0:128] = re.astype(BF16)
                first[16 - k, rows, 128:256] = (-im).astype(BF16)
    low = low_lanes((128, 128))

    def back(k):
        four = dot(table[k], first[k])
        re = four[:128, :128] + four[128:, 128:]
        im = four[:128, 128:] - four[128:, :128]
        pair = [filt[k // 2, part].astype(F32) for part in range(2)]
        if k % 2 == 0:
            fr, fi = [jnp.where(low, f, half_turn(f)) for f in pair]
        else:
            fr, fi = [jnp.where(low, half_turn(f), f) for f in pair]
        product = jnp.concatenate([re * fr - im * fi, re * fi + im * fr], axis=1).astype(BF16)
        four = dot(table_t[k], product)
        return four[:128, :128] - four[128:, 128:], four[128:, :128] + four[:128, 128:]

    sums[0, pl.ds(0, 128)] = back(0)[0]
    sums[8, pl.ds(0, 128)] = back(8)[0]
    for k in range(1, 8):
        one, two = back(k), back(16 - k)
        sums[k, pl.ds(0, 128)] = one[0] + two[0]
        sums[k, pl.ds(128, 128)] = one[1] - two[1]
    for i in range(16):
        rows, below = pl.ds(8 * i, 8), pl.ds(128 + 8 * i, 8)
        scale = 1.0 / 2048
        re = [sums[k, rows, :] * scale for k in range(9)]
        im = [None] + [sums[k, below, :] * scale for k in range(1, 8)] + [None]
        for a in range(5):
            groups = [None] * 4
            for k in range(9):
                ang = 2 * math.pi * (k * a % 16) / 16
                groups[k % 2] = add(groups[k % 2], scaled(re[k], math.cos(ang)))
                groups[2 + k % 2] = sub(groups[2 + k % 2], scaled(im[k], math.sin(ang)))
            ec, oc, es, os = groups
            data[a, rows, :] = add(add(ec, oc), add(es, os)).astype(BF16)
            if 0 < a < 4:
                data[8 - a, rows, :] = sub(sub(add(ec, os), oc), es).astype(BF16)
    for r, out in enumerate(outs):
        base = 2 * lax.rem(z + r, 4)
        out[pl.ds(0, 128), :] = data[base + x]
        out[pl.ds(128, 128), :] = data[base + 1 - x]


def gate_kernel(where, e0, e1, e2, e3, drive, skip, gates, g1, g2, g3, gated, conv):
    z = where[2]
    for r, block in enumerate((e0, e1, e2, e3)):
        conv[lax.rem(z - r + 4, 4)] = block[...]
    low = low_lanes((256, 128))
    for j in range(2):
        lanes = pl.ds(j * 128, 128)
        even, odd = conv[2 * j].astype(F32), conv[2 * j + 1].astype(F32)
        parts = (jnp.where(low, even, half_turn(odd)), jnp.where(low, half_turn(even), odd))
        for p, gate in enumerate((gates, g1, g2, g3)):
            rows = pl.ds(p * 128, 128)
            own = parts[p // 2][(p % 2) * 128 : (p % 2) * 128 + 128]
            direct = skip[:, lanes] * drive[rows, lanes].astype(F32)
            query = gate[:, pl.ds((1792 if p == 3 else 256) + j * 128, 128)].astype(F32)
            gated[rows, lanes] = (query * (own + direct)).astype(BF16)


def sort_weight(where, *refs):
    pieces, keep, give = refs[:4], refs[4], refs[5]
    x, z, c = where[1], where[2], where[3]
    for r in range(4):
        owner = lax.rem(z - r + 4, 4)
        for k in range(2):
            to = 2 * lax.rem(owner, 2) + (1 - x if k else x)

            @pl.when(owner // 2 == c)
            def _():
                keep[to] = pieces[r][k]

            @pl.when(owner // 2 != c)
            def _():
                give[to] = pieces[r][k]


def out_kernel(gated, other, keep, theirs, own, *sends):
    for p in (3, 2, 1, 0):
        rows = pl.ds(p * 128, 128)
        for i in range(4):
            total = dot_t(gated[rows, :], keep[i]) + dot_t(other[rows, :], theirs[i])
            lanes = pl.ds(i * 256, 256)
            if p == 0:
                own[:, lanes] = total
            else:
                sends[p - 1][:, lanes] = total.astype(BF16)


def tables():
    k = np.arange(16)[:, None, None] + 16 * np.arange(128)[None, :, None]
    phase = 2 * np.pi / 2048 * (k * np.arange(128)[None, None, :] % 2048)
    co, si = np.cos(phase), np.sin(phase)
    back = np.concatenate([co.transpose(0, 2, 1), si.transpose(0, 2, 1)], 1)
    return np.concatenate([co, si], 1).astype(jnp.bfloat16), back.astype(jnp.bfloat16)


def planes(tokens, gate_q, gate_k, w_value, skip, filter_spectrum, w_out):
    y, s, c = (lax.axis_index(a) for a in AXES)
    x, z = s % 2, s // 2
    seq, deep = 8, 4
    where = jnp.stack([y, x, z, c]).astype(jnp.int32)

    def permute(values, move):
        pairs = []
        for g in range(2):
            for i in range(seq):
                for k in range(2):
                    g2, z2, x2, k2 = move(g, i // 2, i % 2, k)
                    pairs.append(((g * seq + i) * 2 + k, (g2 * seq + z2 * 2 + x2) * 2 + k2))
        return lax.ppermute(values, AXES, pairs)

    def to_x(values):
        return permute(values, lambda g, z, x, k: (g, z, 1 - x, k))

    def to_core(values):
        return permute(values, lambda g, z, x, k: (g, z, x, 1 - k))

    def to_z(values, r):
        return permute(values, lambda g, z, x, k: (g, (z + r) % deep, x, k))

    def to_peer(values, p):
        return permute(values, lambda g, z, x, k: (g ^ (p // 2), z, x ^ (p % 2), k))

    def after(values, *done):
        return lax.optimization_barrier((values,) + done)[0]

    shape = jax.ShapeDtypeStruct
    block, square = shape((256, 128), BF16), shape((256, 256), BF16)
    inside = pl.BlockSpec(memory_space=pltpu.MemorySpace.HBM)
    laid = [square] * 4 + [shape((128, w), BF16) for w in (2048, 1536, 512)]
    laid.append(shape((2, 2, 128, 256), BF16))
    own_v, away_v, own_o, away_o, message_x, message_y, gates, away_f = pl.pallas_call(
        prologue,
        out_shape=laid,
        in_specs=[pl.BlockSpec(memory_space=pltpu.SMEM)] + [inside] * 6,
        out_specs=[inside] * 8,
        scratch_shapes=[pltpu.SemaphoreType.DMA((15,))],
        compiler_params=pltpu.CompilerParams(vmem_limit_bytes=62 * 1024 * 1024),
    )(where, tokens, gate_k, gate_q, w_value, w_out, filter_spectrum)
    ring = [own_v, to_x(away_v)]
    from_x = to_peer(message_x, 1)
    from_y = to_peer(message_y, 2)
    ring += [to_z(ring[0], 1), to_z(ring[1], 1)]
    received = [from_x, from_y, to_peer(after(from_x, from_y, ring[2]), 2)]
    got = to_x(away_f)
    filters = in_vmem(
        pack_filter,
        [shape((2, 2, 128, 128), BF16)] * 4,
        [pltpu.VMEM((4, 2, 2, 128, 128), BF16)],
        moved=1 << 20,
    )(where, filter_spectrum, got)
    filters = [filters[0]] + [to_z(filters[r], r) for r in (1, 2, 3)]
    mine = [tokens] + received
    other = [to_core(m) for m in mine]
    ring += [to_z(ring[2], 1), to_z(ring[3], 1)]
    ring += [to_z(ring[4], 1), to_z(ring[5], 1)]
    pair = jnp.stack([own_o, to_x(after(away_o, got))])
    hops = [after(pair, ring[4], ring[5])]
    hops.append(to_z(hops[0], 1))
    hops.append(to_z(after(hops[1], ring[6], ring[7]), 1))
    gates = after(gates, *filters)
    drive, *sends = in_vmem(
        value_kernel,
        [shape((512, 256), BF16)] + [block] * 4,
        [pltpu.VMEM((512, 256), F32), pltpu.VMEM((4, 256, 128), BF16)],
        flops=1 << 29,
        moved=4 << 20,
    )(where, *mine, *other, gates, *ring)
    columns = [sends[0]] + [to_z(sends[r], r) for r in (1, 2, 3)]
    table, table_t = tables()
    sends = in_vmem(
        conv_kernel,
        [block] * 4,
        [
            pltpu.VMEM((8, 128, 128), BF16),
            pltpu.VMEM((8, 2, 128, 128), BF16),
            pltpu.VMEM((16, 128, 256), BF16),
            pltpu.VMEM((9, 256, 128), F32),
        ],
        flops=1 << 30,
        moved=5 << 20,
    )(where, *columns, *filters, table, table_t)
    rows = [sends[0]] + [to_z(sends[r], r) for r in (1, 2, 3)]

    hops.append(to_z(after(hops[2], sends[0]), 1))
    hops[3] = after(hops[3], *rows[1:])
    quad = shape((4, 256, 256), BF16)
    keep, give = in_vmem(sort_weight, [quad] * 2, moved=2 << 20)(where, *hops)
    theirs = to_core(give)
    channels = lax.dynamic_slice_in_dim(skip, (y * 2 + x) * 256, 256)[None, :]
    gated = in_vmem(
        gate_kernel, shape((512, 256), BF16), [pltpu.VMEM((4, 256, 128), BF16)], moved=1 << 20
    )(where, *rows, drive, channels, gates, *received)
    gated_other = to_core(gated)
    own, *sends = in_vmem(
        out_kernel,
        [shape((128, 1024), F32)] + [shape((128, 1024), BF16)] * 3,
        smem=0,
        flops=1 << 30,
        moved=4 << 20,
    )(gated, gated_other, keep, theirs)
    total = own
    for p in (3, 2, 1):
        total = total + to_peer(sends[p - 1], p).astype(F32)
    return total.astype(BF16)


def shards(tokens, gate_q, gate_k, w_value, skip, filter_spectrum, w_out):
    seq_count = lax.axis_size("seq")
    position = lax.axis_index("seq")
    length_b = tokens.shape[0]
    columns_each = length_b // seq_count
    freq_rows = 2 * seq_count
    freqs_each = freq_rows // seq_count
    fft_length = freq_rows * length_b
    features = lax.all_gather(tokens, "ch", axis=1, tiled=True)
    value_weight, out_weight = (
        lax.all_gather(w_value, "seq", axis=0, tiled=True),
        lax.all_gather(w_out, "seq", axis=0, tiled=True),
    )
    value = jnp.dot(features, value_weight, preferred_element_type=jnp.float32)
    value = value.astype(jnp.bfloat16)
    drive = (gate_k.astype(jnp.float32) * widened(value)).astype(jnp.bfloat16)
    channels = drive.shape[1]
    columns = lax.all_to_all(drive[None], "seq", split_axis=1, concat_axis=0, tiled=True)
    index_rows = jnp.arange(freq_rows, dtype=jnp.int32)
    index_seq = jnp.arange(seq_count, dtype=jnp.int32)
    index_b = jnp.arange(length_b, dtype=jnp.int32)
    cos_first, sin_first = angles(freq_rows, index_rows, index_seq)
    cos_first = cos_first.astype(jnp.bfloat16)
    sin_first = sin_first.astype(jnp.bfloat16)
    flattened = columns.reshape(seq_count, columns_each * channels)
    real_part = jnp.dot(cos_first, flattened, preferred_element_type=jnp.float32)
    imag_part = jnp.dot(-sin_first, flattened, preferred_element_type=jnp.float32)
    real_part = real_part.reshape(freq_rows, columns_each, channels)
    imag_part = imag_part.reshape(freq_rows, columns_each, channels)
    mine_b = position * columns_each + jnp.arange(columns_each, dtype=jnp.int32)
    twist_cos, twist_sin = angles(fft_length, index_rows, mine_b)
    twist_cos = twist_cos[:, :, None]
    twist_sin = twist_sin[:, :, None]
    section = jnp.stack(
        [
            real_part * twist_cos + imag_part * twist_sin,
            imag_part * twist_cos - real_part * twist_sin,
        ]
    ).astype(jnp.bfloat16)
    spectral = lax.all_to_all(section, "seq", split_axis=1, concat_axis=2, tiled=True)
    cos_seq, sin_seq = angles(length_b, index_b, index_b)
    cos_seq = cos_seq.astype(jnp.bfloat16)
    sin_seq = sin_seq.astype(jnp.bfloat16)
    spectrum_real = jnp.einsum(
        "qb,kbc->kqc", cos_seq, spectral[0], preferred_element_type=jnp.float32
    ) + jnp.einsum("qb,kbc->kqc", sin_seq, spectral[1], preferred_element_type=jnp.float32)
    spectrum_imag = jnp.einsum(
        "qb,kbc->kqc", cos_seq, spectral[1], preferred_element_type=jnp.float32
    ) - jnp.einsum("qb,kbc->kqc", sin_seq, spectral[0], preferred_element_type=jnp.float32)
    filter_real = filter_spectrum[0].astype(jnp.float32)
    filter_imag = filter_spectrum[1].astype(jnp.float32)
    product = jnp.stack(
        [
            spectrum_real * filter_real - spectrum_imag * filter_imag,
            spectrum_real * filter_imag + spectrum_imag * filter_real,
        ]
    ).astype(jnp.bfloat16)
    inverse_real = jnp.einsum(
        "qb,kqc->kbc", cos_seq, product[0], preferred_element_type=jnp.float32
    ) - jnp.einsum("qb,kqc->kbc", sin_seq, product[1], preferred_element_type=jnp.float32)
    inverse_imag = jnp.einsum(
        "qb,kqc->kbc", sin_seq, product[0], preferred_element_type=jnp.float32
    ) + jnp.einsum("qb,kqc->kbc", cos_seq, product[1], preferred_element_type=jnp.float32)
    mine_k = position * freqs_each + jnp.arange(freqs_each, dtype=jnp.int32)
    back_cos, back_sin = angles(fft_length, mine_k, index_b)
    back_cos = back_cos[:, :, None]
    back_sin = back_sin[:, :, None]
    back = jnp.stack(
        [
            inverse_real * back_cos - inverse_imag * back_sin,
            inverse_real * back_sin + inverse_imag * back_cos,
        ]
    ).astype(jnp.bfloat16)
    returned = lax.all_to_all(back, "seq", split_axis=2, concat_axis=1, tiled=True)
    flat_real = returned[0].reshape(freq_rows, columns_each * channels)
    flat_imag = returned[1].reshape(freq_rows, columns_each * channels)
    conv = jnp.dot(cos_first.T, flat_real, preferred_element_type=jnp.float32) - jnp.dot(
        sin_first.T, flat_imag, preferred_element_type=jnp.float32
    )
    conv = (
        (conv * (1.0 / fft_length)).reshape(seq_count, columns_each, channels).astype(jnp.bfloat16)
    )
    conv_rows = lax.all_to_all(conv, "seq", split_axis=0, concat_axis=1, tiled=True)[0]
    gated = (
        gate_q.astype(jnp.float32) * (widened(conv_rows) + skip[None, :] * widened(drive))
    ).astype(jnp.bfloat16)
    partial_value = lax.dot_general(
        gated, out_weight, (((1,), (1,)), ((), ())), preferred_element_type=jnp.float32
    )
    return lax.psum_scatter(
        partial_value.astype(jnp.bfloat16), "ch", scatter_dimension=1, tiled=True
    )


def solution(mesh):
    placed = (
        P(("grp", "seq"), "ch"),
        P(("grp", "seq"), "ch"),
        P(("grp", "seq"), "ch"),
        P("seq", "ch"),
        P("ch"),
        P(None, "seq", None, "ch"),
        P("seq", "ch"),
    )
    sizes = mesh.shape
    body = planes if (sizes["grp"], sizes["seq"], sizes["ch"]) == (2, 8, 2) else shards
    return jax.shard_map(
        body, mesh=mesh, in_specs=placed, out_specs=P(("grp", "seq"), "ch"), check_vma=False
    )
```

```python
import functools
import math

import jax
import jax.numpy as jnp
import numpy as np
from jax import lax
from jax.experimental import pallas as pl
from jax.experimental.pallas import tpu as pltpu
from jax.sharding import PartitionSpec as P

AXES = ("grp", "seq", "ch")
BF16 = jnp.bfloat16
F32 = jnp.float32


def angles(count, first, second):
    phase = 2.0 * math.pi / count * (first[:, None] * second[None, :] % count).astype(jnp.float32)
    return (jnp.cos(phase), jnp.sin(phase))


def widened(values):
    return lax.optimization_barrier(values).astype(jnp.float32)


def dot(a, b):
    return jnp.dot(a, b, preferred_element_type=F32)


def dot_t(a, b):
    return lax.dot_general(a, b, (((1,), (1,)), ((), ())), preferred_element_type=F32)


def in_vmem(kernel, out_shape, scratch=(), smem=1, flops=0, moved=0):
    def call(*operands):
        specs = [pl.BlockSpec(memory_space=pltpu.SMEM)] * smem
        specs += [pl.BlockSpec(memory_space=pltpu.VMEM)] * (len(operands) - smem)
        return pl.pallas_call(
            kernel,
            out_shape=out_shape,
            in_specs=specs,
            out_specs=jax.tree.map(lambda _: pl.BlockSpec(memory_space=pltpu.VMEM), out_shape),
            scratch_shapes=list(scratch),
            compiler_params=pltpu.CompilerParams(vmem_limit_bytes=48 * 1024 * 1024),
            cost_estimate=pl.CostEstimate(flops=flops, bytes_accessed=moved, transcendentals=0),
        )(*operands)

    return call


def low_lanes(shape):
    return lax.broadcasted_iota(jnp.int32, shape, len(shape) - 1) < 64


def half_turn(values):
    return pltpu.roll(values, 64, values.ndim - 1)


def both(first, second, low):
    return (
        jnp.where(low, first, half_turn(second)).astype(BF16),
        jnp.where(low, half_turn(first), second).astype(BF16),
    )


def prologue(where, tokens, key, query, value, out, filt, *refs):
    own_v, away_v, own_o, away_o, m1, m2, m3, own, away_f, sem = refs
    y, x = where[0], where[1]

    def lanes(p):
        row = 1 - y if p // 2 else y
        column = 1 - x if p % 2 else x
        return pl.ds(pl.multiple_of(row * 512 + column * 256, 256), 256)

    moves = [(value.at[:, lanes(0)], own_v), (value.at[:, lanes(1)], away_v)]
    moves.append((filt.at[:, :, :, lanes(1)], away_f))
    for p, message in enumerate((own, m1, m2, m3)):
        moves.append((key.at[:, lanes(p)], message.at[:, pl.ds(0, 256)]))
        moves.append((query.at[:, lanes(p)], message.at[:, pl.ds(256, 256)]))
        if p:
            moves.append((tokens, message.at[:, pl.ds(512, 1024)]))
    moves += [(out.at[:, lanes(0)], own_o), (out.at[:, lanes(1)], away_o)]
    copies = [pltpu.make_async_copy(a, b, sem.at[i]) for i, (a, b) in enumerate(moves)]
    for copy in copies:
        copy.start()
    for copy in copies:
        copy.wait()


def pack_filter(where, filt, near, *outs):
    y, x, z = where[0], where[1], where[2]
    packed, outs = outs[4], outs[:4]
    low = low_lanes((128, 128))
    for k in range(2):
        for j in range(2):
            base = pl.multiple_of(y * 512 + x * 256 + j * 128, 128)
            for part in range(2):
                if k:
                    pair = [near[part, i, :, pl.ds(j * 128, 128)].astype(F32) for i in range(2)]
                else:
                    pair = [filt[part, i, :, pl.ds(base, 128)].astype(F32) for i in range(2)]
                one, two = both(*pair, low)
                packed[2 * j, k, part] = one
                packed[2 * j + 1, k, part] = two
    for r in range(4):
        outs[r][...] = packed[lax.rem(z + r, 4)]


def value_kernel(where, *refs):
    mine, other, gates, pieces = refs[:4], refs[4:8], refs[8], refs[9:17]
    drive, outs = refs[17], refs[18:22]
    acc, packed = refs[22], refs[23]
    x, z, c = where[1], where[2], where[3]
    acc[...] = jnp.zeros_like(acc)

    def gather(blocks, base):
        lanes = [pl.ds(pl.multiple_of(base + (512 if p else 0), 256), 256) for p in range(4)]
        return jnp.concatenate([b[:, at] for b, at in zip(blocks, lanes)], axis=0)

    for r in range(4):
        owner = lax.rem(z - r + 4, 4)
        for k in range(2):
            row = 1 - x if k else x
            base = lax.rem(owner, 2) * 512 + row * 256
            piece = pieces[2 * r + k]

            @pl.when(owner // 2 == c)
            def _():
                acc[...] += dot(gather(mine, base), piece[...])

            @pl.when(owner // 2 != c)
            def _():
                acc[...] += dot(gather(other, base), piece[...])

    for p in range(4):
        rows = pl.ds(p * 128, 128)
        gate = (mine[p] if p else gates)[:, 0:256]
        value = acc[rows, :].astype(BF16).astype(F32)
        drive[rows, :] = (gate.astype(F32) * value).astype(BF16)
    low = low_lanes((256, 128))
    for j in range(2):
        lanes = pl.ds(j * 128, 128)
        first = drive[pl.ds(0, 256), lanes].astype(F32)
        second = drive[pl.ds(256, 256), lanes].astype(F32)
        packed[2 * j], packed[2 * j + 1] = both(first, second, low)
    for r in range(4):
        outs[r][...] = packed[lax.rem(z + r, 4)]


def add(a, b):
    return b if a is None else a if b is None else a + b


def sub(a, b):
    return a if b is None else -b if a is None else a - b


def scaled(a, s):
    if a is None or abs(s) < 1e-9:
        return None
    if abs(s - 1) < 1e-9:
        return a
    if abs(s + 1) < 1e-9:
        return -a
    return a * np.float32(s)


def cmul(a, angle):
    co, si = math.cos(angle), math.sin(angle)
    return (sub(scaled(a[0], co), scaled(a[1], si)), add(scaled(a[0], si), scaled(a[1], co)))


def cadd(a, b):
    return (add(a[0], b[0]), add(a[1], b[1]))


def conj(a):
    return (a[0], None if a[1] is None else -a[1])


def short_transform(values, count, rows):
    if len(values) == 1:
        return [(values[0], None)] * rows
    half = count // 2
    need = half // 2 + 1
    even = short_transform(values[0::2], half, need)
    odd = short_transform(values[1::2], half, need)

    def at(t, k):
        k %= half
        return t[k] if k < need else conj(t[half - k])

    return [cadd(at(even, k), cmul(at(odd, k), -2 * math.pi * k / count)) for k in range(rows)]


def conv_kernel(where, *refs):
    drives, filters, (table, table_t) = refs[:4], refs[4:8], refs[8:10]
    outs, (data, filt, first, sums) = refs[10:14], refs[14:]
    x, z = where[1], where[2]
    for r, block in enumerate(drives):
        base = 2 * lax.rem(z - r + 4, 4)
        filt[base + x] = filters[r][0]
        filt[base + 1 - x] = filters[r][1]
        data[base + x] = block[pl.ds(0, 128), :]
        data[base + 1 - x] = block[pl.ds(128, 128), :]
    for i in range(8):
        rows = pl.ds(16 * i, 16)
        values = [data[a, rows, :].astype(F32) for a in range(8)]
        spectrum = short_transform(values, 16, 9)
        for k in range(9):
            re, im = spectrum[k]
            if im is None:
                im = jnp.zeros_like(re)
            first[k, rows, 0:128] = re.astype(BF16)
            first[k, rows, 128:256] = im.astype(BF16)
            if 0 < k < 8:
                first[16 - k, rows, 0:128] = re.astype(BF16)
                first[16 - k, rows, 128:256] = (-im).astype(BF16)
    low = low_lanes((128, 128))

    def back(k):
        four = dot(table[k], first[k])
        re = four[:128, :128] + four[128:, 128:]
        im = four[:128, 128:] - four[128:, :128]
        pair = [filt[k // 2, part].astype(F32) for part in range(2)]
        if k % 2 == 0:
            fr, fi = [jnp.where(low, f, half_turn(f)) for f in pair]
        else:
            fr, fi = [jnp.where(low, half_turn(f), f) for f in pair]
        product = jnp.concatenate([re * fr - im * fi, re * fi + im * fr], axis=1).astype(BF16)
        four = dot(table_t[k], product)
        return four[:128, :128] - four[128:, 128:], four[128:, :128] + four[:128, 128:]

    sums[0, pl.ds(0, 128)] = back(0)[0]
    sums[8, pl.ds(0, 128)] = back(8)[0]
    for k in range(1, 8):
        one, two = back(k), back(16 - k)
        sums[k, pl.ds(0, 128)] = one[0] + two[0]
        sums[k, pl.ds(128, 128)] = one[1] - two[1]
    for i in range(16):
        rows, below = pl.ds(8 * i, 8), pl.ds(128 + 8 * i, 8)
        scale = 1.0 / 2048
        re = [sums[k, rows, :] * scale for k in range(9)]
        im = [None] + [sums[k, below, :] * scale for k in range(1, 8)] + [None]
        for a in range(5):
            groups = [None] * 4
            for k in range(9):
                ang = 2 * math.pi * (k * a % 16) / 16
                groups[k % 2] = add(groups[k % 2], scaled(re[k], math.cos(ang)))
                groups[2 + k % 2] = sub(groups[2 + k % 2], scaled(im[k], math.sin(ang)))
            ec, oc, es, os = groups
            data[a, rows, :] = add(add(ec, oc), add(es, os)).astype(BF16)
            if 0 < a < 4:
                data[8 - a, rows, :] = sub(sub(add(ec, os), oc), es).astype(BF16)
    for r, out in enumerate(outs):
        base = 2 * lax.rem(z + r, 4)
        out[pl.ds(0, 128), :] = data[base + x]
        out[pl.ds(128, 128), :] = data[base + 1 - x]


def gate_kernel(where, e0, e1, e2, e3, drive, skip, gates, g1, g2, g3, gated, conv):
    z = where[2]
    for r, block in enumerate((e0, e1, e2, e3)):
        conv[lax.rem(z - r + 4, 4)] = block[...]
    low = low_lanes((256, 128))
    for j in range(2):
        lanes = pl.ds(j * 128, 128)
        even, odd = conv[2 * j].astype(F32), conv[2 * j + 1].astype(F32)
        parts = (jnp.where(low, even, half_turn(odd)), jnp.where(low, half_turn(even), odd))
        for p, gate in enumerate((gates, g1, g2, g3)):
            rows = pl.ds(p * 128, 128)
            own = parts[p // 2][(p % 2) * 128 : (p % 2) * 128 + 128]
            direct = skip[:, lanes] * drive[rows, lanes].astype(F32)
            query = gate[:, pl.ds(256 + j * 128, 128)].astype(F32)
            gated[rows, lanes] = (query * (own + direct)).astype(BF16)


def sort_weight(where, *refs):
    pieces, keep, give = refs[:4], refs[4], refs[5]
    x, z, c = where[1], where[2], where[3]
    for r in range(4):
        owner = lax.rem(z - r + 4, 4)
        for k in range(2):
            to = 2 * lax.rem(owner, 2) + (1 - x if k else x)

            @pl.when(owner // 2 == c)
            def _():
                keep[to] = pieces[r][k]

            @pl.when(owner // 2 != c)
            def _():
                give[to] = pieces[r][k]


def out_kernel(gated, other, keep, theirs, own, *sends):
    for p in (3, 2, 1, 0):
        rows = pl.ds(p * 128, 128)
        for i in range(4):
            total = dot_t(gated[rows, :], keep[i]) + dot_t(other[rows, :], theirs[i])
            lanes = pl.ds(i * 256, 256)
            if p == 0:
                own[:, lanes] = total
            else:
                sends[p - 1][:, lanes] = total.astype(BF16)


def tables():
    k = np.arange(16)[:, None, None] + 16 * np.arange(128)[None, :, None]
    phase = 2 * np.pi / 2048 * (k * np.arange(128)[None, None, :] % 2048)
    co, si = np.cos(phase), np.sin(phase)
    back = np.concatenate([co.transpose(0, 2, 1), si.transpose(0, 2, 1)], 1)
    return np.concatenate([co, si], 1).astype(jnp.bfloat16), back.astype(jnp.bfloat16)


def planes(tokens, gate_q, gate_k, w_value, skip, filter_spectrum, w_out):
    y, s, c = (lax.axis_index(a) for a in AXES)
    x, z = s % 2, s // 2
    seq, deep = 8, 4
    where = jnp.stack([y, x, z, c]).astype(jnp.int32)

    def permute(values, move):
        pairs = []
        for g in range(2):
            for i in range(seq):
                for k in range(2):
                    g2, z2, x2, k2 = move(g, i // 2, i % 2, k)
                    pairs.append(((g * seq + i) * 2 + k, (g2 * seq + z2 * 2 + x2) * 2 + k2))
        return lax.ppermute(values, AXES, pairs)

    def to_x(values):
        return permute(values, lambda g, z, x, k: (g, z, 1 - x, k))

    def to_core(values):
        return permute(values, lambda g, z, x, k: (g, z, x, 1 - k))

    def to_z(values, r):
        return permute(values, lambda g, z, x, k: (g, (z + r) % deep, x, k))

    def to_peer(values, p):
        return permute(values, lambda g, z, x, k: (g ^ (p // 2), z, x ^ (p % 2), k))

    def after(values, *done):
        return lax.optimization_barrier((values,) + done)[0]

    shape = jax.ShapeDtypeStruct
    block, square = shape((256, 128), BF16), shape((256, 256), BF16)
    inside = pl.BlockSpec(memory_space=pltpu.MemorySpace.HBM)
    laid = [square] * 4 + [shape((128, w), BF16) for w in (1536, 1536, 1536, 512)]
    laid.append(shape((2, 2, 128, 256), BF16))
    own_v, away_v, own_o, away_o, *messages, gates, away_f = pl.pallas_call(
        prologue,
        out_shape=laid,
        in_specs=[pl.BlockSpec(memory_space=pltpu.SMEM)] + [inside] * 6,
        out_specs=[pl.BlockSpec(memory_space=pltpu.VMEM)] * 9,
        scratch_shapes=[pltpu.SemaphoreType.DMA((16,))],
        compiler_params=pltpu.CompilerParams(vmem_limit_bytes=61 * 1024 * 1024),
    )(where, tokens, gate_k, gate_q, w_value, w_out, filter_spectrum)
    ring = [own_v, to_x(away_v)]
    received = [to_peer(messages[p - 1], p) for p in (1, 2, 3)]
    ring += [to_z(ring[0], 1), to_z(ring[1], 1)]
    got = to_x(away_f)
    filters = in_vmem(
        pack_filter,
        [shape((2, 2, 128, 128), BF16)] * 4,
        [pltpu.VMEM((4, 2, 2, 128, 128), BF16)],
        moved=1 << 20,
    )(where, filter_spectrum, got)
    filters = [filters[0]] + [to_z(filters[r], r) for r in (1, 2, 3)]
    mine = [tokens] + received
    other = [to_core(m) for m in mine]
    ring += [to_z(ring[2], 1), to_z(ring[3], 1)]
    ring += [to_z(after(ring[4], *received[:2]), 1), to_z(ring[5], 1)]
    pair = jnp.stack([own_o, to_x(after(away_o, got))])
    hops = [after(pair, ring[4], ring[5], received[2])]
    hops.append(to_z(hops[0], 1))
    hops.append(to_z(after(hops[1], ring[6], ring[7]), 1))
    gates = after(gates, *filters)
    drive, *sends = in_vmem(
        value_kernel,
        [shape((512, 256), BF16)] + [block] * 4,
        [pltpu.VMEM((512, 256), F32), pltpu.VMEM((4, 256, 128), BF16)],
        flops=1 << 29,
        moved=4 << 20,
    )(where, *mine, *other, gates, *ring)
    columns = [sends[0]] + [to_z(sends[r], r) for r in (1, 2, 3)]
    table, table_t = tables()
    sends = in_vmem(
        conv_kernel,
        [block] * 4,
        [
            pltpu.VMEM((8, 128, 128), BF16),
            pltpu.VMEM((8, 2, 128, 128), BF16),
            pltpu.VMEM((16, 128, 256), BF16),
            pltpu.VMEM((9, 256, 128), F32),
        ],
        flops=1 << 30,
        moved=5 << 20,
    )(where, *columns, *filters, table, table_t)
    rows = [sends[0]] + [to_z(sends[r], r) for r in (1, 2, 3)]

    hops.append(to_z(after(hops[2], sends[0]), 1))
    hops[3] = after(hops[3], *rows[1:])
    quad = shape((4, 256, 256), BF16)
    keep, give = in_vmem(sort_weight, [quad] * 2, moved=2 << 20)(where, *hops)
    theirs = to_core(give)
    channels = lax.dynamic_slice_in_dim(skip, (y * 2 + x) * 256, 256)[None, :]
    gated = in_vmem(
        gate_kernel, shape((512, 256), BF16), [pltpu.VMEM((4, 256, 128), BF16)], moved=1 << 20
    )(where, *rows, drive, channels, gates, *received)
    gated_other = to_core(gated)
    own, *sends = in_vmem(
        out_kernel,
        [shape((128, 1024), F32)] + [shape((128, 1024), BF16)] * 3,
        smem=0,
        flops=1 << 30,
        moved=4 << 20,
    )(gated, gated_other, keep, theirs)
    total = own
    for p in (3, 2, 1):
        total = total + to_peer(sends[p - 1], p).astype(F32)
    return total.astype(BF16)


def shards(tokens, gate_q, gate_k, w_value, skip, filter_spectrum, w_out):
    seq_count = lax.axis_size("seq")
    position = lax.axis_index("seq")
    length_b = tokens.shape[0]
    columns_each = length_b // seq_count
    freq_rows = 2 * seq_count
    freqs_each = freq_rows // seq_count
    fft_length = freq_rows * length_b
    features = lax.all_gather(tokens, "ch", axis=1, tiled=True)
    value_weight, out_weight = (
        lax.all_gather(w_value, "seq", axis=0, tiled=True),
        lax.all_gather(w_out, "seq", axis=0, tiled=True),
    )
    value = jnp.dot(features, value_weight, preferred_element_type=jnp.float32)
    value = value.astype(jnp.bfloat16)
    drive = (gate_k.astype(jnp.float32) * widened(value)).astype(jnp.bfloat16)
    channels = drive.shape[1]
    columns = lax.all_to_all(drive[None], "seq", split_axis=1, concat_axis=0, tiled=True)
    index_rows = jnp.arange(freq_rows, dtype=jnp.int32)
    index_seq = jnp.arange(seq_count, dtype=jnp.int32)
    index_b = jnp.arange(length_b, dtype=jnp.int32)
    cos_first, sin_first = angles(freq_rows, index_rows, index_seq)
    cos_first = cos_first.astype(jnp.bfloat16)
    sin_first = sin_first.astype(jnp.bfloat16)
    flattened = columns.reshape(seq_count, columns_each * channels)
    real_part = jnp.dot(cos_first, flattened, preferred_element_type=jnp.float32)
    imag_part = jnp.dot(-sin_first, flattened, preferred_element_type=jnp.float32)
    real_part = real_part.reshape(freq_rows, columns_each, channels)
    imag_part = imag_part.reshape(freq_rows, columns_each, channels)
    mine_b = position * columns_each + jnp.arange(columns_each, dtype=jnp.int32)
    twist_cos, twist_sin = angles(fft_length, index_rows, mine_b)
    twist_cos = twist_cos[:, :, None]
    twist_sin = twist_sin[:, :, None]
    section = jnp.stack(
        [
            real_part * twist_cos + imag_part * twist_sin,
            imag_part * twist_cos - real_part * twist_sin,
        ]
    ).astype(jnp.bfloat16)
    spectral = lax.all_to_all(section, "seq", split_axis=1, concat_axis=2, tiled=True)
    cos_seq, sin_seq = angles(length_b, index_b, index_b)
    cos_seq = cos_seq.astype(jnp.bfloat16)
    sin_seq = sin_seq.astype(jnp.bfloat16)
    spectrum_real = jnp.einsum(
        "qb,kbc->kqc", cos_seq, spectral[0], preferred_element_type=jnp.float32
    ) + jnp.einsum("qb,kbc->kqc", sin_seq, spectral[1], preferred_element_type=jnp.float32)
    spectrum_imag = jnp.einsum(
        "qb,kbc->kqc", cos_seq, spectral[1], preferred_element_type=jnp.float32
    ) - jnp.einsum("qb,kbc->kqc", sin_seq, spectral[0], preferred_element_type=jnp.float32)
    filter_real = filter_spectrum[0].astype(jnp.float32)
    filter_imag = filter_spectrum[1].astype(jnp.float32)
    product = jnp.stack(
        [
            spectrum_real * filter_real - spectrum_imag * filter_imag,
            spectrum_real * filter_imag + spectrum_imag * filter_real,
        ]
    ).astype(jnp.bfloat16)
    inverse_real = jnp.einsum(
        "qb,kqc->kbc", cos_seq, product[0], preferred_element_type=jnp.float32
    ) - jnp.einsum("qb,kqc->kbc", sin_seq, product[1], preferred_element_type=jnp.float32)
    inverse_imag = jnp.einsum(
        "qb,kqc->kbc", sin_seq, product[0], preferred_element_type=jnp.float32
    ) + jnp.einsum("qb,kqc->kbc", cos_seq, product[1], preferred_element_type=jnp.float32)
    mine_k = position * freqs_each + jnp.arange(freqs_each, dtype=jnp.int32)
    back_cos, back_sin = angles(fft_length, mine_k, index_b)
    back_cos = back_cos[:, :, None]
    back_sin = back_sin[:, :, None]
    back = jnp.stack(
        [
            inverse_real * back_cos - inverse_imag * back_sin,
            inverse_real * back_sin + inverse_imag * back_cos,
        ]
    ).astype(jnp.bfloat16)
    returned = lax.all_to_all(back, "seq", split_axis=2, concat_axis=1, tiled=True)
    flat_real = returned[0].reshape(freq_rows, columns_each * channels)
    flat_imag = returned[1].reshape(freq_rows, columns_each * channels)
    conv = jnp.dot(cos_first.T, flat_real, preferred_element_type=jnp.float32) - jnp.dot(
        sin_first.T, flat_imag, preferred_element_type=jnp.float32
    )
    conv = (
        (conv * (1.0 / fft_length)).reshape(seq_count, columns_each, channels).astype(jnp.bfloat16)
    )
    conv_rows = lax.all_to_all(conv, "seq", split_axis=0, concat_axis=1, tiled=True)[0]
    gated = (
        gate_q.astype(jnp.float32) * (widened(conv_rows) + skip[None, :] * widened(drive))
    ).astype(jnp.bfloat16)
    partial_value = lax.dot_general(
        gated, out_weight, (((1,), (1,)), ((), ())), preferred_element_type=jnp.float32
    )
    return lax.psum_scatter(
        partial_value.astype(jnp.bfloat16), "ch", scatter_dimension=1, tiled=True
    )


def solution(mesh):
    placed = (
        P(("grp", "seq"), "ch"),
        P(("grp", "seq"), "ch"),
        P(("grp", "seq"), "ch"),
        P("seq", "ch"),
        P("ch"),
        P(None, "seq", None, "ch"),
        P("seq", "ch"),
    )
    sizes = mesh.shape
    body = planes if (sizes["grp"], sizes["seq"], sizes["ch"]) == (2, 8, 2) else shards
    return jax.shard_map(
        body, mesh=mesh, in_specs=placed, out_specs=P(("grp", "seq"), "ch"), check_vma=False
    )
```

```python
import functools
import math

import jax
import jax.numpy as jnp
import numpy as np
from jax import lax
from jax.experimental import pallas as pl
from jax.experimental.pallas import tpu as pltpu
from jax.sharding import PartitionSpec as P

AXES = ("grp", "seq", "ch")
BF16 = jnp.bfloat16
F32 = jnp.float32


def angles(count, first, second):
    phase = 2.0 * math.pi / count * (first[:, None] * second[None, :] % count).astype(jnp.float32)
    return (jnp.cos(phase), jnp.sin(phase))


def widened(values):
    return lax.optimization_barrier(values).astype(jnp.float32)


def dot(a, b):
    return jnp.dot(a, b, preferred_element_type=F32)


def dot_t(a, b):
    return lax.dot_general(a, b, (((1,), (1,)), ((), ())), preferred_element_type=F32)


def in_vmem(kernel, out_shape, scratch=(), flops=0, moved=0):
    def call(*operands):
        specs = [pl.BlockSpec(memory_space=pltpu.VMEM)] * len(operands)
        return pl.pallas_call(
            kernel,
            out_shape=out_shape,
            in_specs=specs,
            out_specs=jax.tree.map(lambda _: pl.BlockSpec(memory_space=pltpu.VMEM), out_shape),
            scratch_shapes=list(scratch),
            compiler_params=pltpu.CompilerParams(vmem_limit_bytes=20 * 1024 * 1024),
            cost_estimate=pl.CostEstimate(flops=flops, bytes_accessed=moved, transcendentals=0),
        )(*operands)

    return call


def place():
    y, s, c = (lax.axis_index(a) for a in AXES)
    return y, lax.rem(s, 2), lax.div(s, 2), c


def low_lanes(shape):
    return lax.broadcasted_iota(jnp.int32, shape, len(shape) - 1) < 64


def half_turn(values):
    return pltpu.roll(values, 64, values.ndim - 1)


def both(first, second, low):
    return (
        jnp.where(low, first, half_turn(second)).astype(BF16),
        jnp.where(low, half_turn(first), second).astype(BF16),
    )


def quarter(p):
    y, x, _, _ = place()
    row = 1 - y if p // 2 else y
    column = 1 - x if p % 2 else x
    return pl.ds(pl.multiple_of(row * 512 + column * 256, 256), 256)


def copied(moves, sem):
    copies = [pltpu.make_async_copy(a, b, sem.at[i]) for i, (a, b) in enumerate(moves)]
    for copy in copies:
        copy.start()
    for copy in copies:
        copy.wait()


def cut_weights(value, out, own_v, away_v, own_o, away_o, sem):
    moves = [(value.at[:, quarter(0)], own_v), (value.at[:, quarter(1)], away_v)]
    copied(moves + [(out.at[:, quarter(0)], own_o), (out.at[:, quarter(1)], away_o)], sem)


def cut_messages(tokens, key, query, after, m1, m2, m3, own, sem):
    moves = []
    for p, message in enumerate((own, m1, m2, m3)):
        moves.append((key.at[:, quarter(p)], message.at[:, pl.ds(0, 256)]))
        moves.append((query.at[:, quarter(p)], message.at[:, pl.ds(256, 256)]))
        if p:
            moves.append((tokens, message.at[:, pl.ds(512, 1024)]))
    copied(moves, sem)


def copy_kernel(kernel, out_shape):
    def call(*operands):
        return pl.pallas_call(
            kernel,
            out_shape=out_shape,
            in_specs=[pl.BlockSpec(memory_space=pltpu.MemorySpace.HBM)] * len(operands),
            out_specs=[pl.BlockSpec(memory_space=pltpu.VMEM)] * len(out_shape),
            scratch_shapes=[pltpu.SemaphoreType.DMA((12,))],
            compiler_params=pltpu.CompilerParams(vmem_limit_bytes=61 * 1024 * 1024),
        )(*operands)

    return call


def pack_filter(filt, *refs):
    y, x, z, _ = place()
    packed, outs = refs[4], refs[:4]
    low = low_lanes((128, 128))
    for k in range(2):
        column = 1 - x if k else x
        for j in range(2):
            base = pl.multiple_of(y * 512 + column * 256 + j * 128, 128)
            for part in range(2):
                pair = [filt[part, i, :, pl.ds(base, 128)].astype(F32) for i in range(2)]
                one, two = both(*pair, low)
                packed[2 * j, k, part] = one
                packed[2 * j + 1, k, part] = two
    for r in range(4):
        outs[r][...] = packed[lax.rem(z + r, 4)]


def pass_filter(f0, f1, f2, f3, out):
    for r, block in enumerate((f0, f1, f2, f3)):
        out[r] = block[1]


def join_tokens(m1, m2, m3, out):
    for p, message in enumerate((m1, m2, m3)):
        out[pl.ds(p * 128, 128), :] = message[:, pl.ds(512, 1024)]


def value_kernel(*refs):
    mine, other, gates, pieces = refs[:4], refs[4:6], refs[6], refs[7:15]
    drive, outs = refs[15], refs[16:20]
    acc, packed = refs[20], refs[21]
    _, x, z, c = place()
    acc[...] = jnp.zeros_like(acc)

    def gather(blocks, base):
        near, far = pl.multiple_of(base, 256), pl.multiple_of(base + 512, 256)
        lanes = [near] + [near if len(blocks) == 2 else far] * 3
        return jnp.concatenate([b[:, pl.ds(at, 256)] for b, at in zip(blocks, lanes)], axis=0)

    for r in range(4):
        owner = lax.rem(z - r + 4, 4)
        for k in range(2):
            row = 1 - x if k else x
            base = lax.rem(owner, 2) * 512 + row * 256
            piece = pieces[2 * r + k]

            @pl.when(owner // 2 == c)
            def _():
                acc[...] += dot(gather(mine, base), piece[...])

            @pl.when(owner // 2 != c)
            def _():
                acc[...] += dot(gather(other, base), piece[...])

    for p in range(4):
        rows = pl.ds(p * 128, 128)
        gate = (mine[p] if p else gates)[:, 0:256]
        value = acc[rows, :].astype(BF16).astype(F32)
        drive[rows, :] = (gate.astype(F32) * value).astype(BF16)
    low = low_lanes((256, 128))
    for j in range(2):
        lanes = pl.ds(j * 128, 128)
        first = drive[pl.ds(0, 256), lanes].astype(F32)
        second = drive[pl.ds(256, 256), lanes].astype(F32)
        packed[2 * j], packed[2 * j + 1] = both(first, second, low)
    for r in range(4):
        outs[r][...] = packed[lax.rem(z + r, 4)]


def add(a, b):
    return b if a is None else a if b is None else a + b


def sub(a, b):
    return a if b is None else -b if a is None else a - b


def scaled(a, s):
    if a is None or abs(s) < 1e-9:
        return None
    if abs(s - 1) < 1e-9:
        return a
    if abs(s + 1) < 1e-9:
        return -a
    return a * np.float32(s)


def cmul(a, angle):
    co, si = math.cos(angle), math.sin(angle)
    return (sub(scaled(a[0], co), scaled(a[1], si)), add(scaled(a[0], si), scaled(a[1], co)))


def cadd(a, b):
    return (add(a[0], b[0]), add(a[1], b[1]))


def conj(a):
    return (a[0], None if a[1] is None else -a[1])


def short_transform(values, count, rows):
    if len(values) == 1:
        return [(values[0], None)] * rows
    half = count // 2
    need = half // 2 + 1
    even = short_transform(values[0::2], half, need)
    odd = short_transform(values[1::2], half, need)

    def at(t, k):
        k %= half
        return t[k] if k < need else conj(t[half - k])

    return [cadd(at(even, k), cmul(at(odd, k), -2 * math.pi * k / count)) for k in range(rows)]


def conv_kernel(*refs):
    drives, filters, (beside, table, table_t) = refs[:4], refs[4:8], refs[8:11]
    outs, (data, filt, first, sums) = refs[11:15], refs[15:]
    _, x, z, _ = place()
    for r, block in enumerate(drives):
        base = 2 * lax.rem(z - r + 4, 4)
        filt[base + x] = filters[r][0]
        filt[base + 1 - x] = beside[r]
        data[base + x] = block[pl.ds(0, 128), :]
        data[base + 1 - x] = block[pl.ds(128, 128), :]
    for i in range(8):
        rows = pl.ds(16 * i, 16)
        values = [data[a, rows, :].astype(F32) for a in range(8)]
        spectrum = short_transform(values, 16, 9)
        for k in range(9):
            re, im = spectrum[k]
            if im is None:
                im = jnp.zeros_like(re)
            first[k, rows, 0:128] = re.astype(BF16)
            first[k, rows, 128:256] = im.astype(BF16)
            if 0 < k < 8:
                first[16 - k, rows, 0:128] = re.astype(BF16)
                first[16 - k, rows, 128:256] = (-im).astype(BF16)
    low = low_lanes((128, 128))

    def back(k):
        four = dot(table[k], first[k])
        re = four[:128, :128] + four[128:, 128:]
        im = four[:128, 128:] - four[128:, :128]
        pair = [filt[k // 2, part].astype(F32) for part in range(2)]
        if k % 2 == 0:
            fr, fi = [jnp.where(low, f, half_turn(f)) for f in pair]
        else:
            fr, fi = [jnp.where(low, half_turn(f), f) for f in pair]
        product = jnp.concatenate([re * fr - im * fi, re * fi + im * fr], axis=1).astype(BF16)
        four = dot(table_t[k], product)
        return four[:128, :128] - four[128:, 128:], four[128:, :128] + four[:128, 128:]

    sums[0, pl.ds(0, 128)] = back(0)[0]
    sums[8, pl.ds(0, 128)] = back(8)[0]
    for k in range(1, 8):
        one, two = back(k), back(16 - k)
        sums[k, pl.ds(0, 128)] = one[0] + two[0]
        sums[k, pl.ds(128, 128)] = one[1] - two[1]
    for i in range(16):
        rows, below = pl.ds(8 * i, 8), pl.ds(128 + 8 * i, 8)
        scale = 1.0 / 2048
        re = [sums[k, rows, :] * scale for k in range(9)]
        im = [None] + [sums[k, below, :] * scale for k in range(1, 8)] + [None]
        for a in range(5):
            groups = [None] * 4
            for k in range(9):
                ang = 2 * math.pi * (k * a % 16) / 16
                groups[k % 2] = add(groups[k % 2], scaled(re[k], math.cos(ang)))
                groups[2 + k % 2] = sub(groups[2 + k % 2], scaled(im[k], math.sin(ang)))
            ec, oc, es, os = groups
            data[a, rows, :] = add(add(ec, oc), add(es, os)).astype(BF16)
            if 0 < a < 4:
                data[8 - a, rows, :] = sub(sub(add(ec, os), oc), es).astype(BF16)
    for r, out in enumerate(outs):
        base = 2 * lax.rem(z + r, 4)
        out[pl.ds(0, 128), :] = data[base + x]
        out[pl.ds(128, 128), :] = data[base + 1 - x]


def gate_kernel(e0, e1, e2, e3, drive, skip, gates, g1, g2, g3, gated, conv):
    y, x, z, _ = place()
    for r, block in enumerate((e0, e1, e2, e3)):
        conv[lax.rem(z - r + 4, 4)] = block[...]
    low = low_lanes((256, 128))
    for j in range(2):
        lanes = pl.ds(j * 128, 128)
        even, odd = conv[2 * j].astype(F32), conv[2 * j + 1].astype(F32)
        parts = (jnp.where(low, even, half_turn(odd)), jnp.where(low, half_turn(even), odd))
        for p, gate in enumerate((gates, g1, g2, g3)):
            rows = pl.ds(p * 128, 128)
            own = parts[p // 2][(p % 2) * 128 : (p % 2) * 128 + 128]
            at = pl.ds(pl.multiple_of(y * 512 + x * 256 + j * 128, 128), 128)
            direct = skip[:, at] * drive[rows, lanes].astype(F32)
            query = gate[:, pl.ds(256 + j * 128, 128)].astype(F32)
            gated[rows, lanes] = (query * (own + direct)).astype(BF16)


def sort_weight(*refs):
    pieces, keep, give = refs[:4], refs[4], refs[5]
    _, x, z, c = place()
    for r in range(4):
        owner = lax.rem(z - r + 4, 4)
        for k in range(2):
            to = 2 * lax.rem(owner, 2) + (1 - x if k else x)

            @pl.when(owner // 2 == c)
            def _():
                keep[to] = pieces[r][k]

            @pl.when(owner // 2 != c)
            def _():
                give[to] = pieces[r][k]


def out_kernel(gated, other, keep, theirs, own, *sends):
    for p in (3, 2, 1, 0):
        rows = pl.ds(p * 128, 128)
        for i in range(4):
            total = dot_t(gated[rows, :], keep[i]) + dot_t(other[rows, :], theirs[i])
            lanes = pl.ds(i * 256, 256)
            if p == 0:
                own[:, lanes] = total
            else:
                sends[p - 1][:, lanes] = total.astype(BF16)


def tables():
    k = np.arange(16)[:, None, None] + 16 * np.arange(128)[None, :, None]
    phase = 2 * np.pi / 2048 * (k * np.arange(128)[None, None, :] % 2048)
    co, si = np.cos(phase), np.sin(phase)
    back = np.concatenate([co.transpose(0, 2, 1), si.transpose(0, 2, 1)], 1)
    return np.concatenate([co, si], 1).astype(jnp.bfloat16), back.astype(jnp.bfloat16)


def planes(tokens, gate_q, gate_k, w_value, skip, filter_spectrum, w_out):
    seq, deep = 8, 4

    def permute(values, move):
        pairs = []
        for g in range(2):
            for i in range(seq):
                for k in range(2):
                    g2, z2, x2, k2 = move(g, i // 2, i % 2, k)
                    pairs.append(((g * seq + i) * 2 + k, (g2 * seq + z2 * 2 + x2) * 2 + k2))
        return lax.ppermute(values, AXES, pairs)

    def to_x(values):
        return permute(values, lambda g, z, x, k: (g, z, 1 - x, k))

    def to_core(values):
        return permute(values, lambda g, z, x, k: (g, z, x, 1 - k))

    def to_z(values, r):
        return permute(values, lambda g, z, x, k: (g, (z + r) % deep, x, k))

    def to_peer(values, p):
        return permute(values, lambda g, z, x, k: (g ^ (p // 2), z, x ^ (p % 2), k))

    def after(values, *done):
        return lax.optimization_barrier((values,) + done)[0]

    shape = jax.ShapeDtypeStruct
    block, square = shape((256, 128), BF16), shape((256, 256), BF16)
    own_v, away_v, own_o, away_o = copy_kernel(cut_weights, [square] * 4)(w_value, w_out)
    laid = [shape((128, w), BF16) for w in (1536, 1536, 1536, 512)]
    *messages, gates = copy_kernel(cut_messages, laid)(tokens, gate_k, gate_q, own_v)
    filters = in_vmem(
        pack_filter,
        [shape((2, 2, 128, 128), BF16)] * 4,
        [pltpu.VMEM((4, 2, 2, 128, 128), BF16)],
        moved=1 << 20,
        )(after(filter_spectrum, messages[0]))
    filters = [filters[0]] + [to_z(filters[r], r) for r in (1, 2, 3)]
    received = [to_peer(messages[p - 1], p) for p in (1, 2, 3)]
    b0 = to_x(away_v)
    a1 = to_z(own_v, 1)
    b1 = to_z(b0, 1)
    a2 = to_z(after(a1, b0), 1)
    b2 = to_z(after(b1, a1, received[1]), 1)
    a3 = to_z(after(a2, b1, received[2]), 1)
    got_o = to_x(after(away_o, b0))
    b3 = to_z(after(b2, a2, got_o, *filters[1:]), 1)
    ring = [own_v, b0, a1, b1, a2, b2, a3, b3]
    passed = in_vmem(pass_filter, shape((4, 2, 128, 128), BF16), moved=1 << 20)(
        after(filters[0], b2), *filters[1:]
    )
    beside = to_x(passed)
    mine = [tokens] + received
    first = after(received[0], a3, b3)
    joined = in_vmem(join_tokens, shape((384, 1024), BF16), moved=2 << 20)(first, *received[1:])
    other = [to_core(tokens), to_core(joined)]
    pair = jnp.stack([own_o, got_o])
    hops = [pair, to_z(after(pair, a3), 1)]
    gates = after(gates, passed)
    drive, *sends = in_vmem(
        value_kernel,
        [shape((512, 256), BF16)] + [block] * 4,
        [pltpu.VMEM((512, 256), F32), pltpu.VMEM((4, 256, 128), BF16)],
        flops=1 << 29,
        moved=4 << 20,
    )(*mine, *other, gates, *ring)
    columns = [sends[0]] + [to_z(sends[r], r) for r in (1, 2, 3)]
    hops.append(to_z(after(hops[1], drive), 1))
    hops.append(to_z(after(hops[2], *columns[1:]), 1))
    table, table_t = tables()
    sends = in_vmem(
        conv_kernel,
        [block] * 4,
        [
            pltpu.VMEM((8, 128, 128), BF16),
            pltpu.VMEM((8, 2, 128, 128), BF16),
            pltpu.VMEM((16, 128, 256), BF16),
            pltpu.VMEM((9, 256, 128), F32),
        ],
        flops=1 << 30,
        moved=5 << 20,
    )(*columns, *filters, beside, table, table_t)
    rows = [sends[0]] + [to_z(sends[r], r) for r in (1, 2, 3)]

    hops[3] = after(hops[3], *rows[1:])
    quad = shape((4, 256, 256), BF16)
    keep, give = in_vmem(sort_weight, [quad] * 2, moved=2 << 20)(*hops)
    theirs = to_core(give)
    gated = in_vmem(
        gate_kernel, shape((512, 256), BF16), [pltpu.VMEM((4, 256, 128), BF16)], moved=1 << 20
    )(*rows, drive, skip[None, :], gates, *received)
    gated_other = to_core(gated)
    own, *sends = in_vmem(
        out_kernel,
        [shape((128, 1024), F32)] + [shape((128, 1024), BF16)] * 3,
        flops=1 << 30,
        moved=4 << 20,
    )(gated, gated_other, keep, theirs)
    total = own
    for p in (3, 2, 1):
        total = total + to_peer(sends[p - 1], p).astype(F32)
    return total.astype(BF16)


def shards(tokens, gate_q, gate_k, w_value, skip, filter_spectrum, w_out):
    seq_count = lax.axis_size("seq")
    position = lax.axis_index("seq")
    length_b = tokens.shape[0]
    columns_each = length_b // seq_count
    freq_rows = 2 * seq_count
    freqs_each = freq_rows // seq_count
    fft_length = freq_rows * length_b
    features = lax.all_gather(tokens, "ch", axis=1, tiled=True)
    value_weight, out_weight = (
        lax.all_gather(w_value, "seq", axis=0, tiled=True),
        lax.all_gather(w_out, "seq", axis=0, tiled=True),
    )
    value = jnp.dot(features, value_weight, preferred_element_type=jnp.float32)
    value = value.astype(jnp.bfloat16)
    drive = (gate_k.astype(jnp.float32) * widened(value)).astype(jnp.bfloat16)
    channels = drive.shape[1]
    columns = lax.all_to_all(drive[None], "seq", split_axis=1, concat_axis=0, tiled=True)
    index_rows = jnp.arange(freq_rows, dtype=jnp.int32)
    index_seq = jnp.arange(seq_count, dtype=jnp.int32)
    index_b = jnp.arange(length_b, dtype=jnp.int32)
    cos_first, sin_first = angles(freq_rows, index_rows, index_seq)
    cos_first = cos_first.astype(jnp.bfloat16)
    sin_first = sin_first.astype(jnp.bfloat16)
    flattened = columns.reshape(seq_count, columns_each * channels)
    real_part = jnp.dot(cos_first, flattened, preferred_element_type=jnp.float32)
    imag_part = jnp.dot(-sin_first, flattened, preferred_element_type=jnp.float32)
    real_part = real_part.reshape(freq_rows, columns_each, channels)
    imag_part = imag_part.reshape(freq_rows, columns_each, channels)
    mine_b = position * columns_each + jnp.arange(columns_each, dtype=jnp.int32)
    twist_cos, twist_sin = angles(fft_length, index_rows, mine_b)
    twist_cos = twist_cos[:, :, None]
    twist_sin = twist_sin[:, :, None]
    section = jnp.stack(
        [
            real_part * twist_cos + imag_part * twist_sin,
            imag_part * twist_cos - real_part * twist_sin,
        ]
    ).astype(jnp.bfloat16)
    spectral = lax.all_to_all(section, "seq", split_axis=1, concat_axis=2, tiled=True)
    cos_seq, sin_seq = angles(length_b, index_b, index_b)
    cos_seq = cos_seq.astype(jnp.bfloat16)
    sin_seq = sin_seq.astype(jnp.bfloat16)
    spectrum_real = jnp.einsum(
        "qb,kbc->kqc", cos_seq, spectral[0], preferred_element_type=jnp.float32
    ) + jnp.einsum("qb,kbc->kqc", sin_seq, spectral[1], preferred_element_type=jnp.float32)
    spectrum_imag = jnp.einsum(
        "qb,kbc->kqc", cos_seq, spectral[1], preferred_element_type=jnp.float32
    ) - jnp.einsum("qb,kbc->kqc", sin_seq, spectral[0], preferred_element_type=jnp.float32)
    filter_real = filter_spectrum[0].astype(jnp.float32)
    filter_imag = filter_spectrum[1].astype(jnp.float32)
    product = jnp.stack(
        [
            spectrum_real * filter_real - spectrum_imag * filter_imag,
            spectrum_real * filter_imag + spectrum_imag * filter_real,
        ]
    ).astype(jnp.bfloat16)
    inverse_real = jnp.einsum(
        "qb,kqc->kbc", cos_seq, product[0], preferred_element_type=jnp.float32
    ) - jnp.einsum("qb,kqc->kbc", sin_seq, product[1], preferred_element_type=jnp.float32)
    inverse_imag = jnp.einsum(
        "qb,kqc->kbc", sin_seq, product[0], preferred_element_type=jnp.float32
    ) + jnp.einsum("qb,kqc->kbc", cos_seq, product[1], preferred_element_type=jnp.float32)
    mine_k = position * freqs_each + jnp.arange(freqs_each, dtype=jnp.int32)
    back_cos, back_sin = angles(fft_length, mine_k, index_b)
    back_cos = back_cos[:, :, None]
    back_sin = back_sin[:, :, None]
    back = jnp.stack(
        [
            inverse_real * back_cos - inverse_imag * back_sin,
            inverse_real * back_sin + inverse_imag * back_cos,
        ]
    ).astype(jnp.bfloat16)
    returned = lax.all_to_all(back, "seq", split_axis=2, concat_axis=1, tiled=True)
    flat_real = returned[0].reshape(freq_rows, columns_each * channels)
    flat_imag = returned[1].reshape(freq_rows, columns_each * channels)
    conv = jnp.dot(cos_first.T, flat_real, preferred_element_type=jnp.float32) - jnp.dot(
        sin_first.T, flat_imag, preferred_element_type=jnp.float32
    )
    conv = (
        (conv * (1.0 / fft_length)).reshape(seq_count, columns_each, channels).astype(jnp.bfloat16)
    )
    conv_rows = lax.all_to_all(conv, "seq", split_axis=0, concat_axis=1, tiled=True)[0]
    gated = (
        gate_q.astype(jnp.float32) * (widened(conv_rows) + skip[None, :] * widened(drive))
    ).astype(jnp.bfloat16)
    partial_value = lax.dot_general(
        gated, out_weight, (((1,), (1,)), ((), ())), preferred_element_type=jnp.float32
    )
    return lax.psum_scatter(
        partial_value.astype(jnp.bfloat16), "ch", scatter_dimension=1, tiled=True
    )


def solution(mesh):
    placed = (
        P(("grp", "seq"), "ch"),
        P(("grp", "seq"), "ch"),
        P(("grp", "seq"), "ch"),
        P("seq", "ch"),
        P("ch"),
        P(None, "seq", None, "ch"),
        P("seq", "ch"),
    )
    sizes = mesh.shape
    body = planes if (sizes["grp"], sizes["seq"], sizes["ch"]) == (2, 8, 2) else shards
    return jax.shard_map(
        body, mesh=mesh, in_specs=placed, out_specs=P(("grp", "seq"), "ch"), check_vma=False
    )
```

```python
import functools
import math

import jax
import jax.numpy as jnp
import numpy as np
from jax import lax
from jax.experimental import pallas as pl
from jax.experimental.pallas import tpu as pltpu
from jax.sharding import PartitionSpec as P

AXES = ("grp", "seq", "ch")
BF16 = jnp.bfloat16
F32 = jnp.float32


def angles(count, first, second):
    phase = 2.0 * math.pi / count * (first[:, None] * second[None, :] % count).astype(jnp.float32)
    return (jnp.cos(phase), jnp.sin(phase))


def widened(values):
    return lax.optimization_barrier(values).astype(jnp.float32)


def dot(a, b):
    return jnp.dot(a, b, preferred_element_type=F32)


def dot_t(a, b):
    return lax.dot_general(a, b, (((1,), (1,)), ((), ())), preferred_element_type=F32)


def in_vmem(kernel, out_shape, scratch=(), flops=0, moved=0):
    def call(*operands):
        specs = [pl.BlockSpec(memory_space=pltpu.VMEM)] * len(operands)
        return pl.pallas_call(
            kernel,
            out_shape=out_shape,
            in_specs=specs,
            out_specs=jax.tree.map(lambda _: pl.BlockSpec(memory_space=pltpu.VMEM), out_shape),
            scratch_shapes=list(scratch),
            compiler_params=pltpu.CompilerParams(vmem_limit_bytes=20 * 1024 * 1024),
            cost_estimate=pl.CostEstimate(flops=flops, bytes_accessed=moved, transcendentals=0),
        )(*operands)

    return call


def place():
    y, s, c = (lax.axis_index(a) for a in AXES)
    return y, lax.rem(s, 2), lax.div(s, 2), c


def low_lanes(shape):
    return lax.broadcasted_iota(jnp.int32, shape, len(shape) - 1) < 64


def half_turn(values):
    return pltpu.roll(values, 64, values.ndim - 1)


def both(first, second, low):
    return (
        jnp.where(low, first, half_turn(second)).astype(BF16),
        jnp.where(low, half_turn(first), second).astype(BF16),
    )


def quarter(p):
    y, x, _, _ = place()
    row = 1 - y if p // 2 else y
    column = 1 - x if p % 2 else x
    return pl.ds(pl.multiple_of(row * 512 + column * 256, 256), 256)


def copied(moves, sem):
    copies = [pltpu.make_async_copy(a, b, sem.at[i]) for i, (a, b) in enumerate(moves)]
    for copy in copies:
        copy.start()
    for copy in copies:
        copy.wait()


def cut_first(value, own_v, sem):
    y, _, _, _ = place()
    copied([(value.at[:, pl.ds(pl.multiple_of(y * 512, 512), 512)], own_v)], sem)


def cut_messages(tokens, key, query, out, filt, after, m1, m2, m3, own, own_o, away_o, away_f, sem):
    _, x, _, _ = place()
    moves = [(filt.at[:, :, :, quarter(1)], away_f)]
    for p, message in enumerate((own, m1, m2, m3)):
        column = 1 - x if p % 2 else x
        for i in range(2):
            lanes = pl.ds(pl.multiple_of(i * 512 + column * 256, 256), 256)
            moves.append((tokens.at[:, lanes], message.at[:, pl.ds(512 + i * 256, 256)]))
        moves.append((key.at[:, quarter(p)], message.at[:, pl.ds(0, 256)]))
        moves.append((query.at[:, quarter(p)], message.at[:, pl.ds(256, 256)]))
    moves += [(out.at[:, quarter(0)], own_o), (out.at[:, quarter(1)], away_o)]
    copied(moves, sem)


def copy_kernel(kernel, out_shape):
    def call(*operands):
        return pl.pallas_call(
            kernel,
            out_shape=out_shape,
            in_specs=[pl.BlockSpec(memory_space=pltpu.MemorySpace.HBM)] * len(operands),
            out_specs=[pl.BlockSpec(memory_space=pltpu.VMEM)] * len(out_shape),
            scratch_shapes=[pltpu.SemaphoreType.DMA((19,))],
            compiler_params=pltpu.CompilerParams(vmem_limit_bytes=61 * 1024 * 1024),
        )(*operands)

    return call


def pack_filter(filt, near, *refs):
    y, x, z, _ = place()
    packed, outs = refs[4], refs[:4]
    low = low_lanes((128, 128))
    for k in range(2):
        for j in range(2):
            base = pl.multiple_of(y * 512 + x * 256 + j * 128, 128)
            for part in range(2):
                if k:
                    pair = [near[part, i, :, pl.ds(j * 128, 128)].astype(F32) for i in range(2)]
                else:
                    pair = [filt[part, i, :, pl.ds(base, 128)].astype(F32) for i in range(2)]
                one, two = both(*pair, low)
                packed[2 * j, k, part] = one
                packed[2 * j + 1, k, part] = two
    for r in range(4):
        outs[r][...] = packed[lax.rem(z + r, 4)]


def join_tokens(*refs):
    for p, message in enumerate(refs[:4]):
        refs[4][pl.ds(p * 128, 128), :] = message[:, pl.ds(512, 512)]


def value_kernel(mine, other, w0, w1, w2, w3, keep, give, acc):
    _, x, z, c = place()
    for r, piece in enumerate((w0, w1, w2, w3)):
        owner = lax.rem(z - r + 4, 4)
        lanes = pl.ds(pl.multiple_of(lax.rem(owner, 2) * 256, 256), 256)

        @pl.when(lax.div(owner, 2) == c)
        def _():
            term = dot(mine[:, lanes], piece[...])
            acc[...] = acc[...] + term if r else term

        @pl.when(lax.div(owner, 2) != c)
        def _():
            term = dot(other[:, lanes], piece[...])
            acc[...] = acc[...] + term if r else term

    keep[...] = acc[:, pl.ds(pl.multiple_of(x * 256, 256), 256)]
    away = pl.ds(pl.multiple_of(256 - x * 256, 256), 256)
    for p in range(4):
        give[pl.ds(p * 128, 128), :] = acc[pl.ds((p ^ 1) * 128, 128), away].astype(BF16)


def drive_kernel(keep, taken, g0, g1, g2, g3, skip, direct, o0, o1, o2, o3, drive, packed):
    _, _, z, _ = place()
    for p, gate in enumerate((g0, g1, g2, g3)):
        rows = pl.ds(p * 128, 128)
        value = (keep[rows, :] + taken[rows, :].astype(F32)).astype(BF16).astype(F32)
        held = (gate[:, 0:256].astype(F32) * value).astype(BF16)
        drive[rows, :] = held
        direct[rows, :] = skip[:, quarter(0)] * held.astype(F32)
    low = low_lanes((256, 128))
    for j in range(2):
        lanes = pl.ds(j * 128, 128)
        first = drive[pl.ds(0, 256), lanes].astype(F32)
        second = drive[pl.ds(256, 256), lanes].astype(F32)
        packed[2 * j], packed[2 * j + 1] = both(first, second, low)
    for r, out in enumerate((o0, o1, o2, o3)):
        out[...] = packed[lax.rem(z + r, 4)]


def add(a, b):
    return b if a is None else a if b is None else a + b


def sub(a, b):
    return a if b is None else -b if a is None else a - b


def scaled(a, s):
    if a is None or abs(s) < 1e-9:
        return None
    if abs(s - 1) < 1e-9:
        return a
    if abs(s + 1) < 1e-9:
        return -a
    return a * np.float32(s)


def cmul(a, angle):
    co, si = math.cos(angle), math.sin(angle)
    return (sub(scaled(a[0], co), scaled(a[1], si)), add(scaled(a[0], si), scaled(a[1], co)))


def cadd(a, b):
    return (add(a[0], b[0]), add(a[1], b[1]))


def conj(a):
    return (a[0], None if a[1] is None else -a[1])


def short_transform(values, count, rows):
    if len(values) == 1:
        return [(values[0], None)] * rows
    half = count // 2
    need = half // 2 + 1
    even = short_transform(values[0::2], half, need)
    odd = short_transform(values[1::2], half, need)

    def at(t, k):
        k %= half
        return t[k] if k < need else conj(t[half - k])

    return [cadd(at(even, k), cmul(at(odd, k), -2 * math.pi * k / count)) for k in range(rows)]


def conv_kernel(*refs):
    drives, filters, (table, table_t) = refs[:4], refs[4:8], refs[8:10]
    outs, (data, filt, first, sums) = refs[10:14], refs[14:]
    _, x, z, _ = place()
    for r, block in enumerate(drives):
        base = 2 * lax.rem(z - r + 4, 4)
        filt[base + x] = filters[r][0]
        filt[base + 1 - x] = filters[r][1]
        data[base + x] = block[pl.ds(0, 128), :]
        data[base + 1 - x] = block[pl.ds(128, 128), :]
    for i in range(8):
        rows = pl.ds(16 * i, 16)
        values = [data[a, rows, :].astype(F32) for a in range(8)]
        spectrum = short_transform(values, 16, 9)
        for k in range(9):
            re, im = spectrum[k]
            if im is None:
                im = jnp.zeros_like(re)
            first[k, rows, 0:128] = re.astype(BF16)
            first[k, rows, 128:256] = im.astype(BF16)
            if 0 < k < 8:
                first[16 - k, rows, 0:128] = re.astype(BF16)
                first[16 - k, rows, 128:256] = (-im).astype(BF16)
    low = low_lanes((128, 128))

    def back(k):
        four = dot(table[k], first[k])
        re = four[:128, :128] + four[128:, 128:]
        im = four[:128, 128:] - four[128:, :128]
        pair = [filt[k // 2, part].astype(F32) for part in range(2)]
        if k % 2 == 0:
            fr, fi = [jnp.where(low, f, half_turn(f)) for f in pair]
        else:
            fr, fi = [jnp.where(low, half_turn(f), f) for f in pair]
        product = jnp.concatenate([re * fr - im * fi, re * fi + im * fr], axis=1).astype(BF16)
        four = dot(table_t[k], product)
        return four[:128, :128] - four[128:, 128:], four[128:, :128] + four[:128, 128:]

    sums[0, pl.ds(0, 128)] = back(0)[0]
    sums[8, pl.ds(0, 128)] = back(8)[0]
    for k in range(1, 8):
        one, two = back(k), back(16 - k)
        sums[k, pl.ds(0, 128)] = one[0] + two[0]
        sums[k, pl.ds(128, 128)] = one[1] - two[1]
    for i in range(16):
        rows, below = pl.ds(8 * i, 8), pl.ds(128 + 8 * i, 8)
        scale = 1.0 / 2048
        re = [sums[k, rows, :] * scale for k in range(9)]
        im = [None] + [sums[k, below, :] * scale for k in range(1, 8)] + [None]
        for a in range(5):
            groups = [None] * 4
            for k in range(9):
                ang = 2 * math.pi * (k * a % 16) / 16
                groups[k % 2] = add(groups[k % 2], scaled(re[k], math.cos(ang)))
                groups[2 + k % 2] = sub(groups[2 + k % 2], scaled(im[k], math.sin(ang)))
            ec, oc, es, os = groups
            data[a, rows, :] = add(add(ec, oc), add(es, os)).astype(BF16)
            if 0 < a < 4:
                data[8 - a, rows, :] = sub(sub(add(ec, os), oc), es).astype(BF16)
    for r, out in enumerate(outs):
        base = 2 * lax.rem(z + r, 4)
        out[pl.ds(0, 128), :] = data[base + x]
        out[pl.ds(128, 128), :] = data[base + 1 - x]


def gate_kernel(e0, e1, e2, e3, direct, g0, g1, g2, g3, gated, conv):
    _, _, z, _ = place()
    for r, block in enumerate((e0, e1, e2, e3)):
        conv[lax.rem(z - r + 4, 4)] = block[...]
    low = low_lanes((256, 128))
    for j in range(2):
        lanes = pl.ds(j * 128, 128)
        even, odd = conv[2 * j].astype(F32), conv[2 * j + 1].astype(F32)
        parts = (jnp.where(low, even, half_turn(odd)), jnp.where(low, half_turn(even), odd))
        for p, gate in enumerate((g0, g1, g2, g3)):
            rows = pl.ds(p * 128, 128)
            own = parts[p // 2][(p % 2) * 128 : (p % 2) * 128 + 128]
            query = gate[:, pl.ds(256 + j * 128, 128)].astype(F32)
            gated[rows, lanes] = (query * (own + direct[rows, lanes])).astype(BF16)


def sort_weight(*refs):
    pieces, keep, give = refs[:4], refs[4], refs[5]
    _, x, z, c = place()
    for r in range(4):
        owner = lax.rem(z - r + 4, 4)
        for k in range(2):
            to = 2 * lax.rem(owner, 2) + (1 - x if k else x)

            @pl.when(owner // 2 == c)
            def _():
                keep[to] = pieces[r][k]

            @pl.when(owner // 2 != c)
            def _():
                give[to] = pieces[r][k]


def out_kernel(gated, other, keep, theirs, own, *sends):
    for p in (3, 2, 1, 0):
        rows = pl.ds(p * 128, 128)
        for i in range(4):
            total = dot_t(gated[rows, :], keep[i]) + dot_t(other[rows, :], theirs[i])
            lanes = pl.ds(i * 256, 256)
            if p == 0:
                own[:, lanes] = total
            else:
                sends[p - 1][:, lanes] = total.astype(BF16)


def tables():
    k = np.arange(16)[:, None, None] + 16 * np.arange(128)[None, :, None]
    phase = 2 * np.pi / 2048 * (k * np.arange(128)[None, None, :] % 2048)
    co, si = np.cos(phase), np.sin(phase)
    back = np.concatenate([co.transpose(0, 2, 1), si.transpose(0, 2, 1)], 1)
    return np.concatenate([co, si], 1).astype(jnp.bfloat16), back.astype(jnp.bfloat16)


def planes(tokens, gate_q, gate_k, w_value, skip, filter_spectrum, w_out):
    seq, deep = 8, 4

    def permute(values, move):
        pairs = []
        for g in range(2):
            for i in range(seq):
                for k in range(2):
                    g2, z2, x2, k2 = move(g, i // 2, i % 2, k)
                    pairs.append(((g * seq + i) * 2 + k, (g2 * seq + z2 * 2 + x2) * 2 + k2))
        return lax.ppermute(values, AXES, pairs)

    def to_x(values):
        return permute(values, lambda g, z, x, k: (g, z, 1 - x, k))

    def to_core(values):
        return permute(values, lambda g, z, x, k: (g, z, x, 1 - k))

    def to_z(values, r):
        return permute(values, lambda g, z, x, k: (g, (z + r) % deep, x, k))

    def to_peer(values, p):
        return permute(values, lambda g, z, x, k: (g ^ (p // 2), z, x ^ (p % 2), k))

    def after(values, *done):
        return lax.optimization_barrier((values,) + done)[0]

    shape = jax.ShapeDtypeStruct
    block, square = shape((256, 128), BF16), shape((256, 256), BF16)
    (own_v,) = copy_kernel(cut_first, [shape((256, 512), BF16)])(w_value)
    laid = [shape((128, 1024), BF16)] * 4 + [square] * 2 + [shape((2, 2, 128, 256), BF16)]
    *messages, own, own_o, away_o, away_f = copy_kernel(cut_messages, laid)(
        tokens, gate_k, gate_q, w_out, filter_spectrum, own_v
    )
    near = to_x(away_f)
    received = [to_peer(messages[p - 1], p) for p in (1, 2, 3)]
    plane = [own] + received
    filters = in_vmem(
        pack_filter,
        [shape((2, 2, 128, 128), BF16)] * 4,
        [pltpu.VMEM((4, 2, 2, 128, 128), BF16)],
        moved=1 << 20,
    )(filter_spectrum, near)
    filters = [filters[0]] + [to_z(filters[r], r) for r in (1, 2, 3)]
    v1 = to_z(own_v, 1)
    v2 = to_z(after(v1, received[0], received[1]), 1)
    mine = in_vmem(join_tokens, shape((512, 512), BF16), moved=1 << 20)(after(own, v2), *received)
    v3 = to_z(after(v2, mine), 1)
    other = to_core(mine)
    got_o = to_x(after(away_o, v2))
    pair = jnp.stack([own_o, got_o])
    hops = [pair, to_z(after(pair, v3), 1)]
    keep, give = in_vmem(
        value_kernel,
        [shape((512, 256), F32), shape((512, 256), BF16)],
        [pltpu.VMEM((512, 512), F32)],
        flops=1 << 29,
        moved=2 << 20,
    )(after(mine, *filters[1:]), other, own_v, v1, v2, v3)
    drive, *sends = in_vmem(
        drive_kernel,
        [shape((512, 256), F32)] + [block] * 4,
        [pltpu.VMEM((512, 256), BF16), pltpu.VMEM((4, 256, 128), BF16)],
        moved=2 << 20,
    )(keep, to_x(give), *plane, skip[None, :])
    columns = [sends[0]] + [to_z(sends[r], r) for r in (1, 2, 3)]
    hops.append(to_z(after(hops[1], drive), 1))
    hops.append(to_z(after(hops[2], *columns[1:]), 1))
    table, table_t = tables()
    sends = in_vmem(
        conv_kernel,
        [block] * 4,
        [
            pltpu.VMEM((8, 128, 128), BF16),
            pltpu.VMEM((8, 2, 128, 128), BF16),
            pltpu.VMEM((16, 128, 256), BF16),
            pltpu.VMEM((9, 256, 128), F32),
        ],
        flops=1 << 30,
        moved=5 << 20,
    )(*columns, *filters, table, table_t)
    rows = [sends[0]] + [to_z(sends[r], r) for r in (1, 2, 3)]

    hops[3] = after(hops[3], *rows[1:])
    quad = shape((4, 256, 256), BF16)
    keep, give = in_vmem(sort_weight, [quad] * 2, moved=2 << 20)(*hops)
    theirs = to_core(give)
    gated = in_vmem(
        gate_kernel, shape((512, 256), BF16), [pltpu.VMEM((4, 256, 128), BF16)], moved=1 << 20
    )(*rows, drive, *plane)
    gated_other = to_core(gated)
    own, *sends = in_vmem(
        out_kernel,
        [shape((128, 1024), F32)] + [shape((128, 1024), BF16)] * 3,
        flops=1 << 30,
        moved=4 << 20,
    )(gated, gated_other, keep, theirs)
    total = own
    for p in (3, 2, 1):
        total = total + to_peer(sends[p - 1], p).astype(F32)
    return total.astype(BF16)


def shards(tokens, gate_q, gate_k, w_value, skip, filter_spectrum, w_out):
    seq_count = lax.axis_size("seq")
    position = lax.axis_index("seq")
    length_b = tokens.shape[0]
    columns_each = length_b // seq_count
    freq_rows = 2 * seq_count
    freqs_each = freq_rows // seq_count
    fft_length = freq_rows * length_b
    features = lax.all_gather(tokens, "ch", axis=1, tiled=True)
    value_weight, out_weight = (
        lax.all_gather(w_value, "seq", axis=0, tiled=True),
        lax.all_gather(w_out, "seq", axis=0, tiled=True),
    )
    value = jnp.dot(features, value_weight, preferred_element_type=jnp.float32)
    value = value.astype(jnp.bfloat16)
    drive = (gate_k.astype(jnp.float32) * widened(value)).astype(jnp.bfloat16)
    channels = drive.shape[1]
    columns = lax.all_to_all(drive[None], "seq", split_axis=1, concat_axis=0, tiled=True)
    index_rows = jnp.arange(freq_rows, dtype=jnp.int32)
    index_seq = jnp.arange(seq_count, dtype=jnp.int32)
    index_b = jnp.arange(length_b, dtype=jnp.int32)
    cos_first, sin_first = angles(freq_rows, index_rows, index_seq)
    cos_first = cos_first.astype(jnp.bfloat16)
    sin_first = sin_first.astype(jnp.bfloat16)
    flattened = columns.reshape(seq_count, columns_each * channels)
    real_part = jnp.dot(cos_first, flattened, preferred_element_type=jnp.float32)
    imag_part = jnp.dot(-sin_first, flattened, preferred_element_type=jnp.float32)
    real_part = real_part.reshape(freq_rows, columns_each, channels)
    imag_part = imag_part.reshape(freq_rows, columns_each, channels)
    mine_b = position * columns_each + jnp.arange(columns_each, dtype=jnp.int32)
    twist_cos, twist_sin = angles(fft_length, index_rows, mine_b)
    twist_cos = twist_cos[:, :, None]
    twist_sin = twist_sin[:, :, None]
    section = jnp.stack(
        [
            real_part * twist_cos + imag_part * twist_sin,
            imag_part * twist_cos - real_part * twist_sin,
        ]
    ).astype(jnp.bfloat16)
    spectral = lax.all_to_all(section, "seq", split_axis=1, concat_axis=2, tiled=True)
    cos_seq, sin_seq = angles(length_b, index_b, index_b)
    cos_seq = cos_seq.astype(jnp.bfloat16)
    sin_seq = sin_seq.astype(jnp.bfloat16)
    spectrum_real = jnp.einsum(
        "qb,kbc->kqc", cos_seq, spectral[0], preferred_element_type=jnp.float32
    ) + jnp.einsum("qb,kbc->kqc", sin_seq, spectral[1], preferred_element_type=jnp.float32)
    spectrum_imag = jnp.einsum(
        "qb,kbc->kqc", cos_seq, spectral[1], preferred_element_type=jnp.float32
    ) - jnp.einsum("qb,kbc->kqc", sin_seq, spectral[0], preferred_element_type=jnp.float32)
    filter_real = filter_spectrum[0].astype(jnp.float32)
    filter_imag = filter_spectrum[1].astype(jnp.float32)
    product = jnp.stack(
        [
            spectrum_real * filter_real - spectrum_imag * filter_imag,
            spectrum_real * filter_imag + spectrum_imag * filter_real,
        ]
    ).astype(jnp.bfloat16)
    inverse_real = jnp.einsum(
        "qb,kqc->kbc", cos_seq, product[0], preferred_element_type=jnp.float32
    ) - jnp.einsum("qb,kqc->kbc", sin_seq, product[1], preferred_element_type=jnp.float32)
    inverse_imag = jnp.einsum(
        "qb,kqc->kbc", sin_seq, product[0], preferred_element_type=jnp.float32
    ) + jnp.einsum("qb,kqc->kbc", cos_seq, product[1], preferred_element_type=jnp.float32)
    mine_k = position * freqs_each + jnp.arange(freqs_each, dtype=jnp.int32)
    back_cos, back_sin = angles(fft_length, mine_k, index_b)
    back_cos = back_cos[:, :, None]
    back_sin = back_sin[:, :, None]
    back = jnp.stack(
        [
            inverse_real * back_cos - inverse_imag * back_sin,
            inverse_real * back_sin + inverse_imag * back_cos,
        ]
    ).astype(jnp.bfloat16)
    returned = lax.all_to_all(back, "seq", split_axis=2, concat_axis=1, tiled=True)
    flat_real = returned[0].reshape(freq_rows, columns_each * channels)
    flat_imag = returned[1].reshape(freq_rows, columns_each * channels)
    conv = jnp.dot(cos_first.T, flat_real, preferred_element_type=jnp.float32) - jnp.dot(
        sin_first.T, flat_imag, preferred_element_type=jnp.float32
    )
    conv = (
        (conv * (1.0 / fft_length)).reshape(seq_count, columns_each, channels).astype(jnp.bfloat16)
    )
    conv_rows = lax.all_to_all(conv, "seq", split_axis=0, concat_axis=1, tiled=True)[0]
    gated = (
        gate_q.astype(jnp.float32) * (widened(conv_rows) + skip[None, :] * widened(drive))
    ).astype(jnp.bfloat16)
    partial_value = lax.dot_general(
        gated, out_weight, (((1,), (1,)), ((), ())), preferred_element_type=jnp.float32
    )
    return lax.psum_scatter(
        partial_value.astype(jnp.bfloat16), "ch", scatter_dimension=1, tiled=True
    )


def solution(mesh):
    placed = (
        P(("grp", "seq"), "ch"),
        P(("grp", "seq"), "ch"),
        P(("grp", "seq"), "ch"),
        P("seq", "ch"),
        P("ch"),
        P(None, "seq", None, "ch"),
        P("seq", "ch"),
    )
    sizes = mesh.shape
    body = planes if (sizes["grp"], sizes["seq"], sizes["ch"]) == (2, 8, 2) else shards
    return jax.shard_map(
        body, mesh=mesh, in_specs=placed, out_specs=P(("grp", "seq"), "ch"), check_vma=False
    )
```

```python
import functools
import math

import jax
import jax.numpy as jnp
import numpy as np
from jax import lax
from jax.experimental import pallas as pl
from jax.experimental.pallas import tpu as pltpu
from jax.sharding import PartitionSpec as P

AXES = ("grp", "seq", "ch")
BF16 = jnp.bfloat16
F32 = jnp.float32


def angles(count, first, second):
    phase = 2.0 * math.pi / count * (first[:, None] * second[None, :] % count).astype(jnp.float32)
    return (jnp.cos(phase), jnp.sin(phase))


def widened(values):
    return lax.optimization_barrier(values).astype(jnp.float32)


def dot(a, b):
    return jnp.dot(a, b, preferred_element_type=F32)


def dot_t(a, b):
    return lax.dot_general(a, b, (((1,), (1,)), ((), ())), preferred_element_type=F32)


def in_vmem(kernel, out_shape, scratch=(), flops=0, moved=0):
    def call(*operands):
        specs = [pl.BlockSpec(memory_space=pltpu.VMEM)] * len(operands)
        return pl.pallas_call(
            kernel,
            out_shape=out_shape,
            in_specs=specs,
            out_specs=jax.tree.map(lambda _: pl.BlockSpec(memory_space=pltpu.VMEM), out_shape),
            scratch_shapes=list(scratch),
            compiler_params=pltpu.CompilerParams(vmem_limit_bytes=20 * 1024 * 1024),
            cost_estimate=pl.CostEstimate(flops=flops, bytes_accessed=moved, transcendentals=0),
        )(*operands)

    return call


def place():
    y, s, c = (lax.axis_index(a) for a in AXES)
    return y, lax.rem(s, 2), lax.div(s, 2), c


def low_lanes(shape):
    return lax.broadcasted_iota(jnp.int32, shape, len(shape) - 1) < 64


def half_turn(values):
    return pltpu.roll(values, 64, values.ndim - 1)


def both(first, second, low):
    return (
        jnp.where(low, first, half_turn(second)).astype(BF16),
        jnp.where(low, half_turn(first), second).astype(BF16),
    )


def quarter(p):
    y, x, _, _ = place()
    row = 1 - y if p // 2 else y
    column = 1 - x if p % 2 else x
    return pl.ds(pl.multiple_of(row * 512 + column * 256, 256), 256)


def copied(moves, sem):
    copies = [pltpu.make_async_copy(a, b, sem.at[i]) for i, (a, b) in enumerate(moves)]
    for copy in copies:
        copy.start()
    for copy in copies:
        copy.wait()


def cut_first(value, own_v, sem):
    y, _, _, _ = place()
    copied([(value.at[:, pl.ds(pl.multiple_of(y * 512, 512), 512)], own_v)], sem)


def cut_messages(tokens, key, query, out, filt, after, m1, m2, m3, own, own_o, away_o, away_f, sem):
    _, x, _, _ = place()
    moves = [(filt.at[:, :, :, quarter(1)], away_f)]
    for p, message in enumerate((own, m1, m2, m3)):
        column = 1 - x if p % 2 else x
        for i in range(2):
            lanes = pl.ds(pl.multiple_of(i * 512 + column * 256, 256), 256)
            moves.append((tokens.at[:, lanes], message.at[:, pl.ds(512 + i * 256, 256)]))
        moves.append((key.at[:, quarter(p)], message.at[:, pl.ds(0, 256)]))
        moves.append((query.at[:, quarter(p)], message.at[:, pl.ds(256, 256)]))
    moves += [(out.at[:, quarter(0)], own_o), (out.at[:, quarter(1)], away_o)]
    copied(moves, sem)


def copy_kernel(kernel, out_shape):
    def call(*operands):
        return pl.pallas_call(
            kernel,
            out_shape=out_shape,
            in_specs=[pl.BlockSpec(memory_space=pltpu.MemorySpace.HBM)] * len(operands),
            out_specs=[pl.BlockSpec(memory_space=pltpu.VMEM)] * len(out_shape),
            scratch_shapes=[pltpu.SemaphoreType.DMA((19,))],
            compiler_params=pltpu.CompilerParams(vmem_limit_bytes=61 * 1024 * 1024),
        )(*operands)

    return call


def pack_filter(filt, near, *refs):
    y, x, z, _ = place()
    packed, outs = refs[4], refs[:4]
    low = low_lanes((128, 128))
    for k in range(2):
        for j in range(2):
            base = pl.multiple_of(y * 512 + x * 256 + j * 128, 128)
            for part in range(2):
                if k:
                    pair = [near[part, i, :, pl.ds(j * 128, 128)].astype(F32) for i in range(2)]
                else:
                    pair = [filt[part, i, :, pl.ds(base, 128)].astype(F32) for i in range(2)]
                one, two = both(*pair, low)
                packed[2 * j, k, part] = one
                packed[2 * j + 1, k, part] = two
    for r in range(4):
        outs[r][...] = packed[lax.rem(z + r, 4)]


def join_tokens(*refs):
    for p, message in enumerate(refs[:4]):
        refs[4][pl.ds(p * 128, 128), :] = message[:, pl.ds(512, 512)]


def value_kernel(mine, other, w0, w1, w2, w3, keep, give, acc):
    _, x, z, c = place()
    for r, piece in enumerate((w0, w1, w2, w3)):
        owner = lax.rem(z - r + 4, 4)
        lanes = pl.ds(pl.multiple_of(lax.rem(owner, 2) * 256, 256), 256)

        @pl.when(lax.div(owner, 2) == c)
        def _():
            term = dot(mine[:, lanes], piece[...])
            acc[...] = acc[...] + term if r else term

        @pl.when(lax.div(owner, 2) != c)
        def _():
            term = dot(other[:, lanes], piece[...])
            acc[...] = acc[...] + term if r else term

    keep[...] = acc[:, pl.ds(pl.multiple_of(x * 256, 256), 256)]
    away = pl.ds(pl.multiple_of(256 - x * 256, 256), 256)
    for p in range(4):
        give[pl.ds(p * 128, 128), :] = acc[pl.ds((p ^ 1) * 128, 128), away].astype(BF16)


def drive_kernel(keep, taken, g0, g1, g2, g3, skip, direct, o0, o1, o2, o3, drive, packed):
    _, _, z, _ = place()
    for p, gate in enumerate((g0, g1, g2, g3)):
        rows = pl.ds(p * 128, 128)
        value = (keep[rows, :] + taken[rows, :].astype(F32)).astype(BF16).astype(F32)
        held = (gate[:, 0:256].astype(F32) * value).astype(BF16)
        drive[rows, :] = held
        direct[rows, :] = skip[:, quarter(0)] * held.astype(F32)
    low = low_lanes((256, 128))
    for j in range(2):
        lanes = pl.ds(j * 128, 128)
        first = drive[pl.ds(0, 256), lanes].astype(F32)
        second = drive[pl.ds(256, 256), lanes].astype(F32)
        packed[2 * j], packed[2 * j + 1] = both(first, second, low)
    for r, out in enumerate((o0, o1, o2, o3)):
        out[...] = packed[lax.rem(z + r, 4)]


def add(a, b):
    return b if a is None else a if b is None else a + b


def sub(a, b):
    return a if b is None else -b if a is None else a - b


def scaled(a, s):
    if a is None or abs(s) < 1e-9:
        return None
    if abs(s - 1) < 1e-9:
        return a
    if abs(s + 1) < 1e-9:
        return -a
    return a * np.float32(s)


def cmul(a, angle):
    co, si = math.cos(angle), math.sin(angle)
    return (sub(scaled(a[0], co), scaled(a[1], si)), add(scaled(a[0], si), scaled(a[1], co)))


def cadd(a, b):
    return (add(a[0], b[0]), add(a[1], b[1]))


def conj(a):
    return (a[0], None if a[1] is None else -a[1])


def short_transform(values, count, rows):
    if len(values) == 1:
        return [(values[0], None)] * rows
    half = count // 2
    need = half // 2 + 1
    even = short_transform(values[0::2], half, need)
    odd = short_transform(values[1::2], half, need)

    def at(t, k):
        k %= half
        return t[k] if k < need else conj(t[half - k])

    return [cadd(at(even, k), cmul(at(odd, k), -2 * math.pi * k / count)) for k in range(rows)]


def conv_kernel(*refs):
    drives, filters, (table, table_t) = refs[:4], refs[4:8], refs[8:10]
    outs, (data, filt, first, sums) = refs[10:14], refs[14:]
    _, x, z, _ = place()
    for r, block in enumerate(drives):
        base = 2 * lax.rem(z - r + 4, 4)
        filt[base + x] = filters[r][0]
        filt[base + 1 - x] = filters[r][1]
        data[base + x] = block[pl.ds(0, 128), :]
        data[base + 1 - x] = block[pl.ds(128, 128), :]
    for i in range(8):
        rows = pl.ds(16 * i, 16)
        values = [data[a, rows, :].astype(F32) for a in range(8)]
        spectrum = short_transform(values, 16, 9)
        for k in range(9):
            re, im = spectrum[k]
            if im is None:
                im = jnp.zeros_like(re)
            first[k, rows, 0:128] = re.astype(BF16)
            first[k, rows, 128:256] = im.astype(BF16)
            if 0 < k < 8:
                first[16 - k, rows, 0:128] = re.astype(BF16)
                first[16 - k, rows, 128:256] = (-im).astype(BF16)
    low = low_lanes((128, 128))

    def back(k):
        four = dot(table[k], first[k])
        re = four[:128, :128] + four[128:, 128:]
        im = four[:128, 128:] - four[128:, :128]
        pair = [filt[k // 2, part].astype(F32) for part in range(2)]
        if k % 2 == 0:
            fr, fi = [jnp.where(low, f, half_turn(f)) for f in pair]
        else:
            fr, fi = [jnp.where(low, half_turn(f), f) for f in pair]
        product = jnp.concatenate([re * fr - im * fi, re * fi + im * fr], axis=1).astype(BF16)
        four = dot(table_t[k], product)
        return four[:128, :128] - four[128:, 128:], four[128:, :128] + four[:128, 128:]

    sums[0, pl.ds(0, 128)] = back(0)[0]
    sums[8, pl.ds(0, 128)] = back(8)[0]
    for k in range(1, 8):
        one, two = back(k), back(16 - k)
        sums[k, pl.ds(0, 128)] = one[0] + two[0]
        sums[k, pl.ds(128, 128)] = one[1] - two[1]
    for i in range(16):
        rows, below = pl.ds(8 * i, 8), pl.ds(128 + 8 * i, 8)
        scale = 1.0 / 2048
        re = [sums[k, rows, :] * scale for k in range(9)]
        im = [None] + [sums[k, below, :] * scale for k in range(1, 8)] + [None]
        for a in range(5):
            groups = [None] * 4
            for k in range(9):
                ang = 2 * math.pi * (k * a % 16) / 16
                groups[k % 2] = add(groups[k % 2], scaled(re[k], math.cos(ang)))
                groups[2 + k % 2] = sub(groups[2 + k % 2], scaled(im[k], math.sin(ang)))
            ec, oc, es, os = groups
            data[a, rows, :] = add(add(ec, oc), add(es, os)).astype(BF16)
            if 0 < a < 4:
                data[8 - a, rows, :] = sub(sub(add(ec, os), oc), es).astype(BF16)
    for r, out in enumerate(outs):
        base = 2 * lax.rem(z + r, 4)
        out[pl.ds(0, 128), :] = data[base + x]
        out[pl.ds(128, 128), :] = data[base + 1 - x]


def gate_kernel(e0, e1, e2, e3, direct, g0, g1, g2, g3, gated, conv):
    _, _, z, _ = place()
    for r, block in enumerate((e0, e1, e2, e3)):
        conv[lax.rem(z - r + 4, 4)] = block[...]
    low = low_lanes((256, 128))
    for j in range(2):
        lanes = pl.ds(j * 128, 128)
        even, odd = conv[2 * j].astype(F32), conv[2 * j + 1].astype(F32)
        parts = (jnp.where(low, even, half_turn(odd)), jnp.where(low, half_turn(even), odd))
        for p, gate in enumerate((g0, g1, g2, g3)):
            rows = pl.ds(p * 128, 128)
            own = parts[p // 2][(p % 2) * 128 : (p % 2) * 128 + 128]
            query = gate[:, pl.ds(256 + j * 128, 128)].astype(F32)
            gated[rows, lanes] = (query * (own + direct[rows, lanes])).astype(BF16)


def sort_weight(*refs):
    pieces, keep, give = refs[:8], refs[8], refs[9]
    _, x, z, c = place()
    for r in range(4):
        owner = lax.rem(z - r + 4, 4)
        for k in range(2):
            to = 2 * lax.rem(owner, 2) + (1 - x if k else x)

            @pl.when(owner // 2 == c)
            def _():
                keep[to] = pieces[2 * r + k][...]

            @pl.when(owner // 2 != c)
            def _():
                give[to] = pieces[2 * r + k][...]


def out_kernel(gated, other, keep, theirs, own, *sends):
    for p in (3, 2, 1, 0):
        rows = pl.ds(p * 128, 128)
        for i in range(4):
            total = dot_t(gated[rows, :], keep[i]) + dot_t(other[rows, :], theirs[i])
            lanes = pl.ds(i * 256, 256)
            if p == 0:
                own[:, lanes] = total
            else:
                sends[p - 1][:, lanes] = total.astype(BF16)


def tables():
    k = np.arange(16)[:, None, None] + 16 * np.arange(128)[None, :, None]
    phase = 2 * np.pi / 2048 * (k * np.arange(128)[None, None, :] % 2048)
    co, si = np.cos(phase), np.sin(phase)
    back = np.concatenate([co.transpose(0, 2, 1), si.transpose(0, 2, 1)], 1)
    return np.concatenate([co, si], 1).astype(jnp.bfloat16), back.astype(jnp.bfloat16)


def planes(tokens, gate_q, gate_k, w_value, skip, filter_spectrum, w_out):
    seq, deep = 8, 4

    def permute(values, move):
        pairs = []
        for g in range(2):
            for i in range(seq):
                for k in range(2):
                    g2, z2, x2, k2 = move(g, i // 2, i % 2, k)
                    pairs.append(((g * seq + i) * 2 + k, (g2 * seq + z2 * 2 + x2) * 2 + k2))
        return lax.ppermute(values, AXES, pairs)

    def to_x(values):
        return permute(values, lambda g, z, x, k: (g, z, 1 - x, k))

    def to_core(values):
        return permute(values, lambda g, z, x, k: (g, z, x, 1 - k))

    def to_z(values, r):
        return permute(values, lambda g, z, x, k: (g, (z + r) % deep, x, k))

    def to_peer(values, p):
        return permute(values, lambda g, z, x, k: (g ^ (p // 2), z, x ^ (p % 2), k))

    def after(values, *done):
        return lax.optimization_barrier((values,) + done)[0]

    shape = jax.ShapeDtypeStruct
    block, square = shape((256, 128), BF16), shape((256, 256), BF16)
    (own_v,) = copy_kernel(cut_first, [shape((256, 512), BF16)])(w_value)
    laid = [shape((128, 1024), BF16)] * 4 + [square] * 2 + [shape((2, 2, 128, 256), BF16)]
    *messages, own, own_o, away_o, away_f = copy_kernel(cut_messages, laid)(
        tokens, gate_k, gate_q, w_out, filter_spectrum, own_v
    )
    near = to_x(away_f)
    received = [to_peer(messages[p - 1], p) for p in (1, 2, 3)]
    plane = [own] + received
    filters = in_vmem(
        pack_filter,
        [shape((2, 2, 128, 128), BF16)] * 4,
        [pltpu.VMEM((4, 2, 2, 128, 128), BF16)],
        moved=1 << 20,
    )(filter_spectrum, near)
    filters = [filters[0]] + [to_z(filters[r], r) for r in (1, 2, 3)]
    v1 = to_z(own_v, 1)
    q1 = to_z(own_o, 1)
    v2 = to_z(after(v1, near, received[1], q1), 1)
    q2 = to_z(q1, 1)
    mine = in_vmem(join_tokens, shape((512, 512), BF16), moved=1 << 20)(after(own, v2, q2, *filters[1:]), *received)
    v3 = to_z(after(v2, filters[1]), 1)
    q3 = to_z(q2, 1)
    other = to_core(mine)
    got_o = to_x(after(away_o, v2))
    r1 = to_z(after(got_o, v3), 1)
    keep, give = in_vmem(
        value_kernel,
        [shape((512, 256), F32), shape((512, 256), BF16)],
        [pltpu.VMEM((512, 512), F32)],
        flops=1 << 29,
        moved=2 << 20,
    )(after(mine, q3), other, own_v, v1, v2, v3)
    r2 = to_z(after(r1, keep), 1)
    drive, *sends = in_vmem(
        drive_kernel,
        [shape((512, 256), F32)] + [block] * 4,
        [pltpu.VMEM((512, 256), BF16), pltpu.VMEM((4, 256, 128), BF16)],
        moved=2 << 20,
    )(keep, to_x(give), *plane, skip[None, :])
    columns = [sends[0]] + [to_z(sends[r], r) for r in (1, 2, 3)]
    r3 = to_z(after(r2, *columns[1:]), 1)
    table, table_t = tables()
    sends = in_vmem(
        conv_kernel,
        [block] * 4,
        [
            pltpu.VMEM((8, 128, 128), BF16),
            pltpu.VMEM((8, 2, 128, 128), BF16),
            pltpu.VMEM((16, 128, 256), BF16),
            pltpu.VMEM((9, 256, 128), F32),
        ],
        flops=1 << 30,
        moved=5 << 20,
    )(*columns, *filters, table, table_t)
    rows = [sends[0]] + [to_z(sends[r], r) for r in (1, 2, 3)]

    hops = [own_o, got_o, q1, r1, q2, r2, q3, after(r3, *rows[1:])]
    quad = shape((4, 256, 256), BF16)
    keep, give = in_vmem(sort_weight, [quad] * 2, moved=2 << 20)(*hops)
    theirs = to_core(give)
    gated = in_vmem(
        gate_kernel, shape((512, 256), BF16), [pltpu.VMEM((4, 256, 128), BF16)], moved=1 << 20
    )(*rows, drive, *plane)
    gated_other = to_core(gated)
    own, *sends = in_vmem(
        out_kernel,
        [shape((128, 1024), F32)] + [shape((128, 1024), BF16)] * 3,
        flops=1 << 30,
        moved=4 << 20,
    )(gated, gated_other, keep, theirs)
    total = own
    for p in (3, 2, 1):
        total = total + to_peer(sends[p - 1], p).astype(F32)
    return total.astype(BF16)


def shards(tokens, gate_q, gate_k, w_value, skip, filter_spectrum, w_out):
    seq_count = lax.axis_size("seq")
    position = lax.axis_index("seq")
    length_b = tokens.shape[0]
    columns_each = length_b // seq_count
    freq_rows = 2 * seq_count
    freqs_each = freq_rows // seq_count
    fft_length = freq_rows * length_b
    features = lax.all_gather(tokens, "ch", axis=1, tiled=True)
    value_weight, out_weight = (
        lax.all_gather(w_value, "seq", axis=0, tiled=True),
        lax.all_gather(w_out, "seq", axis=0, tiled=True),
    )
    value = jnp.dot(features, value_weight, preferred_element_type=jnp.float32)
    value = value.astype(jnp.bfloat16)
    drive = (gate_k.astype(jnp.float32) * widened(value)).astype(jnp.bfloat16)
    channels = drive.shape[1]
    columns = lax.all_to_all(drive[None], "seq", split_axis=1, concat_axis=0, tiled=True)
    index_rows = jnp.arange(freq_rows, dtype=jnp.int32)
    index_seq = jnp.arange(seq_count, dtype=jnp.int32)
    index_b = jnp.arange(length_b, dtype=jnp.int32)
    cos_first, sin_first = angles(freq_rows, index_rows, index_seq)
    cos_first = cos_first.astype(jnp.bfloat16)
    sin_first = sin_first.astype(jnp.bfloat16)
    flattened = columns.reshape(seq_count, columns_each * channels)
    real_part = jnp.dot(cos_first, flattened, preferred_element_type=jnp.float32)
    imag_part = jnp.dot(-sin_first, flattened, preferred_element_type=jnp.float32)
    real_part = real_part.reshape(freq_rows, columns_each, channels)
    imag_part = imag_part.reshape(freq_rows, columns_each, channels)
    mine_b = position * columns_each + jnp.arange(columns_each, dtype=jnp.int32)
    twist_cos, twist_sin = angles(fft_length, index_rows, mine_b)
    twist_cos = twist_cos[:, :, None]
    twist_sin = twist_sin[:, :, None]
    section = jnp.stack(
        [
            real_part * twist_cos + imag_part * twist_sin,
            imag_part * twist_cos - real_part * twist_sin,
        ]
    ).astype(jnp.bfloat16)
    spectral = lax.all_to_all(section, "seq", split_axis=1, concat_axis=2, tiled=True)
    cos_seq, sin_seq = angles(length_b, index_b, index_b)
    cos_seq = cos_seq.astype(jnp.bfloat16)
    sin_seq = sin_seq.astype(jnp.bfloat16)
    spectrum_real = jnp.einsum(
        "qb,kbc->kqc", cos_seq, spectral[0], preferred_element_type=jnp.float32
    ) + jnp.einsum("qb,kbc->kqc", sin_seq, spectral[1], preferred_element_type=jnp.float32)
    spectrum_imag = jnp.einsum(
        "qb,kbc->kqc", cos_seq, spectral[1], preferred_element_type=jnp.float32
    ) - jnp.einsum("qb,kbc->kqc", sin_seq, spectral[0], preferred_element_type=jnp.float32)
    filter_real = filter_spectrum[0].astype(jnp.float32)
    filter_imag = filter_spectrum[1].astype(jnp.float32)
    product = jnp.stack(
        [
            spectrum_real * filter_real - spectrum_imag * filter_imag,
            spectrum_real * filter_imag + spectrum_imag * filter_real,
        ]
    ).astype(jnp.bfloat16)
    inverse_real = jnp.einsum(
        "qb,kqc->kbc", cos_seq, product[0], preferred_element_type=jnp.float32
    ) - jnp.einsum("qb,kqc->kbc", sin_seq, product[1], preferred_element_type=jnp.float32)
    inverse_imag = jnp.einsum(
        "qb,kqc->kbc", sin_seq, product[0], preferred_element_type=jnp.float32
    ) + jnp.einsum("qb,kqc->kbc", cos_seq, product[1], preferred_element_type=jnp.float32)
    mine_k = position * freqs_each + jnp.arange(freqs_each, dtype=jnp.int32)
    back_cos, back_sin = angles(fft_length, mine_k, index_b)
    back_cos = back_cos[:, :, None]
    back_sin = back_sin[:, :, None]
    back = jnp.stack(
        [
            inverse_real * back_cos - inverse_imag * back_sin,
            inverse_real * back_sin + inverse_imag * back_cos,
        ]
    ).astype(jnp.bfloat16)
    returned = lax.all_to_all(back, "seq", split_axis=2, concat_axis=1, tiled=True)
    flat_real = returned[0].reshape(freq_rows, columns_each * channels)
    flat_imag = returned[1].reshape(freq_rows, columns_each * channels)
    conv = jnp.dot(cos_first.T, flat_real, preferred_element_type=jnp.float32) - jnp.dot(
        sin_first.T, flat_imag, preferred_element_type=jnp.float32
    )
    conv = (
        (conv * (1.0 / fft_length)).reshape(seq_count, columns_each, channels).astype(jnp.bfloat16)
    )
    conv_rows = lax.all_to_all(conv, "seq", split_axis=0, concat_axis=1, tiled=True)[0]
    gated = (
        gate_q.astype(jnp.float32) * (widened(conv_rows) + skip[None, :] * widened(drive))
    ).astype(jnp.bfloat16)
    partial_value = lax.dot_general(
        gated, out_weight, (((1,), (1,)), ((), ())), preferred_element_type=jnp.float32
    )
    return lax.psum_scatter(
        partial_value.astype(jnp.bfloat16), "ch", scatter_dimension=1, tiled=True
    )


def solution(mesh):
    placed = (
        P(("grp", "seq"), "ch"),
        P(("grp", "seq"), "ch"),
        P(("grp", "seq"), "ch"),
        P("seq", "ch"),
        P("ch"),
        P(None, "seq", None, "ch"),
        P("seq", "ch"),
    )
    sizes = mesh.shape
    body = planes if (sizes["grp"], sizes["seq"], sizes["ch"]) == (2, 8, 2) else shards
    return jax.shard_map(
        body, mesh=mesh, in_specs=placed, out_specs=P(("grp", "seq"), "ch"), check_vma=False
    )
```

```python
import functools
import math

import jax
import jax.numpy as jnp
import numpy as np
from jax import lax
from jax.experimental import pallas as pl
from jax.experimental.pallas import tpu as pltpu
from jax.sharding import PartitionSpec as P

AXES = ("grp", "seq", "ch")
BF16 = jnp.bfloat16
F32 = jnp.float32


def angles(count, first, second):
    phase = 2.0 * math.pi / count * (first[:, None] * second[None, :] % count).astype(jnp.float32)
    return (jnp.cos(phase), jnp.sin(phase))


def widened(values):
    return lax.optimization_barrier(values).astype(jnp.float32)


def dot(a, b):
    return jnp.dot(a, b, preferred_element_type=F32)


def dot_t(a, b):
    return lax.dot_general(a, b, (((1,), (1,)), ((), ())), preferred_element_type=F32)


def in_vmem(kernel, out_shape, scratch=(), flops=0, moved=0):
    def call(*operands):
        specs = [pl.BlockSpec(memory_space=pltpu.VMEM)] * len(operands)
        return pl.pallas_call(
            kernel,
            out_shape=out_shape,
            in_specs=specs,
            out_specs=jax.tree.map(lambda _: pl.BlockSpec(memory_space=pltpu.VMEM), out_shape),
            scratch_shapes=list(scratch),
            compiler_params=pltpu.CompilerParams(vmem_limit_bytes=20 * 1024 * 1024),
            cost_estimate=pl.CostEstimate(flops=flops, bytes_accessed=moved, transcendentals=0),
        )(*operands)

    return call


def place():
    y, s, c = (lax.axis_index(a) for a in AXES)
    return y, lax.rem(s, 2), lax.div(s, 2), c


def low_lanes(shape):
    return lax.broadcasted_iota(jnp.int32, shape, len(shape) - 1) < 64


def half_turn(values):
    return pltpu.roll(values, 64, values.ndim - 1)


def both(first, second, low):
    return (
        jnp.where(low, first, half_turn(second)).astype(BF16),
        jnp.where(low, half_turn(first), second).astype(BF16),
    )


def quarter(p):
    y, x, _, _ = place()
    row = 1 - y if p // 2 else y
    column = 1 - x if p % 2 else x
    return pl.ds(pl.multiple_of(row * 512 + column * 256, 256), 256)


def copied(moves, sem):
    copies = [pltpu.make_async_copy(a, b, sem.at[i]) for i, (a, b) in enumerate(moves)]
    for copy in copies:
        copy.start()
    for copy in copies:
        copy.wait()


def cut_first(value, own_v, sem):
    y, _, _, _ = place()
    copied([(value.at[:, pl.ds(pl.multiple_of(y * 512, 512), 512)], own_v)], sem)


def cut_messages(tokens, key, query, out, filt, after, m1, m2, m3, own, own_o, away_o, away_f, sem):
    _, x, _, _ = place()
    moves = [(filt.at[:, :, :, quarter(1)], away_f)]
    for p, message in enumerate((own, m1, m2, m3)):
        column = 1 - x if p % 2 else x
        for i in range(2):
            lanes = pl.ds(pl.multiple_of(i * 512 + column * 256, 256), 256)
            moves.append((tokens.at[:, lanes], message.at[:, pl.ds(512 + i * 256, 256)]))
        moves.append((key.at[:, quarter(p)], message.at[:, pl.ds(0, 256)]))
        moves.append((query.at[:, quarter(p)], message.at[:, pl.ds(256, 256)]))
    moves += [(out.at[:, quarter(0)], own_o), (out.at[:, quarter(1)], away_o)]
    copied(moves, sem)


def copy_kernel(kernel, out_shape):
    def call(*operands):
        return pl.pallas_call(
            kernel,
            out_shape=out_shape,
            in_specs=[pl.BlockSpec(memory_space=pltpu.MemorySpace.HBM)] * len(operands),
            out_specs=[pl.BlockSpec(memory_space=pltpu.VMEM)] * len(out_shape),
            scratch_shapes=[pltpu.SemaphoreType.DMA((19,))],
            compiler_params=pltpu.CompilerParams(vmem_limit_bytes=61 * 1024 * 1024),
        )(*operands)

    return call


def pack_filter(filt, near, *refs):
    y, x, z, _ = place()
    packed, outs = refs[4], refs[:4]
    low = low_lanes((128, 128))
    for k in range(2):
        for j in range(2):
            base = pl.multiple_of(y * 512 + x * 256 + j * 128, 128)
            for part in range(2):
                if k:
                    pair = [near[part, i, :, pl.ds(j * 128, 128)].astype(F32) for i in range(2)]
                else:
                    pair = [filt[part, i, :, pl.ds(base, 128)].astype(F32) for i in range(2)]
                one, two = both(*pair, low)
                packed[2 * j, k, part] = one
                packed[2 * j + 1, k, part] = two
    for r in range(4):
        outs[r][...] = packed[lax.rem(z + r, 4)]


def join_tokens(*refs):
    for p, message in enumerate(refs[:4]):
        refs[4][pl.ds(p * 128, 128), :] = message[:, pl.ds(512, 512)]


def value_kernel(mine, other, w0, w1, w2, w3, keep, give, acc):
    _, x, z, c = place()
    for r, piece in enumerate((w0, w1, w2, w3)):
        owner = lax.rem(z - r + 4, 4)
        lanes = pl.ds(pl.multiple_of(lax.rem(owner, 2) * 256, 256), 256)

        @pl.when(lax.div(owner, 2) == c)
        def _():
            term = dot(mine[:, lanes], piece[...])
            acc[...] = acc[...] + term if r else term

        @pl.when(lax.div(owner, 2) != c)
        def _():
            term = dot(other[:, lanes], piece[...])
            acc[...] = acc[...] + term if r else term

    keep[...] = acc[:, pl.ds(pl.multiple_of(x * 256, 256), 256)]
    away = pl.ds(pl.multiple_of(256 - x * 256, 256), 256)
    for p in range(4):
        give[pl.ds(p * 128, 128), :] = acc[pl.ds((p ^ 1) * 128, 128), away].astype(BF16)


def drive_kernel(keep, taken, g0, g1, g2, g3, skip, direct, o0, o1, o2, o3, drive, packed):
    _, _, z, _ = place()
    for p, gate in enumerate((g0, g1, g2, g3)):
        rows = pl.ds(p * 128, 128)
        value = (keep[rows, :] + taken[rows, :].astype(F32)).astype(BF16).astype(F32)
        held = (gate[:, 0:256].astype(F32) * value).astype(BF16)
        drive[rows, :] = held
        direct[rows, :] = skip[:, quarter(0)] * held.astype(F32)
    low = low_lanes((256, 128))
    for j in range(2):
        lanes = pl.ds(j * 128, 128)
        first = drive[pl.ds(0, 256), lanes].astype(F32)
        second = drive[pl.ds(256, 256), lanes].astype(F32)
        packed[2 * j], packed[2 * j + 1] = both(first, second, low)
    for r, out in enumerate((o0, o1, o2, o3)):
        out[...] = packed[lax.rem(z + r, 4)]


def add(a, b):
    return b if a is None else a if b is None else a + b


def sub(a, b):
    return a if b is None else -b if a is None else a - b


def scaled(a, s):
    if a is None or abs(s) < 1e-9:
        return None
    if abs(s - 1) < 1e-9:
        return a
    if abs(s + 1) < 1e-9:
        return -a
    return a * np.float32(s)


def cmul(a, angle):
    co, si = math.cos(angle), math.sin(angle)
    return (sub(scaled(a[0], co), scaled(a[1], si)), add(scaled(a[0], si), scaled(a[1], co)))


def cadd(a, b):
    return (add(a[0], b[0]), add(a[1], b[1]))


def conj(a):
    return (a[0], None if a[1] is None else -a[1])


def short_transform(values, count, rows):
    if len(values) == 1:
        return [(values[0], None)] * rows
    half = count // 2
    need = half // 2 + 1
    even = short_transform(values[0::2], half, need)
    odd = short_transform(values[1::2], half, need)

    def at(t, k):
        k %= half
        return t[k] if k < need else conj(t[half - k])

    return [cadd(at(even, k), cmul(at(odd, k), -2 * math.pi * k / count)) for k in range(rows)]


def conv_kernel(*refs):
    drives, filters, (table, table_t) = refs[:4], refs[4:8], refs[8:10]
    outs, (data, filt, first, sums) = refs[10:14], refs[14:]
    _, x, z, _ = place()
    for r, block in enumerate(drives):
        base = 2 * lax.rem(z - r + 4, 4)
        filt[base + x] = filters[r][0]
        filt[base + 1 - x] = filters[r][1]
        data[base + x] = block[pl.ds(0, 128), :]
        data[base + 1 - x] = block[pl.ds(128, 128), :]
    for i in range(8):
        rows = pl.ds(16 * i, 16)
        values = [data[a, rows, :].astype(F32) for a in range(8)]
        spectrum = short_transform(values, 16, 9)
        for k in range(9):
            re, im = spectrum[k]
            if im is None:
                im = jnp.zeros_like(re)
            first[k, rows, 0:128] = re.astype(BF16)
            first[k, rows, 128:256] = im.astype(BF16)
            if 0 < k < 8:
                first[16 - k, rows, 0:128] = re.astype(BF16)
                first[16 - k, rows, 128:256] = (-im).astype(BF16)
    low = low_lanes((128, 128))

    def back(k):
        four = dot(table[k], first[k])
        re = four[:128, :128] + four[128:, 128:]
        im = four[:128, 128:] - four[128:, :128]
        pair = [filt[k // 2, part].astype(F32) for part in range(2)]
        if k % 2 == 0:
            fr, fi = [jnp.where(low, f, half_turn(f)) for f in pair]
        else:
            fr, fi = [jnp.where(low, half_turn(f), f) for f in pair]
        product = jnp.concatenate([re * fr - im * fi, re * fi + im * fr], axis=1).astype(BF16)
        four = dot(table_t[k], product)
        return four[:128, :128] - four[128:, 128:], four[128:, :128] + four[:128, 128:]

    sums[0, pl.ds(0, 128)] = back(0)[0]
    sums[8, pl.ds(0, 128)] = back(8)[0]
    for k in range(1, 8):
        one, two = back(k), back(16 - k)
        sums[k, pl.ds(0, 128)] = one[0] + two[0]
        sums[k, pl.ds(128, 128)] = one[1] - two[1]
    for i in range(16):
        rows, below = pl.ds(8 * i, 8), pl.ds(128 + 8 * i, 8)
        scale = 1.0 / 2048
        re = [sums[k, rows, :] * scale for k in range(9)]
        im = [None] + [sums[k, below, :] * scale for k in range(1, 8)] + [None]
        for a in range(5):
            groups = [None] * 4
            for k in range(9):
                ang = 2 * math.pi * (k * a % 16) / 16
                groups[k % 2] = add(groups[k % 2], scaled(re[k], math.cos(ang)))
                groups[2 + k % 2] = sub(groups[2 + k % 2], scaled(im[k], math.sin(ang)))
            ec, oc, es, os = groups
            data[a, rows, :] = add(add(ec, oc), add(es, os)).astype(BF16)
            if 0 < a < 4:
                data[8 - a, rows, :] = sub(sub(add(ec, os), oc), es).astype(BF16)
    for r, out in enumerate(outs):
        base = 2 * lax.rem(z + r, 4)
        out[pl.ds(0, 128), :] = data[base + x]
        out[pl.ds(128, 128), :] = data[base + 1 - x]


def gate_kernel(e0, e1, e2, e3, direct, g0, g1, g2, g3, gated, conv):
    _, _, z, _ = place()
    for r, block in enumerate((e0, e1, e2, e3)):
        conv[lax.rem(z - r + 4, 4)] = block[...]
    low = low_lanes((256, 128))
    for j in range(2):
        lanes = pl.ds(j * 128, 128)
        even, odd = conv[2 * j].astype(F32), conv[2 * j + 1].astype(F32)
        parts = (jnp.where(low, even, half_turn(odd)), jnp.where(low, half_turn(even), odd))
        for p, gate in enumerate((g0, g1, g2, g3)):
            rows = pl.ds(p * 128, 128)
            own = parts[p // 2][(p % 2) * 128 : (p % 2) * 128 + 128]
            query = gate[:, pl.ds(256 + j * 128, 128)].astype(F32)
            gated[rows, lanes] = (query * (own + direct[rows, lanes])).astype(BF16)


def sort_weight(*refs):
    pieces, keep, give = refs[:8], refs[8], refs[9]
    _, x, z, c = place()
    for r in range(4):
        owner = lax.rem(z - r + 4, 4)
        for k in range(2):
            to = 2 * lax.rem(owner, 2) + (1 - x if k else x)

            @pl.when(owner // 2 == c)
            def _():
                keep[to] = pieces[2 * r + k][...]

            @pl.when(owner // 2 != c)
            def _():
                give[to] = pieces[2 * r + k][...]


def out_kernel(gated, other, keep, theirs, own, *sends):
    for p in (3, 2, 1, 0):
        rows = pl.ds(p * 128, 128)
        for i in range(4):
            total = dot_t(gated[rows, :], keep[i]) + dot_t(other[rows, :], theirs[i])
            lanes = pl.ds(i * 256, 256)
            if p == 0:
                own[:, lanes] = total
            else:
                sends[p - 1][:, lanes] = total.astype(BF16)


def tables():
    k = np.arange(16)[:, None, None] + 16 * np.arange(128)[None, :, None]
    phase = 2 * np.pi / 2048 * (k * np.arange(128)[None, None, :] % 2048)
    co, si = np.cos(phase), np.sin(phase)
    back = np.concatenate([co.transpose(0, 2, 1), si.transpose(0, 2, 1)], 1)
    return np.concatenate([co, si], 1).astype(jnp.bfloat16), back.astype(jnp.bfloat16)


def planes(tokens, gate_q, gate_k, w_value, skip, filter_spectrum, w_out):
    seq, deep = 8, 4

    def permute(values, move):
        pairs = []
        for g in range(2):
            for i in range(seq):
                for k in range(2):
                    g2, z2, x2, k2 = move(g, i // 2, i % 2, k)
                    pairs.append(((g * seq + i) * 2 + k, (g2 * seq + z2 * 2 + x2) * 2 + k2))
        return lax.ppermute(values, AXES, pairs)

    def to_x(values):
        return permute(values, lambda g, z, x, k: (g, z, 1 - x, k))

    def to_core(values):
        return permute(values, lambda g, z, x, k: (g, z, x, 1 - k))

    def to_z(values, r):
        return permute(values, lambda g, z, x, k: (g, (z + r) % deep, x, k))

    def to_peer(values, p):
        return permute(values, lambda g, z, x, k: (g ^ (p // 2), z, x ^ (p % 2), k))

    def after(values, *done):
        return lax.optimization_barrier((values,) + done)[0]

    shape = jax.ShapeDtypeStruct
    block, square = shape((256, 128), BF16), shape((256, 256), BF16)
    (own_v,) = copy_kernel(cut_first, [shape((256, 512), BF16)])(w_value)
    laid = [shape((128, 1024), BF16)] * 4 + [square] * 2 + [shape((2, 2, 128, 256), BF16)]
    *messages, own, own_o, away_o, away_f = copy_kernel(cut_messages, laid)(
        tokens, gate_k, gate_q, w_out, filter_spectrum, own_v
    )
    near = to_x(away_f)
    received = [to_peer(messages[p - 1], p) for p in (1, 2, 3)]
    plane = [own] + received
    filters = in_vmem(
        pack_filter,
        [shape((2, 2, 128, 128), BF16)] * 4,
        [pltpu.VMEM((4, 2, 2, 128, 128), BF16)],
        moved=1 << 20,
    )(filter_spectrum, near)
    filters = [filters[0]] + [to_z(filters[r], r) for r in (1, 2, 3)]
    v1 = to_z(own_v, 1)
    q1 = to_z(own_o, 1)
    v2 = to_z(after(v1, received[0], received[1]), 1)
    q2 = to_z(after(q1, v1), 1)
    mine = in_vmem(join_tokens, shape((512, 512), BF16), moved=1 << 20)(after(own, v2, q2), *received)
    v3 = to_z(after(v2, mine), 1)
    q3 = to_z(q2, 1)
    other = to_core(mine)
    got_o = to_x(after(away_o, v2))
    r1 = to_z(after(got_o, v3), 1)
    keep, give = in_vmem(
        value_kernel,
        [shape((512, 256), F32), shape((512, 256), BF16)],
        [pltpu.VMEM((512, 512), F32)],
        flops=1 << 29,
        moved=2 << 20,
    )(after(mine, q3, near, got_o), other, own_v, v1, v2, v3)
    r2 = to_z(after(r1, keep), 1)
    drive, *sends = in_vmem(
        drive_kernel,
        [shape((512, 256), F32)] + [block] * 4,
        [pltpu.VMEM((512, 256), BF16), pltpu.VMEM((4, 256, 128), BF16)],
        moved=2 << 20,
    )(after(keep, filters[1], filters[2]), to_x(give), *plane, skip[None, :])
    columns = [sends[0]] + [to_z(sends[r], r) for r in (1, 2, 3)]
    r3 = to_z(after(r2, *columns[1:]), 1)
    table, table_t = tables()
    sends = in_vmem(
        conv_kernel,
        [block] * 4,
        [
            pltpu.VMEM((8, 128, 128), BF16),
            pltpu.VMEM((8, 2, 128, 128), BF16),
            pltpu.VMEM((16, 128, 256), BF16),
            pltpu.VMEM((9, 256, 128), F32),
        ],
        flops=1 << 30,
        moved=5 << 20,
    )(*columns, *filters, table, table_t)
    rows = [sends[0]] + [to_z(sends[r], r) for r in (1, 2, 3)]

    hops = [own_o, got_o, q1, r1, q2, r2, q3, after(r3, *rows[1:])]
    quad = shape((4, 256, 256), BF16)
    keep, give = in_vmem(sort_weight, [quad] * 2, moved=2 << 20)(*hops)
    theirs = to_core(give)
    gated = in_vmem(
        gate_kernel, shape((512, 256), BF16), [pltpu.VMEM((4, 256, 128), BF16)], moved=1 << 20
    )(*rows, drive, *plane)
    gated_other = to_core(gated)
    own, *sends = in_vmem(
        out_kernel,
        [shape((128, 1024), F32)] + [shape((128, 1024), BF16)] * 3,
        flops=1 << 30,
        moved=4 << 20,
    )(gated, gated_other, keep, theirs)
    total = own
    for p in (3, 2, 1):
        total = total + to_peer(sends[p - 1], p).astype(F32)
    return total.astype(BF16)


def shards(tokens, gate_q, gate_k, w_value, skip, filter_spectrum, w_out):
    seq_count = lax.axis_size("seq")
    position = lax.axis_index("seq")
    length_b = tokens.shape[0]
    columns_each = length_b // seq_count
    freq_rows = 2 * seq_count
    freqs_each = freq_rows // seq_count
    fft_length = freq_rows * length_b
    features = lax.all_gather(tokens, "ch", axis=1, tiled=True)
    value_weight, out_weight = (
        lax.all_gather(w_value, "seq", axis=0, tiled=True),
        lax.all_gather(w_out, "seq", axis=0, tiled=True),
    )
    value = jnp.dot(features, value_weight, preferred_element_type=jnp.float32)
    value = value.astype(jnp.bfloat16)
    drive = (gate_k.astype(jnp.float32) * widened(value)).astype(jnp.bfloat16)
    channels = drive.shape[1]
    columns = lax.all_to_all(drive[None], "seq", split_axis=1, concat_axis=0, tiled=True)
    index_rows = jnp.arange(freq_rows, dtype=jnp.int32)
    index_seq = jnp.arange(seq_count, dtype=jnp.int32)
    index_b = jnp.arange(length_b, dtype=jnp.int32)
    cos_first, sin_first = angles(freq_rows, index_rows, index_seq)
    cos_first = cos_first.astype(jnp.bfloat16)
    sin_first = sin_first.astype(jnp.bfloat16)
    flattened = columns.reshape(seq_count, columns_each * channels)
    real_part = jnp.dot(cos_first, flattened, preferred_element_type=jnp.float32)
    imag_part = jnp.dot(-sin_first, flattened, preferred_element_type=jnp.float32)
    real_part = real_part.reshape(freq_rows, columns_each, channels)
    imag_part = imag_part.reshape(freq_rows, columns_each, channels)
    mine_b = position * columns_each + jnp.arange(columns_each, dtype=jnp.int32)
    twist_cos, twist_sin = angles(fft_length, index_rows, mine_b)
    twist_cos = twist_cos[:, :, None]
    twist_sin = twist_sin[:, :, None]
    section = jnp.stack(
        [
            real_part * twist_cos + imag_part * twist_sin,
            imag_part * twist_cos - real_part * twist_sin,
        ]
    ).astype(jnp.bfloat16)
    spectral = lax.all_to_all(section, "seq", split_axis=1, concat_axis=2, tiled=True)
    cos_seq, sin_seq = angles(length_b, index_b, index_b)
    cos_seq = cos_seq.astype(jnp.bfloat16)
    sin_seq = sin_seq.astype(jnp.bfloat16)
    spectrum_real = jnp.einsum(
        "qb,kbc->kqc", cos_seq, spectral[0], preferred_element_type=jnp.float32
    ) + jnp.einsum("qb,kbc->kqc", sin_seq, spectral[1], preferred_element_type=jnp.float32)
    spectrum_imag = jnp.einsum(
        "qb,kbc->kqc", cos_seq, spectral[1], preferred_element_type=jnp.float32
    ) - jnp.einsum("qb,kbc->kqc", sin_seq, spectral[0], preferred_element_type=jnp.float32)
    filter_real = filter_spectrum[0].astype(jnp.float32)
    filter_imag = filter_spectrum[1].astype(jnp.float32)
    product = jnp.stack(
        [
            spectrum_real * filter_real - spectrum_imag * filter_imag,
            spectrum_real * filter_imag + spectrum_imag * filter_real,
        ]
    ).astype(jnp.bfloat16)
    inverse_real = jnp.einsum(
        "qb,kqc->kbc", cos_seq, product[0], preferred_element_type=jnp.float32
    ) - jnp.einsum("qb,kqc->kbc", sin_seq, product[1], preferred_element_type=jnp.float32)
    inverse_imag = jnp.einsum(
        "qb,kqc->kbc", sin_seq, product[0], preferred_element_type=jnp.float32
    ) + jnp.einsum("qb,kqc->kbc", cos_seq, product[1], preferred_element_type=jnp.float32)
    mine_k = position * freqs_each + jnp.arange(freqs_each, dtype=jnp.int32)
    back_cos, back_sin = angles(fft_length, mine_k, index_b)
    back_cos = back_cos[:, :, None]
    back_sin = back_sin[:, :, None]
    back = jnp.stack(
        [
            inverse_real * back_cos - inverse_imag * back_sin,
            inverse_real * back_sin + inverse_imag * back_cos,
        ]
    ).astype(jnp.bfloat16)
    returned = lax.all_to_all(back, "seq", split_axis=2, concat_axis=1, tiled=True)
    flat_real = returned[0].reshape(freq_rows, columns_each * channels)
    flat_imag = returned[1].reshape(freq_rows, columns_each * channels)
    conv = jnp.dot(cos_first.T, flat_real, preferred_element_type=jnp.float32) - jnp.dot(
        sin_first.T, flat_imag, preferred_element_type=jnp.float32
    )
    conv = (
        (conv * (1.0 / fft_length)).reshape(seq_count, columns_each, channels).astype(jnp.bfloat16)
    )
    conv_rows = lax.all_to_all(conv, "seq", split_axis=0, concat_axis=1, tiled=True)[0]
    gated = (
        gate_q.astype(jnp.float32) * (widened(conv_rows) + skip[None, :] * widened(drive))
    ).astype(jnp.bfloat16)
    partial_value = lax.dot_general(
        gated, out_weight, (((1,), (1,)), ((), ())), preferred_element_type=jnp.float32
    )
    return lax.psum_scatter(
        partial_value.astype(jnp.bfloat16), "ch", scatter_dimension=1, tiled=True
    )


def solution(mesh):
    placed = (
        P(("grp", "seq"), "ch"),
        P(("grp", "seq"), "ch"),
        P(("grp", "seq"), "ch"),
        P("seq", "ch"),
        P("ch"),
        P(None, "seq", None, "ch"),
        P("seq", "ch"),
    )
    sizes = mesh.shape
    body = planes if (sizes["grp"], sizes["seq"], sizes["ch"]) == (2, 8, 2) else shards
    return jax.shard_map(
        body, mesh=mesh, in_specs=placed, out_specs=P(("grp", "seq"), "ch"), check_vma=False
    )
```

```python
import functools
import math

import jax
import jax.numpy as jnp
import numpy as np
from jax import lax
from jax.experimental import pallas as pl
from jax.experimental.pallas import tpu as pltpu
from jax.sharding import PartitionSpec as P

AXES = ("grp", "seq", "ch")
BF16 = jnp.bfloat16
F32 = jnp.float32


def angles(count, first, second):
    phase = 2.0 * math.pi / count * (first[:, None] * second[None, :] % count).astype(jnp.float32)
    return (jnp.cos(phase), jnp.sin(phase))


def widened(values):
    return lax.optimization_barrier(values).astype(jnp.float32)


def dot(a, b):
    return jnp.dot(a, b, preferred_element_type=F32)


def dot_t(a, b):
    return lax.dot_general(a, b, (((1,), (1,)), ((), ())), preferred_element_type=F32)


def in_vmem(kernel, out_shape, scratch=(), flops=0, moved=0):
    def call(*operands):
        specs = [pl.BlockSpec(memory_space=pltpu.VMEM)] * len(operands)
        return pl.pallas_call(
            kernel,
            out_shape=out_shape,
            in_specs=specs,
            out_specs=jax.tree.map(lambda _: pl.BlockSpec(memory_space=pltpu.VMEM), out_shape),
            scratch_shapes=list(scratch),
            compiler_params=pltpu.CompilerParams(vmem_limit_bytes=20 * 1024 * 1024),
            cost_estimate=pl.CostEstimate(flops=flops, bytes_accessed=moved, transcendentals=0),
        )(*operands)

    return call


def place():
    y, s, c = (lax.axis_index(a) for a in AXES)
    return y, lax.rem(s, 2), lax.div(s, 2), c


def low_lanes(shape):
    return lax.broadcasted_iota(jnp.int32, shape, len(shape) - 1) < 64


def half_turn(values):
    return pltpu.roll(values, 64, values.ndim - 1)


def both(first, second, low):
    return (
        jnp.where(low, first, half_turn(second)).astype(BF16),
        jnp.where(low, half_turn(first), second).astype(BF16),
    )


def quarter(p):
    y, x, _, _ = place()
    row = 1 - y if p // 2 else y
    column = 1 - x if p % 2 else x
    return pl.ds(pl.multiple_of(row * 512 + column * 256, 256), 256)


def copied(moves, sem):
    copies = [pltpu.make_async_copy(a, b, sem.at[i]) for i, (a, b) in enumerate(moves)]
    for copy in copies:
        copy.start()
    for copy in copies:
        copy.wait()


def cut_messages(tokens, key, query, out, filt, after, m1, m2, m3, own_o, away_o, away_f, sem):
    _, x, _, _ = place()
    moves = [(filt.at[:, :, :, quarter(1)], away_f)]
    for p, message in enumerate((m1, m2, m3), 1):
        column = 1 - x if p % 2 else x
        for i in range(2):
            lanes = pl.ds(pl.multiple_of(i * 512 + column * 256, 256), 256)
            moves.append((tokens.at[:, lanes], message.at[:, pl.ds(512 + i * 256, 256)]))
        moves.append((key.at[:, quarter(p)], message.at[:, pl.ds(0, 256)]))
        moves.append((query.at[:, quarter(p)], message.at[:, pl.ds(256, 256)]))
    moves += [(out.at[:, quarter(0)], own_o), (out.at[:, quarter(1)], away_o)]
    copied(moves, sem)


def copy_kernel(kernel, out_shape):
    def call(*operands):
        return pl.pallas_call(
            kernel,
            out_shape=out_shape,
            in_specs=[pl.BlockSpec(memory_space=pltpu.MemorySpace.HBM)] * len(operands),
            out_specs=[pl.BlockSpec(memory_space=pltpu.VMEM)] * len(out_shape),
            scratch_shapes=[pltpu.SemaphoreType.DMA((19,))],
            compiler_params=pltpu.CompilerParams(vmem_limit_bytes=61 * 1024 * 1024),
        )(*operands)

    return call


def pack_filter(filt, near, *refs):
    y, x, z, _ = place()
    packed, outs = refs[4], refs[:4]
    low = low_lanes((128, 128))
    for k in range(2):
        for j in range(2):
            base = pl.multiple_of(y * 512 + x * 256 + j * 128, 128)
            for part in range(2):
                if k:
                    pair = [near[part, i, :, pl.ds(j * 128, 128)].astype(F32) for i in range(2)]
                else:
                    pair = [filt[part, i, :, pl.ds(base, 128)].astype(F32) for i in range(2)]
                one, two = both(*pair, low)
                packed[2 * j, k, part] = one
                packed[2 * j + 1, k, part] = two
    for r in range(4):
        outs[r][...] = packed[lax.rem(z + r, 4)]


def join_tokens(*refs):
    _, x, _, _ = place()
    for i in range(2):
        lanes = pl.ds(pl.multiple_of(i * 512 + x * 256, 256), 256)
        refs[4][pl.ds(0, 128), pl.ds(i * 256, 256)] = refs[0][:, lanes]
    for p in (1, 2, 3):
        refs[4][pl.ds(p * 128, 128), :] = refs[p][:, pl.ds(512, 512)]


def value_kernel(mine, other, w0, w1, w2, w3, keep, give, acc):
    _, x, z, c = place()
    for r, piece in enumerate((w0, w1, w2, w3)):
        owner = lax.rem(z - r + 4, 4)
        lanes = pl.ds(pl.multiple_of(lax.rem(owner, 2) * 256, 256), 256)

        @pl.when(lax.div(owner, 2) == c)
        def _():
            term = dot(mine[:, lanes], piece[...])
            acc[...] = acc[...] + term if r else term

        @pl.when(lax.div(owner, 2) != c)
        def _():
            term = dot(other[:, lanes], piece[...])
            acc[...] = acc[...] + term if r else term

    keep[...] = acc[:, pl.ds(pl.multiple_of(x * 256, 256), 256)]
    away = pl.ds(pl.multiple_of(256 - x * 256, 256), 256)
    for p in range(4):
        give[pl.ds(p * 128, 128), :] = acc[pl.ds((p ^ 1) * 128, 128), away].astype(BF16)


def drive_kernel(keep, taken, g0, g1, g2, g3, skip, direct, o0, o1, o2, o3, drive, packed):
    _, _, z, _ = place()
    for p, gate in enumerate((g0, g1, g2, g3)):
        rows = pl.ds(p * 128, 128)
        value = (keep[rows, :] + taken[rows, :].astype(F32)).astype(BF16).astype(F32)
        held = ((gate[:, 0:256] if p else gate[:, quarter(0)]).astype(F32) * value).astype(BF16)
        drive[rows, :] = held
        direct[rows, :] = skip[:, quarter(0)] * held.astype(F32)
    low = low_lanes((256, 128))
    for j in range(2):
        lanes = pl.ds(j * 128, 128)
        first = drive[pl.ds(0, 256), lanes].astype(F32)
        second = drive[pl.ds(256, 256), lanes].astype(F32)
        packed[2 * j], packed[2 * j + 1] = both(first, second, low)
    for r, out in enumerate((o0, o1, o2, o3)):
        out[...] = packed[lax.rem(z + r, 4)]


def add(a, b):
    return b if a is None else a if b is None else a + b


def sub(a, b):
    return a if b is None else -b if a is None else a - b


def scaled(a, s):
    if a is None or abs(s) < 1e-9:
        return None
    if abs(s - 1) < 1e-9:
        return a
    if abs(s + 1) < 1e-9:
        return -a
    return a * np.float32(s)


def cmul(a, angle):
    co, si = math.cos(angle), math.sin(angle)
    return (sub(scaled(a[0], co), scaled(a[1], si)), add(scaled(a[0], si), scaled(a[1], co)))


def cadd(a, b):
    return (add(a[0], b[0]), add(a[1], b[1]))


def conj(a):
    return (a[0], None if a[1] is None else -a[1])


def short_transform(values, count, rows):
    if len(values) == 1:
        return [(values[0], None)] * rows
    half = count // 2
    need = half // 2 + 1
    even = short_transform(values[0::2], half, need)
    odd = short_transform(values[1::2], half, need)

    def at(t, k):
        k %= half
        return t[k] if k < need else conj(t[half - k])

    return [cadd(at(even, k), cmul(at(odd, k), -2 * math.pi * k / count)) for k in range(rows)]


def conv_kernel(*refs):
    drives, filters, (table, table_t) = refs[:4], refs[4:8], refs[8:10]
    outs, (data, filt, first, sums) = refs[10:14], refs[14:]
    _, x, z, _ = place()
    for r, block in enumerate(drives):
        base = 2 * lax.rem(z - r + 4, 4)
        filt[base + x] = filters[r][0]
        filt[base + 1 - x] = filters[r][1]
        data[base + x] = block[pl.ds(0, 128), :]
        data[base + 1 - x] = block[pl.ds(128, 128), :]
    for i in range(8):
        rows = pl.ds(16 * i, 16)
        values = [data[a, rows, :].astype(F32) for a in range(8)]
        spectrum = short_transform(values, 16, 9)
        for k in range(9):
            re, im = spectrum[k]
            if im is None:
                im = jnp.zeros_like(re)
            first[k, rows, 0:128] = re.astype(BF16)
            first[k, rows, 128:256] = im.astype(BF16)
            if 0 < k < 8:
                first[16 - k, rows, 0:128] = re.astype(BF16)
                first[16 - k, rows, 128:256] = (-im).astype(BF16)
    low = low_lanes((128, 128))

    def back(k):
        four = dot(table[k], first[k])
        re = four[:128, :128] + four[128:, 128:]
        im = four[:128, 128:] - four[128:, :128]
        pair = [filt[k // 2, part].astype(F32) for part in range(2)]
        if k % 2 == 0:
            fr, fi = [jnp.where(low, f, half_turn(f)) for f in pair]
        else:
            fr, fi = [jnp.where(low, half_turn(f), f) for f in pair]
        product = jnp.concatenate([re * fr - im * fi, re * fi + im * fr], axis=1).astype(BF16)
        four = dot(table_t[k], product)
        return four[:128, :128] - four[128:, 128:], four[128:, :128] + four[:128, 128:]

    sums[0, pl.ds(0, 128)] = back(0)[0]
    sums[8, pl.ds(0, 128)] = back(8)[0]
    for k in range(1, 8):
        one, two = back(k), back(16 - k)
        sums[k, pl.ds(0, 128)] = one[0] + two[0]
        sums[k, pl.ds(128, 128)] = one[1] - two[1]
    for i in range(16):
        rows, below = pl.ds(8 * i, 8), pl.ds(128 + 8 * i, 8)
        scale = 1.0 / 2048
        re = [sums[k, rows, :] * scale for k in range(9)]
        im = [None] + [sums[k, below, :] * scale for k in range(1, 8)] + [None]
        for a in range(5):
            groups = [None] * 4
            for k in range(9):
                ang = 2 * math.pi * (k * a % 16) / 16
                groups[k % 2] = add(groups[k % 2], scaled(re[k], math.cos(ang)))
                groups[2 + k % 2] = sub(groups[2 + k % 2], scaled(im[k], math.sin(ang)))
            ec, oc, es, os = groups
            data[a, rows, :] = add(add(ec, oc), add(es, os)).astype(BF16)
            if 0 < a < 4:
                data[8 - a, rows, :] = sub(sub(add(ec, os), oc), es).astype(BF16)
    for r, out in enumerate(outs):
        base = 2 * lax.rem(z + r, 4)
        out[pl.ds(0, 128), :] = data[base + x]
        out[pl.ds(128, 128), :] = data[base + 1 - x]


def gate_kernel(e0, e1, e2, e3, direct, g0, g1, g2, g3, gated, conv):
    _, _, z, _ = place()
    for r, block in enumerate((e0, e1, e2, e3)):
        conv[lax.rem(z - r + 4, 4)] = block[...]
    low = low_lanes((256, 128))
    for j in range(2):
        lanes = pl.ds(j * 128, 128)
        even, odd = conv[2 * j].astype(F32), conv[2 * j + 1].astype(F32)
        parts = (jnp.where(low, even, half_turn(odd)), jnp.where(low, half_turn(even), odd))
        for p, gate in enumerate((g0, g1, g2, g3)):
            rows = pl.ds(p * 128, 128)
            own = parts[p // 2][(p % 2) * 128 : (p % 2) * 128 + 128]
            y, x, _, _ = place()
            base = y * 512 + x * 256 if p == 0 else 256
            query = gate[:, pl.ds(pl.multiple_of(base + j * 128, 128), 128)].astype(F32)
            gated[rows, lanes] = (query * (own + direct[rows, lanes])).astype(BF16)


def sort_weight(*refs):
    pieces, keep, give = refs[:8], refs[8], refs[9]
    _, x, z, c = place()
    for r in range(4):
        owner = lax.rem(z - r + 4, 4)
        for k in range(2):
            to = 2 * lax.rem(owner, 2) + (1 - x if k else x)

            @pl.when(owner // 2 == c)
            def _():
                keep[to] = pieces[2 * r + k][...]

            @pl.when(owner // 2 != c)
            def _():
                give[to] = pieces[2 * r + k][...]


def out_kernel(gated, other, keep, theirs, own, *sends):
    for p in (3, 2, 1, 0):
        rows = pl.ds(p * 128, 128)
        for i in range(4):
            total = dot_t(gated[rows, :], keep[i]) + dot_t(other[rows, :], theirs[i])
            lanes = pl.ds(i * 256, 256)
            if p == 0:
                own[:, lanes] = total
            else:
                sends[p - 1][:, lanes] = total.astype(BF16)


def tables():
    k = np.arange(16)[:, None, None] + 16 * np.arange(128)[None, :, None]
    phase = 2 * np.pi / 2048 * (k * np.arange(128)[None, None, :] % 2048)
    co, si = np.cos(phase), np.sin(phase)
    back = np.concatenate([co.transpose(0, 2, 1), si.transpose(0, 2, 1)], 1)
    return np.concatenate([co, si], 1).astype(jnp.bfloat16), back.astype(jnp.bfloat16)


def planes(tokens, gate_q, gate_k, w_value, skip, filter_spectrum, w_out):
    seq, deep = 8, 4

    def permute(values, move):
        pairs = []
        for g in range(2):
            for i in range(seq):
                for k in range(2):
                    g2, z2, x2, k2 = move(g, i // 2, i % 2, k)
                    pairs.append(((g * seq + i) * 2 + k, (g2 * seq + z2 * 2 + x2) * 2 + k2))
        return lax.ppermute(values, AXES, pairs)

    def to_x(values):
        return permute(values, lambda g, z, x, k: (g, z, 1 - x, k))

    def to_core(values):
        return permute(values, lambda g, z, x, k: (g, z, x, 1 - k))

    def to_z(values, r):
        return permute(values, lambda g, z, x, k: (g, (z + r) % deep, x, k))

    def to_peer(values, p):
        return permute(values, lambda g, z, x, k: (g ^ (p // 2), z, x ^ (p % 2), k))

    def after(values, *done):
        return lax.optimization_barrier((values,) + done)[0]

    shape = jax.ShapeDtypeStruct
    block, square = shape((256, 128), BF16), shape((256, 256), BF16)
    own_v = lax.dynamic_slice_in_dim(w_value, lax.axis_index("grp") * 512, 512, axis=1)
    laid = [shape((128, 1024), BF16)] * 3 + [square] * 2 + [shape((2, 2, 128, 256), BF16)]
    *messages, own_o, away_o, away_f = copy_kernel(cut_messages, laid)(
        tokens, gate_k, gate_q, w_out, filter_spectrum, own_v
    )
    near = to_x(away_f)
    received = [to_peer(messages[p - 1], p) for p in (1, 2, 3)]
    filters = in_vmem(
        pack_filter,
        [shape((2, 2, 128, 128), BF16)] * 4,
        [pltpu.VMEM((4, 2, 2, 128, 128), BF16)],
        moved=1 << 20,
    )(filter_spectrum, near)
    filters = [filters[0]] + [to_z(filters[r], r) for r in (1, 2, 3)]
    v1 = to_z(own_v, 1)
    q1 = to_z(own_o, 1)
    v2 = to_z(v1, 1)
    q2 = to_z(after(q1, v1), 1)
    mine = in_vmem(join_tokens, shape((512, 512), BF16), moved=1 << 20)(tokens, after(received[0], q2), *received[1:])
    v3 = to_z(v2, 1)
    q3 = to_z(q2, 1)
    other = to_core(mine)
    got_o = to_x(after(away_o, v2))
    r1 = to_z(after(got_o, v3), 1)
    keep, give = in_vmem(
        value_kernel,
        [shape((512, 256), F32), shape((512, 256), BF16)],
        [pltpu.VMEM((512, 512), F32)],
        flops=1 << 29,
        moved=2 << 20,
    )(after(mine, q3, near, got_o), other, own_v, v1, v2, v3)
    r2 = to_z(after(r1, keep), 1)
    drive, *sends = in_vmem(
        drive_kernel,
        [shape((512, 256), F32)] + [block] * 4,
        [pltpu.VMEM((512, 256), BF16), pltpu.VMEM((4, 256, 128), BF16)],
        moved=2 << 20,
    )(after(keep, filters[1], filters[2]), to_x(give), gate_k, *received, skip[None, :])
    columns = [sends[0]] + [to_z(sends[r], r) for r in (1, 2, 3)]
    r3 = to_z(after(r2, *columns[1:]), 1)
    table, table_t = tables()
    sends = in_vmem(
        conv_kernel,
        [block] * 4,
        [
            pltpu.VMEM((8, 128, 128), BF16),
            pltpu.VMEM((8, 2, 128, 128), BF16),
            pltpu.VMEM((16, 128, 256), BF16),
            pltpu.VMEM((9, 256, 128), F32),
        ],
        flops=1 << 30,
        moved=5 << 20,
    )(*columns, *filters, table, table_t)
    rows = [sends[0]] + [to_z(sends[r], r) for r in (1, 2, 3)]

    hops = [own_o, got_o, q1, r1, q2, r2, q3, after(r3, *rows[1:])]
    quad = shape((4, 256, 256), BF16)
    keep, give = in_vmem(sort_weight, [quad] * 2, moved=2 << 20)(*hops)
    theirs = to_core(give)
    gated = in_vmem(
        gate_kernel, shape((512, 256), BF16), [pltpu.VMEM((4, 256, 128), BF16)], moved=1 << 20
    )(*rows, drive, gate_q, *received)
    gated_other = to_core(gated)
    own, *sends = in_vmem(
        out_kernel,
        [shape((128, 1024), F32)] + [shape((128, 1024), BF16)] * 3,
        flops=1 << 30,
        moved=4 << 20,
    )(gated, gated_other, keep, theirs)
    total = own
    for p in (3, 2, 1):
        total = total + to_peer(sends[p - 1], p).astype(F32)
    return total.astype(BF16)


def shards(tokens, gate_q, gate_k, w_value, skip, filter_spectrum, w_out):
    seq_count = lax.axis_size("seq")
    position = lax.axis_index("seq")
    length_b = tokens.shape[0]
    columns_each = length_b // seq_count
    freq_rows = 2 * seq_count
    freqs_each = freq_rows // seq_count
    fft_length = freq_rows * length_b
    features = lax.all_gather(tokens, "ch", axis=1, tiled=True)
    value_weight, out_weight = (
        lax.all_gather(w_value, "seq", axis=0, tiled=True),
        lax.all_gather(w_out, "seq", axis=0, tiled=True),
    )
    value = jnp.dot(features, value_weight, preferred_element_type=jnp.float32)
    value = value.astype(jnp.bfloat16)
    drive = (gate_k.astype(jnp.float32) * widened(value)).astype(jnp.bfloat16)
    channels = drive.shape[1]
    columns = lax.all_to_all(drive[None], "seq", split_axis=1, concat_axis=0, tiled=True)
    index_rows = jnp.arange(freq_rows, dtype=jnp.int32)
    index_seq = jnp.arange(seq_count, dtype=jnp.int32)
    index_b = jnp.arange(length_b, dtype=jnp.int32)
    cos_first, sin_first = angles(freq_rows, index_rows, index_seq)
    cos_first = cos_first.astype(jnp.bfloat16)
    sin_first = sin_first.astype(jnp.bfloat16)
    flattened = columns.reshape(seq_count, columns_each * channels)
    real_part = jnp.dot(cos_first, flattened, preferred_element_type=jnp.float32)
    imag_part = jnp.dot(-sin_first, flattened, preferred_element_type=jnp.float32)
    real_part = real_part.reshape(freq_rows, columns_each, channels)
    imag_part = imag_part.reshape(freq_rows, columns_each, channels)
    mine_b = position * columns_each + jnp.arange(columns_each, dtype=jnp.int32)
    twist_cos, twist_sin = angles(fft_length, index_rows, mine_b)
    twist_cos = twist_cos[:, :, None]
    twist_sin = twist_sin[:, :, None]
    section = jnp.stack(
        [
            real_part * twist_cos + imag_part * twist_sin,
            imag_part * twist_cos - real_part * twist_sin,
        ]
    ).astype(jnp.bfloat16)
    spectral = lax.all_to_all(section, "seq", split_axis=1, concat_axis=2, tiled=True)
    cos_seq, sin_seq = angles(length_b, index_b, index_b)
    cos_seq = cos_seq.astype(jnp.bfloat16)
    sin_seq = sin_seq.astype(jnp.bfloat16)
    spectrum_real = jnp.einsum(
        "qb,kbc->kqc", cos_seq, spectral[0], preferred_element_type=jnp.float32
    ) + jnp.einsum("qb,kbc->kqc", sin_seq, spectral[1], preferred_element_type=jnp.float32)
    spectrum_imag = jnp.einsum(
        "qb,kbc->kqc", cos_seq, spectral[1], preferred_element_type=jnp.float32
    ) - jnp.einsum("qb,kbc->kqc", sin_seq, spectral[0], preferred_element_type=jnp.float32)
    filter_real = filter_spectrum[0].astype(jnp.float32)
    filter_imag = filter_spectrum[1].astype(jnp.float32)
    product = jnp.stack(
        [
            spectrum_real * filter_real - spectrum_imag * filter_imag,
            spectrum_real * filter_imag + spectrum_imag * filter_real,
        ]
    ).astype(jnp.bfloat16)
    inverse_real = jnp.einsum(
        "qb,kqc->kbc", cos_seq, product[0], preferred_element_type=jnp.float32
    ) - jnp.einsum("qb,kqc->kbc", sin_seq, product[1], preferred_element_type=jnp.float32)
    inverse_imag = jnp.einsum(
        "qb,kqc->kbc", sin_seq, product[0], preferred_element_type=jnp.float32
    ) + jnp.einsum("qb,kqc->kbc", cos_seq, product[1], preferred_element_type=jnp.float32)
    mine_k = position * freqs_each + jnp.arange(freqs_each, dtype=jnp.int32)
    back_cos, back_sin = angles(fft_length, mine_k, index_b)
    back_cos = back_cos[:, :, None]
    back_sin = back_sin[:, :, None]
    back = jnp.stack(
        [
            inverse_real * back_cos - inverse_imag * back_sin,
            inverse_real * back_sin + inverse_imag * back_cos,
        ]
    ).astype(jnp.bfloat16)
    returned = lax.all_to_all(back, "seq", split_axis=2, concat_axis=1, tiled=True)
    flat_real = returned[0].reshape(freq_rows, columns_each * channels)
    flat_imag = returned[1].reshape(freq_rows, columns_each * channels)
    conv = jnp.dot(cos_first.T, flat_real, preferred_element_type=jnp.float32) - jnp.dot(
        sin_first.T, flat_imag, preferred_element_type=jnp.float32
    )
    conv = (
        (conv * (1.0 / fft_length)).reshape(seq_count, columns_each, channels).astype(jnp.bfloat16)
    )
    conv_rows = lax.all_to_all(conv, "seq", split_axis=0, concat_axis=1, tiled=True)[0]
    gated = (
        gate_q.astype(jnp.float32) * (widened(conv_rows) + skip[None, :] * widened(drive))
    ).astype(jnp.bfloat16)
    partial_value = lax.dot_general(
        gated, out_weight, (((1,), (1,)), ((), ())), preferred_element_type=jnp.float32
    )
    return lax.psum_scatter(
        partial_value.astype(jnp.bfloat16), "ch", scatter_dimension=1, tiled=True
    )


def solution(mesh):
    placed = (
        P(("grp", "seq"), "ch"),
        P(("grp", "seq"), "ch"),
        P(("grp", "seq"), "ch"),
        P("seq", "ch"),
        P("ch"),
        P(None, "seq", None, "ch"),
        P("seq", "ch"),
    )
    sizes = mesh.shape
    body = planes if (sizes["grp"], sizes["seq"], sizes["ch"]) == (2, 8, 2) else shards
    return jax.shard_map(
        body, mesh=mesh, in_specs=placed, out_specs=P(("grp", "seq"), "ch"), check_vma=False
    )
```

```python
import functools
import math

import jax
import jax.numpy as jnp
import numpy as np
from jax import lax
from jax.experimental import pallas as pl
from jax.experimental.pallas import tpu as pltpu
from jax.sharding import PartitionSpec as P

AXES = ("grp", "seq", "ch")
BF16 = jnp.bfloat16
F32 = jnp.float32


def angles(count, first, second):
    phase = 2.0 * math.pi / count * (first[:, None] * second[None, :] % count).astype(jnp.float32)
    return (jnp.cos(phase), jnp.sin(phase))


def widened(values):
    return lax.optimization_barrier(values).astype(jnp.float32)


def dot(a, b):
    return jnp.dot(a, b, preferred_element_type=F32)


def dot_t(a, b):
    return lax.dot_general(a, b, (((1,), (1,)), ((), ())), preferred_element_type=F32)


def in_vmem(kernel, out_shape, scratch=(), flops=0, moved=0):
    def call(*operands):
        specs = [pl.BlockSpec(memory_space=pltpu.VMEM)] * len(operands)
        return pl.pallas_call(
            kernel,
            out_shape=out_shape,
            in_specs=specs,
            out_specs=jax.tree.map(lambda _: pl.BlockSpec(memory_space=pltpu.VMEM), out_shape),
            scratch_shapes=list(scratch),
            compiler_params=pltpu.CompilerParams(vmem_limit_bytes=20 * 1024 * 1024),
            cost_estimate=pl.CostEstimate(flops=flops, bytes_accessed=moved, transcendentals=0),
        )(*operands)

    return call


def place():
    y, s, c = (lax.axis_index(a) for a in AXES)
    return y, lax.rem(s, 2), lax.div(s, 2), c


def low_lanes(shape):
    return lax.broadcasted_iota(jnp.int32, shape, len(shape) - 1) < 64


def half_turn(values):
    return pltpu.roll(values, 64, values.ndim - 1)


def both(first, second, low):
    return (
        jnp.where(low, first, half_turn(second)).astype(BF16),
        jnp.where(low, half_turn(first), second).astype(BF16),
    )


def quarter(p):
    y, x, _, _ = place()
    row = 1 - y if p // 2 else y
    column = 1 - x if p % 2 else x
    return pl.ds(pl.multiple_of(row * 512 + column * 256, 256), 256)


def copied(moves, sem):
    copies = [pltpu.make_async_copy(a, b, sem.at[i]) for i, (a, b) in enumerate(moves)]
    for copy in copies:
        copy.start()
    for copy in copies:
        copy.wait()


def cut_messages(tokens, key, query, out, filt, after, m1, m2, m3, own_o, away_o, away_f, sem):
    _, x, _, _ = place()
    moves = [(filt.at[:, :, :, quarter(1)], away_f)]
    for p, message in enumerate((m1, m2, m3), 1):
        column = 1 - x if p % 2 else x
        for i in range(2):
            lanes = pl.ds(pl.multiple_of(i * 512 + column * 256, 256), 256)
            moves.append((tokens.at[:, lanes], message.at[:, pl.ds(512 + i * 256, 256)]))
        moves.append((key.at[:, quarter(p)], message.at[:, pl.ds(0, 256)]))
        moves.append((query.at[:, quarter(p)], message.at[:, pl.ds(256, 256)]))
    moves += [(out.at[:, quarter(0)], own_o), (out.at[:, quarter(1)], away_o)]
    copied(moves, sem)


def copy_kernel(kernel, out_shape):
    def call(*operands):
        return pl.pallas_call(
            kernel,
            out_shape=out_shape,
            in_specs=[pl.BlockSpec(memory_space=pltpu.MemorySpace.HBM)] * len(operands),
            out_specs=[pl.BlockSpec(memory_space=pltpu.VMEM)] * len(out_shape),
            scratch_shapes=[pltpu.SemaphoreType.DMA((19,))],
            compiler_params=pltpu.CompilerParams(vmem_limit_bytes=61 * 1024 * 1024),
        )(*operands)

    return call


def pack_filter(filt, near, *refs):
    y, x, z, _ = place()
    packed, outs = refs[4], refs[:4]
    low = low_lanes((128, 128))
    for k in range(2):
        for j in range(2):
            base = pl.multiple_of(y * 512 + x * 256 + j * 128, 128)
            for part in range(2):
                if k:
                    pair = [near[part, i, :, pl.ds(j * 128, 128)].astype(F32) for i in range(2)]
                else:
                    pair = [filt[part, i, :, pl.ds(base, 128)].astype(F32) for i in range(2)]
                one, two = both(*pair, low)
                packed[2 * j, k, part] = one
                packed[2 * j + 1, k, part] = two
    for r in range(4):
        outs[r][...] = packed[lax.rem(z + r, 4)]


def join_tokens(*refs):
    _, x, _, _ = place()
    for i in range(2):
        lanes = pl.ds(pl.multiple_of(i * 512 + x * 256, 256), 256)
        refs[4][pl.ds(0, 128), pl.ds(i * 256, 256)] = refs[0][:, lanes]
    for p in (1, 2, 3):
        refs[4][pl.ds(p * 128, 128), :] = refs[p][:, pl.ds(512, 512)]


def value_kernel(mine, other, w0, w1, w2, w3, keep, give, acc):
    _, x, z, c = place()
    for r, piece in enumerate((w0, w1, w2, w3)):
        owner = lax.rem(z - r + 4, 4)
        lanes = pl.ds(pl.multiple_of(lax.rem(owner, 2) * 256, 256), 256)

        @pl.when(lax.div(owner, 2) == c)
        def _():
            term = dot(mine[:, lanes], piece[...])
            acc[...] = acc[...] + term if r else term

        @pl.when(lax.div(owner, 2) != c)
        def _():
            term = dot(other[:, lanes], piece[...])
            acc[...] = acc[...] + term if r else term

    keep[...] = acc[:, pl.ds(pl.multiple_of(x * 256, 256), 256)]
    away = pl.ds(pl.multiple_of(256 - x * 256, 256), 256)
    for p in range(4):
        give[pl.ds(p * 128, 128), :] = acc[pl.ds((p ^ 1) * 128, 128), away].astype(BF16)


def drive_kernel(keep, taken, g0, g1, g2, g3, skip, direct, o0, o1, o2, o3, drive, packed):
    _, _, z, _ = place()
    for p, gate in enumerate((g0, g1, g2, g3)):
        rows = pl.ds(p * 128, 128)
        value = (keep[rows, :] + taken[rows, :].astype(F32)).astype(BF16).astype(F32)
        held = ((gate[:, 0:256] if p else gate[:, quarter(0)]).astype(F32) * value).astype(BF16)
        drive[rows, :] = held
        direct[rows, :] = skip[:, quarter(0)] * held.astype(F32)
    low = low_lanes((256, 128))
    for j in range(2):
        lanes = pl.ds(j * 128, 128)
        first = drive[pl.ds(0, 256), lanes].astype(F32)
        second = drive[pl.ds(256, 256), lanes].astype(F32)
        packed[2 * j], packed[2 * j + 1] = both(first, second, low)
    for r, out in enumerate((o0, o1, o2, o3)):
        out[...] = packed[lax.rem(z + r, 4)]


def add(a, b):
    return b if a is None else a if b is None else a + b


def sub(a, b):
    return a if b is None else -b if a is None else a - b


def scaled(a, s):
    if a is None or abs(s) < 1e-9:
        return None
    if abs(s - 1) < 1e-9:
        return a
    if abs(s + 1) < 1e-9:
        return -a
    return a * np.float32(s)


def cmul(a, angle):
    co, si = math.cos(angle), math.sin(angle)
    return (sub(scaled(a[0], co), scaled(a[1], si)), add(scaled(a[0], si), scaled(a[1], co)))


def cadd(a, b):
    return (add(a[0], b[0]), add(a[1], b[1]))


def conj(a):
    return (a[0], None if a[1] is None else -a[1])


def short_transform(values, count, rows):
    if len(values) == 1:
        return [(values[0], None)] * rows
    half = count // 2
    need = half // 2 + 1
    even = short_transform(values[0::2], half, need)
    odd = short_transform(values[1::2], half, need)

    def at(t, k):
        k %= half
        return t[k] if k < need else conj(t[half - k])

    return [cadd(at(even, k), cmul(at(odd, k), -2 * math.pi * k / count)) for k in range(rows)]


def conv_kernel(*refs):
    drives, filters, (table, table_t) = refs[:4], refs[4:8], refs[8:10]
    outs, (data, filt, first, sums) = refs[10:14], refs[14:]
    _, x, z, _ = place()
    for r, block in enumerate(drives):
        base = 2 * lax.rem(z - r + 4, 4)
        filt[base + x] = filters[r][0]
        filt[base + 1 - x] = filters[r][1]
        data[base + x] = block[pl.ds(0, 128), :]
        data[base + 1 - x] = block[pl.ds(128, 128), :]
    for i in range(8):
        rows = pl.ds(16 * i, 16)
        values = [data[a, rows, :].astype(F32) for a in range(8)]
        spectrum = short_transform(values, 16, 9)
        for k in range(9):
            re, im = spectrum[k]
            if im is None:
                im = jnp.zeros_like(re)
            first[k, rows, 0:128] = re.astype(BF16)
            first[k, rows, 128:256] = im.astype(BF16)
            if 0 < k < 8:
                first[16 - k, rows, 0:128] = re.astype(BF16)
                first[16 - k, rows, 128:256] = (-im).astype(BF16)
    low = low_lanes((128, 128))

    def back(k):
        four = dot(table[k], first[k])
        re = four[:128, :128] + four[128:, 128:]
        im = four[:128, 128:] - four[128:, :128]
        pair = [filt[k // 2, part].astype(F32) for part in range(2)]
        if k % 2 == 0:
            fr, fi = [jnp.where(low, f, half_turn(f)) for f in pair]
        else:
            fr, fi = [jnp.where(low, half_turn(f), f) for f in pair]
        product = jnp.concatenate([re * fr - im * fi, re * fi + im * fr], axis=1).astype(BF16)
        four = dot(table_t[k], product)
        return four[:128, :128] - four[128:, 128:], four[128:, :128] + four[:128, 128:]

    sums[0, pl.ds(0, 128)] = back(0)[0]
    sums[8, pl.ds(0, 128)] = back(8)[0]
    for k in range(1, 8):
        one, two = back(k), back(16 - k)
        sums[k, pl.ds(0, 128)] = one[0] + two[0]
        sums[k, pl.ds(128, 128)] = one[1] - two[1]
    for i in range(16):
        rows, below = pl.ds(8 * i, 8), pl.ds(128 + 8 * i, 8)
        scale = 1.0 / 2048
        re = [sums[k, rows, :] * scale for k in range(9)]
        im = [None] + [sums[k, below, :] * scale for k in range(1, 8)] + [None]
        for a in range(5):
            groups = [None] * 4
            for k in range(9):
                ang = 2 * math.pi * (k * a % 16) / 16
                groups[k % 2] = add(groups[k % 2], scaled(re[k], math.cos(ang)))
                groups[2 + k % 2] = sub(groups[2 + k % 2], scaled(im[k], math.sin(ang)))
            ec, oc, es, os = groups
            data[a, rows, :] = add(add(ec, oc), add(es, os)).astype(BF16)
            if 0 < a < 4:
                data[8 - a, rows, :] = sub(sub(add(ec, os), oc), es).astype(BF16)
    for r, out in enumerate(outs):
        base = 2 * lax.rem(z + r, 4)
        out[pl.ds(0, 128), :] = data[base + x]
        out[pl.ds(128, 128), :] = data[base + 1 - x]


def gate_kernel(e0, e1, e2, e3, direct, g0, g1, g2, g3, gated, conv):
    _, _, z, _ = place()
    for r, block in enumerate((e0, e1, e2, e3)):
        conv[lax.rem(z - r + 4, 4)] = block[...]
    low = low_lanes((256, 128))
    for j in range(2):
        lanes = pl.ds(j * 128, 128)
        even, odd = conv[2 * j].astype(F32), conv[2 * j + 1].astype(F32)
        parts = (jnp.where(low, even, half_turn(odd)), jnp.where(low, half_turn(even), odd))
        for p, gate in enumerate((g0, g1, g2, g3)):
            rows = pl.ds(p * 128, 128)
            own = parts[p // 2][(p % 2) * 128 : (p % 2) * 128 + 128]
            y, x, _, _ = place()
            base = y * 512 + x * 256 if p == 0 else 256
            query = gate[:, pl.ds(pl.multiple_of(base + j * 128, 128), 128)].astype(F32)
            gated[rows, lanes] = (query * (own + direct[rows, lanes])).astype(BF16)


def sort_weight(*refs):
    pieces, keep, give = refs[:8], refs[8], refs[9]
    _, x, z, c = place()
    for r in range(4):
        owner = lax.rem(z - r + 4, 4)
        for k in range(2):
            to = 2 * lax.rem(owner, 2) + (1 - x if k else x)

            @pl.when(owner // 2 == c)
            def _():
                keep[to] = pieces[2 * r + k][...]

            @pl.when(owner // 2 != c)
            def _():
                give[to] = pieces[2 * r + k][...]


def out_kernel(blocks, gated, other, keep, theirs, *outs):
    for p, out in zip(blocks, outs):
        rows = pl.ds(p * 128, 128)
        for i in range(4):
            total = dot_t(gated[rows, :], keep[i]) + dot_t(other[rows, :], theirs[i])
            out[:, pl.ds(i * 256, 256)] = total.astype(out.dtype)


def tables():
    k = np.arange(16)[:, None, None] + 16 * np.arange(128)[None, :, None]
    phase = 2 * np.pi / 2048 * (k * np.arange(128)[None, None, :] % 2048)
    co, si = np.cos(phase), np.sin(phase)
    back = np.concatenate([co.transpose(0, 2, 1), si.transpose(0, 2, 1)], 1)
    return np.concatenate([co, si], 1).astype(jnp.bfloat16), back.astype(jnp.bfloat16)


def planes(tokens, gate_q, gate_k, w_value, skip, filter_spectrum, w_out):
    seq, deep = 8, 4

    def permute(values, move):
        pairs = []
        for g in range(2):
            for i in range(seq):
                for k in range(2):
                    g2, z2, x2, k2 = move(g, i // 2, i % 2, k)
                    pairs.append(((g * seq + i) * 2 + k, (g2 * seq + z2 * 2 + x2) * 2 + k2))
        return lax.ppermute(values, AXES, pairs)

    def to_x(values):
        return permute(values, lambda g, z, x, k: (g, z, 1 - x, k))

    def to_core(values):
        return permute(values, lambda g, z, x, k: (g, z, x, 1 - k))

    def to_z(values, r):
        return permute(values, lambda g, z, x, k: (g, (z + r) % deep, x, k))

    def to_peer(values, p):
        return permute(values, lambda g, z, x, k: (g ^ (p // 2), z, x ^ (p % 2), k))

    def after(values, *done):
        return lax.optimization_barrier((values,) + done)[0]

    shape = jax.ShapeDtypeStruct
    block, square = shape((256, 128), BF16), shape((256, 256), BF16)
    own_v = lax.dynamic_slice_in_dim(w_value, lax.axis_index("grp") * 512, 512, axis=1)
    laid = [shape((128, 1024), BF16)] * 3 + [square] * 2 + [shape((2, 2, 128, 256), BF16)]
    *messages, own_o, away_o, away_f = copy_kernel(cut_messages, laid)(
        tokens, gate_k, gate_q, w_out, filter_spectrum, own_v
    )
    near = to_x(away_f)
    received = [to_peer(messages[p - 1], p) for p in (1, 2, 3)]
    filters = in_vmem(
        pack_filter,
        [shape((2, 2, 128, 128), BF16)] * 4,
        [pltpu.VMEM((4, 2, 2, 128, 128), BF16)],
        moved=1 << 20,
    )(filter_spectrum, near)
    filters = [filters[0]] + [to_z(filters[r], r) for r in (1, 2, 3)]
    v1 = to_z(own_v, 1)
    q1 = to_z(own_o, 1)
    v2 = to_z(v1, 1)
    q2 = to_z(after(q1, v1), 1)
    mine = in_vmem(join_tokens, shape((512, 512), BF16), moved=1 << 20)(tokens, after(received[0], q2), *received[1:])
    v3 = to_z(v2, 1)
    other = to_core(mine)
    got_o = to_x(after(away_o, v2))
    r1 = to_z(after(got_o, v3), 1)
    keep, give = in_vmem(
        value_kernel,
        [shape((512, 256), F32), shape((512, 256), BF16)],
        [pltpu.VMEM((512, 512), F32)],
        flops=1 << 29,
        moved=2 << 20,
    )(after(mine, filters[1], got_o), other, own_v, v1, v2, v3)
    r2 = to_z(after(r1, keep), 1)
    drive, *sends = in_vmem(
        drive_kernel,
        [shape((512, 256), F32)] + [block] * 4,
        [pltpu.VMEM((512, 256), BF16), pltpu.VMEM((4, 256, 128), BF16)],
        moved=2 << 20,
    )(after(keep, filters[1], filters[2]), to_x(give), gate_k, *received, skip[None, :])
    columns = [sends[0]] + [to_z(sends[r], r) for r in (1, 2, 3)]
    q3 = to_z(after(q2, columns[1]), 1)
    r3 = to_z(after(r2, *columns[1:]), 1)
    table, table_t = tables()
    sends = in_vmem(
        conv_kernel,
        [block] * 4,
        [
            pltpu.VMEM((8, 128, 128), BF16),
            pltpu.VMEM((8, 2, 128, 128), BF16),
            pltpu.VMEM((16, 128, 256), BF16),
            pltpu.VMEM((9, 256, 128), F32),
        ],
        flops=1 << 30,
        moved=5 << 20,
    )(*columns, *filters, table, table_t)
    rows = [sends[0]] + [to_z(sends[r], r) for r in (1, 2, 3)]

    hops = [own_o, got_o, q1, r1, q2, r2, q3, after(r3, *rows[1:])]
    quad = shape((4, 256, 256), BF16)
    keep, give = in_vmem(sort_weight, [quad] * 2, moved=2 << 20)(*hops)
    theirs = to_core(give)
    gated = in_vmem(
        gate_kernel, shape((512, 256), BF16), [pltpu.VMEM((4, 256, 128), BF16)], moved=1 << 20
    )(*rows, drive, gate_q, *received)
    gated_other = to_core(gated)
    summed = (gated, gated_other, keep, theirs)
    send = shape((128, 1024), BF16)
    far = in_vmem(functools.partial(out_kernel, (3, 1)), [send] * 2, flops=1 << 29, moved=2 << 20)
    close = in_vmem(
        functools.partial(out_kernel, (2, 0)),
        [send, shape((128, 1024), F32)],
        flops=1 << 29,
        moved=2 << 20,
    )
    to_xy, to_row = far(*summed)
    parts = [to_peer(to_xy, 3), to_peer(to_row, 1)]
    to_column, total = close(*summed)
    parts.append(to_peer(to_column, 2))
    for part in parts:
        total = total + part.astype(F32)
    return total.astype(BF16)


def shards(tokens, gate_q, gate_k, w_value, skip, filter_spectrum, w_out):
    seq_count = lax.axis_size("seq")
    position = lax.axis_index("seq")
    length_b = tokens.shape[0]
    columns_each = length_b // seq_count
    freq_rows = 2 * seq_count
    freqs_each = freq_rows // seq_count
    fft_length = freq_rows * length_b
    features = lax.all_gather(tokens, "ch", axis=1, tiled=True)
    value_weight, out_weight = (
        lax.all_gather(w_value, "seq", axis=0, tiled=True),
        lax.all_gather(w_out, "seq", axis=0, tiled=True),
    )
    value = jnp.dot(features, value_weight, preferred_element_type=jnp.float32)
    value = value.astype(jnp.bfloat16)
    drive = (gate_k.astype(jnp.float32) * widened(value)).astype(jnp.bfloat16)
    channels = drive.shape[1]
    columns = lax.all_to_all(drive[None], "seq", split_axis=1, concat_axis=0, tiled=True)
    index_rows = jnp.arange(freq_rows, dtype=jnp.int32)
    index_seq = jnp.arange(seq_count, dtype=jnp.int32)
    index_b = jnp.arange(length_b, dtype=jnp.int32)
    cos_first, sin_first = angles(freq_rows, index_rows, index_seq)
    cos_first = cos_first.astype(jnp.bfloat16)
    sin_first = sin_first.astype(jnp.bfloat16)
    flattened = columns.reshape(seq_count, columns_each * channels)
    real_part = jnp.dot(cos_first, flattened, preferred_element_type=jnp.float32)
    imag_part = jnp.dot(-sin_first, flattened, preferred_element_type=jnp.float32)
    real_part = real_part.reshape(freq_rows, columns_each, channels)
    imag_part = imag_part.reshape(freq_rows, columns_each, channels)
    mine_b = position * columns_each + jnp.arange(columns_each, dtype=jnp.int32)
    twist_cos, twist_sin = angles(fft_length, index_rows, mine_b)
    twist_cos = twist_cos[:, :, None]
    twist_sin = twist_sin[:, :, None]
    section = jnp.stack(
        [
            real_part * twist_cos + imag_part * twist_sin,
            imag_part * twist_cos - real_part * twist_sin,
        ]
    ).astype(jnp.bfloat16)
    spectral = lax.all_to_all(section, "seq", split_axis=1, concat_axis=2, tiled=True)
    cos_seq, sin_seq = angles(length_b, index_b, index_b)
    cos_seq = cos_seq.astype(jnp.bfloat16)
    sin_seq = sin_seq.astype(jnp.bfloat16)
    spectrum_real = jnp.einsum(
        "qb,kbc->kqc", cos_seq, spectral[0], preferred_element_type=jnp.float32
    ) + jnp.einsum("qb,kbc->kqc", sin_seq, spectral[1], preferred_element_type=jnp.float32)
    spectrum_imag = jnp.einsum(
        "qb,kbc->kqc", cos_seq, spectral[1], preferred_element_type=jnp.float32
    ) - jnp.einsum("qb,kbc->kqc", sin_seq, spectral[0], preferred_element_type=jnp.float32)
    filter_real = filter_spectrum[0].astype(jnp.float32)
    filter_imag = filter_spectrum[1].astype(jnp.float32)
    product = jnp.stack(
        [
            spectrum_real * filter_real - spectrum_imag * filter_imag,
            spectrum_real * filter_imag + spectrum_imag * filter_real,
        ]
    ).astype(jnp.bfloat16)
    inverse_real = jnp.einsum(
        "qb,kqc->kbc", cos_seq, product[0], preferred_element_type=jnp.float32
    ) - jnp.einsum("qb,kqc->kbc", sin_seq, product[1], preferred_element_type=jnp.float32)
    inverse_imag = jnp.einsum(
        "qb,kqc->kbc", sin_seq, product[0], preferred_element_type=jnp.float32
    ) + jnp.einsum("qb,kqc->kbc", cos_seq, product[1], preferred_element_type=jnp.float32)
    mine_k = position * freqs_each + jnp.arange(freqs_each, dtype=jnp.int32)
    back_cos, back_sin = angles(fft_length, mine_k, index_b)
    back_cos = back_cos[:, :, None]
    back_sin = back_sin[:, :, None]
    back = jnp.stack(
        [
            inverse_real * back_cos - inverse_imag * back_sin,
            inverse_real * back_sin + inverse_imag * back_cos,
        ]
    ).astype(jnp.bfloat16)
    returned = lax.all_to_all(back, "seq", split_axis=2, concat_axis=1, tiled=True)
    flat_real = returned[0].reshape(freq_rows, columns_each * channels)
    flat_imag = returned[1].reshape(freq_rows, columns_each * channels)
    conv = jnp.dot(cos_first.T, flat_real, preferred_element_type=jnp.float32) - jnp.dot(
        sin_first.T, flat_imag, preferred_element_type=jnp.float32
    )
    conv = (
        (conv * (1.0 / fft_length)).reshape(seq_count, columns_each, channels).astype(jnp.bfloat16)
    )
    conv_rows = lax.all_to_all(conv, "seq", split_axis=0, concat_axis=1, tiled=True)[0]
    gated = (
        gate_q.astype(jnp.float32) * (widened(conv_rows) + skip[None, :] * widened(drive))
    ).astype(jnp.bfloat16)
    partial_value = lax.dot_general(
        gated, out_weight, (((1,), (1,)), ((), ())), preferred_element_type=jnp.float32
    )
    return lax.psum_scatter(
        partial_value.astype(jnp.bfloat16), "ch", scatter_dimension=1, tiled=True
    )


def solution(mesh):
    placed = (
        P(("grp", "seq"), "ch"),
        P(("grp", "seq"), "ch"),
        P(("grp", "seq"), "ch"),
        P("seq", "ch"),
        P("ch"),
        P(None, "seq", None, "ch"),
        P("seq", "ch"),
    )
    sizes = mesh.shape
    body = planes if (sizes["grp"], sizes["seq"], sizes["ch"]) == (2, 8, 2) else shards
    return jax.shard_map(
        body, mesh=mesh, in_specs=placed, out_specs=P(("grp", "seq"), "ch"), check_vma=False
    )
```

```python
import functools
import math

import jax
import jax.numpy as jnp
import numpy as np
from jax import lax
from jax.experimental import pallas as pl
from jax.experimental.pallas import tpu as pltpu
from jax.sharding import PartitionSpec as P

AXES = ("grp", "seq", "ch")
BF16 = jnp.bfloat16
F32 = jnp.float32


def angles(count, first, second):
    phase = 2.0 * math.pi / count * (first[:, None] * second[None, :] % count).astype(jnp.float32)
    return (jnp.cos(phase), jnp.sin(phase))


def widened(values):
    return lax.optimization_barrier(values).astype(jnp.float32)


def dot(a, b):
    return jnp.dot(a, b, preferred_element_type=F32)


def dot_t(a, b):
    return lax.dot_general(a, b, (((1,), (1,)), ((), ())), preferred_element_type=F32)


def in_vmem(kernel, out_shape, scratch=(), flops=0, moved=0):
    def call(*operands):
        specs = [pl.BlockSpec(memory_space=pltpu.VMEM)] * len(operands)
        return pl.pallas_call(
            kernel,
            out_shape=out_shape,
            in_specs=specs,
            out_specs=jax.tree.map(lambda _: pl.BlockSpec(memory_space=pltpu.VMEM), out_shape),
            scratch_shapes=list(scratch),
            compiler_params=pltpu.CompilerParams(vmem_limit_bytes=20 * 1024 * 1024),
            cost_estimate=pl.CostEstimate(flops=flops, bytes_accessed=moved, transcendentals=0),
        )(*operands)

    return call


def place():
    y, s, c = (lax.axis_index(a) for a in AXES)
    return y, lax.rem(s, 2), lax.div(s, 2), c


def low_lanes(shape):
    return lax.broadcasted_iota(jnp.int32, shape, len(shape) - 1) < 64


def half_turn(values):
    return pltpu.roll(values, 64, values.ndim - 1)


def both(first, second, low):
    return (
        jnp.where(low, first, half_turn(second)).astype(BF16),
        jnp.where(low, half_turn(first), second).astype(BF16),
    )


def quarter(p):
    y, x, _, _ = place()
    row = 1 - y if p // 2 else y
    column = 1 - x if p % 2 else x
    return pl.ds(pl.multiple_of(row * 512 + column * 256, 256), 256)


def copied(moves, sem):
    copies = [pltpu.make_async_copy(a, b, sem.at[i]) for i, (a, b) in enumerate(moves)]
    for copy in copies:
        copy.start()
    for copy in copies:
        copy.wait()


def cut_messages(tokens, key, query, out, filt, after, m1, m2, m3, own_o, away_o, away_f, sem):
    _, x, _, _ = place()
    moves = [(filt.at[:, :, :, quarter(1)], away_f)]
    for p, message in enumerate((m1, m2, m3), 1):
        column = 1 - x if p % 2 else x
        for i in range(2):
            lanes = pl.ds(pl.multiple_of(i * 512 + column * 256, 256), 256)
            moves.append((tokens.at[:, lanes], message.at[:, pl.ds(512 + i * 256, 256)]))
        moves.append((key.at[:, quarter(p)], message.at[:, pl.ds(0, 256)]))
        moves.append((query.at[:, quarter(p)], message.at[:, pl.ds(256, 256)]))
    moves += [(out.at[:, quarter(0)], own_o), (out.at[:, quarter(1)], away_o)]
    copied(moves, sem)


def copy_kernel(kernel, out_shape):
    def call(*operands):
        return pl.pallas_call(
            kernel,
            out_shape=out_shape,
            in_specs=[pl.BlockSpec(memory_space=pltpu.MemorySpace.HBM)] * len(operands),
            out_specs=[pl.BlockSpec(memory_space=pltpu.VMEM)] * len(out_shape),
            scratch_shapes=[pltpu.SemaphoreType.DMA((19,))],
            compiler_params=pltpu.CompilerParams(vmem_limit_bytes=61 * 1024 * 1024),
        )(*operands)

    return call


def pack_filter(filt, near, *refs):
    y, x, z, _ = place()
    packed, outs = refs[4], refs[:4]
    low = low_lanes((128, 128))
    for k in range(2):
        for j in range(2):
            base = pl.multiple_of(y * 512 + x * 256 + j * 128, 128)
            for part in range(2):
                if k:
                    pair = [near[part, i, :, pl.ds(j * 128, 128)].astype(F32) for i in range(2)]
                else:
                    pair = [filt[part, i, :, pl.ds(base, 128)].astype(F32) for i in range(2)]
                one, two = both(*pair, low)
                packed[2 * j, k, part] = one
                packed[2 * j + 1, k, part] = two
    for r in range(4):
        outs[r][...] = packed[z ^ r]


def join_tokens(*refs):
    _, x, _, _ = place()
    for i in range(2):
        lanes = pl.ds(pl.multiple_of(i * 512 + x * 256, 256), 256)
        refs[4][pl.ds(0, 128), pl.ds(i * 256, 256)] = refs[0][:, lanes]
    for p in (1, 2, 3):
        refs[4][pl.ds(p * 128, 128), :] = refs[p][:, pl.ds(512, 512)]


def value_kernel(mine, other, w0, w1, w2, w3, keep, give, acc):
    _, x, z, c = place()
    for r, piece in enumerate((w0, w1, w2, w3)):
        owner = lax.rem(z - r + 4, 4)
        lanes = pl.ds(pl.multiple_of(lax.rem(owner, 2) * 256, 256), 256)

        @pl.when(lax.div(owner, 2) == c)
        def _():
            term = dot(mine[:, lanes], piece[...])
            acc[...] = acc[...] + term if r else term

        @pl.when(lax.div(owner, 2) != c)
        def _():
            term = dot(other[:, lanes], piece[...])
            acc[...] = acc[...] + term if r else term

    keep[...] = acc[:, pl.ds(pl.multiple_of(x * 256, 256), 256)]
    away = pl.ds(pl.multiple_of(256 - x * 256, 256), 256)
    for p in range(4):
        give[pl.ds(p * 128, 128), :] = acc[pl.ds((p ^ 1) * 128, 128), away].astype(BF16)


def drive_kernel(keep, taken, g0, g1, g2, g3, skip, direct, o0, o1, o2, o3, drive, packed):
    _, _, z, _ = place()
    for p, gate in enumerate((g0, g1, g2, g3)):
        rows = pl.ds(p * 128, 128)
        value = (keep[rows, :] + taken[rows, :].astype(F32)).astype(BF16).astype(F32)
        held = ((gate[:, 0:256] if p else gate[:, quarter(0)]).astype(F32) * value).astype(BF16)
        drive[rows, :] = held
        direct[rows, :] = skip[:, quarter(0)] * held.astype(F32)
    low = low_lanes((256, 128))
    for j in range(2):
        lanes = pl.ds(j * 128, 128)
        first = drive[pl.ds(0, 256), lanes].astype(F32)
        second = drive[pl.ds(256, 256), lanes].astype(F32)
        packed[2 * j], packed[2 * j + 1] = both(first, second, low)
    for r, out in enumerate((o0, o1, o2, o3)):
        out[...] = packed[z ^ r]


def add(a, b):
    return b if a is None else a if b is None else a + b


def sub(a, b):
    return a if b is None else -b if a is None else a - b


def scaled(a, s):
    if a is None or abs(s) < 1e-9:
        return None
    if abs(s - 1) < 1e-9:
        return a
    if abs(s + 1) < 1e-9:
        return -a
    return a * np.float32(s)


def cmul(a, angle):
    co, si = math.cos(angle), math.sin(angle)
    return (sub(scaled(a[0], co), scaled(a[1], si)), add(scaled(a[0], si), scaled(a[1], co)))


def cadd(a, b):
    return (add(a[0], b[0]), add(a[1], b[1]))


def conj(a):
    return (a[0], None if a[1] is None else -a[1])


def short_transform(values, count, rows):
    if len(values) == 1:
        return [(values[0], None)] * rows
    half = count // 2
    need = half // 2 + 1
    even = short_transform(values[0::2], half, need)
    odd = short_transform(values[1::2], half, need)

    def at(t, k):
        k %= half
        return t[k] if k < need else conj(t[half - k])

    return [cadd(at(even, k), cmul(at(odd, k), -2 * math.pi * k / count)) for k in range(rows)]


def conv_kernel(*refs):
    drives, filters, (table, table_t) = refs[:4], refs[4:8], refs[8:10]
    outs, (data, filt, first, sums) = refs[10:14], refs[14:]
    _, x, z, _ = place()
    for r, block in enumerate(drives):
        base = 2 * (z ^ r)
        filt[base + x] = filters[r][0]
        filt[base + 1 - x] = filters[r][1]
        data[base + x] = block[pl.ds(0, 128), :]
        data[base + 1 - x] = block[pl.ds(128, 128), :]
    for i in range(8):
        rows = pl.ds(16 * i, 16)
        values = [data[a, rows, :].astype(F32) for a in range(8)]
        spectrum = short_transform(values, 16, 9)
        for k in range(9):
            re, im = spectrum[k]
            if im is None:
                im = jnp.zeros_like(re)
            first[k, rows, 0:128] = re.astype(BF16)
            first[k, rows, 128:256] = im.astype(BF16)
            if 0 < k < 8:
                first[16 - k, rows, 0:128] = re.astype(BF16)
                first[16 - k, rows, 128:256] = (-im).astype(BF16)
    low = low_lanes((128, 128))

    def back(k):
        four = dot(table[k], first[k])
        re = four[:128, :128] + four[128:, 128:]
        im = four[:128, 128:] - four[128:, :128]
        pair = [filt[k // 2, part].astype(F32) for part in range(2)]
        if k % 2 == 0:
            fr, fi = [jnp.where(low, f, half_turn(f)) for f in pair]
        else:
            fr, fi = [jnp.where(low, half_turn(f), f) for f in pair]
        product = jnp.concatenate([re * fr - im * fi, re * fi + im * fr], axis=1).astype(BF16)
        four = dot(table_t[k], product)
        return four[:128, :128] - four[128:, 128:], four[128:, :128] + four[:128, 128:]

    sums[0, pl.ds(0, 128)] = back(0)[0]
    sums[8, pl.ds(0, 128)] = back(8)[0]
    for k in range(1, 8):
        one, two = back(k), back(16 - k)
        sums[k, pl.ds(0, 128)] = one[0] + two[0]
        sums[k, pl.ds(128, 128)] = one[1] - two[1]
    for i in range(16):
        rows, below = pl.ds(8 * i, 8), pl.ds(128 + 8 * i, 8)
        scale = 1.0 / 2048
        re = [sums[k, rows, :] * scale for k in range(9)]
        im = [None] + [sums[k, below, :] * scale for k in range(1, 8)] + [None]
        for a in range(5):
            groups = [None] * 4
            for k in range(9):
                ang = 2 * math.pi * (k * a % 16) / 16
                groups[k % 2] = add(groups[k % 2], scaled(re[k], math.cos(ang)))
                groups[2 + k % 2] = sub(groups[2 + k % 2], scaled(im[k], math.sin(ang)))
            ec, oc, es, os = groups
            data[a, rows, :] = add(add(ec, oc), add(es, os)).astype(BF16)
            if 0 < a < 4:
                data[8 - a, rows, :] = sub(sub(add(ec, os), oc), es).astype(BF16)
    for r, out in enumerate(outs):
        base = 2 * (z ^ r)
        out[pl.ds(0, 128), :] = data[base + x]
        out[pl.ds(128, 128), :] = data[base + 1 - x]


def gate_kernel(e0, e1, e2, e3, direct, g0, g1, g2, g3, gated, conv):
    _, _, z, _ = place()
    for r, block in enumerate((e0, e1, e2, e3)):
        conv[z ^ r] = block[...]
    low = low_lanes((256, 128))
    for j in range(2):
        lanes = pl.ds(j * 128, 128)
        even, odd = conv[2 * j].astype(F32), conv[2 * j + 1].astype(F32)
        parts = (jnp.where(low, even, half_turn(odd)), jnp.where(low, half_turn(even), odd))
        for p, gate in enumerate((g0, g1, g2, g3)):
            rows = pl.ds(p * 128, 128)
            own = parts[p // 2][(p % 2) * 128 : (p % 2) * 128 + 128]
            y, x, _, _ = place()
            base = y * 512 + x * 256 if p == 0 else 256
            query = gate[:, pl.ds(pl.multiple_of(base + j * 128, 128), 128)].astype(F32)
            gated[rows, lanes] = (query * (own + direct[rows, lanes])).astype(BF16)


def sort_weight(*refs):
    pieces, keep, give = refs[:8], refs[8], refs[9]
    _, x, z, c = place()
    for r in range(4):
        owner = lax.rem(z - r + 4, 4)
        for k in range(2):
            to = 2 * lax.rem(owner, 2) + (1 - x if k else x)

            @pl.when(owner // 2 == c)
            def _():
                keep[to] = pieces[2 * r + k][...]

            @pl.when(owner // 2 != c)
            def _():
                give[to] = pieces[2 * r + k][...]


def out_kernel(blocks, gated, other, keep, theirs, *outs):
    for p, out in zip(blocks, outs):
        rows = pl.ds(p * 128, 128)
        for i in range(4):
            total = dot_t(gated[rows, :], keep[i]) + dot_t(other[rows, :], theirs[i])
            out[:, pl.ds(i * 256, 256)] = total.astype(out.dtype)


def tables():
    k = np.arange(16)[:, None, None] + 16 * np.arange(128)[None, :, None]
    phase = 2 * np.pi / 2048 * (k * np.arange(128)[None, None, :] % 2048)
    co, si = np.cos(phase), np.sin(phase)
    back = np.concatenate([co.transpose(0, 2, 1), si.transpose(0, 2, 1)], 1)
    return np.concatenate([co, si], 1).astype(jnp.bfloat16), back.astype(jnp.bfloat16)


def planes(tokens, gate_q, gate_k, w_value, skip, filter_spectrum, w_out):
    seq, deep = 8, 4

    def permute(values, move):
        pairs = []
        for g in range(2):
            for i in range(seq):
                for k in range(2):
                    g2, z2, x2, k2 = move(g, i // 2, i % 2, k)
                    pairs.append(((g * seq + i) * 2 + k, (g2 * seq + z2 * 2 + x2) * 2 + k2))
        return lax.ppermute(values, AXES, pairs)

    def to_x(values):
        return permute(values, lambda g, z, x, k: (g, z, 1 - x, k))

    def to_core(values):
        return permute(values, lambda g, z, x, k: (g, z, x, 1 - k))

    def with_z(values, r):
        return permute(values, lambda g, z, x, k: (g, z ^ r, x, k))

    def to_z(values, r):
        return permute(values, lambda g, z, x, k: (g, (z + r) % deep, x, k))

    def to_peer(values, p):
        return permute(values, lambda g, z, x, k: (g ^ (p // 2), z, x ^ (p % 2), k))

    def after(values, *done):
        return lax.optimization_barrier((values,) + done)[0]

    shape = jax.ShapeDtypeStruct
    block, square = shape((256, 128), BF16), shape((256, 256), BF16)
    own_v = lax.dynamic_slice_in_dim(w_value, lax.axis_index("grp") * 512, 512, axis=1)
    laid = [shape((128, 1024), BF16)] * 3 + [square] * 2 + [shape((2, 2, 128, 256), BF16)]
    *messages, own_o, away_o, away_f = copy_kernel(cut_messages, laid)(
        tokens, gate_k, gate_q, w_out, filter_spectrum, own_v
    )
    near = to_x(away_f)
    received = [to_peer(messages[p - 1], p) for p in (1, 2, 3)]
    filters = in_vmem(
        pack_filter,
        [shape((2, 2, 128, 128), BF16)] * 4,
        [pltpu.VMEM((4, 2, 2, 128, 128), BF16)],
        moved=1 << 20,
    )(filter_spectrum, near)
    filters = [filters[0]] + [with_z(filters[r], r) for r in (1, 2, 3)]
    v1 = to_z(own_v, 1)
    q1 = to_z(own_o, 1)
    v2 = to_z(v1, 1)
    q2 = to_z(after(q1, v1), 1)
    mine = in_vmem(join_tokens, shape((512, 512), BF16), moved=1 << 20)(tokens, after(received[0], q2), *received[1:])
    v3 = to_z(v2, 1)
    q3 = to_z(q2, 1)
    other = to_core(mine)
    got_o = to_x(after(away_o, v2))
    r1 = to_z(after(got_o, v3), 1)
    keep, give = in_vmem(
        value_kernel,
        [shape((512, 256), F32), shape((512, 256), BF16)],
        [pltpu.VMEM((512, 512), F32)],
        flops=1 << 29,
        moved=2 << 20,
    )(after(mine, q3, near, got_o), other, own_v, v1, v2, v3)
    r2 = to_z(after(r1, keep), 1)
    drive, *sends = in_vmem(
        drive_kernel,
        [shape((512, 256), F32)] + [block] * 4,
        [pltpu.VMEM((512, 256), BF16), pltpu.VMEM((4, 256, 128), BF16)],
        moved=2 << 20,
    )(after(keep, filters[1], filters[2]), to_x(give), gate_k, *received, skip[None, :])
    columns = [sends[0]] + [with_z(sends[r], r) for r in (1, 2, 3)]
    r3 = to_z(after(r2, *columns[1:]), 1)
    table, table_t = tables()
    sends = in_vmem(
        conv_kernel,
        [block] * 4,
        [
            pltpu.VMEM((8, 128, 128), BF16),
            pltpu.VMEM((8, 2, 128, 128), BF16),
            pltpu.VMEM((16, 128, 256), BF16),
            pltpu.VMEM((9, 256, 128), F32),
        ],
        flops=1 << 30,
        moved=5 << 20,
    )(*columns, *filters, table, table_t)
    rows = [sends[0]] + [with_z(sends[r], r) for r in (1, 2, 3)]

    hops = [own_o, got_o, q1, r1, q2, r2, q3, after(r3, *rows[1:])]
    quad = shape((4, 256, 256), BF16)
    keep, give = in_vmem(sort_weight, [quad] * 2, moved=2 << 20)(*hops)
    theirs = to_core(give)
    gated = in_vmem(
        gate_kernel, shape((512, 256), BF16), [pltpu.VMEM((4, 256, 128), BF16)], moved=1 << 20
    )(*rows, drive, gate_q, *received)
    gated_other = to_core(gated)
    summed = (gated, gated_other, keep, theirs)
    send = shape((128, 1024), BF16)
    far = in_vmem(functools.partial(out_kernel, (3, 1)), [send] * 2, flops=1 << 29, moved=2 << 20)
    close = in_vmem(
        functools.partial(out_kernel, (2, 0)),
        [send, shape((128, 1024), F32)],
        flops=1 << 29,
        moved=2 << 20,
    )
    to_xy, to_row = far(*summed)
    parts = [to_peer(to_xy, 3), to_peer(to_row, 1)]
    to_column, total = close(*summed)
    parts.append(to_peer(to_column, 2))
    for part in parts:
        total = total + part.astype(F32)
    return total.astype(BF16)


def shards(tokens, gate_q, gate_k, w_value, skip, filter_spectrum, w_out):
    seq_count = lax.axis_size("seq")
    position = lax.axis_index("seq")
    length_b = tokens.shape[0]
    columns_each = length_b // seq_count
    freq_rows = 2 * seq_count
    freqs_each = freq_rows // seq_count
    fft_length = freq_rows * length_b
    features = lax.all_gather(tokens, "ch", axis=1, tiled=True)
    value_weight, out_weight = (
        lax.all_gather(w_value, "seq", axis=0, tiled=True),
        lax.all_gather(w_out, "seq", axis=0, tiled=True),
    )
    value = jnp.dot(features, value_weight, preferred_element_type=jnp.float32)
    value = value.astype(jnp.bfloat16)
    drive = (gate_k.astype(jnp.float32) * widened(value)).astype(jnp.bfloat16)
    channels = drive.shape[1]
    columns = lax.all_to_all(drive[None], "seq", split_axis=1, concat_axis=0, tiled=True)
    index_rows = jnp.arange(freq_rows, dtype=jnp.int32)
    index_seq = jnp.arange(seq_count, dtype=jnp.int32)
    index_b = jnp.arange(length_b, dtype=jnp.int32)
    cos_first, sin_first = angles(freq_rows, index_rows, index_seq)
    cos_first = cos_first.astype(jnp.bfloat16)
    sin_first = sin_first.astype(jnp.bfloat16)
    flattened = columns.reshape(seq_count, columns_each * channels)
    real_part = jnp.dot(cos_first, flattened, preferred_element_type=jnp.float32)
    imag_part = jnp.dot(-sin_first, flattened, preferred_element_type=jnp.float32)
    real_part = real_part.reshape(freq_rows, columns_each, channels)
    imag_part = imag_part.reshape(freq_rows, columns_each, channels)
    mine_b = position * columns_each + jnp.arange(columns_each, dtype=jnp.int32)
    twist_cos, twist_sin = angles(fft_length, index_rows, mine_b)
    twist_cos = twist_cos[:, :, None]
    twist_sin = twist_sin[:, :, None]
    section = jnp.stack(
        [
            real_part * twist_cos + imag_part * twist_sin,
            imag_part * twist_cos - real_part * twist_sin,
        ]
    ).astype(jnp.bfloat16)
    spectral = lax.all_to_all(section, "seq", split_axis=1, concat_axis=2, tiled=True)
    cos_seq, sin_seq = angles(length_b, index_b, index_b)
    cos_seq = cos_seq.astype(jnp.bfloat16)
    sin_seq = sin_seq.astype(jnp.bfloat16)
    spectrum_real = jnp.einsum(
        "qb,kbc->kqc", cos_seq, spectral[0], preferred_element_type=jnp.float32
    ) + jnp.einsum("qb,kbc->kqc", sin_seq, spectral[1], preferred_element_type=jnp.float32)
    spectrum_imag = jnp.einsum(
        "qb,kbc->kqc", cos_seq, spectral[1], preferred_element_type=jnp.float32
    ) - jnp.einsum("qb,kbc->kqc", sin_seq, spectral[0], preferred_element_type=jnp.float32)
    filter_real = filter_spectrum[0].astype(jnp.float32)
    filter_imag = filter_spectrum[1].astype(jnp.float32)
    product = jnp.stack(
        [
            spectrum_real * filter_real - spectrum_imag * filter_imag,
            spectrum_real * filter_imag + spectrum_imag * filter_real,
        ]
    ).astype(jnp.bfloat16)
    inverse_real = jnp.einsum(
        "qb,kqc->kbc", cos_seq, product[0], preferred_element_type=jnp.float32
    ) - jnp.einsum("qb,kqc->kbc", sin_seq, product[1], preferred_element_type=jnp.float32)
    inverse_imag = jnp.einsum(
        "qb,kqc->kbc", sin_seq, product[0], preferred_element_type=jnp.float32
    ) + jnp.einsum("qb,kqc->kbc", cos_seq, product[1], preferred_element_type=jnp.float32)
    mine_k = position * freqs_each + jnp.arange(freqs_each, dtype=jnp.int32)
    back_cos, back_sin = angles(fft_length, mine_k, index_b)
    back_cos = back_cos[:, :, None]
    back_sin = back_sin[:, :, None]
    back = jnp.stack(
        [
            inverse_real * back_cos - inverse_imag * back_sin,
            inverse_real * back_sin + inverse_imag * back_cos,
        ]
    ).astype(jnp.bfloat16)
    returned = lax.all_to_all(back, "seq", split_axis=2, concat_axis=1, tiled=True)
    flat_real = returned[0].reshape(freq_rows, columns_each * channels)
    flat_imag = returned[1].reshape(freq_rows, columns_each * channels)
    conv = jnp.dot(cos_first.T, flat_real, preferred_element_type=jnp.float32) - jnp.dot(
        sin_first.T, flat_imag, preferred_element_type=jnp.float32
    )
    conv = (
        (conv * (1.0 / fft_length)).reshape(seq_count, columns_each, channels).astype(jnp.bfloat16)
    )
    conv_rows = lax.all_to_all(conv, "seq", split_axis=0, concat_axis=1, tiled=True)[0]
    gated = (
        gate_q.astype(jnp.float32) * (widened(conv_rows) + skip[None, :] * widened(drive))
    ).astype(jnp.bfloat16)
    partial_value = lax.dot_general(
        gated, out_weight, (((1,), (1,)), ((), ())), preferred_element_type=jnp.float32
    )
    return lax.psum_scatter(
        partial_value.astype(jnp.bfloat16), "ch", scatter_dimension=1, tiled=True
    )


def solution(mesh):
    placed = (
        P(("grp", "seq"), "ch"),
        P(("grp", "seq"), "ch"),
        P(("grp", "seq"), "ch"),
        P("seq", "ch"),
        P("ch"),
        P(None, "seq", None, "ch"),
        P("seq", "ch"),
    )
    sizes = mesh.shape
    body = planes if (sizes["grp"], sizes["seq"], sizes["ch"]) == (2, 8, 2) else shards
    return jax.shard_map(
        body, mesh=mesh, in_specs=placed, out_specs=P(("grp", "seq"), "ch"), check_vma=False
    )
```

```python
import functools
import math

import jax
import jax.numpy as jnp
import numpy as np
from jax import lax
from jax.experimental import pallas as pl
from jax.experimental.pallas import tpu as pltpu
from jax.sharding import PartitionSpec as P

AXES = ("grp", "seq", "ch")
BF16 = jnp.bfloat16
F32 = jnp.float32


def angles(count, first, second):
    phase = 2.0 * math.pi / count * (first[:, None] * second[None, :] % count).astype(jnp.float32)
    return (jnp.cos(phase), jnp.sin(phase))


def widened(values):
    return lax.optimization_barrier(values).astype(jnp.float32)


def dot(a, b):
    return jnp.dot(a, b, preferred_element_type=F32)


def dot_t(a, b):
    return lax.dot_general(a, b, (((1,), (1,)), ((), ())), preferred_element_type=F32)


def in_vmem(kernel, out_shape, scratch=(), flops=0, moved=0):
    def call(*operands):
        specs = [pl.BlockSpec(memory_space=pltpu.VMEM)] * len(operands)
        return pl.pallas_call(
            kernel,
            out_shape=out_shape,
            in_specs=specs,
            out_specs=jax.tree.map(lambda _: pl.BlockSpec(memory_space=pltpu.VMEM), out_shape),
            scratch_shapes=list(scratch),
            compiler_params=pltpu.CompilerParams(vmem_limit_bytes=20 * 1024 * 1024),
            cost_estimate=pl.CostEstimate(flops=flops, bytes_accessed=moved, transcendentals=0),
        )(*operands)

    return call


def place():
    y, s, c = (lax.axis_index(a) for a in AXES)
    return y, lax.rem(s, 2), lax.div(s, 2), c


def low_lanes(shape):
    return lax.broadcasted_iota(jnp.int32, shape, len(shape) - 1) < 64


def half_turn(values):
    return pltpu.roll(values, 64, values.ndim - 1)


def both(first, second, low):
    return (
        jnp.where(low, first, half_turn(second)).astype(BF16),
        jnp.where(low, half_turn(first), second).astype(BF16),
    )


def quarter(p):
    y, x, _, _ = place()
    row = 1 - y if p // 2 else y
    column = 1 - x if p % 2 else x
    return pl.ds(pl.multiple_of(row * 512 + column * 256, 256), 256)


def copied(moves, sem):
    copies = [pltpu.make_async_copy(a, b, sem.at[i]) for i, (a, b) in enumerate(moves)]
    for copy in copies:
        copy.start()
    for copy in copies:
        copy.wait()


def cut_messages(tokens, key, query, out, filt, after, m1, m2, m3, own_o, away_o, away_f, sem):
    _, x, _, _ = place()
    moves = [(filt.at[:, :, :, quarter(1)], away_f)]
    for p, message in enumerate((m1, m2, m3), 1):
        column = 1 - x if p % 2 else x
        for i in range(2):
            lanes = pl.ds(pl.multiple_of(i * 512 + column * 256, 256), 256)
            moves.append((tokens.at[:, lanes], message.at[:, pl.ds(512 + i * 256, 256)]))
        moves.append((key.at[:, quarter(p)], message.at[:, pl.ds(0, 256)]))
        moves.append((query.at[:, quarter(p)], message.at[:, pl.ds(256, 256)]))
    moves += [(out.at[:, quarter(0)], own_o), (out.at[:, quarter(1)], away_o)]
    copied(moves, sem)


def copy_kernel(kernel, out_shape):
    def call(*operands):
        return pl.pallas_call(
            kernel,
            out_shape=out_shape,
            in_specs=[pl.BlockSpec(memory_space=pltpu.MemorySpace.HBM)] * len(operands),
            out_specs=[pl.BlockSpec(memory_space=pltpu.VMEM)] * len(out_shape),
            scratch_shapes=[pltpu.SemaphoreType.DMA((19,))],
            compiler_params=pltpu.CompilerParams(vmem_limit_bytes=61 * 1024 * 1024),
        )(*operands)

    return call


def pack_filter(filt, near, *refs):
    y, x, z, _ = place()
    packed, outs = refs[4], refs[:4]
    low = low_lanes((128, 128))
    for k in range(2):
        for j in range(2):
            base = pl.multiple_of(y * 512 + x * 256 + j * 128, 128)
            for part in range(2):
                if k:
                    pair = [near[part, i, :, pl.ds(j * 128, 128)].astype(F32) for i in range(2)]
                else:
                    pair = [filt[part, i, :, pl.ds(base, 128)].astype(F32) for i in range(2)]
                one, two = both(*pair, low)
                packed[2 * j, k, part] = one
                packed[2 * j + 1, k, part] = two
    for r in range(4):
        outs[r][...] = packed[lax.rem(z + r, 4)]


def join_tokens(*refs):
    _, x, _, _ = place()
    for i in range(2):
        lanes = pl.ds(pl.multiple_of(i * 512 + x * 256, 256), 256)
        refs[4][pl.ds(0, 128), pl.ds(i * 256, 256)] = refs[0][:, lanes]
    for p in (1, 2, 3):
        refs[4][pl.ds(p * 128, 128), :] = refs[p][:, pl.ds(512, 512)]


def value_kernel(mine, other, w0, w1, w2, w3, keep, give, acc):
    _, x, z, c = place()
    for r, piece in enumerate((w0, w1, w2, w3)):
        owner = lax.rem(z - r + 4, 4)
        lanes = pl.ds(pl.multiple_of(lax.rem(owner, 2) * 256, 256), 256)

        @pl.when(lax.div(owner, 2) == c)
        def _():
            term = dot(mine[:, lanes], piece[...])
            acc[...] = acc[...] + term if r else term

        @pl.when(lax.div(owner, 2) != c)
        def _():
            term = dot(other[:, lanes], piece[...])
            acc[...] = acc[...] + term if r else term

    keep[...] = acc[:, pl.ds(pl.multiple_of(x * 256, 256), 256)]
    away = pl.ds(pl.multiple_of(256 - x * 256, 256), 256)
    for p in range(4):
        give[pl.ds(p * 128, 128), :] = acc[pl.ds((p ^ 1) * 128, 128), away].astype(BF16)


def drive_kernel(keep, taken, g0, g1, g2, g3, skip, direct, o0, o1, o2, o3, drive, packed):
    _, _, z, _ = place()
    for p, gate in enumerate((g0, g1, g2, g3)):
        rows = pl.ds(p * 128, 128)
        value = (keep[rows, :] + taken[rows, :].astype(F32)).astype(BF16).astype(F32)
        held = ((gate[:, 0:256] if p else gate[:, quarter(0)]).astype(F32) * value).astype(BF16)
        drive[rows, :] = held
        direct[rows, :] = skip[:, quarter(0)] * held.astype(F32)
    low = low_lanes((256, 128))
    for j in range(2):
        lanes = pl.ds(j * 128, 128)
        first = drive[pl.ds(0, 256), lanes].astype(F32)
        second = drive[pl.ds(256, 256), lanes].astype(F32)
        packed[2 * j], packed[2 * j + 1] = both(first, second, low)
    for r, out in enumerate((o0, o1, o2, o3)):
        out[...] = packed[lax.rem(z + r, 4)]


def add(a, b):
    return b if a is None else a if b is None else a + b


def sub(a, b):
    return a if b is None else -b if a is None else a - b


def scaled(a, s):
    if a is None or abs(s) < 1e-9:
        return None
    if abs(s - 1) < 1e-9:
        return a
    if abs(s + 1) < 1e-9:
        return -a
    return a * np.float32(s)


def cmul(a, angle):
    co, si = math.cos(angle), math.sin(angle)
    return (sub(scaled(a[0], co), scaled(a[1], si)), add(scaled(a[0], si), scaled(a[1], co)))


def cadd(a, b):
    return (add(a[0], b[0]), add(a[1], b[1]))


def conj(a):
    return (a[0], None if a[1] is None else -a[1])


def short_transform(values, count, rows):
    if len(values) == 1:
        return [(values[0], None)] * rows
    half = count // 2
    need = half // 2 + 1
    even = short_transform(values[0::2], half, need)
    odd = short_transform(values[1::2], half, need)

    def at(t, k):
        k %= half
        return t[k] if k < need else conj(t[half - k])

    return [cadd(at(even, k), cmul(at(odd, k), -2 * math.pi * k / count)) for k in range(rows)]


def conv_kernel(*refs):
    drives, filters, (table, table_t) = refs[:4], refs[4:8], refs[8:10]
    outs, (data, filt, first, sums) = refs[10:14], refs[14:]
    _, x, z, _ = place()
    for r, block in enumerate(drives):
        base = 2 * lax.rem(z - r + 4, 4)
        filt[base + x] = filters[r][0]
        filt[base + 1 - x] = filters[r][1]
        data[base + x] = block[pl.ds(0, 128), :]
        data[base + 1 - x] = block[pl.ds(128, 128), :]
    for i in range(8):
        rows = pl.ds(16 * i, 16)
        values = [data[a, rows, :].astype(F32) for a in range(8)]
        spectrum = short_transform(values, 16, 9)
        for k in range(9):
            re, im = spectrum[k]
            if im is None:
                im = jnp.zeros_like(re)
            first[k, rows, 0:128] = re.astype(BF16)
            first[k, rows, 128:256] = im.astype(BF16)
            if 0 < k < 8:
                first[16 - k, rows, 0:128] = re.astype(BF16)
                first[16 - k, rows, 128:256] = (-im).astype(BF16)
    low = low_lanes((128, 128))

    def back(k):
        four = dot(table[k], first[k])
        re = four[:128, :128] + four[128:, 128:]
        im = four[:128, 128:] - four[128:, :128]
        pair = [filt[k // 2, part].astype(F32) for part in range(2)]
        if k % 2 == 0:
            fr, fi = [jnp.where(low, f, half_turn(f)) for f in pair]
        else:
            fr, fi = [jnp.where(low, half_turn(f), f) for f in pair]
        product = jnp.concatenate([re * fr - im * fi, re * fi + im * fr], axis=1).astype(BF16)
        four = dot(table_t[k], product)
        return four[:128, :128] - four[128:, 128:], four[128:, :128] + four[:128, 128:]

    sums[0, pl.ds(0, 128)] = back(0)[0]
    sums[8, pl.ds(0, 128)] = back(8)[0]
    for k in range(1, 8):
        one, two = back(k), back(16 - k)
        sums[k, pl.ds(0, 128)] = one[0] + two[0]
        sums[k, pl.ds(128, 128)] = one[1] - two[1]
    for i in range(16):
        rows, below = pl.ds(8 * i, 8), pl.ds(128 + 8 * i, 8)
        scale = 1.0 / 2048
        re = [sums[k, rows, :] * scale for k in range(9)]
        im = [None] + [sums[k, below, :] * scale for k in range(1, 8)] + [None]
        for a in range(5):
            groups = [None] * 4
            for k in range(9):
                ang = 2 * math.pi * (k * a % 16) / 16
                groups[k % 2] = add(groups[k % 2], scaled(re[k], math.cos(ang)))
                groups[2 + k % 2] = sub(groups[2 + k % 2], scaled(im[k], math.sin(ang)))
            ec, oc, es, os = groups
            data[a, rows, :] = add(add(ec, oc), add(es, os)).astype(BF16)
            if 0 < a < 4:
                data[8 - a, rows, :] = sub(sub(add(ec, os), oc), es).astype(BF16)
    for r, out in enumerate(outs):
        base = 2 * lax.rem(z + r, 4)
        out[pl.ds(0, 128), :] = data[base + x]
        out[pl.ds(128, 128), :] = data[base + 1 - x]


def gate_kernel(e0, e1, e2, e3, direct, g0, g1, g2, g3, gated, conv):
    _, _, z, _ = place()
    for r, block in enumerate((e0, e1, e2, e3)):
        conv[lax.rem(z - r + 4, 4)] = block[...]
    low = low_lanes((256, 128))
    for j in range(2):
        lanes = pl.ds(j * 128, 128)
        even, odd = conv[2 * j].astype(F32), conv[2 * j + 1].astype(F32)
        parts = (jnp.where(low, even, half_turn(odd)), jnp.where(low, half_turn(even), odd))
        for p, gate in enumerate((g0, g1, g2, g3)):
            rows = pl.ds(p * 128, 128)
            own = parts[p // 2][(p % 2) * 128 : (p % 2) * 128 + 128]
            y, x, _, _ = place()
            base = y * 512 + x * 256 if p == 0 else 256
            query = gate[:, pl.ds(pl.multiple_of(base + j * 128, 128), 128)].astype(F32)
            gated[rows, lanes] = (query * (own + direct[rows, lanes])).astype(BF16)


def sort_weight(*refs):
    pieces, keep, give = refs[:8], refs[8], refs[9]
    _, x, z, c = place()
    for r in range(4):
        owner = lax.rem(z - r + 4, 4)
        for k in range(2):
            to = 2 * lax.rem(owner, 2) + (1 - x if k else x)

            @pl.when(owner // 2 == c)
            def _():
                keep[to] = pieces[2 * r + k][...]

            @pl.when(owner // 2 != c)
            def _():
                give[to] = pieces[2 * r + k][...]


def out_kernel(blocks, gated, other, keep, theirs, *outs):
    for p, out in zip(blocks, outs):
        rows = pl.ds(p * 128, 128)
        for i in range(4):
            total = dot_t(gated[rows, :], keep[i]) + dot_t(other[rows, :], theirs[i])
            out[:, pl.ds(i * 256, 256)] = total.astype(out.dtype)


def tables():
    k = np.arange(16)[:, None, None] + 16 * np.arange(128)[None, :, None]
    phase = 2 * np.pi / 2048 * (k * np.arange(128)[None, None, :] % 2048)
    co, si = np.cos(phase), np.sin(phase)
    back = np.concatenate([co.transpose(0, 2, 1), si.transpose(0, 2, 1)], 1)
    return np.concatenate([co, si], 1).astype(jnp.bfloat16), back.astype(jnp.bfloat16)


def planes(tokens, gate_q, gate_k, w_value, skip, filter_spectrum, w_out):
    seq, deep = 8, 4

    def permute(values, move):
        pairs = []
        for g in range(2):
            for i in range(seq):
                for k in range(2):
                    g2, z2, x2, k2 = move(g, i // 2, i % 2, k)
                    pairs.append(((g * seq + i) * 2 + k, (g2 * seq + z2 * 2 + x2) * 2 + k2))
        return lax.ppermute(values, AXES, pairs)

    def to_x(values):
        return permute(values, lambda g, z, x, k: (g, z, 1 - x, k))

    def to_core(values):
        return permute(values, lambda g, z, x, k: (g, z, x, 1 - k))

    def to_z(values, r):
        return permute(values, lambda g, z, x, k: (g, (z + r) % deep, x, k))

    def to_peer(values, p):
        return permute(values, lambda g, z, x, k: (g ^ (p // 2), z, x ^ (p % 2), k))

    def after(values, *done):
        return lax.optimization_barrier((values,) + done)[0]

    shape = jax.ShapeDtypeStruct
    block, square = shape((256, 128), BF16), shape((256, 256), BF16)
    own_v = lax.dynamic_slice_in_dim(w_value, lax.axis_index("grp") * 512, 512, axis=1)
    laid = [shape((128, 1024), BF16)] * 3 + [square] * 2 + [shape((2, 2, 128, 256), BF16)]
    *messages, own_o, away_o, away_f = copy_kernel(cut_messages, laid)(
        tokens, gate_k, gate_q, w_out, filter_spectrum, own_v
    )
    near = to_x(away_f)
    received = [to_peer(messages[p - 1], p) for p in (1, 2, 3)]
    filters = in_vmem(
        pack_filter,
        [shape((2, 2, 128, 128), BF16)] * 4,
        [pltpu.VMEM((4, 2, 2, 128, 128), BF16)],
        moved=1 << 20,
    )(filter_spectrum, near)
    filters = [filters[0]] + [to_z(filters[r], r) for r in (1, 2, 3)]
    v1 = to_z(own_v, 1)
    q1 = to_z(own_o, 1)
    v2 = to_z(v1, 1)
    q2 = to_z(after(q1, v1), 1)
    mine = in_vmem(join_tokens, shape((512, 512), BF16), moved=1 << 20)(tokens, after(received[0], q2), *received[1:])
    v3 = to_z(v2, 1)
    other = to_core(mine)
    got_o = to_x(after(away_o, v1))
    r1 = to_z(after(got_o, v2), 1)
    keep, give = in_vmem(
        value_kernel,
        [shape((512, 256), F32), shape((512, 256), BF16)],
        [pltpu.VMEM((512, 512), F32)],
        flops=1 << 29,
        moved=2 << 20,
    )(after(mine, r1, near), other, own_v, v1, v2, v3)
    r2 = to_z(after(r1, keep), 1)
    drive, *sends = in_vmem(
        drive_kernel,
        [shape((512, 256), F32)] + [block] * 4,
        [pltpu.VMEM((512, 256), BF16), pltpu.VMEM((4, 256, 128), BF16)],
        moved=2 << 20,
    )(after(keep, filters[1]), to_x(give), gate_k, *received, skip[None, :])
    columns = [sends[0]] + [to_z(sends[r], r) for r in (1, 2, 3)]
    r3 = to_z(after(r2, *filters[2:], columns[1]), 1)
    q3 = to_z(after(q2, *columns[1:]), 1)
    table, table_t = tables()
    sends = in_vmem(
        conv_kernel,
        [block] * 4,
        [
            pltpu.VMEM((8, 128, 128), BF16),
            pltpu.VMEM((8, 2, 128, 128), BF16),
            pltpu.VMEM((16, 128, 256), BF16),
            pltpu.VMEM((9, 256, 128), F32),
        ],
        flops=1 << 30,
        moved=5 << 20,
    )(*columns, *filters, table, table_t)
    rows = [sends[0]] + [to_z(sends[r], r) for r in (1, 2, 3)]

    hops = [own_o, got_o, q1, r1, q2, r2, q3, after(r3, *rows[1:])]
    quad = shape((4, 256, 256), BF16)
    keep, give = in_vmem(sort_weight, [quad] * 2, moved=2 << 20)(*hops)
    theirs = to_core(give)
    gated = in_vmem(
        gate_kernel, shape((512, 256), BF16), [pltpu.VMEM((4, 256, 128), BF16)], moved=1 << 20
    )(*rows, drive, gate_q, *received)
    gated_other = to_core(gated)
    summed = (gated, gated_other, keep, theirs)
    send = shape((128, 1024), BF16)
    far = in_vmem(functools.partial(out_kernel, (3, 1)), [send] * 2, flops=1 << 29, moved=2 << 20)
    close = in_vmem(
        functools.partial(out_kernel, (2, 0)),
        [send, shape((128, 1024), F32)],
        flops=1 << 29,
        moved=2 << 20,
    )
    to_xy, to_row = far(*summed)
    parts = [to_peer(to_xy, 3), to_peer(to_row, 1)]
    to_column, total = close(*summed)
    parts.append(to_peer(to_column, 2))
    for part in parts:
        total = total + part.astype(F32)
    return total.astype(BF16)


def shards(tokens, gate_q, gate_k, w_value, skip, filter_spectrum, w_out):
    seq_count = lax.axis_size("seq")
    position = lax.axis_index("seq")
    length_b = tokens.shape[0]
    columns_each = length_b // seq_count
    freq_rows = 2 * seq_count
    freqs_each = freq_rows // seq_count
    fft_length = freq_rows * length_b
    features = lax.all_gather(tokens, "ch", axis=1, tiled=True)
    value_weight, out_weight = (
        lax.all_gather(w_value, "seq", axis=0, tiled=True),
        lax.all_gather(w_out, "seq", axis=0, tiled=True),
    )
    value = jnp.dot(features, value_weight, preferred_element_type=jnp.float32)
    value = value.astype(jnp.bfloat16)
    drive = (gate_k.astype(jnp.float32) * widened(value)).astype(jnp.bfloat16)
    channels = drive.shape[1]
    columns = lax.all_to_all(drive[None], "seq", split_axis=1, concat_axis=0, tiled=True)
    index_rows = jnp.arange(freq_rows, dtype=jnp.int32)
    index_seq = jnp.arange(seq_count, dtype=jnp.int32)
    index_b = jnp.arange(length_b, dtype=jnp.int32)
    cos_first, sin_first = angles(freq_rows, index_rows, index_seq)
    cos_first = cos_first.astype(jnp.bfloat16)
    sin_first = sin_first.astype(jnp.bfloat16)
    flattened = columns.reshape(seq_count, columns_each * channels)
    real_part = jnp.dot(cos_first, flattened, preferred_element_type=jnp.float32)
    imag_part = jnp.dot(-sin_first, flattened, preferred_element_type=jnp.float32)
    real_part = real_part.reshape(freq_rows, columns_each, channels)
    imag_part = imag_part.reshape(freq_rows, columns_each, channels)
    mine_b = position * columns_each + jnp.arange(columns_each, dtype=jnp.int32)
    twist_cos, twist_sin = angles(fft_length, index_rows, mine_b)
    twist_cos = twist_cos[:, :, None]
    twist_sin = twist_sin[:, :, None]
    section = jnp.stack(
        [
            real_part * twist_cos + imag_part * twist_sin,
            imag_part * twist_cos - real_part * twist_sin,
        ]
    ).astype(jnp.bfloat16)
    spectral = lax.all_to_all(section, "seq", split_axis=1, concat_axis=2, tiled=True)
    cos_seq, sin_seq = angles(length_b, index_b, index_b)
    cos_seq = cos_seq.astype(jnp.bfloat16)
    sin_seq = sin_seq.astype(jnp.bfloat16)
    spectrum_real = jnp.einsum(
        "qb,kbc->kqc", cos_seq, spectral[0], preferred_element_type=jnp.float32
    ) + jnp.einsum("qb,kbc->kqc", sin_seq, spectral[1], preferred_element_type=jnp.float32)
    spectrum_imag = jnp.einsum(
        "qb,kbc->kqc", cos_seq, spectral[1], preferred_element_type=jnp.float32
    ) - jnp.einsum("qb,kbc->kqc", sin_seq, spectral[0], preferred_element_type=jnp.float32)
    filter_real = filter_spectrum[0].astype(jnp.float32)
    filter_imag = filter_spectrum[1].astype(jnp.float32)
    product = jnp.stack(
        [
            spectrum_real * filter_real - spectrum_imag * filter_imag,
            spectrum_real * filter_imag + spectrum_imag * filter_real,
        ]
    ).astype(jnp.bfloat16)
    inverse_real = jnp.einsum(
        "qb,kqc->kbc", cos_seq, product[0], preferred_element_type=jnp.float32
    ) - jnp.einsum("qb,kqc->kbc", sin_seq, product[1], preferred_element_type=jnp.float32)
    inverse_imag = jnp.einsum(
        "qb,kqc->kbc", sin_seq, product[0], preferred_element_type=jnp.float32
    ) + jnp.einsum("qb,kqc->kbc", cos_seq, product[1], preferred_element_type=jnp.float32)
    mine_k = position * freqs_each + jnp.arange(freqs_each, dtype=jnp.int32)
    back_cos, back_sin = angles(fft_length, mine_k, index_b)
    back_cos = back_cos[:, :, None]
    back_sin = back_sin[:, :, None]
    back = jnp.stack(
        [
            inverse_real * back_cos - inverse_imag * back_sin,
            inverse_real * back_sin + inverse_imag * back_cos,
        ]
    ).astype(jnp.bfloat16)
    returned = lax.all_to_all(back, "seq", split_axis=2, concat_axis=1, tiled=True)
    flat_real = returned[0].reshape(freq_rows, columns_each * channels)
    flat_imag = returned[1].reshape(freq_rows, columns_each * channels)
    conv = jnp.dot(cos_first.T, flat_real, preferred_element_type=jnp.float32) - jnp.dot(
        sin_first.T, flat_imag, preferred_element_type=jnp.float32
    )
    conv = (
        (conv * (1.0 / fft_length)).reshape(seq_count, columns_each, channels).astype(jnp.bfloat16)
    )
    conv_rows = lax.all_to_all(conv, "seq", split_axis=0, concat_axis=1, tiled=True)[0]
    gated = (
        gate_q.astype(jnp.float32) * (widened(conv_rows) + skip[None, :] * widened(drive))
    ).astype(jnp.bfloat16)
    partial_value = lax.dot_general(
        gated, out_weight, (((1,), (1,)), ((), ())), preferred_element_type=jnp.float32
    )
    return lax.psum_scatter(
        partial_value.astype(jnp.bfloat16), "ch", scatter_dimension=1, tiled=True
    )


def solution(mesh):
    placed = (
        P(("grp", "seq"), "ch"),
        P(("grp", "seq"), "ch"),
        P(("grp", "seq"), "ch"),
        P("seq", "ch"),
        P("ch"),
        P(None, "seq", None, "ch"),
        P("seq", "ch"),
    )
    sizes = mesh.shape
    body = planes if (sizes["grp"], sizes["seq"], sizes["ch"]) == (2, 8, 2) else shards
    return jax.shard_map(
        body, mesh=mesh, in_specs=placed, out_specs=P(("grp", "seq"), "ch"), check_vma=False
    )
```

```python
import functools
import math

import jax
import jax.numpy as jnp
import numpy as np
from jax import lax
from jax.experimental import pallas as pl
from jax.experimental.pallas import tpu as pltpu
from jax.sharding import PartitionSpec as P

AXES = ("grp", "seq", "ch")
BF16 = jnp.bfloat16
F32 = jnp.float32


def angles(count, first, second):
    phase = 2.0 * math.pi / count * (first[:, None] * second[None, :] % count).astype(jnp.float32)
    return (jnp.cos(phase), jnp.sin(phase))


def widened(values):
    return lax.optimization_barrier(values).astype(jnp.float32)


def dot(a, b):
    return jnp.dot(a, b, preferred_element_type=F32)


def dot_t(a, b):
    return lax.dot_general(a, b, (((1,), (1,)), ((), ())), preferred_element_type=F32)


def in_vmem(kernel, out_shape, scratch=(), flops=0, moved=0):
    def call(*operands):
        specs = [pl.BlockSpec(memory_space=pltpu.VMEM)] * len(operands)
        return pl.pallas_call(
            kernel,
            out_shape=out_shape,
            in_specs=specs,
            out_specs=jax.tree.map(lambda _: pl.BlockSpec(memory_space=pltpu.VMEM), out_shape),
            scratch_shapes=list(scratch),
            compiler_params=pltpu.CompilerParams(vmem_limit_bytes=20 * 1024 * 1024),
            cost_estimate=pl.CostEstimate(flops=flops, bytes_accessed=moved, transcendentals=0),
        )(*operands)

    return call


def place():
    y, s, c = (lax.axis_index(a) for a in AXES)
    return y, lax.rem(s, 2), lax.div(s, 2), c


def low_lanes(shape):
    return lax.broadcasted_iota(jnp.int32, shape, len(shape) - 1) < 64


def half_turn(values):
    return pltpu.roll(values, 64, values.ndim - 1)


def both(first, second, low):
    return (
        jnp.where(low, first, half_turn(second)).astype(BF16),
        jnp.where(low, half_turn(first), second).astype(BF16),
    )


def quarter(p):
    y, x, _, _ = place()
    row = 1 - y if p // 2 else y
    column = 1 - x if p % 2 else x
    return pl.ds(pl.multiple_of(row * 512 + column * 256, 256), 256)


def copied(moves, sem):
    copies = [pltpu.make_async_copy(a, b, sem.at[i]) for i, (a, b) in enumerate(moves)]
    for copy in copies:
        copy.start()
    for copy in copies:
        copy.wait()


def cut_messages(tokens, key, query, out, filt, after, m1, m2, m3, own_o, away_o, away_f, sem):
    _, x, _, _ = place()
    moves = [(filt.at[:, :, :, quarter(1)], away_f)]
    for p, message in enumerate((m1, m2, m3), 1):
        column = 1 - x if p % 2 else x
        for i in range(2):
            lanes = pl.ds(pl.multiple_of(i * 512 + column * 256, 256), 256)
            moves.append((tokens.at[:, lanes], message.at[:, pl.ds(512 + i * 256, 256)]))
        moves.append((key.at[:, quarter(p)], message.at[:, pl.ds(0, 256)]))
        moves.append((query.at[:, quarter(p)], message.at[:, pl.ds(256, 256)]))
    moves += [(out.at[:, quarter(0)], own_o), (out.at[:, quarter(1)], away_o)]
    copied(moves, sem)


def copy_kernel(kernel, out_shape):
    def call(*operands):
        return pl.pallas_call(
            kernel,
            out_shape=out_shape,
            in_specs=[pl.BlockSpec(memory_space=pltpu.MemorySpace.HBM)] * len(operands),
            out_specs=[pl.BlockSpec(memory_space=pltpu.VMEM)] * len(out_shape),
            scratch_shapes=[pltpu.SemaphoreType.DMA((19,))],
            compiler_params=pltpu.CompilerParams(vmem_limit_bytes=61 * 1024 * 1024),
        )(*operands)

    return call


def pack_filter(filt, near, *refs):
    y, x, z, _ = place()
    packed, outs = refs[4], refs[:4]
    low = low_lanes((128, 128))
    for k in range(2):
        for j in range(2):
            base = pl.multiple_of(y * 512 + x * 256 + j * 128, 128)
            for part in range(2):
                if k:
                    pair = [near[part, i, :, pl.ds(j * 128, 128)].astype(F32) for i in range(2)]
                else:
                    pair = [filt[part, i, :, pl.ds(base, 128)].astype(F32) for i in range(2)]
                one, two = both(*pair, low)
                packed[2 * j, k, part] = one
                packed[2 * j + 1, k, part] = two
    for r in range(4):
        outs[r][...] = packed[lax.rem(z + r, 4)]


def join_tokens(*refs):
    _, x, _, _ = place()
    for i in range(2):
        lanes = pl.ds(pl.multiple_of(i * 512 + x * 256, 256), 256)
        refs[4][pl.ds(0, 128), pl.ds(i * 256, 256)] = refs[0][:, lanes]
    for p in (1, 2, 3):
        refs[4][pl.ds(p * 128, 128), :] = refs[p][:, pl.ds(512, 512)]


def value_kernel(mine, other, w0, w1, w2, w3, keep, give, acc):
    _, x, z, c = place()
    for r, piece in enumerate((w0, w1, w2, w3)):
        owner = lax.rem(z - r + 4, 4)
        lanes = pl.ds(pl.multiple_of(lax.rem(owner, 2) * 256, 256), 256)

        @pl.when(lax.div(owner, 2) == c)
        def _():
            term = dot(mine[:, lanes], piece[...])
            acc[...] = acc[...] + term if r else term

        @pl.when(lax.div(owner, 2) != c)
        def _():
            term = dot(other[:, lanes], piece[...])
            acc[...] = acc[...] + term if r else term

    keep[...] = acc[:, pl.ds(pl.multiple_of(x * 256, 256), 256)]
    away = pl.ds(pl.multiple_of(256 - x * 256, 256), 256)
    for p in range(4):
        give[pl.ds(p * 128, 128), :] = acc[pl.ds((p ^ 1) * 128, 128), away].astype(BF16)


def drive_kernel(keep, taken, g0, g1, g2, g3, skip, direct, o0, o1, o2, o3, drive, packed):
    _, _, z, _ = place()
    for p, gate in enumerate((g0, g1, g2, g3)):
        rows = pl.ds(p * 128, 128)
        value = (keep[rows, :] + taken[rows, :].astype(F32)).astype(BF16).astype(F32)
        held = ((gate[:, 0:256] if p else gate[:, quarter(0)]).astype(F32) * value).astype(BF16)
        drive[rows, :] = held
        direct[rows, :] = skip[:, quarter(0)] * held.astype(F32)
    low = low_lanes((256, 128))
    for j in range(2):
        lanes = pl.ds(j * 128, 128)
        first = drive[pl.ds(0, 256), lanes].astype(F32)
        second = drive[pl.ds(256, 256), lanes].astype(F32)
        packed[2 * j], packed[2 * j + 1] = both(first, second, low)
    for r, out in enumerate((o0, o1, o2, o3)):
        out[...] = packed[lax.rem(z + r, 4)]


def add(a, b):
    return b if a is None else a if b is None else a + b


def sub(a, b):
    return a if b is None else -b if a is None else a - b


def scaled(a, s):
    if a is None or abs(s) < 1e-9:
        return None
    if abs(s - 1) < 1e-9:
        return a
    if abs(s + 1) < 1e-9:
        return -a
    return a * np.float32(s)


def cmul(a, angle):
    co, si = math.cos(angle), math.sin(angle)
    return (sub(scaled(a[0], co), scaled(a[1], si)), add(scaled(a[0], si), scaled(a[1], co)))


def cadd(a, b):
    return (add(a[0], b[0]), add(a[1], b[1]))


def conj(a):
    return (a[0], None if a[1] is None else -a[1])


def short_transform(values, count, rows):
    if len(values) == 1:
        return [(values[0], None)] * rows
    half = count // 2
    need = half // 2 + 1
    even = short_transform(values[0::2], half, need)
    odd = short_transform(values[1::2], half, need)

    def at(t, k):
        k %= half
        return t[k] if k < need else conj(t[half - k])

    return [cadd(at(even, k), cmul(at(odd, k), -2 * math.pi * k / count)) for k in range(rows)]


def conv_kernel(*refs):
    drives, filters, (table, table_t) = refs[:4], refs[4:8], refs[8:10]
    outs, (data, filt, first, sums) = refs[10:14], refs[14:]
    _, x, z, _ = place()
    for r, block in enumerate(drives):
        base = 2 * lax.rem(z - r + 4, 4)
        filt[base + x] = filters[r][0]
        filt[base + 1 - x] = filters[r][1]
        data[base + x] = block[pl.ds(0, 128), :]
        data[base + 1 - x] = block[pl.ds(128, 128), :]
    for i in range(8):
        rows = pl.ds(16 * i, 16)
        values = [data[a, rows, :].astype(F32) for a in range(8)]
        spectrum = short_transform(values, 16, 9)
        for k in range(9):
            re, im = spectrum[k]
            if im is None:
                im = jnp.zeros_like(re)
            first[k, rows, 0:128] = re.astype(BF16)
            first[k, rows, 128:256] = im.astype(BF16)
            if 0 < k < 8:
                first[16 - k, rows, 0:128] = re.astype(BF16)
                first[16 - k, rows, 128:256] = (-im).astype(BF16)
    low = low_lanes((128, 128))

    def back(k):
        four = dot(table[k], first[k])
        re = four[:128, :128] + four[128:, 128:]
        im = four[:128, 128:] - four[128:, :128]
        pair = [filt[k // 2, part].astype(F32) for part in range(2)]
        if k % 2 == 0:
            fr, fi = [jnp.where(low, f, half_turn(f)) for f in pair]
        else:
            fr, fi = [jnp.where(low, half_turn(f), f) for f in pair]
        product = jnp.concatenate([re * fr - im * fi, re * fi + im * fr], axis=1).astype(BF16)
        four = dot(table_t[k], product)
        return four[:128, :128] - four[128:, 128:], four[128:, :128] + four[:128, 128:]

    sums[0, pl.ds(0, 128)] = back(0)[0]
    sums[8, pl.ds(0, 128)] = back(8)[0]
    for k in range(1, 8):
        one, two = back(k), back(16 - k)
        sums[k, pl.ds(0, 128)] = one[0] + two[0]
        sums[k, pl.ds(128, 128)] = one[1] - two[1]
    for i in range(16):
        rows, below = pl.ds(8 * i, 8), pl.ds(128 + 8 * i, 8)
        scale = 1.0 / 2048
        re = [sums[k, rows, :] * scale for k in range(9)]
        im = [None] + [sums[k, below, :] * scale for k in range(1, 8)] + [None]
        for a in range(5):
            groups = [None] * 4
            for k in range(9):
                ang = 2 * math.pi * (k * a % 16) / 16
                groups[k % 2] = add(groups[k % 2], scaled(re[k], math.cos(ang)))
                groups[2 + k % 2] = sub(groups[2 + k % 2], scaled(im[k], math.sin(ang)))
            ec, oc, es, os = groups
            data[a, rows, :] = add(add(ec, oc), add(es, os)).astype(BF16)
            if 0 < a < 4:
                data[8 - a, rows, :] = sub(sub(add(ec, os), oc), es).astype(BF16)
    for r, out in enumerate(outs):
        base = 2 * lax.rem(z + r, 4)
        out[pl.ds(0, 128), :] = data[base + x]
        out[pl.ds(128, 128), :] = data[base + 1 - x]


def gate_kernel(e0, e1, e2, e3, direct, g0, g1, g2, g3, gated, conv):
    _, _, z, _ = place()
    for r, block in enumerate((e0, e1, e2, e3)):
        conv[lax.rem(z - r + 4, 4)] = block[...]
    low = low_lanes((256, 128))
    for j in range(2):
        lanes = pl.ds(j * 128, 128)
        even, odd = conv[2 * j].astype(F32), conv[2 * j + 1].astype(F32)
        parts = (jnp.where(low, even, half_turn(odd)), jnp.where(low, half_turn(even), odd))
        for p, gate in enumerate((g0, g1, g2, g3)):
            rows = pl.ds(p * 128, 128)
            own = parts[p // 2][(p % 2) * 128 : (p % 2) * 128 + 128]
            y, x, _, _ = place()
            base = y * 512 + x * 256 if p == 0 else 256
            query = gate[:, pl.ds(pl.multiple_of(base + j * 128, 128), 128)].astype(F32)
            gated[rows, lanes] = (query * (own + direct[rows, lanes])).astype(BF16)


def sort_weight(*refs):
    pieces, keep, give = refs[:8], refs[8], refs[9]
    _, x, z, c = place()
    for r in range(4):
        owner = lax.rem(z - r + 4, 4)
        for k in range(2):
            to = 2 * lax.rem(owner, 2) + (1 - x if k else x)

            @pl.when(owner // 2 == c)
            def _():
                keep[to] = pieces[2 * r + k][...]

            @pl.when(owner // 2 != c)
            def _():
                give[to] = pieces[2 * r + k][...]


def out_kernel(blocks, gated, other, keep, theirs, *outs):
    for p, out in zip(blocks, outs):
        rows = pl.ds(p * 128, 128)
        for i in range(4):
            total = dot_t(gated[rows, :], keep[i]) + dot_t(other[rows, :], theirs[i])
            out[:, pl.ds(i * 256, 256)] = total.astype(out.dtype)


def tables():
    k = np.arange(16)[:, None, None] + 16 * np.arange(128)[None, :, None]
    phase = 2 * np.pi / 2048 * (k * np.arange(128)[None, None, :] % 2048)
    co, si = np.cos(phase), np.sin(phase)
    back = np.concatenate([co.transpose(0, 2, 1), si.transpose(0, 2, 1)], 1)
    return np.concatenate([co, si], 1).astype(jnp.bfloat16), back.astype(jnp.bfloat16)


def planes(tokens, gate_q, gate_k, w_value, skip, filter_spectrum, w_out):
    seq, deep = 8, 4

    def permute(values, move):
        pairs = []
        for g in range(2):
            for i in range(seq):
                for k in range(2):
                    g2, z2, x2, k2 = move(g, i // 2, i % 2, k)
                    pairs.append(((g * seq + i) * 2 + k, (g2 * seq + z2 * 2 + x2) * 2 + k2))
        return lax.ppermute(values, AXES, pairs)

    def to_x(values):
        return permute(values, lambda g, z, x, k: (g, z, 1 - x, k))

    def to_core(values):
        return permute(values, lambda g, z, x, k: (g, z, x, 1 - k))

    def to_z(values, r):
        return permute(values, lambda g, z, x, k: (g, (z + r) % deep, x, k))

    def to_peer(values, p):
        return permute(values, lambda g, z, x, k: (g ^ (p // 2), z, x ^ (p % 2), k))

    def after(values, *done):
        return lax.optimization_barrier((values,) + done)[0]

    shape = jax.ShapeDtypeStruct
    block, square = shape((256, 128), BF16), shape((256, 256), BF16)
    own_v = lax.dynamic_slice_in_dim(w_value, lax.axis_index("grp") * 512, 512, axis=1)
    laid = [shape((128, 1024), BF16)] * 3 + [square] * 2 + [shape((2, 2, 128, 256), BF16)]
    *messages, own_o, away_o, away_f = copy_kernel(cut_messages, laid)(
        tokens, gate_k, gate_q, w_out, filter_spectrum, own_v
    )
    near = to_x(away_f)
    received = [to_peer(messages[p - 1], p) for p in (1, 2, 3)]
    filters = in_vmem(
        pack_filter,
        [shape((2, 2, 128, 128), BF16)] * 4,
        [pltpu.VMEM((4, 2, 2, 128, 128), BF16)],
        moved=1 << 20,
    )(filter_spectrum, near)
    filters = [filters[0]] + [to_z(filters[r], r) for r in (1, 2, 3)]
    v1 = to_z(own_v, 1)
    q1 = to_z(after(own_o, v1), 1)
    v2 = to_z(v1, 1)
    q2 = to_z(after(q1, v2), 1)
    mine = in_vmem(join_tokens, shape((512, 512), BF16), moved=1 << 20)(tokens, after(received[0], q1), *received[1:])
    v3 = to_z(v2, 1)
    other = to_core(mine)
    got_o = to_x(after(away_o, v1))
    r1 = to_z(after(got_o, v2), 1)
    keep, give = in_vmem(
        value_kernel,
        [shape((512, 256), F32), shape((512, 256), BF16)],
        [pltpu.VMEM((512, 512), F32)],
        flops=1 << 29,
        moved=2 << 20,
    )(after(mine, q2, r1, near), other, own_v, v1, v2, v3)
    r2 = to_z(after(r1, keep), 1)
    drive, *sends = in_vmem(
        drive_kernel,
        [shape((512, 256), F32)] + [block] * 4,
        [pltpu.VMEM((512, 256), BF16), pltpu.VMEM((4, 256, 128), BF16)],
        moved=2 << 20,
    )(after(keep, filters[1]), to_x(give), gate_k, *received, skip[None, :])
    columns = [sends[0]] + [to_z(sends[r], r) for r in (1, 2, 3)]
    r3 = to_z(after(r2, *filters[2:], columns[1]), 1)
    q3 = to_z(after(q2, columns[1]), 1)
    table, table_t = tables()
    sends = in_vmem(
        conv_kernel,
        [block] * 4,
        [
            pltpu.VMEM((8, 128, 128), BF16),
            pltpu.VMEM((8, 2, 128, 128), BF16),
            pltpu.VMEM((16, 128, 256), BF16),
            pltpu.VMEM((9, 256, 128), F32),
        ],
        flops=1 << 30,
        moved=5 << 20,
    )(*columns, *filters, table, table_t)
    rows = [sends[0]] + [to_z(sends[r], r) for r in (1, 2, 3)]

    hops = [own_o, got_o, q1, r1, q2, r2, q3, after(r3, *rows[1:])]
    quad = shape((4, 256, 256), BF16)
    keep, give = in_vmem(sort_weight, [quad] * 2, moved=2 << 20)(*hops)
    theirs = to_core(give)
    gated = in_vmem(
        gate_kernel, shape((512, 256), BF16), [pltpu.VMEM((4, 256, 128), BF16)], moved=1 << 20
    )(*rows, drive, gate_q, *received)
    gated_other = to_core(gated)
    summed = (gated, gated_other, keep, theirs)
    send = shape((128, 1024), BF16)
    far = in_vmem(functools.partial(out_kernel, (3, 1)), [send] * 2, flops=1 << 29, moved=2 << 20)
    close = in_vmem(
        functools.partial(out_kernel, (2, 0)),
        [send, shape((128, 1024), F32)],
        flops=1 << 29,
        moved=2 << 20,
    )
    to_xy, to_row = far(*summed)
    parts = [to_peer(to_xy, 3), to_peer(to_row, 1)]
    to_column, total = close(*summed)
    parts.append(to_peer(to_column, 2))
    for part in parts:
        total = total + part.astype(F32)
    return total.astype(BF16)


def shards(tokens, gate_q, gate_k, w_value, skip, filter_spectrum, w_out):
    seq_count = lax.axis_size("seq")
    position = lax.axis_index("seq")
    length_b = tokens.shape[0]
    columns_each = length_b // seq_count
    freq_rows = 2 * seq_count
    freqs_each = freq_rows // seq_count
    fft_length = freq_rows * length_b
    features = lax.all_gather(tokens, "ch", axis=1, tiled=True)
    value_weight, out_weight = (
        lax.all_gather(w_value, "seq", axis=0, tiled=True),
        lax.all_gather(w_out, "seq", axis=0, tiled=True),
    )
    value = jnp.dot(features, value_weight, preferred_element_type=jnp.float32)
    value = value.astype(jnp.bfloat16)
    drive = (gate_k.astype(jnp.float32) * widened(value)).astype(jnp.bfloat16)
    channels = drive.shape[1]
    columns = lax.all_to_all(drive[None], "seq", split_axis=1, concat_axis=0, tiled=True)
    index_rows = jnp.arange(freq_rows, dtype=jnp.int32)
    index_seq = jnp.arange(seq_count, dtype=jnp.int32)
    index_b = jnp.arange(length_b, dtype=jnp.int32)
    cos_first, sin_first = angles(freq_rows, index_rows, index_seq)
    cos_first = cos_first.astype(jnp.bfloat16)
    sin_first = sin_first.astype(jnp.bfloat16)
    flattened = columns.reshape(seq_count, columns_each * channels)
    real_part = jnp.dot(cos_first, flattened, preferred_element_type=jnp.float32)
    imag_part = jnp.dot(-sin_first, flattened, preferred_element_type=jnp.float32)
    real_part = real_part.reshape(freq_rows, columns_each, channels)
    imag_part = imag_part.reshape(freq_rows, columns_each, channels)
    mine_b = position * columns_each + jnp.arange(columns_each, dtype=jnp.int32)
    twist_cos, twist_sin = angles(fft_length, index_rows, mine_b)
    twist_cos = twist_cos[:, :, None]
    twist_sin = twist_sin[:, :, None]
    section = jnp.stack(
        [
            real_part * twist_cos + imag_part * twist_sin,
            imag_part * twist_cos - real_part * twist_sin,
        ]
    ).astype(jnp.bfloat16)
    spectral = lax.all_to_all(section, "seq", split_axis=1, concat_axis=2, tiled=True)
    cos_seq, sin_seq = angles(length_b, index_b, index_b)
    cos_seq = cos_seq.astype(jnp.bfloat16)
    sin_seq = sin_seq.astype(jnp.bfloat16)
    spectrum_real = jnp.einsum(
        "qb,kbc->kqc", cos_seq, spectral[0], preferred_element_type=jnp.float32
    ) + jnp.einsum("qb,kbc->kqc", sin_seq, spectral[1], preferred_element_type=jnp.float32)
    spectrum_imag = jnp.einsum(
        "qb,kbc->kqc", cos_seq, spectral[1], preferred_element_type=jnp.float32
    ) - jnp.einsum("qb,kbc->kqc", sin_seq, spectral[0], preferred_element_type=jnp.float32)
    filter_real = filter_spectrum[0].astype(jnp.float32)
    filter_imag = filter_spectrum[1].astype(jnp.float32)
    product = jnp.stack(
        [
            spectrum_real * filter_real - spectrum_imag * filter_imag,
            spectrum_real * filter_imag + spectrum_imag * filter_real,
        ]
    ).astype(jnp.bfloat16)
    inverse_real = jnp.einsum(
        "qb,kqc->kbc", cos_seq, product[0], preferred_element_type=jnp.float32
    ) - jnp.einsum("qb,kqc->kbc", sin_seq, product[1], preferred_element_type=jnp.float32)
    inverse_imag = jnp.einsum(
        "qb,kqc->kbc", sin_seq, product[0], preferred_element_type=jnp.float32
    ) + jnp.einsum("qb,kqc->kbc", cos_seq, product[1], preferred_element_type=jnp.float32)
    mine_k = position * freqs_each + jnp.arange(freqs_each, dtype=jnp.int32)
    back_cos, back_sin = angles(fft_length, mine_k, index_b)
    back_cos = back_cos[:, :, None]
    back_sin = back_sin[:, :, None]
    back = jnp.stack(
        [
            inverse_real * back_cos - inverse_imag * back_sin,
            inverse_real * back_sin + inverse_imag * back_cos,
        ]
    ).astype(jnp.bfloat16)
    returned = lax.all_to_all(back, "seq", split_axis=2, concat_axis=1, tiled=True)
    flat_real = returned[0].reshape(freq_rows, columns_each * channels)
    flat_imag = returned[1].reshape(freq_rows, columns_each * channels)
    conv = jnp.dot(cos_first.T, flat_real, preferred_element_type=jnp.float32) - jnp.dot(
        sin_first.T, flat_imag, preferred_element_type=jnp.float32
    )
    conv = (
        (conv * (1.0 / fft_length)).reshape(seq_count, columns_each, channels).astype(jnp.bfloat16)
    )
    conv_rows = lax.all_to_all(conv, "seq", split_axis=0, concat_axis=1, tiled=True)[0]
    gated = (
        gate_q.astype(jnp.float32) * (widened(conv_rows) + skip[None, :] * widened(drive))
    ).astype(jnp.bfloat16)
    partial_value = lax.dot_general(
        gated, out_weight, (((1,), (1,)), ((), ())), preferred_element_type=jnp.float32
    )
    return lax.psum_scatter(
        partial_value.astype(jnp.bfloat16), "ch", scatter_dimension=1, tiled=True
    )


def solution(mesh):
    placed = (
        P(("grp", "seq"), "ch"),
        P(("grp", "seq"), "ch"),
        P(("grp", "seq"), "ch"),
        P("seq", "ch"),
        P("ch"),
        P(None, "seq", None, "ch"),
        P("seq", "ch"),
    )
    sizes = mesh.shape
    body = planes if (sizes["grp"], sizes["seq"], sizes["ch"]) == (2, 8, 2) else shards
    return jax.shard_map(
        body, mesh=mesh, in_specs=placed, out_specs=P(("grp", "seq"), "ch"), check_vma=False
    )
```

```python
import functools
import math

import jax
import jax.numpy as jnp
import numpy as np
from jax import lax
from jax.experimental import pallas as pl
from jax.experimental.pallas import tpu as pltpu
from jax.sharding import PartitionSpec as P

AXES = ("grp", "seq", "ch")
BF16 = jnp.bfloat16
F32 = jnp.float32


def angles(count, first, second):
    phase = 2.0 * math.pi / count * (first[:, None] * second[None, :] % count).astype(jnp.float32)
    return (jnp.cos(phase), jnp.sin(phase))


def widened(values):
    return lax.optimization_barrier(values).astype(jnp.float32)


def dot(a, b):
    return jnp.dot(a, b, preferred_element_type=F32)


def dot_t(a, b):
    return lax.dot_general(a, b, (((1,), (1,)), ((), ())), preferred_element_type=F32)


def in_vmem(kernel, out_shape, scratch=(), flops=0, moved=0):
    def call(*operands):
        specs = [pl.BlockSpec(memory_space=pltpu.VMEM)] * len(operands)
        return pl.pallas_call(
            kernel,
            out_shape=out_shape,
            in_specs=specs,
            out_specs=jax.tree.map(lambda _: pl.BlockSpec(memory_space=pltpu.VMEM), out_shape),
            scratch_shapes=list(scratch),
            compiler_params=pltpu.CompilerParams(vmem_limit_bytes=20 * 1024 * 1024),
            cost_estimate=pl.CostEstimate(flops=flops, bytes_accessed=moved, transcendentals=0),
        )(*operands)

    return call


def place():
    y, s, c = (lax.axis_index(a) for a in AXES)
    return y, lax.rem(s, 2), lax.div(s, 2), c


def before(z, r):
    at = lax.rem((z ^ lax.div(z, 2)) - r + 4, 4)
    return at ^ lax.div(at, 2)


def low_lanes(shape):
    return lax.broadcasted_iota(jnp.int32, shape, len(shape) - 1) < 64


def half_turn(values):
    return pltpu.roll(values, 64, values.ndim - 1)


def both(first, second, low):
    return (
        jnp.where(low, first, half_turn(second)).astype(BF16),
        jnp.where(low, half_turn(first), second).astype(BF16),
    )


def quarter(p):
    y, x, _, _ = place()
    row = 1 - y if p // 2 else y
    column = 1 - x if p % 2 else x
    return pl.ds(pl.multiple_of(row * 512 + column * 256, 256), 256)


def copied(moves, sem):
    copies = [pltpu.make_async_copy(a, b, sem.at[i]) for i, (a, b) in enumerate(moves)]
    for copy in copies:
        copy.start()
    for copy in copies:
        copy.wait()


def cut_messages(tokens, key, query, out, filt, after, m1, m2, m3, own_o, away_o, away_f, sem):
    _, x, _, _ = place()
    moves = [(filt.at[:, :, :, quarter(1)], away_f)]
    for p, message in enumerate((m1, m2, m3), 1):
        column = 1 - x if p % 2 else x
        for i in range(2):
            lanes = pl.ds(pl.multiple_of(i * 512 + column * 256, 256), 256)
            moves.append((tokens.at[:, lanes], message.at[:, pl.ds(512 + i * 256, 256)]))
        moves.append((key.at[:, quarter(p)], message.at[:, pl.ds(0, 256)]))
        moves.append((query.at[:, quarter(p)], message.at[:, pl.ds(256, 256)]))
    moves += [(out.at[:, quarter(0)], own_o), (out.at[:, quarter(1)], away_o)]
    copied(moves, sem)


def copy_kernel(kernel, out_shape):
    def call(*operands):
        return pl.pallas_call(
            kernel,
            out_shape=out_shape,
            in_specs=[pl.BlockSpec(memory_space=pltpu.MemorySpace.HBM)] * len(operands),
            out_specs=[pl.BlockSpec(memory_space=pltpu.VMEM)] * len(out_shape),
            scratch_shapes=[pltpu.SemaphoreType.DMA((19,))],
            compiler_params=pltpu.CompilerParams(vmem_limit_bytes=61 * 1024 * 1024),
        )(*operands)

    return call


def pack_filter(filt, near, *refs):
    y, x, z, _ = place()
    packed, outs = refs[4], refs[:4]
    low = low_lanes((128, 128))
    for k in range(2):
        for j in range(2):
            base = pl.multiple_of(y * 512 + x * 256 + j * 128, 128)
            for part in range(2):
                if k:
                    pair = [near[part, i, :, pl.ds(j * 128, 128)].astype(F32) for i in range(2)]
                else:
                    pair = [filt[part, i, :, pl.ds(base, 128)].astype(F32) for i in range(2)]
                one, two = both(*pair, low)
                packed[2 * j, k, part] = one
                packed[2 * j + 1, k, part] = two
    for r in range(4):
        outs[r][...] = packed[lax.rem(z + r, 4)]


def join_tokens(*refs):
    _, x, _, _ = place()
    for i in range(2):
        lanes = pl.ds(pl.multiple_of(i * 512 + x * 256, 256), 256)
        refs[4][pl.ds(0, 128), pl.ds(i * 256, 256)] = refs[0][:, lanes]
    for p in (1, 2, 3):
        refs[4][pl.ds(p * 128, 128), :] = refs[p][:, pl.ds(512, 512)]


def value_kernel(mine, other, w0, w1, w2, w3, keep, give, acc):
    _, x, z, c = place()
    for r, piece in enumerate((w0, w1, w2, w3)):
        owner = before(z, r)
        lanes = pl.ds(pl.multiple_of(lax.rem(owner, 2) * 256, 256), 256)

        @pl.when(lax.div(owner, 2) == c)
        def _():
            term = dot(mine[:, lanes], piece[...])
            acc[...] = acc[...] + term if r else term

        @pl.when(lax.div(owner, 2) != c)
        def _():
            term = dot(other[:, lanes], piece[...])
            acc[...] = acc[...] + term if r else term

    keep[...] = acc[:, pl.ds(pl.multiple_of(x * 256, 256), 256)]
    away = pl.ds(pl.multiple_of(256 - x * 256, 256), 256)
    for p in range(4):
        give[pl.ds(p * 128, 128), :] = acc[pl.ds((p ^ 1) * 128, 128), away].astype(BF16)


def drive_kernel(keep, taken, g0, g1, g2, g3, skip, direct, o0, o1, o2, o3, drive, packed):
    _, _, z, _ = place()
    for p, gate in enumerate((g0, g1, g2, g3)):
        rows = pl.ds(p * 128, 128)
        value = (keep[rows, :] + taken[rows, :].astype(F32)).astype(BF16).astype(F32)
        held = ((gate[:, 0:256] if p else gate[:, quarter(0)]).astype(F32) * value).astype(BF16)
        drive[rows, :] = held
        direct[rows, :] = skip[:, quarter(0)] * held.astype(F32)
    low = low_lanes((256, 128))
    for j in range(2):
        lanes = pl.ds(j * 128, 128)
        first = drive[pl.ds(0, 256), lanes].astype(F32)
        second = drive[pl.ds(256, 256), lanes].astype(F32)
        packed[2 * j], packed[2 * j + 1] = both(first, second, low)
    for r, out in enumerate((o0, o1, o2, o3)):
        out[...] = packed[lax.rem(z + r, 4)]


def add(a, b):
    return b if a is None else a if b is None else a + b


def sub(a, b):
    return a if b is None else -b if a is None else a - b


def scaled(a, s):
    if a is None or abs(s) < 1e-9:
        return None
    if abs(s - 1) < 1e-9:
        return a
    if abs(s + 1) < 1e-9:
        return -a
    return a * np.float32(s)


def cmul(a, angle):
    co, si = math.cos(angle), math.sin(angle)
    return (sub(scaled(a[0], co), scaled(a[1], si)), add(scaled(a[0], si), scaled(a[1], co)))


def cadd(a, b):
    return (add(a[0], b[0]), add(a[1], b[1]))


def conj(a):
    return (a[0], None if a[1] is None else -a[1])


def short_transform(values, count, rows):
    if len(values) == 1:
        return [(values[0], None)] * rows
    half = count // 2
    need = half // 2 + 1
    even = short_transform(values[0::2], half, need)
    odd = short_transform(values[1::2], half, need)

    def at(t, k):
        k %= half
        return t[k] if k < need else conj(t[half - k])

    return [cadd(at(even, k), cmul(at(odd, k), -2 * math.pi * k / count)) for k in range(rows)]


def conv_kernel(*refs):
    drives, filters, (table, table_t) = refs[:4], refs[4:8], refs[8:10]
    outs, (data, filt, first, sums) = refs[10:14], refs[14:]
    _, x, z, _ = place()
    for r, block in enumerate(drives):
        base = 2 * lax.rem(z - r + 4, 4)
        filt[base + x] = filters[r][0]
        filt[base + 1 - x] = filters[r][1]
        data[base + x] = block[pl.ds(0, 128), :]
        data[base + 1 - x] = block[pl.ds(128, 128), :]
    for i in range(8):
        rows = pl.ds(16 * i, 16)
        values = [data[a, rows, :].astype(F32) for a in range(8)]
        spectrum = short_transform(values, 16, 9)
        for k in range(9):
            re, im = spectrum[k]
            if im is None:
                im = jnp.zeros_like(re)
            first[k, rows, 0:128] = re.astype(BF16)
            first[k, rows, 128:256] = im.astype(BF16)
            if 0 < k < 8:
                first[16 - k, rows, 0:128] = re.astype(BF16)
                first[16 - k, rows, 128:256] = (-im).astype(BF16)
    low = low_lanes((128, 128))

    def back(k):
        four = dot(table[k], first[k])
        re = four[:128, :128] + four[128:, 128:]
        im = four[:128, 128:] - four[128:, :128]
        pair = [filt[k // 2, part].astype(F32) for part in range(2)]
        if k % 2 == 0:
            fr, fi = [jnp.where(low, f, half_turn(f)) for f in pair]
        else:
            fr, fi = [jnp.where(low, half_turn(f), f) for f in pair]
        product = jnp.concatenate([re * fr - im * fi, re * fi + im * fr], axis=1).astype(BF16)
        four = dot(table_t[k], product)
        return four[:128, :128] - four[128:, 128:], four[128:, :128] + four[:128, 128:]

    sums[0, pl.ds(0, 128)] = back(0)[0]
    sums[8, pl.ds(0, 128)] = back(8)[0]
    for k in range(1, 8):
        one, two = back(k), back(16 - k)
        sums[k, pl.ds(0, 128)] = one[0] + two[0]
        sums[k, pl.ds(128, 128)] = one[1] - two[1]
    for i in range(16):
        rows, below = pl.ds(8 * i, 8), pl.ds(128 + 8 * i, 8)
        scale = 1.0 / 2048
        re = [sums[k, rows, :] * scale for k in range(9)]
        im = [None] + [sums[k, below, :] * scale for k in range(1, 8)] + [None]
        for a in range(5):
            groups = [None] * 4
            for k in range(9):
                ang = 2 * math.pi * (k * a % 16) / 16
                groups[k % 2] = add(groups[k % 2], scaled(re[k], math.cos(ang)))
                groups[2 + k % 2] = sub(groups[2 + k % 2], scaled(im[k], math.sin(ang)))
            ec, oc, es, os = groups
            data[a, rows, :] = add(add(ec, oc), add(es, os)).astype(BF16)
            if 0 < a < 4:
                data[8 - a, rows, :] = sub(sub(add(ec, os), oc), es).astype(BF16)
    for r, out in enumerate(outs):
        base = 2 * lax.rem(z + r, 4)
        out[pl.ds(0, 128), :] = data[base + x]
        out[pl.ds(128, 128), :] = data[base + 1 - x]


def gate_kernel(e0, e1, e2, e3, direct, g0, g1, g2, g3, gated, conv):
    _, _, z, _ = place()
    for r, block in enumerate((e0, e1, e2, e3)):
        conv[lax.rem(z - r + 4, 4)] = block[...]
    low = low_lanes((256, 128))
    for j in range(2):
        lanes = pl.ds(j * 128, 128)
        even, odd = conv[2 * j].astype(F32), conv[2 * j + 1].astype(F32)
        parts = (jnp.where(low, even, half_turn(odd)), jnp.where(low, half_turn(even), odd))
        for p, gate in enumerate((g0, g1, g2, g3)):
            rows = pl.ds(p * 128, 128)
            own = parts[p // 2][(p % 2) * 128 : (p % 2) * 128 + 128]
            y, x, _, _ = place()
            base = y * 512 + x * 256 if p == 0 else 256
            query = gate[:, pl.ds(pl.multiple_of(base + j * 128, 128), 128)].astype(F32)
            gated[rows, lanes] = (query * (own + direct[rows, lanes])).astype(BF16)


def sort_weight(*refs):
    pieces, keep, give = refs[:8], refs[8], refs[9]
    _, x, z, c = place()
    for r in range(4):
        owner = before(z, r)
        for k in range(2):
            to = 2 * lax.rem(owner, 2) + (1 - x if k else x)

            @pl.when(owner // 2 == c)
            def _():
                keep[to] = pieces[2 * r + k][...]

            @pl.when(owner // 2 != c)
            def _():
                give[to] = pieces[2 * r + k][...]


def out_kernel(blocks, gated, other, keep, theirs, *outs):
    for p, out in zip(blocks, outs):
        rows = pl.ds(p * 128, 128)
        for i in range(4):
            total = dot_t(gated[rows, :], keep[i]) + dot_t(other[rows, :], theirs[i])
            out[:, pl.ds(i * 256, 256)] = total.astype(out.dtype)


def tables():
    k = np.arange(16)[:, None, None] + 16 * np.arange(128)[None, :, None]
    phase = 2 * np.pi / 2048 * (k * np.arange(128)[None, None, :] % 2048)
    co, si = np.cos(phase), np.sin(phase)
    back = np.concatenate([co.transpose(0, 2, 1), si.transpose(0, 2, 1)], 1)
    return np.concatenate([co, si], 1).astype(jnp.bfloat16), back.astype(jnp.bfloat16)


def planes(tokens, gate_q, gate_k, w_value, skip, filter_spectrum, w_out):
    seq, deep = 8, 4

    def permute(values, move):
        pairs = []
        for g in range(2):
            for i in range(seq):
                for k in range(2):
                    g2, z2, x2, k2 = move(g, i // 2, i % 2, k)
                    pairs.append(((g * seq + i) * 2 + k, (g2 * seq + z2 * 2 + x2) * 2 + k2))
        return lax.ppermute(values, AXES, pairs)

    def to_x(values):
        return permute(values, lambda g, z, x, k: (g, z, 1 - x, k))

    def to_core(values):
        return permute(values, lambda g, z, x, k: (g, z, x, 1 - k))

    def onward(values):
        ring = (1, 3, 0, 2)
        return permute(values, lambda g, z, x, k: (g, ring[z], x, k))

    def to_z(values, r):
        return permute(values, lambda g, z, x, k: (g, (z + r) % deep, x, k))

    def to_peer(values, p):
        return permute(values, lambda g, z, x, k: (g ^ (p // 2), z, x ^ (p % 2), k))

    def after(values, *done):
        return lax.optimization_barrier((values,) + done)[0]

    shape = jax.ShapeDtypeStruct
    block, square = shape((256, 128), BF16), shape((256, 256), BF16)
    own_v = lax.dynamic_slice_in_dim(w_value, lax.axis_index("grp") * 512, 512, axis=1)
    laid = [shape((128, 1024), BF16)] * 3 + [square] * 2 + [shape((2, 2, 128, 256), BF16)]
    *messages, own_o, away_o, away_f = copy_kernel(cut_messages, laid)(
        tokens, gate_k, gate_q, w_out, filter_spectrum, own_v
    )
    near = to_x(away_f)
    received = [to_peer(messages[p - 1], p) for p in (1, 2, 3)]
    filters = in_vmem(
        pack_filter,
        [shape((2, 2, 128, 128), BF16)] * 4,
        [pltpu.VMEM((4, 2, 2, 128, 128), BF16)],
        moved=1 << 20,
    )(filter_spectrum, near)
    filters = [filters[0]] + [to_z(filters[r], r) for r in (1, 2, 3)]
    v1 = onward(own_v)
    q1 = onward(own_o)
    v2 = onward(v1)
    q2 = onward(after(q1, v1))
    mine = in_vmem(join_tokens, shape((512, 512), BF16), moved=1 << 20)(tokens, after(received[0], q2), *received[1:])
    v3 = onward(v2)
    other = to_core(mine)
    got_o = to_x(after(away_o, v1))
    r1 = onward(after(got_o, v2))
    keep, give = in_vmem(
        value_kernel,
        [shape((512, 256), F32), shape((512, 256), BF16)],
        [pltpu.VMEM((512, 512), F32)],
        flops=1 << 29,
        moved=2 << 20,
    )(after(mine, r1, near), other, own_v, v1, v2, v3)
    r2 = onward(after(r1, keep))
    drive, *sends = in_vmem(
        drive_kernel,
        [shape((512, 256), F32)] + [block] * 4,
        [pltpu.VMEM((512, 256), BF16), pltpu.VMEM((4, 256, 128), BF16)],
        moved=2 << 20,
    )(after(keep, filters[1]), to_x(give), gate_k, *received, skip[None, :])
    columns = [sends[0]] + [to_z(sends[r], r) for r in (1, 2, 3)]
    r3 = onward(after(r2, *filters[2:], columns[1]))
    q3 = onward(after(q2, *columns[1:]))
    table, table_t = tables()
    sends = in_vmem(
        conv_kernel,
        [block] * 4,
        [
            pltpu.VMEM((8, 128, 128), BF16),
            pltpu.VMEM((8, 2, 128, 128), BF16),
            pltpu.VMEM((16, 128, 256), BF16),
            pltpu.VMEM((9, 256, 128), F32),
        ],
        flops=1 << 30,
        moved=5 << 20,
    )(*columns, *filters, table, table_t)
    rows = [sends[0]] + [to_z(sends[r], r) for r in (1, 2, 3)]

    hops = [own_o, got_o, q1, r1, q2, r2, q3, after(r3, *rows[1:])]
    quad = shape((4, 256, 256), BF16)
    keep, give = in_vmem(sort_weight, [quad] * 2, moved=2 << 20)(*hops)
    theirs = to_core(give)
    gated = in_vmem(
        gate_kernel, shape((512, 256), BF16), [pltpu.VMEM((4, 256, 128), BF16)], moved=1 << 20
    )(*rows, drive, gate_q, *received)
    gated_other = to_core(gated)
    summed = (gated, gated_other, keep, theirs)
    send = shape((128, 1024), BF16)
    far = in_vmem(functools.partial(out_kernel, (3, 1)), [send] * 2, flops=1 << 29, moved=2 << 20)
    close = in_vmem(
        functools.partial(out_kernel, (2, 0)),
        [send, shape((128, 1024), F32)],
        flops=1 << 29,
        moved=2 << 20,
    )
    to_xy, to_row = far(*summed)
    parts = [to_peer(to_xy, 3), to_peer(to_row, 1)]
    to_column, total = close(*summed)
    parts.append(to_peer(to_column, 2))
    for part in parts:
        total = total + part.astype(F32)
    return total.astype(BF16)


def shards(tokens, gate_q, gate_k, w_value, skip, filter_spectrum, w_out):
    seq_count = lax.axis_size("seq")
    position = lax.axis_index("seq")
    length_b = tokens.shape[0]
    columns_each = length_b // seq_count
    freq_rows = 2 * seq_count
    freqs_each = freq_rows // seq_count
    fft_length = freq_rows * length_b
    features = lax.all_gather(tokens, "ch", axis=1, tiled=True)
    value_weight, out_weight = (
        lax.all_gather(w_value, "seq", axis=0, tiled=True),
        lax.all_gather(w_out, "seq", axis=0, tiled=True),
    )
    value = jnp.dot(features, value_weight, preferred_element_type=jnp.float32)
    value = value.astype(jnp.bfloat16)
    drive = (gate_k.astype(jnp.float32) * widened(value)).astype(jnp.bfloat16)
    channels = drive.shape[1]
    columns = lax.all_to_all(drive[None], "seq", split_axis=1, concat_axis=0, tiled=True)
    index_rows = jnp.arange(freq_rows, dtype=jnp.int32)
    index_seq = jnp.arange(seq_count, dtype=jnp.int32)
    index_b = jnp.arange(length_b, dtype=jnp.int32)
    cos_first, sin_first = angles(freq_rows, index_rows, index_seq)
    cos_first = cos_first.astype(jnp.bfloat16)
    sin_first = sin_first.astype(jnp.bfloat16)
    flattened = columns.reshape(seq_count, columns_each * channels)
    real_part = jnp.dot(cos_first, flattened, preferred_element_type=jnp.float32)
    imag_part = jnp.dot(-sin_first, flattened, preferred_element_type=jnp.float32)
    real_part = real_part.reshape(freq_rows, columns_each, channels)
    imag_part = imag_part.reshape(freq_rows, columns_each, channels)
    mine_b = position * columns_each + jnp.arange(columns_each, dtype=jnp.int32)
    twist_cos, twist_sin = angles(fft_length, index_rows, mine_b)
    twist_cos = twist_cos[:, :, None]
    twist_sin = twist_sin[:, :, None]
    section = jnp.stack(
        [
            real_part * twist_cos + imag_part * twist_sin,
            imag_part * twist_cos - real_part * twist_sin,
        ]
    ).astype(jnp.bfloat16)
    spectral = lax.all_to_all(section, "seq", split_axis=1, concat_axis=2, tiled=True)
    cos_seq, sin_seq = angles(length_b, index_b, index_b)
    cos_seq = cos_seq.astype(jnp.bfloat16)
    sin_seq = sin_seq.astype(jnp.bfloat16)
    spectrum_real = jnp.einsum(
        "qb,kbc->kqc", cos_seq, spectral[0], preferred_element_type=jnp.float32
    ) + jnp.einsum("qb,kbc->kqc", sin_seq, spectral[1], preferred_element_type=jnp.float32)
    spectrum_imag = jnp.einsum(
        "qb,kbc->kqc", cos_seq, spectral[1], preferred_element_type=jnp.float32
    ) - jnp.einsum("qb,kbc->kqc", sin_seq, spectral[0], preferred_element_type=jnp.float32)
    filter_real = filter_spectrum[0].astype(jnp.float32)
    filter_imag = filter_spectrum[1].astype(jnp.float32)
    product = jnp.stack(
        [
            spectrum_real * filter_real - spectrum_imag * filter_imag,
            spectrum_real * filter_imag + spectrum_imag * filter_real,
        ]
    ).astype(jnp.bfloat16)
    inverse_real = jnp.einsum(
        "qb,kqc->kbc", cos_seq, product[0], preferred_element_type=jnp.float32
    ) - jnp.einsum("qb,kqc->kbc", sin_seq, product[1], preferred_element_type=jnp.float32)
    inverse_imag = jnp.einsum(
        "qb,kqc->kbc", sin_seq, product[0], preferred_element_type=jnp.float32
    ) + jnp.einsum("qb,kqc->kbc", cos_seq, product[1], preferred_element_type=jnp.float32)
    mine_k = position * freqs_each + jnp.arange(freqs_each, dtype=jnp.int32)
    back_cos, back_sin = angles(fft_length, mine_k, index_b)
    back_cos = back_cos[:, :, None]
    back_sin = back_sin[:, :, None]
    back = jnp.stack(
        [
            inverse_real * back_cos - inverse_imag * back_sin,
            inverse_real * back_sin + inverse_imag * back_cos,
        ]
    ).astype(jnp.bfloat16)
    returned = lax.all_to_all(back, "seq", split_axis=2, concat_axis=1, tiled=True)
    flat_real = returned[0].reshape(freq_rows, columns_each * channels)
    flat_imag = returned[1].reshape(freq_rows, columns_each * channels)
    conv = jnp.dot(cos_first.T, flat_real, preferred_element_type=jnp.float32) - jnp.dot(
        sin_first.T, flat_imag, preferred_element_type=jnp.float32
    )
    conv = (
        (conv * (1.0 / fft_length)).reshape(seq_count, columns_each, channels).astype(jnp.bfloat16)
    )
    conv_rows = lax.all_to_all(conv, "seq", split_axis=0, concat_axis=1, tiled=True)[0]
    gated = (
        gate_q.astype(jnp.float32) * (widened(conv_rows) + skip[None, :] * widened(drive))
    ).astype(jnp.bfloat16)
    partial_value = lax.dot_general(
        gated, out_weight, (((1,), (1,)), ((), ())), preferred_element_type=jnp.float32
    )
    return lax.psum_scatter(
        partial_value.astype(jnp.bfloat16), "ch", scatter_dimension=1, tiled=True
    )


def solution(mesh):
    placed = (
        P(("grp", "seq"), "ch"),
        P(("grp", "seq"), "ch"),
        P(("grp", "seq"), "ch"),
        P("seq", "ch"),
        P("ch"),
        P(None, "seq", None, "ch"),
        P("seq", "ch"),
    )
    sizes = mesh.shape
    body = planes if (sizes["grp"], sizes["seq"], sizes["ch"]) == (2, 8, 2) else shards
    return jax.shard_map(
        body, mesh=mesh, in_specs=placed, out_specs=P(("grp", "seq"), "ch"), check_vma=False
    )
```

```python
import functools
import math

import jax
import jax.numpy as jnp
import numpy as np
from jax import lax
from jax.experimental import pallas as pl
from jax.experimental.pallas import tpu as pltpu
from jax.sharding import PartitionSpec as P

AXES = ("grp", "seq", "ch")
BF16 = jnp.bfloat16
F32 = jnp.float32


def angles(count, first, second):
    phase = 2.0 * math.pi / count * (first[:, None] * second[None, :] % count).astype(jnp.float32)
    return (jnp.cos(phase), jnp.sin(phase))


def widened(values):
    return lax.optimization_barrier(values).astype(jnp.float32)


def dot(a, b):
    return jnp.dot(a, b, preferred_element_type=F32)


def dot_t(a, b):
    return lax.dot_general(a, b, (((1,), (1,)), ((), ())), preferred_element_type=F32)


def in_vmem(kernel, out_shape, scratch=(), flops=0, moved=0):
    def call(*operands):
        specs = [pl.BlockSpec(memory_space=pltpu.VMEM)] * len(operands)
        return pl.pallas_call(
            kernel,
            out_shape=out_shape,
            in_specs=specs,
            out_specs=jax.tree.map(lambda _: pl.BlockSpec(memory_space=pltpu.VMEM), out_shape),
            scratch_shapes=list(scratch),
            compiler_params=pltpu.CompilerParams(vmem_limit_bytes=20 * 1024 * 1024),
            cost_estimate=pl.CostEstimate(flops=flops, bytes_accessed=moved, transcendentals=0),
        )(*operands)

    return call


def place():
    y, s, c = (lax.axis_index(a) for a in AXES)
    return y, lax.rem(s, 2), lax.div(s, 2), c


def low_lanes(shape):
    return lax.broadcasted_iota(jnp.int32, shape, len(shape) - 1) < 64


def half_turn(values):
    return pltpu.roll(values, 64, values.ndim - 1)


def both(first, second, low):
    return (
        jnp.where(low, first, half_turn(second)).astype(BF16),
        jnp.where(low, half_turn(first), second).astype(BF16),
    )


def quarter(p):
    y, x, _, _ = place()
    row = 1 - y if p // 2 else y
    column = 1 - x if p % 2 else x
    return pl.ds(pl.multiple_of(row * 512 + column * 256, 256), 256)


def copied(moves, sem):
    copies = [pltpu.make_async_copy(a, b, sem.at[i]) for i, (a, b) in enumerate(moves)]
    for copy in copies:
        copy.start()
    for copy in copies:
        copy.wait()


def cut_messages(tokens, key, query, out, filt, after, m1, m2, m3, own_o, away_o, away_f, sem):
    _, x, _, _ = place()
    moves = [(filt.at[:, :, :, quarter(1)], away_f)]
    for p, message in enumerate((m1, m2, m3), 1):
        column = 1 - x if p % 2 else x
        for i in range(2):
            lanes = pl.ds(pl.multiple_of(i * 512 + column * 256, 256), 256)
            moves.append((tokens.at[:, lanes], message.at[:, pl.ds(512 + i * 256, 256)]))
        moves.append((key.at[:, quarter(p)], message.at[:, pl.ds(0, 256)]))
        moves.append((query.at[:, quarter(p)], message.at[:, pl.ds(256, 256)]))
    moves += [(out.at[:, quarter(0)], own_o), (out.at[:, quarter(1)], away_o)]
    copied(moves, sem)


def copy_kernel(kernel, out_shape):
    def call(*operands):
        return pl.pallas_call(
            kernel,
            out_shape=out_shape,
            in_specs=[pl.BlockSpec(memory_space=pltpu.MemorySpace.HBM)] * len(operands),
            out_specs=[pl.BlockSpec(memory_space=pltpu.VMEM)] * len(out_shape),
            scratch_shapes=[pltpu.SemaphoreType.DMA((19,))],
            compiler_params=pltpu.CompilerParams(vmem_limit_bytes=61 * 1024 * 1024),
        )(*operands)

    return call


def pack_filter(filt, near, *refs):
    y, x, z, _ = place()
    packed, outs = refs[4], refs[:4]
    low = low_lanes((128, 128))
    for k in range(2):
        for j in range(2):
            base = pl.multiple_of(y * 512 + x * 256 + j * 128, 128)
            for part in range(2):
                if k:
                    pair = [near[part, i, :, pl.ds(j * 128, 128)].astype(F32) for i in range(2)]
                else:
                    pair = [filt[part, i, :, pl.ds(base, 128)].astype(F32) for i in range(2)]
                one, two = both(*pair, low)
                packed[2 * j, k, part] = one
                packed[2 * j + 1, k, part] = two
    for r in range(4):
        outs[r][...] = packed[lax.rem(z + r, 4)]


def join_tokens(*refs):
    _, x, _, _ = place()
    for i in range(2):
        lanes = pl.ds(pl.multiple_of(i * 512 + x * 256, 256), 256)
        refs[4][pl.ds(0, 128), pl.ds(i * 256, 256)] = refs[0][:, lanes]
    for p in (1, 2, 3):
        refs[4][pl.ds(p * 128, 128), :] = refs[p][:, pl.ds(512, 512)]


def value_kernel(mine, other, w0, w1, w2, w3, keep, give, acc):
    _, x, z, c = place()
    for r, piece in enumerate((w0, w1, w2, w3)):
        owner = z ^ (0, 1, 3, 2)[r]
        lanes = pl.ds(pl.multiple_of(lax.rem(owner, 2) * 256, 256), 256)

        @pl.when(lax.div(owner, 2) == c)
        def _():
            term = dot(mine[:, lanes], piece[...])
            acc[...] = acc[...] + term if r else term

        @pl.when(lax.div(owner, 2) != c)
        def _():
            term = dot(other[:, lanes], piece[...])
            acc[...] = acc[...] + term if r else term

    keep[...] = acc[:, pl.ds(pl.multiple_of(x * 256, 256), 256)]
    away = pl.ds(pl.multiple_of(256 - x * 256, 256), 256)
    for p in range(4):
        give[pl.ds(p * 128, 128), :] = acc[pl.ds((p ^ 1) * 128, 128), away].astype(BF16)


def drive_kernel(keep, taken, g0, g1, g2, g3, skip, direct, o0, o1, o2, o3, drive, packed):
    _, _, z, _ = place()
    for p, gate in enumerate((g0, g1, g2, g3)):
        rows = pl.ds(p * 128, 128)
        value = (keep[rows, :] + taken[rows, :].astype(F32)).astype(BF16).astype(F32)
        held = ((gate[:, 0:256] if p else gate[:, quarter(0)]).astype(F32) * value).astype(BF16)
        drive[rows, :] = held
        direct[rows, :] = skip[:, quarter(0)] * held.astype(F32)
    low = low_lanes((256, 128))
    for j in range(2):
        lanes = pl.ds(j * 128, 128)
        first = drive[pl.ds(0, 256), lanes].astype(F32)
        second = drive[pl.ds(256, 256), lanes].astype(F32)
        packed[2 * j], packed[2 * j + 1] = both(first, second, low)
    for r, out in enumerate((o0, o1, o2, o3)):
        out[...] = packed[lax.rem(z + r, 4)]


def add(a, b):
    return b if a is None else a if b is None else a + b


def sub(a, b):
    return a if b is None else -b if a is None else a - b


def scaled(a, s):
    if a is None or abs(s) < 1e-9:
        return None
    if abs(s - 1) < 1e-9:
        return a
    if abs(s + 1) < 1e-9:
        return -a
    return a * np.float32(s)


def cmul(a, angle):
    co, si = math.cos(angle), math.sin(angle)
    return (sub(scaled(a[0], co), scaled(a[1], si)), add(scaled(a[0], si), scaled(a[1], co)))


def cadd(a, b):
    return (add(a[0], b[0]), add(a[1], b[1]))


def conj(a):
    return (a[0], None if a[1] is None else -a[1])


def short_transform(values, count, rows):
    if len(values) == 1:
        return [(values[0], None)] * rows
    half = count // 2
    need = half // 2 + 1
    even = short_transform(values[0::2], half, need)
    odd = short_transform(values[1::2], half, need)

    def at(t, k):
        k %= half
        return t[k] if k < need else conj(t[half - k])

    return [cadd(at(even, k), cmul(at(odd, k), -2 * math.pi * k / count)) for k in range(rows)]


def conv_kernel(*refs):
    drives, filters, (table, table_t) = refs[:4], refs[4:8], refs[8:10]
    outs, (data, filt, first, sums) = refs[10:14], refs[14:]
    _, x, z, _ = place()
    for r, block in enumerate(drives):
        base = 2 * lax.rem(z - r + 4, 4)
        filt[base + x] = filters[r][0]
        filt[base + 1 - x] = filters[r][1]
        data[base + x] = block[pl.ds(0, 128), :]
        data[base + 1 - x] = block[pl.ds(128, 128), :]
    for i in range(8):
        rows = pl.ds(16 * i, 16)
        values = [data[a, rows, :].astype(F32) for a in range(8)]
        spectrum = short_transform(values, 16, 9)
        for k in range(9):
            re, im = spectrum[k]
            if im is None:
                im = jnp.zeros_like(re)
            first[k, rows, 0:128] = re.astype(BF16)
            first[k, rows, 128:256] = im.astype(BF16)
            if 0 < k < 8:
                first[16 - k, rows, 0:128] = re.astype(BF16)
                first[16 - k, rows, 128:256] = (-im).astype(BF16)
    low = low_lanes((128, 128))

    def back(k):
        four = dot(table[k], first[k])
        re = four[:128, :128] + four[128:, 128:]
        im = four[:128, 128:] - four[128:, :128]
        pair = [filt[k // 2, part].astype(F32) for part in range(2)]
        if k % 2 == 0:
            fr, fi = [jnp.where(low, f, half_turn(f)) for f in pair]
        else:
            fr, fi = [jnp.where(low, half_turn(f), f) for f in pair]
        product = jnp.concatenate([re * fr - im * fi, re * fi + im * fr], axis=1).astype(BF16)
        four = dot(table_t[k], product)
        return four[:128, :128] - four[128:, 128:], four[128:, :128] + four[:128, 128:]

    sums[0, pl.ds(0, 128)] = back(0)[0]
    sums[8, pl.ds(0, 128)] = back(8)[0]
    for k in range(1, 8):
        one, two = back(k), back(16 - k)
        sums[k, pl.ds(0, 128)] = one[0] + two[0]
        sums[k, pl.ds(128, 128)] = one[1] - two[1]
    for i in range(16):
        rows, below = pl.ds(8 * i, 8), pl.ds(128 + 8 * i, 8)
        scale = 1.0 / 2048
        re = [sums[k, rows, :] * scale for k in range(9)]
        im = [None] + [sums[k, below, :] * scale for k in range(1, 8)] + [None]
        for a in range(5):
            groups = [None] * 4
            for k in range(9):
                ang = 2 * math.pi * (k * a % 16) / 16
                groups[k % 2] = add(groups[k % 2], scaled(re[k], math.cos(ang)))
                groups[2 + k % 2] = sub(groups[2 + k % 2], scaled(im[k], math.sin(ang)))
            ec, oc, es, os = groups
            data[a, rows, :] = add(add(ec, oc), add(es, os)).astype(BF16)
            if 0 < a < 4:
                data[8 - a, rows, :] = sub(sub(add(ec, os), oc), es).astype(BF16)
    for r, out in enumerate(outs):
        base = 2 * lax.rem(z + r, 4)
        out[pl.ds(0, 128), :] = data[base + x]
        out[pl.ds(128, 128), :] = data[base + 1 - x]


def gate_kernel(e0, e1, e2, e3, direct, g0, g1, g2, g3, gated, conv):
    _, _, z, _ = place()
    for r, block in enumerate((e0, e1, e2, e3)):
        conv[lax.rem(z - r + 4, 4)] = block[...]
    low = low_lanes((256, 128))
    for j in range(2):
        lanes = pl.ds(j * 128, 128)
        even, odd = conv[2 * j].astype(F32), conv[2 * j + 1].astype(F32)
        parts = (jnp.where(low, even, half_turn(odd)), jnp.where(low, half_turn(even), odd))
        for p, gate in enumerate((g0, g1, g2, g3)):
            rows = pl.ds(p * 128, 128)
            own = parts[p // 2][(p % 2) * 128 : (p % 2) * 128 + 128]
            y, x, _, _ = place()
            base = y * 512 + x * 256 if p == 0 else 256
            query = gate[:, pl.ds(pl.multiple_of(base + j * 128, 128), 128)].astype(F32)
            gated[rows, lanes] = (query * (own + direct[rows, lanes])).astype(BF16)


def sort_weight(*refs):
    pieces, keep, give = refs[:8], refs[8], refs[9]
    _, x, z, c = place()
    for r in range(4):
        owner = z ^ (0, 1, 3, 2)[r]
        for k in range(2):
            to = 2 * lax.rem(owner, 2) + (1 - x if k else x)

            @pl.when(owner // 2 == c)
            def _():
                keep[to] = pieces[2 * r + k][...]

            @pl.when(owner // 2 != c)
            def _():
                give[to] = pieces[2 * r + k][...]


def out_kernel(blocks, gated, other, keep, theirs, *outs):
    for p, out in zip(blocks, outs):
        rows = pl.ds(p * 128, 128)
        for i in range(4):
            total = dot_t(gated[rows, :], keep[i]) + dot_t(other[rows, :], theirs[i])
            out[:, pl.ds(i * 256, 256)] = total.astype(out.dtype)


def tables():
    k = np.arange(16)[:, None, None] + 16 * np.arange(128)[None, :, None]
    phase = 2 * np.pi / 2048 * (k * np.arange(128)[None, None, :] % 2048)
    co, si = np.cos(phase), np.sin(phase)
    back = np.concatenate([co.transpose(0, 2, 1), si.transpose(0, 2, 1)], 1)
    return np.concatenate([co, si], 1).astype(jnp.bfloat16), back.astype(jnp.bfloat16)


def planes(tokens, gate_q, gate_k, w_value, skip, filter_spectrum, w_out):
    seq, deep = 8, 4

    def permute(values, move):
        pairs = []
        for g in range(2):
            for i in range(seq):
                for k in range(2):
                    g2, z2, x2, k2 = move(g, i // 2, i % 2, k)
                    pairs.append(((g * seq + i) * 2 + k, (g2 * seq + z2 * 2 + x2) * 2 + k2))
        return lax.ppermute(values, AXES, pairs)

    def to_x(values):
        return permute(values, lambda g, z, x, k: (g, z, 1 - x, k))

    def to_core(values):
        return permute(values, lambda g, z, x, k: (g, z, x, 1 - k))

    def with_z(values, r):
        return permute(values, lambda g, z, x, k: (g, z ^ r, x, k))

    def to_z(values, r):
        return permute(values, lambda g, z, x, k: (g, (z + r) % deep, x, k))

    def to_peer(values, p):
        return permute(values, lambda g, z, x, k: (g ^ (p // 2), z, x ^ (p % 2), k))

    def after(values, *done):
        return lax.optimization_barrier((values,) + done)[0]

    shape = jax.ShapeDtypeStruct
    block, square = shape((256, 128), BF16), shape((256, 256), BF16)
    own_v = lax.dynamic_slice_in_dim(w_value, lax.axis_index("grp") * 512, 512, axis=1)
    laid = [shape((128, 1024), BF16)] * 3 + [square] * 2 + [shape((2, 2, 128, 256), BF16)]
    *messages, own_o, away_o, away_f = copy_kernel(cut_messages, laid)(
        tokens, gate_k, gate_q, w_out, filter_spectrum, own_v
    )
    near = to_x(away_f)
    received = [to_peer(messages[p - 1], p) for p in (1, 2, 3)]
    filters = in_vmem(
        pack_filter,
        [shape((2, 2, 128, 128), BF16)] * 4,
        [pltpu.VMEM((4, 2, 2, 128, 128), BF16)],
        moved=1 << 20,
    )(filter_spectrum, near)
    filters = [filters[0]] + [to_z(filters[r], r) for r in (1, 2, 3)]
    v2 = with_z(own_v, 3)
    v1 = with_z(own_v, 1)
    q2 = with_z(after(own_o, v2), 3)
    v3 = with_z(after(v2, v1), 1)
    q3 = with_z(q2, 1)
    q1 = with_z(after(own_o, v2), 1)
    mine = in_vmem(join_tokens, shape((512, 512), BF16), moved=1 << 20)(
        tokens, after(received[0], q2), *received[1:]
    )
    other = to_core(mine)
    got_o = to_x(after(away_o, v2))
    keep, give = in_vmem(
        value_kernel,
        [shape((512, 256), F32), shape((512, 256), BF16)],
        [pltpu.VMEM((512, 512), F32)],
        flops=1 << 29,
        moved=2 << 20,
    )(after(mine, q1, q3, near, got_o), other, own_v, v1, v2, v3)
    r2 = with_z(after(got_o, keep), 3)
    r1 = with_z(after(got_o, keep), 1)
    drive, *sends = in_vmem(
        drive_kernel,
        [shape((512, 256), F32)] + [block] * 4,
        [pltpu.VMEM((512, 256), BF16), pltpu.VMEM((4, 256, 128), BF16)],
        moved=2 << 20,
    )(after(keep, filters[1]), to_x(give), gate_k, *received, skip[None, :])
    columns = [sends[0]] + [to_z(sends[r], r) for r in (1, 2, 3)]
    r3 = with_z(after(r2, r1, *filters[2:], columns[1]), 1)
    table, table_t = tables()
    sends = in_vmem(
        conv_kernel,
        [block] * 4,
        [
            pltpu.VMEM((8, 128, 128), BF16),
            pltpu.VMEM((8, 2, 128, 128), BF16),
            pltpu.VMEM((16, 128, 256), BF16),
            pltpu.VMEM((9, 256, 128), F32),
        ],
        flops=1 << 30,
        moved=5 << 20,
    )(*columns, *filters, table, table_t)
    rows = [sends[0]] + [to_z(sends[r], r) for r in (1, 2, 3)]

    hops = [own_o, got_o, q1, r1, q2, r2, q3, after(r3, *rows[1:])]
    quad = shape((4, 256, 256), BF16)
    keep, give = in_vmem(sort_weight, [quad] * 2, moved=2 << 20)(*hops)
    theirs = to_core(give)
    gated = in_vmem(
        gate_kernel, shape((512, 256), BF16), [pltpu.VMEM((4, 256, 128), BF16)], moved=1 << 20
    )(*rows, drive, gate_q, *received)
    gated_other = to_core(gated)
    summed = (gated, gated_other, keep, theirs)
    send = shape((128, 1024), BF16)
    far = in_vmem(functools.partial(out_kernel, (3, 1)), [send] * 2, flops=1 << 29, moved=2 << 20)
    close = in_vmem(
        functools.partial(out_kernel, (2, 0)),
        [send, shape((128, 1024), F32)],
        flops=1 << 29,
        moved=2 << 20,
    )
    to_xy, to_row = far(*summed)
    parts = [to_peer(to_xy, 3), to_peer(to_row, 1)]
    to_column, total = close(*summed)
    parts.append(to_peer(to_column, 2))
    for part in parts:
        total = total + part.astype(F32)
    return total.astype(BF16)


def shards(tokens, gate_q, gate_k, w_value, skip, filter_spectrum, w_out):
    seq_count = lax.axis_size("seq")
    position = lax.axis_index("seq")
    length_b = tokens.shape[0]
    columns_each = length_b // seq_count
    freq_rows = 2 * seq_count
    freqs_each = freq_rows // seq_count
    fft_length = freq_rows * length_b
    features = lax.all_gather(tokens, "ch", axis=1, tiled=True)
    value_weight, out_weight = (
        lax.all_gather(w_value, "seq", axis=0, tiled=True),
        lax.all_gather(w_out, "seq", axis=0, tiled=True),
    )
    value = jnp.dot(features, value_weight, preferred_element_type=jnp.float32)
    value = value.astype(jnp.bfloat16)
    drive = (gate_k.astype(jnp.float32) * widened(value)).astype(jnp.bfloat16)
    channels = drive.shape[1]
    columns = lax.all_to_all(drive[None], "seq", split_axis=1, concat_axis=0, tiled=True)
    index_rows = jnp.arange(freq_rows, dtype=jnp.int32)
    index_seq = jnp.arange(seq_count, dtype=jnp.int32)
    index_b = jnp.arange(length_b, dtype=jnp.int32)
    cos_first, sin_first = angles(freq_rows, index_rows, index_seq)
    cos_first = cos_first.astype(jnp.bfloat16)
    sin_first = sin_first.astype(jnp.bfloat16)
    flattened = columns.reshape(seq_count, columns_each * channels)
    real_part = jnp.dot(cos_first, flattened, preferred_element_type=jnp.float32)
    imag_part = jnp.dot(-sin_first, flattened, preferred_element_type=jnp.float32)
    real_part = real_part.reshape(freq_rows, columns_each, channels)
    imag_part = imag_part.reshape(freq_rows, columns_each, channels)
    mine_b = position * columns_each + jnp.arange(columns_each, dtype=jnp.int32)
    twist_cos, twist_sin = angles(fft_length, index_rows, mine_b)
    twist_cos = twist_cos[:, :, None]
    twist_sin = twist_sin[:, :, None]
    section = jnp.stack(
        [
            real_part * twist_cos + imag_part * twist_sin,
            imag_part * twist_cos - real_part * twist_sin,
        ]
    ).astype(jnp.bfloat16)
    spectral = lax.all_to_all(section, "seq", split_axis=1, concat_axis=2, tiled=True)
    cos_seq, sin_seq = angles(length_b, index_b, index_b)
    cos_seq = cos_seq.astype(jnp.bfloat16)
    sin_seq = sin_seq.astype(jnp.bfloat16)
    spectrum_real = jnp.einsum(
        "qb,kbc->kqc", cos_seq, spectral[0], preferred_element_type=jnp.float32
    ) + jnp.einsum("qb,kbc->kqc", sin_seq, spectral[1], preferred_element_type=jnp.float32)
    spectrum_imag = jnp.einsum(
        "qb,kbc->kqc", cos_seq, spectral[1], preferred_element_type=jnp.float32
    ) - jnp.einsum("qb,kbc->kqc", sin_seq, spectral[0], preferred_element_type=jnp.float32)
    filter_real = filter_spectrum[0].astype(jnp.float32)
    filter_imag = filter_spectrum[1].astype(jnp.float32)
    product = jnp.stack(
        [
            spectrum_real * filter_real - spectrum_imag * filter_imag,
            spectrum_real * filter_imag + spectrum_imag * filter_real,
        ]
    ).astype(jnp.bfloat16)
    inverse_real = jnp.einsum(
        "qb,kqc->kbc", cos_seq, product[0], preferred_element_type=jnp.float32
    ) - jnp.einsum("qb,kqc->kbc", sin_seq, product[1], preferred_element_type=jnp.float32)
    inverse_imag = jnp.einsum(
        "qb,kqc->kbc", sin_seq, product[0], preferred_element_type=jnp.float32
    ) + jnp.einsum("qb,kqc->kbc", cos_seq, product[1], preferred_element_type=jnp.float32)
    mine_k = position * freqs_each + jnp.arange(freqs_each, dtype=jnp.int32)
    back_cos, back_sin = angles(fft_length, mine_k, index_b)
    back_cos = back_cos[:, :, None]
    back_sin = back_sin[:, :, None]
    back = jnp.stack(
        [
            inverse_real * back_cos - inverse_imag * back_sin,
            inverse_real * back_sin + inverse_imag * back_cos,
        ]
    ).astype(jnp.bfloat16)
    returned = lax.all_to_all(back, "seq", split_axis=2, concat_axis=1, tiled=True)
    flat_real = returned[0].reshape(freq_rows, columns_each * channels)
    flat_imag = returned[1].reshape(freq_rows, columns_each * channels)
    conv = jnp.dot(cos_first.T, flat_real, preferred_element_type=jnp.float32) - jnp.dot(
        sin_first.T, flat_imag, preferred_element_type=jnp.float32
    )
    conv = (
        (conv * (1.0 / fft_length)).reshape(seq_count, columns_each, channels).astype(jnp.bfloat16)
    )
    conv_rows = lax.all_to_all(conv, "seq", split_axis=0, concat_axis=1, tiled=True)[0]
    gated = (
        gate_q.astype(jnp.float32) * (widened(conv_rows) + skip[None, :] * widened(drive))
    ).astype(jnp.bfloat16)
    partial_value = lax.dot_general(
        gated, out_weight, (((1,), (1,)), ((), ())), preferred_element_type=jnp.float32
    )
    return lax.psum_scatter(
        partial_value.astype(jnp.bfloat16), "ch", scatter_dimension=1, tiled=True
    )


def solution(mesh):
    placed = (
        P(("grp", "seq"), "ch"),
        P(("grp", "seq"), "ch"),
        P(("grp", "seq"), "ch"),
        P("seq", "ch"),
        P("ch"),
        P(None, "seq", None, "ch"),
        P("seq", "ch"),
    )
    sizes = mesh.shape
    body = planes if (sizes["grp"], sizes["seq"], sizes["ch"]) == (2, 8, 2) else shards
    return jax.shard_map(
        body, mesh=mesh, in_specs=placed, out_specs=P(("grp", "seq"), "ch"), check_vma=False
    )
```

```python
import functools
import math

import jax
import jax.numpy as jnp
import numpy as np
from jax import lax
from jax.experimental import pallas as pl
from jax.experimental.pallas import tpu as pltpu
from jax.sharding import PartitionSpec as P

AXES = ("grp", "seq", "ch")
BF16 = jnp.bfloat16
F32 = jnp.float32


def angles(count, first, second):
    phase = 2.0 * math.pi / count * (first[:, None] * second[None, :] % count).astype(jnp.float32)
    return (jnp.cos(phase), jnp.sin(phase))


def widened(values):
    return lax.optimization_barrier(values).astype(jnp.float32)


def dot(a, b):
    return jnp.dot(a, b, preferred_element_type=F32)


def dot_t(a, b):
    return lax.dot_general(a, b, (((1,), (1,)), ((), ())), preferred_element_type=F32)


def in_vmem(kernel, out_shape, scratch=(), flops=0, moved=0):
    def call(*operands):
        specs = [pl.BlockSpec(memory_space=pltpu.VMEM)] * len(operands)
        return pl.pallas_call(
            kernel,
            out_shape=out_shape,
            in_specs=specs,
            out_specs=jax.tree.map(lambda _: pl.BlockSpec(memory_space=pltpu.VMEM), out_shape),
            scratch_shapes=list(scratch),
            compiler_params=pltpu.CompilerParams(vmem_limit_bytes=20 * 1024 * 1024),
            cost_estimate=pl.CostEstimate(flops=flops, bytes_accessed=moved, transcendentals=0),
        )(*operands)

    return call


def place():
    y, s, c = (lax.axis_index(a) for a in AXES)
    return y, lax.rem(s, 2), lax.div(s, 2), c


def around(z, r):
    at = lax.rem((z ^ lax.div(z, 2)) + r + 4, 4)
    return at ^ lax.div(at, 2)


def low_lanes(shape):
    return lax.broadcasted_iota(jnp.int32, shape, len(shape) - 1) < 64


def half_turn(values):
    return pltpu.roll(values, 64, values.ndim - 1)


def both(first, second, low):
    return (
        jnp.where(low, first, half_turn(second)).astype(BF16),
        jnp.where(low, half_turn(first), second).astype(BF16),
    )


def quarter(p):
    y, x, _, _ = place()
    row = 1 - y if p // 2 else y
    column = 1 - x if p % 2 else x
    return pl.ds(pl.multiple_of(row * 512 + column * 256, 256), 256)


def copied(moves, sem):
    copies = [pltpu.make_async_copy(a, b, sem.at[i]) for i, (a, b) in enumerate(moves)]
    for copy in copies:
        copy.start()
    for copy in copies:
        copy.wait()


def cut_messages(tokens, key, query, out, filt, after, m1, m2, m3, own_o, away_o, away_f, sem):
    _, x, _, _ = place()
    moves = [(filt.at[:, :, :, quarter(1)], away_f)]
    for p, message in enumerate((m1, m2, m3), 1):
        column = 1 - x if p % 2 else x
        for i in range(2):
            lanes = pl.ds(pl.multiple_of(i * 512 + column * 256, 256), 256)
            moves.append((tokens.at[:, lanes], message.at[:, pl.ds(512 + i * 256, 256)]))
        moves.append((key.at[:, quarter(p)], message.at[:, pl.ds(0, 256)]))
        moves.append((query.at[:, quarter(p)], message.at[:, pl.ds(256, 256)]))
    moves += [(out.at[:, quarter(0)], own_o), (out.at[:, quarter(1)], away_o)]
    copied(moves, sem)


def copy_kernel(kernel, out_shape):
    def call(*operands):
        return pl.pallas_call(
            kernel,
            out_shape=out_shape,
            in_specs=[pl.BlockSpec(memory_space=pltpu.MemorySpace.HBM)] * len(operands),
            out_specs=[pl.BlockSpec(memory_space=pltpu.VMEM)] * len(out_shape),
            scratch_shapes=[pltpu.SemaphoreType.DMA((19,))],
            compiler_params=pltpu.CompilerParams(vmem_limit_bytes=61 * 1024 * 1024),
        )(*operands)

    return call


def pack_filter(filt, near, *refs):
    y, x, z, _ = place()
    packed, outs = refs[4], refs[:4]
    low = low_lanes((128, 128))
    for k in range(2):
        for j in range(2):
            base = pl.multiple_of(y * 512 + x * 256 + j * 128, 128)
            for part in range(2):
                if k:
                    pair = [near[part, i, :, pl.ds(j * 128, 128)].astype(F32) for i in range(2)]
                else:
                    pair = [filt[part, i, :, pl.ds(base, 128)].astype(F32) for i in range(2)]
                one, two = both(*pair, low)
                packed[2 * j, k, part] = one
                packed[2 * j + 1, k, part] = two
    for r in range(4):
        outs[r][...] = packed[around(z, r)]


def join_tokens(*refs):
    _, x, _, _ = place()
    for i in range(2):
        lanes = pl.ds(pl.multiple_of(i * 512 + x * 256, 256), 256)
        refs[4][pl.ds(0, 128), pl.ds(i * 256, 256)] = refs[0][:, lanes]
    for p in (1, 2, 3):
        refs[4][pl.ds(p * 128, 128), :] = refs[p][:, pl.ds(512, 512)]


def value_kernel(mine, other, w0, w1, w2, w3, keep, give, acc):
    _, x, z, c = place()
    for r, piece in enumerate((w0, w1, w2, w3)):
        owner = around(z, -r)
        lanes = pl.ds(pl.multiple_of(lax.rem(owner, 2) * 256, 256), 256)

        @pl.when(lax.div(owner, 2) == c)
        def _():
            term = dot(mine[:, lanes], piece[...])
            acc[...] = acc[...] + term if r else term

        @pl.when(lax.div(owner, 2) != c)
        def _():
            term = dot(other[:, lanes], piece[...])
            acc[...] = acc[...] + term if r else term

    keep[...] = acc[:, pl.ds(pl.multiple_of(x * 256, 256), 256)]
    away = pl.ds(pl.multiple_of(256 - x * 256, 256), 256)
    for p in range(4):
        give[pl.ds(p * 128, 128), :] = acc[pl.ds((p ^ 1) * 128, 128), away].astype(BF16)


def drive_kernel(keep, taken, g0, g1, g2, g3, skip, direct, o0, o1, o2, o3, drive, packed):
    _, _, z, _ = place()
    for p, gate in enumerate((g0, g1, g2, g3)):
        rows = pl.ds(p * 128, 128)
        value = (keep[rows, :] + taken[rows, :].astype(F32)).astype(BF16).astype(F32)
        held = ((gate[:, 0:256] if p else gate[:, quarter(0)]).astype(F32) * value).astype(BF16)
        drive[rows, :] = held
        direct[rows, :] = skip[:, quarter(0)] * held.astype(F32)
    low = low_lanes((256, 128))
    for j in range(2):
        lanes = pl.ds(j * 128, 128)
        first = drive[pl.ds(0, 256), lanes].astype(F32)
        second = drive[pl.ds(256, 256), lanes].astype(F32)
        packed[2 * j], packed[2 * j + 1] = both(first, second, low)
    for r, out in enumerate((o0, o1, o2, o3)):
        out[...] = packed[around(z, r)]


def add(a, b):
    return b if a is None else a if b is None else a + b


def sub(a, b):
    return a if b is None else -b if a is None else a - b


def scaled(a, s):
    if a is None or abs(s) < 1e-9:
        return None
    if abs(s - 1) < 1e-9:
        return a
    if abs(s + 1) < 1e-9:
        return -a
    return a * np.float32(s)


def cmul(a, angle):
    co, si = math.cos(angle), math.sin(angle)
    return (sub(scaled(a[0], co), scaled(a[1], si)), add(scaled(a[0], si), scaled(a[1], co)))


def cadd(a, b):
    return (add(a[0], b[0]), add(a[1], b[1]))


def conj(a):
    return (a[0], None if a[1] is None else -a[1])


def short_transform(values, count, rows):
    if len(values) == 1:
        return [(values[0], None)] * rows
    half = count // 2
    need = half // 2 + 1
    even = short_transform(values[0::2], half, need)
    odd = short_transform(values[1::2], half, need)

    def at(t, k):
        k %= half
        return t[k] if k < need else conj(t[half - k])

    return [cadd(at(even, k), cmul(at(odd, k), -2 * math.pi * k / count)) for k in range(rows)]


def conv_kernel(*refs):
    drives, filters, (table, table_t) = refs[:4], refs[4:8], refs[8:10]
    outs, (data, filt, first, sums) = refs[10:14], refs[14:]
    _, x, z, _ = place()
    for r, block in enumerate(drives):
        base = 2 * around(z, -r)
        filt[base + x] = filters[r][0]
        filt[base + 1 - x] = filters[r][1]
        data[base + x] = block[pl.ds(0, 128), :]
        data[base + 1 - x] = block[pl.ds(128, 128), :]
    for i in range(8):
        rows = pl.ds(16 * i, 16)
        values = [data[a, rows, :].astype(F32) for a in range(8)]
        spectrum = short_transform(values, 16, 9)
        for k in range(9):
            re, im = spectrum[k]
            if im is None:
                im = jnp.zeros_like(re)
            first[k, rows, 0:128] = re.astype(BF16)
            first[k, rows, 128:256] = im.astype(BF16)
            if 0 < k < 8:
                first[16 - k, rows, 0:128] = re.astype(BF16)
                first[16 - k, rows, 128:256] = (-im).astype(BF16)
    low = low_lanes((128, 128))

    def back(k):
        four = dot(table[k], first[k])
        re = four[:128, :128] + four[128:, 128:]
        im = four[:128, 128:] - four[128:, :128]
        pair = [filt[k // 2, part].astype(F32) for part in range(2)]
        if k % 2 == 0:
            fr, fi = [jnp.where(low, f, half_turn(f)) for f in pair]
        else:
            fr, fi = [jnp.where(low, half_turn(f), f) for f in pair]
        product = jnp.concatenate([re * fr - im * fi, re * fi + im * fr], axis=1).astype(BF16)
        four = dot(table_t[k], product)
        return four[:128, :128] - four[128:, 128:], four[128:, :128] + four[:128, 128:]

    sums[0, pl.ds(0, 128)] = back(0)[0]
    sums[8, pl.ds(0, 128)] = back(8)[0]
    for k in range(1, 8):
        one, two = back(k), back(16 - k)
        sums[k, pl.ds(0, 128)] = one[0] + two[0]
        sums[k, pl.ds(128, 128)] = one[1] - two[1]
    for i in range(16):
        rows, below = pl.ds(8 * i, 8), pl.ds(128 + 8 * i, 8)
        scale = 1.0 / 2048
        re = [sums[k, rows, :] * scale for k in range(9)]
        im = [None] + [sums[k, below, :] * scale for k in range(1, 8)] + [None]
        for a in range(5):
            groups = [None] * 4
            for k in range(9):
                ang = 2 * math.pi * (k * a % 16) / 16
                groups[k % 2] = add(groups[k % 2], scaled(re[k], math.cos(ang)))
                groups[2 + k % 2] = sub(groups[2 + k % 2], scaled(im[k], math.sin(ang)))
            ec, oc, es, os = groups
            data[a, rows, :] = add(add(ec, oc), add(es, os)).astype(BF16)
            if 0 < a < 4:
                data[8 - a, rows, :] = sub(sub(add(ec, os), oc), es).astype(BF16)
    for r, out in enumerate(outs):
        base = 2 * around(z, r)
        out[pl.ds(0, 128), :] = data[base + x]
        out[pl.ds(128, 128), :] = data[base + 1 - x]


def gate_kernel(e0, e1, e2, e3, direct, g0, g1, g2, g3, gated, conv):
    _, _, z, _ = place()
    for r, block in enumerate((e0, e1, e2, e3)):
        conv[around(z, -r)] = block[...]
    low = low_lanes((256, 128))
    for j in range(2):
        lanes = pl.ds(j * 128, 128)
        even, odd = conv[2 * j].astype(F32), conv[2 * j + 1].astype(F32)
        parts = (jnp.where(low, even, half_turn(odd)), jnp.where(low, half_turn(even), odd))
        for p, gate in enumerate((g0, g1, g2, g3)):
            rows = pl.ds(p * 128, 128)
            own = parts[p // 2][(p % 2) * 128 : (p % 2) * 128 + 128]
            y, x, _, _ = place()
            base = y * 512 + x * 256 if p == 0 else 256
            query = gate[:, pl.ds(pl.multiple_of(base + j * 128, 128), 128)].astype(F32)
            gated[rows, lanes] = (query * (own + direct[rows, lanes])).astype(BF16)


def sort_weight(*refs):
    pieces, keep, give = refs[:8], refs[8], refs[9]
    _, x, z, c = place()
    for r in range(4):
        owner = around(z, -r)
        for k in range(2):
            to = 2 * lax.rem(owner, 2) + (1 - x if k else x)

            @pl.when(owner // 2 == c)
            def _():
                keep[to] = pieces[2 * r + k][...]

            @pl.when(owner // 2 != c)
            def _():
                give[to] = pieces[2 * r + k][...]


def out_kernel(blocks, gated, other, keep, theirs, *outs):
    for p, out in zip(blocks, outs):
        rows = pl.ds(p * 128, 128)
        for i in range(4):
            total = dot_t(gated[rows, :], keep[i]) + dot_t(other[rows, :], theirs[i])
            out[:, pl.ds(i * 256, 256)] = total.astype(out.dtype)


def tables():
    k = np.arange(16)[:, None, None] + 16 * np.arange(128)[None, :, None]
    phase = 2 * np.pi / 2048 * (k * np.arange(128)[None, None, :] % 2048)
    co, si = np.cos(phase), np.sin(phase)
    back = np.concatenate([co.transpose(0, 2, 1), si.transpose(0, 2, 1)], 1)
    return np.concatenate([co, si], 1).astype(jnp.bfloat16), back.astype(jnp.bfloat16)


def planes(tokens, gate_q, gate_k, w_value, skip, filter_spectrum, w_out):
    seq, deep = 8, 4

    def permute(values, move):
        pairs = []
        for g in range(2):
            for i in range(seq):
                for k in range(2):
                    g2, z2, x2, k2 = move(g, i // 2, i % 2, k)
                    pairs.append(((g * seq + i) * 2 + k, (g2 * seq + z2 * 2 + x2) * 2 + k2))
        return lax.ppermute(values, AXES, pairs)

    def to_x(values):
        return permute(values, lambda g, z, x, k: (g, z, 1 - x, k))

    def to_core(values):
        return permute(values, lambda g, z, x, k: (g, z, x, 1 - k))

    def to_z(values, r):
        ring = (0, 1, 3, 2)
        at = [ring.index(z) for z in range(deep)]
        return permute(values, lambda g, z, x, k: (g, ring[(at[z] + r) % deep], x, k))

    def onward(values):
        return to_z(values, 1)

    def to_peer(values, p):
        return permute(values, lambda g, z, x, k: (g ^ (p // 2), z, x ^ (p % 2), k))

    def after(values, *done):
        return lax.optimization_barrier((values,) + done)[0]

    shape = jax.ShapeDtypeStruct
    block, square = shape((256, 128), BF16), shape((256, 256), BF16)
    own_v = lax.dynamic_slice_in_dim(w_value, lax.axis_index("grp") * 512, 512, axis=1)
    laid = [shape((128, 1024), BF16)] * 3 + [square] * 2 + [shape((2, 2, 128, 256), BF16)]
    *messages, own_o, away_o, away_f = copy_kernel(cut_messages, laid)(
        tokens, gate_k, gate_q, w_out, filter_spectrum, own_v
    )
    near = to_x(away_f)
    received = [to_peer(messages[p - 1], p) for p in (1, 2, 3)]
    filters = in_vmem(
        pack_filter,
        [shape((2, 2, 128, 128), BF16)] * 4,
        [pltpu.VMEM((4, 2, 2, 128, 128), BF16)],
        moved=1 << 20,
    )(filter_spectrum, near)
    filters = [filters[0]] + [to_z(filters[r], r) for r in (1, 2, 3)]
    v1 = onward(own_v)
    q1 = onward(own_o)
    v2 = onward(v1)
    q2 = onward(after(q1, v1))
    mine = in_vmem(join_tokens, shape((512, 512), BF16), moved=1 << 20)(tokens, after(received[0], q2), *received[1:])
    v3 = onward(v2)
    other = to_core(mine)
    got_o = to_x(after(away_o, v1))
    r1 = onward(after(got_o, v2))
    keep, give = in_vmem(
        value_kernel,
        [shape((512, 256), F32), shape((512, 256), BF16)],
        [pltpu.VMEM((512, 512), F32)],
        flops=1 << 29,
        moved=2 << 20,
    )(after(mine, r1, filters[0]), other, own_v, v1, v2, v3)
    r2 = onward(after(r1, keep))
    drive, *sends = in_vmem(
        drive_kernel,
        [shape((512, 256), F32)] + [block] * 4,
        [pltpu.VMEM((512, 256), BF16), pltpu.VMEM((4, 256, 128), BF16)],
        moved=2 << 20,
    )(after(keep, filters[1]), to_x(give), gate_k, *received, skip[None, :])
    columns = [sends[0]] + [to_z(sends[r], r) for r in (1, 2, 3)]
    r3 = onward(after(r2, *filters[2:], columns[1]))
    q3 = onward(after(q2, *columns[1:]))
    table, table_t = tables()
    sends = in_vmem(
        conv_kernel,
        [block] * 4,
        [
            pltpu.VMEM((8, 128, 128), BF16),
            pltpu.VMEM((8, 2, 128, 128), BF16),
            pltpu.VMEM((16, 128, 256), BF16),
            pltpu.VMEM((9, 256, 128), F32),
        ],
        flops=1 << 30,
        moved=5 << 20,
    )(*columns, *filters, table, table_t)
    rows = [sends[0]] + [to_z(sends[r], r) for r in (1, 2, 3)]

    hops = [own_o, got_o, q1, r1, q2, r2, q3, after(r3, *rows[1:])]
    quad = shape((4, 256, 256), BF16)
    keep, give = in_vmem(sort_weight, [quad] * 2, moved=2 << 20)(*hops)
    theirs = to_core(give)
    gated = in_vmem(
        gate_kernel, shape((512, 256), BF16), [pltpu.VMEM((4, 256, 128), BF16)], moved=1 << 20
    )(*rows, drive, gate_q, *received)
    gated_other = to_core(gated)
    summed = (gated, gated_other, keep, theirs)
    send = shape((128, 1024), BF16)
    far = in_vmem(functools.partial(out_kernel, (3, 1)), [send] * 2, flops=1 << 29, moved=2 << 20)
    close = in_vmem(
        functools.partial(out_kernel, (2, 0)),
        [send, shape((128, 1024), F32)],
        flops=1 << 29,
        moved=2 << 20,
    )
    to_xy, to_row = far(*summed)
    parts = [to_peer(to_xy, 3), to_peer(to_row, 1)]
    to_column, total = close(*summed)
    parts.append(to_peer(to_column, 2))
    for part in parts:
        total = total + part.astype(F32)
    return total.astype(BF16)


def shards(tokens, gate_q, gate_k, w_value, skip, filter_spectrum, w_out):
    seq_count = lax.axis_size("seq")
    position = lax.axis_index("seq")
    length_b = tokens.shape[0]
    columns_each = length_b // seq_count
    freq_rows = 2 * seq_count
    freqs_each = freq_rows // seq_count
    fft_length = freq_rows * length_b
    features = lax.all_gather(tokens, "ch", axis=1, tiled=True)
    value_weight, out_weight = (
        lax.all_gather(w_value, "seq", axis=0, tiled=True),
        lax.all_gather(w_out, "seq", axis=0, tiled=True),
    )
    value = jnp.dot(features, value_weight, preferred_element_type=jnp.float32)
    value = value.astype(jnp.bfloat16)
    drive = (gate_k.astype(jnp.float32) * widened(value)).astype(jnp.bfloat16)
    channels = drive.shape[1]
    columns = lax.all_to_all(drive[None], "seq", split_axis=1, concat_axis=0, tiled=True)
    index_rows = jnp.arange(freq_rows, dtype=jnp.int32)
    index_seq = jnp.arange(seq_count, dtype=jnp.int32)
    index_b = jnp.arange(length_b, dtype=jnp.int32)
    cos_first, sin_first = angles(freq_rows, index_rows, index_seq)
    cos_first = cos_first.astype(jnp.bfloat16)
    sin_first = sin_first.astype(jnp.bfloat16)
    flattened = columns.reshape(seq_count, columns_each * channels)
    real_part = jnp.dot(cos_first, flattened, preferred_element_type=jnp.float32)
    imag_part = jnp.dot(-sin_first, flattened, preferred_element_type=jnp.float32)
    real_part = real_part.reshape(freq_rows, columns_each, channels)
    imag_part = imag_part.reshape(freq_rows, columns_each, channels)
    mine_b = position * columns_each + jnp.arange(columns_each, dtype=jnp.int32)
    twist_cos, twist_sin = angles(fft_length, index_rows, mine_b)
    twist_cos = twist_cos[:, :, None]
    twist_sin = twist_sin[:, :, None]
    section = jnp.stack(
        [
            real_part * twist_cos + imag_part * twist_sin,
            imag_part * twist_cos - real_part * twist_sin,
        ]
    ).astype(jnp.bfloat16)
    spectral = lax.all_to_all(section, "seq", split_axis=1, concat_axis=2, tiled=True)
    cos_seq, sin_seq = angles(length_b, index_b, index_b)
    cos_seq = cos_seq.astype(jnp.bfloat16)
    sin_seq = sin_seq.astype(jnp.bfloat16)
    spectrum_real = jnp.einsum(
        "qb,kbc->kqc", cos_seq, spectral[0], preferred_element_type=jnp.float32
    ) + jnp.einsum("qb,kbc->kqc", sin_seq, spectral[1], preferred_element_type=jnp.float32)
    spectrum_imag = jnp.einsum(
        "qb,kbc->kqc", cos_seq, spectral[1], preferred_element_type=jnp.float32
    ) - jnp.einsum("qb,kbc->kqc", sin_seq, spectral[0], preferred_element_type=jnp.float32)
    filter_real = filter_spectrum[0].astype(jnp.float32)
    filter_imag = filter_spectrum[1].astype(jnp.float32)
    product = jnp.stack(
        [
            spectrum_real * filter_real - spectrum_imag * filter_imag,
            spectrum_real * filter_imag + spectrum_imag * filter_real,
        ]
    ).astype(jnp.bfloat16)
    inverse_real = jnp.einsum(
        "qb,kqc->kbc", cos_seq, product[0], preferred_element_type=jnp.float32
    ) - jnp.einsum("qb,kqc->kbc", sin_seq, product[1], preferred_element_type=jnp.float32)
    inverse_imag = jnp.einsum(
        "qb,kqc->kbc", sin_seq, product[0], preferred_element_type=jnp.float32
    ) + jnp.einsum("qb,kqc->kbc", cos_seq, product[1], preferred_element_type=jnp.float32)
    mine_k = position * freqs_each + jnp.arange(freqs_each, dtype=jnp.int32)
    back_cos, back_sin = angles(fft_length, mine_k, index_b)
    back_cos = back_cos[:, :, None]
    back_sin = back_sin[:, :, None]
    back = jnp.stack(
        [
            inverse_real * back_cos - inverse_imag * back_sin,
            inverse_real * back_sin + inverse_imag * back_cos,
        ]
    ).astype(jnp.bfloat16)
    returned = lax.all_to_all(back, "seq", split_axis=2, concat_axis=1, tiled=True)
    flat_real = returned[0].reshape(freq_rows, columns_each * channels)
    flat_imag = returned[1].reshape(freq_rows, columns_each * channels)
    conv = jnp.dot(cos_first.T, flat_real, preferred_element_type=jnp.float32) - jnp.dot(
        sin_first.T, flat_imag, preferred_element_type=jnp.float32
    )
    conv = (
        (conv * (1.0 / fft_length)).reshape(seq_count, columns_each, channels).astype(jnp.bfloat16)
    )
    conv_rows = lax.all_to_all(conv, "seq", split_axis=0, concat_axis=1, tiled=True)[0]
    gated = (
        gate_q.astype(jnp.float32) * (widened(conv_rows) + skip[None, :] * widened(drive))
    ).astype(jnp.bfloat16)
    partial_value = lax.dot_general(
        gated, out_weight, (((1,), (1,)), ((), ())), preferred_element_type=jnp.float32
    )
    return lax.psum_scatter(
        partial_value.astype(jnp.bfloat16), "ch", scatter_dimension=1, tiled=True
    )


def solution(mesh):
    placed = (
        P(("grp", "seq"), "ch"),
        P(("grp", "seq"), "ch"),
        P(("grp", "seq"), "ch"),
        P("seq", "ch"),
        P("ch"),
        P(None, "seq", None, "ch"),
        P("seq", "ch"),
    )
    sizes = mesh.shape
    body = planes if (sizes["grp"], sizes["seq"], sizes["ch"]) == (2, 8, 2) else shards
    return jax.shard_map(
        body, mesh=mesh, in_specs=placed, out_specs=P(("grp", "seq"), "ch"), check_vma=False
    )
```

```python
import functools
import math

import jax
import jax.numpy as jnp
import numpy as np
from jax import lax
from jax.experimental import pallas as pl
from jax.experimental.pallas import tpu as pltpu
from jax.sharding import PartitionSpec as P

AXES = ("grp", "seq", "ch")
BF16 = jnp.bfloat16
F32 = jnp.float32


def angles(count, first, second):
    phase = 2.0 * math.pi / count * (first[:, None] * second[None, :] % count).astype(jnp.float32)
    return (jnp.cos(phase), jnp.sin(phase))


def widened(values):
    return lax.optimization_barrier(values).astype(jnp.float32)


def dot(a, b):
    return jnp.dot(a, b, preferred_element_type=F32)


def dot_t(a, b):
    return lax.dot_general(a, b, (((1,), (1,)), ((), ())), preferred_element_type=F32)


def in_vmem(kernel, out_shape, scratch=(), flops=0, moved=0):
    def call(*operands):
        specs = [pl.BlockSpec(memory_space=pltpu.VMEM)] * len(operands)
        return pl.pallas_call(
            kernel,
            out_shape=out_shape,
            in_specs=specs,
            out_specs=jax.tree.map(lambda _: pl.BlockSpec(memory_space=pltpu.VMEM), out_shape),
            scratch_shapes=list(scratch),
            compiler_params=pltpu.CompilerParams(vmem_limit_bytes=20 * 1024 * 1024),
            cost_estimate=pl.CostEstimate(flops=flops, bytes_accessed=moved, transcendentals=0),
        )(*operands)

    return call


def place():
    y, s, c = (lax.axis_index(a) for a in AXES)
    return y, lax.rem(s, 2), lax.div(s, 2), c


def around(z, r):
    at = lax.rem((z ^ lax.div(z, 2)) + r + 4, 4)
    return at ^ lax.div(at, 2)


def low_lanes(shape):
    return lax.broadcasted_iota(jnp.int32, shape, len(shape) - 1) < 64


def half_turn(values):
    return pltpu.roll(values, 64, values.ndim - 1)


def both(first, second, low):
    return (
        jnp.where(low, first, half_turn(second)).astype(BF16),
        jnp.where(low, half_turn(first), second).astype(BF16),
    )


def quarter(p):
    y, x, _, _ = place()
    row = 1 - y if p // 2 else y
    column = 1 - x if p % 2 else x
    return pl.ds(pl.multiple_of(row * 512 + column * 256, 256), 256)


def copied(moves, sem):
    copies = [pltpu.make_async_copy(a, b, sem.at[i]) for i, (a, b) in enumerate(moves)]
    for copy in copies:
        copy.start()
    for copy in copies:
        copy.wait()


def cut_messages(tokens, key, query, out, filt, after, m1, m2, m3, own_o, away_o, away_f, sem):
    _, x, _, _ = place()
    moves = [(filt.at[:, :, :, quarter(1)], away_f)]
    for p, message in enumerate((m1, m2, m3), 1):
        column = 1 - x if p % 2 else x
        for i in range(2):
            lanes = pl.ds(pl.multiple_of(i * 512 + column * 256, 256), 256)
            moves.append((tokens.at[:, lanes], message.at[:, pl.ds(512 + i * 256, 256)]))
        moves.append((key.at[:, quarter(p)], message.at[:, pl.ds(0, 256)]))
        moves.append((query.at[:, quarter(p)], message.at[:, pl.ds(256, 256)]))
    moves += [(out.at[:, quarter(0)], own_o), (out.at[:, quarter(1)], away_o)]
    copied(moves, sem)


def copy_kernel(kernel, out_shape):
    def call(*operands):
        return pl.pallas_call(
            kernel,
            out_shape=out_shape,
            in_specs=[pl.BlockSpec(memory_space=pltpu.MemorySpace.HBM)] * len(operands),
            out_specs=[pl.BlockSpec(memory_space=pltpu.VMEM)] * len(out_shape),
            scratch_shapes=[pltpu.SemaphoreType.DMA((19,))],
            compiler_params=pltpu.CompilerParams(vmem_limit_bytes=61 * 1024 * 1024),
        )(*operands)

    return call


def pack_filter(filt, near, *refs):
    y, x, z, _ = place()
    packed, outs = refs[4], refs[:4]
    low = low_lanes((128, 128))
    for k in range(2):
        for j in range(2):
            base = pl.multiple_of(y * 512 + x * 256 + j * 128, 128)
            for part in range(2):
                if k:
                    pair = [near[part, i, :, pl.ds(j * 128, 128)].astype(F32) for i in range(2)]
                else:
                    pair = [filt[part, i, :, pl.ds(base, 128)].astype(F32) for i in range(2)]
                one, two = both(*pair, low)
                packed[2 * j, k, part] = one
                packed[2 * j + 1, k, part] = two
    for r in range(4):
        outs[r][...] = packed[around(z, r)]


def join_tokens(*refs):
    _, x, _, _ = place()
    for i in range(2):
        lanes = pl.ds(pl.multiple_of(i * 512 + x * 256, 256), 256)
        refs[4][pl.ds(0, 128), pl.ds(i * 256, 256)] = refs[0][:, lanes]
    for p in (1, 2, 3):
        refs[4][pl.ds(p * 128, 128), :] = refs[p][:, pl.ds(512, 512)]


def value_kernel(mine, other, w0, w1, w2, w3, keep, give, acc):
    _, x, z, c = place()
    for r, piece in enumerate((w0, w1, w2, w3)):
        owner = around(z, -r)
        lanes = pl.ds(pl.multiple_of(lax.rem(owner, 2) * 256, 256), 256)

        @pl.when(lax.div(owner, 2) == c)
        def _():
            term = dot(mine[:, lanes], piece[...])
            acc[...] = acc[...] + term if r else term

        @pl.when(lax.div(owner, 2) != c)
        def _():
            term = dot(other[:, lanes], piece[...])
            acc[...] = acc[...] + term if r else term

    keep[...] = acc[:, pl.ds(pl.multiple_of(x * 256, 256), 256)]
    away = pl.ds(pl.multiple_of(256 - x * 256, 256), 256)
    for p in range(4):
        give[pl.ds(p * 128, 128), :] = acc[pl.ds((p ^ 1) * 128, 128), away].astype(BF16)


def drive_kernel(keep, taken, g0, g1, g2, g3, skip, direct, o0, o1, o2, o3, drive, packed):
    _, _, z, _ = place()
    for p, gate in enumerate((g0, g1, g2, g3)):
        rows = pl.ds(p * 128, 128)
        value = (keep[rows, :] + taken[rows, :].astype(F32)).astype(BF16).astype(F32)
        held = ((gate[:, 0:256] if p else gate[:, quarter(0)]).astype(F32) * value).astype(BF16)
        drive[rows, :] = held
        direct[rows, :] = skip[:, quarter(0)] * held.astype(F32)
    low = low_lanes((256, 128))
    for j in range(2):
        lanes = pl.ds(j * 128, 128)
        first = drive[pl.ds(0, 256), lanes].astype(F32)
        second = drive[pl.ds(256, 256), lanes].astype(F32)
        packed[2 * j], packed[2 * j + 1] = both(first, second, low)
    for r, out in enumerate((o0, o1, o2, o3)):
        out[...] = packed[around(z, r)]


def add(a, b):
    return b if a is None else a if b is None else a + b


def sub(a, b):
    return a if b is None else -b if a is None else a - b


def scaled(a, s):
    if a is None or abs(s) < 1e-9:
        return None
    if abs(s - 1) < 1e-9:
        return a
    if abs(s + 1) < 1e-9:
        return -a
    return a * np.float32(s)


def cmul(a, angle):
    co, si = math.cos(angle), math.sin(angle)
    return (sub(scaled(a[0], co), scaled(a[1], si)), add(scaled(a[0], si), scaled(a[1], co)))


def cadd(a, b):
    return (add(a[0], b[0]), add(a[1], b[1]))


def conj(a):
    return (a[0], None if a[1] is None else -a[1])


def short_transform(values, count, rows):
    if len(values) == 1:
        return [(values[0], None)] * rows
    half = count // 2
    need = half // 2 + 1
    even = short_transform(values[0::2], half, need)
    odd = short_transform(values[1::2], half, need)

    def at(t, k):
        k %= half
        return t[k] if k < need else conj(t[half - k])

    return [cadd(at(even, k), cmul(at(odd, k), -2 * math.pi * k / count)) for k in range(rows)]


def conv_kernel(*refs):
    drives, filters, (table, table_t) = refs[:4], refs[4:8], refs[8:10]
    outs, (data, filt, first, sums) = refs[10:14], refs[14:]
    _, x, z, _ = place()
    for r, block in enumerate(drives):
        base = 2 * around(z, -r)
        filt[base + x] = filters[r][0]
        filt[base + 1 - x] = filters[r][1]
        data[base + x] = block[pl.ds(0, 128), :]
        data[base + 1 - x] = block[pl.ds(128, 128), :]
    for i in range(8):
        rows = pl.ds(16 * i, 16)
        values = [data[a, rows, :].astype(F32) for a in range(8)]
        spectrum = short_transform(values, 16, 9)
        for k in range(9):
            re, im = spectrum[k]
            if im is None:
                im = jnp.zeros_like(re)
            first[k, rows, 0:128] = re.astype(BF16)
            first[k, rows, 128:256] = im.astype(BF16)
            if 0 < k < 8:
                first[16 - k, rows, 0:128] = re.astype(BF16)
                first[16 - k, rows, 128:256] = (-im).astype(BF16)
    low = low_lanes((128, 128))

    def back(k):
        four = dot(table[k], first[k])
        re = four[:128, :128] + four[128:, 128:]
        im = four[:128, 128:] - four[128:, :128]
        pair = [filt[k // 2, part].astype(F32) for part in range(2)]
        if k % 2 == 0:
            fr, fi = [jnp.where(low, f, half_turn(f)) for f in pair]
        else:
            fr, fi = [jnp.where(low, half_turn(f), f) for f in pair]
        product = jnp.concatenate([re * fr - im * fi, re * fi + im * fr], axis=1).astype(BF16)
        four = dot(table_t[k], product)
        return four[:128, :128] - four[128:, 128:], four[128:, :128] + four[:128, 128:]

    sums[0, pl.ds(0, 128)] = back(0)[0]
    sums[8, pl.ds(0, 128)] = back(8)[0]
    for k in range(1, 8):
        one, two = back(k), back(16 - k)
        sums[k, pl.ds(0, 128)] = one[0] + two[0]
        sums[k, pl.ds(128, 128)] = one[1] - two[1]
    for i in range(16):
        rows, below = pl.ds(8 * i, 8), pl.ds(128 + 8 * i, 8)
        scale = 1.0 / 2048
        re = [sums[k, rows, :] * scale for k in range(9)]
        im = [None] + [sums[k, below, :] * scale for k in range(1, 8)] + [None]
        for a in range(5):
            groups = [None] * 4
            for k in range(9):
                ang = 2 * math.pi * (k * a % 16) / 16
                groups[k % 2] = add(groups[k % 2], scaled(re[k], math.cos(ang)))
                groups[2 + k % 2] = sub(groups[2 + k % 2], scaled(im[k], math.sin(ang)))
            ec, oc, es, os = groups
            data[a, rows, :] = add(add(ec, oc), add(es, os)).astype(BF16)
            if 0 < a < 4:
                data[8 - a, rows, :] = sub(sub(add(ec, os), oc), es).astype(BF16)
    for r, out in enumerate(outs):
        base = 2 * around(z, r)
        out[pl.ds(0, 128), :] = data[base + x]
        out[pl.ds(128, 128), :] = data[base + 1 - x]


def gate_kernel(e0, e1, e2, e3, direct, g0, g1, g2, g3, gated, conv):
    _, _, z, _ = place()
    for r, block in enumerate((e0, e1, e2, e3)):
        conv[around(z, -r)] = block[...]
    low = low_lanes((256, 128))
    for j in range(2):
        lanes = pl.ds(j * 128, 128)
        even, odd = conv[2 * j].astype(F32), conv[2 * j + 1].astype(F32)
        parts = (jnp.where(low, even, half_turn(odd)), jnp.where(low, half_turn(even), odd))
        for p, gate in enumerate((g0, g1, g2, g3)):
            rows = pl.ds(p * 128, 128)
            own = parts[p // 2][(p % 2) * 128 : (p % 2) * 128 + 128]
            y, x, _, _ = place()
            base = y * 512 + x * 256 if p == 0 else 256
            query = gate[:, pl.ds(pl.multiple_of(base + j * 128, 128), 128)].astype(F32)
            gated[rows, lanes] = (query * (own + direct[rows, lanes])).astype(BF16)


def sort_weight(*refs):
    pieces, keep, give = refs[:8], refs[8], refs[9]
    _, x, z, c = place()
    for r in range(4):
        owner = around(z, -r)
        for k in range(2):
            to = 2 * lax.rem(owner, 2) + (1 - x if k else x)

            @pl.when(owner // 2 == c)
            def _():
                keep[to] = pieces[2 * r + k][...]

            @pl.when(owner // 2 != c)
            def _():
                give[to] = pieces[2 * r + k][...]


def out_kernel(blocks, gated, other, keep, theirs, *outs):
    for p, out in zip(blocks, outs):
        rows = pl.ds(p * 128, 128)
        for i in range(4):
            total = dot_t(gated[rows, :], keep[i]) + dot_t(other[rows, :], theirs[i])
            out[:, pl.ds(i * 256, 256)] = total.astype(out.dtype)


def tables():
    k = np.arange(16)[:, None, None] + 16 * np.arange(128)[None, :, None]
    phase = 2 * np.pi / 2048 * (k * np.arange(128)[None, None, :] % 2048)
    co, si = np.cos(phase), np.sin(phase)
    back = np.concatenate([co.transpose(0, 2, 1), si.transpose(0, 2, 1)], 1)
    return np.concatenate([co, si], 1).astype(jnp.bfloat16), back.astype(jnp.bfloat16)


def planes(tokens, gate_q, gate_k, w_value, skip, filter_spectrum, w_out):
    seq, deep = 8, 4

    def permute(values, move):
        pairs = []
        for g in range(2):
            for i in range(seq):
                for k in range(2):
                    g2, z2, x2, k2 = move(g, i // 2, i % 2, k)
                    pairs.append(((g * seq + i) * 2 + k, (g2 * seq + z2 * 2 + x2) * 2 + k2))
        return lax.ppermute(values, AXES, pairs)

    def to_x(values):
        return permute(values, lambda g, z, x, k: (g, z, 1 - x, k))

    def to_core(values):
        return permute(values, lambda g, z, x, k: (g, z, x, 1 - k))

    def to_z(values, r):
        ring = (0, 1, 3, 2)
        at = [ring.index(z) for z in range(deep)]
        return permute(values, lambda g, z, x, k: (g, ring[(at[z] + r) % deep], x, k))

    def onward(values):
        return to_z(values, 1)

    def to_peer(values, p):
        return permute(values, lambda g, z, x, k: (g ^ (p // 2), z, x ^ (p % 2), k))

    def after(values, *done):
        return lax.optimization_barrier((values,) + done)[0]

    shape = jax.ShapeDtypeStruct
    block, square = shape((256, 128), BF16), shape((256, 256), BF16)
    own_v = lax.dynamic_slice_in_dim(w_value, lax.axis_index("grp") * 512, 512, axis=1)
    laid = [shape((128, 1024), BF16)] * 3 + [square] * 2 + [shape((2, 2, 128, 256), BF16)]
    *messages, own_o, away_o, away_f = copy_kernel(cut_messages, laid)(
        tokens, gate_k, gate_q, w_out, filter_spectrum, own_v
    )
    near = to_x(away_f)
    received = [to_peer(messages[p - 1], p) for p in (1, 2, 3)]
    filters = in_vmem(
        pack_filter,
        [shape((2, 2, 128, 128), BF16)] * 4,
        [pltpu.VMEM((4, 2, 2, 128, 128), BF16)],
        moved=1 << 20,
    )(filter_spectrum, near)
    filters = [filters[0]] + [to_z(filters[r], r) for r in (1, 2, 3)]
    v1 = onward(own_v)
    q1 = onward(own_o)
    v2 = onward(v1)
    q2 = onward(after(q1, v1))
    mine = in_vmem(join_tokens, shape((512, 512), BF16), moved=1 << 20)(tokens, after(received[0], q2), *received[1:])
    v3 = onward(v2)
    other = to_core(mine)
    got_o = to_x(after(away_o, v1))
    r1 = onward(after(got_o, v2))
    keep, give = in_vmem(
        value_kernel,
        [shape((512, 256), F32), shape((512, 256), BF16)],
        [pltpu.VMEM((512, 512), F32)],
        flops=1 << 29,
        moved=2 << 20,
    )(after(mine, r1, filters[0]), other, own_v, v1, v2, v3)
    r2 = onward(after(r1, keep))
    drive, *sends = in_vmem(
        drive_kernel,
        [shape((512, 256), F32)] + [block] * 4,
        [pltpu.VMEM((512, 256), BF16), pltpu.VMEM((4, 256, 128), BF16)],
        moved=2 << 20,
    )(keep, to_x(give), gate_k, *received, skip[None, :])
    columns = [sends[0]] + [to_z(sends[r], r) for r in (1, 2, 3)]
    r3 = onward(after(r2, filters[3], columns[1]))
    q3 = onward(after(q2, *columns[1:]))
    table, table_t = tables()
    sends = in_vmem(
        conv_kernel,
        [block] * 4,
        [
            pltpu.VMEM((8, 128, 128), BF16),
            pltpu.VMEM((8, 2, 128, 128), BF16),
            pltpu.VMEM((16, 128, 256), BF16),
            pltpu.VMEM((9, 256, 128), F32),
        ],
        flops=1 << 30,
        moved=5 << 20,
    )(*columns, *filters, table, table_t)
    rows = [sends[0]] + [to_z(sends[r], r) for r in (1, 2, 3)]

    hops = [own_o, got_o, q1, r1, q2, r2, q3, after(r3, *rows[1:])]
    quad = shape((4, 256, 256), BF16)
    keep, give = in_vmem(sort_weight, [quad] * 2, moved=2 << 20)(*hops)
    theirs = to_core(give)
    gated = in_vmem(
        gate_kernel, shape((512, 256), BF16), [pltpu.VMEM((4, 256, 128), BF16)], moved=1 << 20
    )(*rows, drive, gate_q, *received)
    gated_other = to_core(gated)
    summed = (gated, gated_other, keep, theirs)
    send = shape((128, 1024), BF16)
    far = in_vmem(functools.partial(out_kernel, (3, 1)), [send] * 2, flops=1 << 29, moved=2 << 20)
    close = in_vmem(
        functools.partial(out_kernel, (2, 0)),
        [send, shape((128, 1024), F32)],
        flops=1 << 29,
        moved=2 << 20,
    )
    to_xy, to_row = far(*summed)
    parts = [to_peer(to_xy, 3), to_peer(to_row, 1)]
    to_column, total = close(*summed)
    parts.append(to_peer(to_column, 2))
    for part in parts:
        total = total + part.astype(F32)
    return total.astype(BF16)


def shards(tokens, gate_q, gate_k, w_value, skip, filter_spectrum, w_out):
    seq_count = lax.axis_size("seq")
    position = lax.axis_index("seq")
    length_b = tokens.shape[0]
    columns_each = length_b // seq_count
    freq_rows = 2 * seq_count
    freqs_each = freq_rows // seq_count
    fft_length = freq_rows * length_b
    features = lax.all_gather(tokens, "ch", axis=1, tiled=True)
    value_weight, out_weight = (
        lax.all_gather(w_value, "seq", axis=0, tiled=True),
        lax.all_gather(w_out, "seq", axis=0, tiled=True),
    )
    value = jnp.dot(features, value_weight, preferred_element_type=jnp.float32)
    value = value.astype(jnp.bfloat16)
    drive = (gate_k.astype(jnp.float32) * widened(value)).astype(jnp.bfloat16)
    channels = drive.shape[1]
    columns = lax.all_to_all(drive[None], "seq", split_axis=1, concat_axis=0, tiled=True)
    index_rows = jnp.arange(freq_rows, dtype=jnp.int32)
    index_seq = jnp.arange(seq_count, dtype=jnp.int32)
    index_b = jnp.arange(length_b, dtype=jnp.int32)
    cos_first, sin_first = angles(freq_rows, index_rows, index_seq)
    cos_first = cos_first.astype(jnp.bfloat16)
    sin_first = sin_first.astype(jnp.bfloat16)
    flattened = columns.reshape(seq_count, columns_each * channels)
    real_part = jnp.dot(cos_first, flattened, preferred_element_type=jnp.float32)
    imag_part = jnp.dot(-sin_first, flattened, preferred_element_type=jnp.float32)
    real_part = real_part.reshape(freq_rows, columns_each, channels)
    imag_part = imag_part.reshape(freq_rows, columns_each, channels)
    mine_b = position * columns_each + jnp.arange(columns_each, dtype=jnp.int32)
    twist_cos, twist_sin = angles(fft_length, index_rows, mine_b)
    twist_cos = twist_cos[:, :, None]
    twist_sin = twist_sin[:, :, None]
    section = jnp.stack(
        [
            real_part * twist_cos + imag_part * twist_sin,
            imag_part * twist_cos - real_part * twist_sin,
        ]
    ).astype(jnp.bfloat16)
    spectral = lax.all_to_all(section, "seq", split_axis=1, concat_axis=2, tiled=True)
    cos_seq, sin_seq = angles(length_b, index_b, index_b)
    cos_seq = cos_seq.astype(jnp.bfloat16)
    sin_seq = sin_seq.astype(jnp.bfloat16)
    spectrum_real = jnp.einsum(
        "qb,kbc->kqc", cos_seq, spectral[0], preferred_element_type=jnp.float32
    ) + jnp.einsum("qb,kbc->kqc", sin_seq, spectral[1], preferred_element_type=jnp.float32)
    spectrum_imag = jnp.einsum(
        "qb,kbc->kqc", cos_seq, spectral[1], preferred_element_type=jnp.float32
    ) - jnp.einsum("qb,kbc->kqc", sin_seq, spectral[0], preferred_element_type=jnp.float32)
    filter_real = filter_spectrum[0].astype(jnp.float32)
    filter_imag = filter_spectrum[1].astype(jnp.float32)
    product = jnp.stack(
        [
            spectrum_real * filter_real - spectrum_imag * filter_imag,
            spectrum_real * filter_imag + spectrum_imag * filter_real,
        ]
    ).astype(jnp.bfloat16)
    inverse_real = jnp.einsum(
        "qb,kqc->kbc", cos_seq, product[0], preferred_element_type=jnp.float32
    ) - jnp.einsum("qb,kqc->kbc", sin_seq, product[1], preferred_element_type=jnp.float32)
    inverse_imag = jnp.einsum(
        "qb,kqc->kbc", sin_seq, product[0], preferred_element_type=jnp.float32
    ) + jnp.einsum("qb,kqc->kbc", cos_seq, product[1], preferred_element_type=jnp.float32)
    mine_k = position * freqs_each + jnp.arange(freqs_each, dtype=jnp.int32)
    back_cos, back_sin = angles(fft_length, mine_k, index_b)
    back_cos = back_cos[:, :, None]
    back_sin = back_sin[:, :, None]
    back = jnp.stack(
        [
            inverse_real * back_cos - inverse_imag * back_sin,
            inverse_real * back_sin + inverse_imag * back_cos,
        ]
    ).astype(jnp.bfloat16)
    returned = lax.all_to_all(back, "seq", split_axis=2, concat_axis=1, tiled=True)
    flat_real = returned[0].reshape(freq_rows, columns_each * channels)
    flat_imag = returned[1].reshape(freq_rows, columns_each * channels)
    conv = jnp.dot(cos_first.T, flat_real, preferred_element_type=jnp.float32) - jnp.dot(
        sin_first.T, flat_imag, preferred_element_type=jnp.float32
    )
    conv = (
        (conv * (1.0 / fft_length)).reshape(seq_count, columns_each, channels).astype(jnp.bfloat16)
    )
    conv_rows = lax.all_to_all(conv, "seq", split_axis=0, concat_axis=1, tiled=True)[0]
    gated = (
        gate_q.astype(jnp.float32) * (widened(conv_rows) + skip[None, :] * widened(drive))
    ).astype(jnp.bfloat16)
    partial_value = lax.dot_general(
        gated, out_weight, (((1,), (1,)), ((), ())), preferred_element_type=jnp.float32
    )
    return lax.psum_scatter(
        partial_value.astype(jnp.bfloat16), "ch", scatter_dimension=1, tiled=True
    )


def solution(mesh):
    placed = (
        P(("grp", "seq"), "ch"),
        P(("grp", "seq"), "ch"),
        P(("grp", "seq"), "ch"),
        P("seq", "ch"),
        P("ch"),
        P(None, "seq", None, "ch"),
        P("seq", "ch"),
    )
    sizes = mesh.shape
    body = planes if (sizes["grp"], sizes["seq"], sizes["ch"]) == (2, 8, 2) else shards
    return jax.shard_map(
        body, mesh=mesh, in_specs=placed, out_specs=P(("grp", "seq"), "ch"), check_vma=False
    )
```

```python
import functools
import math

import jax
import jax.numpy as jnp
import numpy as np
from jax import lax
from jax.experimental import pallas as pl
from jax.experimental.pallas import tpu as pltpu
from jax.sharding import PartitionSpec as P

AXES = ("grp", "seq", "ch")
BF16 = jnp.bfloat16
F32 = jnp.float32


def angles(count, first, second):
    phase = 2.0 * math.pi / count * (first[:, None] * second[None, :] % count).astype(jnp.float32)
    return (jnp.cos(phase), jnp.sin(phase))


def widened(values):
    return lax.optimization_barrier(values).astype(jnp.float32)


def dot(a, b):
    return jnp.dot(a, b, preferred_element_type=F32)


def dot_t(a, b):
    return lax.dot_general(a, b, (((1,), (1,)), ((), ())), preferred_element_type=F32)


def in_vmem(kernel, out_shape, scratch=(), flops=0, moved=0):
    def call(*operands):
        specs = [pl.BlockSpec(memory_space=pltpu.VMEM)] * len(operands)
        return pl.pallas_call(
            kernel,
            out_shape=out_shape,
            in_specs=specs,
            out_specs=jax.tree.map(lambda _: pl.BlockSpec(memory_space=pltpu.VMEM), out_shape),
            scratch_shapes=list(scratch),
            compiler_params=pltpu.CompilerParams(vmem_limit_bytes=20 * 1024 * 1024),
            cost_estimate=pl.CostEstimate(flops=flops, bytes_accessed=moved, transcendentals=0),
        )(*operands)

    return call


def place():
    y, s, c = (lax.axis_index(a) for a in AXES)
    return y, lax.rem(s, 2), lax.div(s, 2), c


def around(z, r):
    at = lax.rem((z ^ lax.div(z, 2)) + r + 4, 4)
    return at ^ lax.div(at, 2)


def low_lanes(shape):
    return lax.broadcasted_iota(jnp.int32, shape, len(shape) - 1) < 64


def half_turn(values):
    return pltpu.roll(values, 64, values.ndim - 1)


def both(first, second, low):
    return (
        jnp.where(low, first, half_turn(second)).astype(BF16),
        jnp.where(low, half_turn(first), second).astype(BF16),
    )


def quarter(p):
    y, x, _, _ = place()
    row = 1 - y if p // 2 else y
    column = 1 - x if p % 2 else x
    return pl.ds(pl.multiple_of(row * 512 + column * 256, 256), 256)


def copied(moves, sem):
    copies = [pltpu.make_async_copy(a, b, sem.at[i]) for i, (a, b) in enumerate(moves)]
    for copy in copies:
        copy.start()
    for copy in copies:
        copy.wait()


def cut_messages(tokens, key, query, out, filt, after, m1, m2, m3, own_o, away_o, away_f, sem):
    _, x, _, _ = place()
    moves = [(filt.at[:, :, :, quarter(1)], away_f)]
    for p, message in enumerate((m1, m2, m3), 1):
        column = 1 - x if p % 2 else x
        for i in range(2):
            lanes = pl.ds(pl.multiple_of(i * 512 + column * 256, 256), 256)
            moves.append((tokens.at[:, lanes], message.at[:, pl.ds(512 + i * 256, 256)]))
        moves.append((key.at[:, quarter(p)], message.at[:, pl.ds(0, 256)]))
        moves.append((query.at[:, quarter(p)], message.at[:, pl.ds(256, 256)]))
    moves += [(out.at[:, quarter(0)], own_o), (out.at[:, quarter(1)], away_o)]
    copied(moves, sem)


def copy_kernel(kernel, out_shape):
    def call(*operands):
        return pl.pallas_call(
            kernel,
            out_shape=out_shape,
            in_specs=[pl.BlockSpec(memory_space=pltpu.MemorySpace.HBM)] * len(operands),
            out_specs=[pl.BlockSpec(memory_space=pltpu.VMEM)] * len(out_shape),
            scratch_shapes=[pltpu.SemaphoreType.DMA((19,))],
            compiler_params=pltpu.CompilerParams(vmem_limit_bytes=61 * 1024 * 1024),
        )(*operands)

    return call


def pack_filter(filt, near, *refs):
    y, x, z, _ = place()
    packed, outs = refs[4], refs[:4]
    low = low_lanes((128, 128))
    for k in range(2):
        for j in range(2):
            base = pl.multiple_of(y * 512 + x * 256 + j * 128, 128)
            for part in range(2):
                if k:
                    pair = [near[part, i, :, pl.ds(j * 128, 128)].astype(F32) for i in range(2)]
                else:
                    pair = [filt[part, i, :, pl.ds(base, 128)].astype(F32) for i in range(2)]
                one, two = both(*pair, low)
                packed[2 * j, k, part] = one
                packed[2 * j + 1, k, part] = two
    for r in range(4):
        outs[r][...] = packed[around(z, r)]


def join_tokens(*refs):
    _, x, _, _ = place()
    for i in range(2):
        lanes = pl.ds(pl.multiple_of(i * 512 + x * 256, 256), 256)
        refs[4][pl.ds(0, 128), pl.ds(i * 256, 256)] = refs[0][:, lanes]
    for p in (1, 2, 3):
        refs[4][pl.ds(p * 128, 128), :] = refs[p][:, pl.ds(512, 512)]


def value_kernel(mine, other, w0, w1, w2, w3, keep, give, acc):
    _, x, z, c = place()
    for r, piece in enumerate((w0, w1, w2, w3)):
        owner = around(z, -r)
        lanes = pl.ds(pl.multiple_of(lax.rem(owner, 2) * 256, 256), 256)

        @pl.when(lax.div(owner, 2) == c)
        def _():
            term = dot(mine[:, lanes], piece[...])
            acc[...] = acc[...] + term if r else term

        @pl.when(lax.div(owner, 2) != c)
        def _():
            term = dot(other[:, lanes], piece[...])
            acc[...] = acc[...] + term if r else term

    keep[...] = acc[:, pl.ds(pl.multiple_of(x * 256, 256), 256)]
    away = pl.ds(pl.multiple_of(256 - x * 256, 256), 256)
    for p in range(4):
        give[pl.ds(p * 128, 128), :] = acc[pl.ds((p ^ 1) * 128, 128), away].astype(BF16)


def drive_kernel(keep, taken, g0, g1, g2, g3, skip, direct, o0, o1, o2, o3, drive, packed):
    _, _, z, _ = place()
    for p, gate in enumerate((g0, g1, g2, g3)):
        rows = pl.ds(p * 128, 128)
        value = (keep[rows, :] + taken[rows, :].astype(F32)).astype(BF16).astype(F32)
        held = ((gate[:, 0:256] if p else gate[:, quarter(0)]).astype(F32) * value).astype(BF16)
        drive[rows, :] = held
        direct[rows, :] = skip[:, quarter(0)] * held.astype(F32)
    low = low_lanes((256, 128))
    for j in range(2):
        lanes = pl.ds(j * 128, 128)
        first = drive[pl.ds(0, 256), lanes].astype(F32)
        second = drive[pl.ds(256, 256), lanes].astype(F32)
        packed[2 * j], packed[2 * j + 1] = both(first, second, low)
    for r, out in enumerate((o0, o1, o2, o3)):
        out[...] = packed[around(z, r)]


def add(a, b):
    return b if a is None else a if b is None else a + b


def sub(a, b):
    return a if b is None else -b if a is None else a - b


def scaled(a, s):
    if a is None or abs(s) < 1e-9:
        return None
    if abs(s - 1) < 1e-9:
        return a
    if abs(s + 1) < 1e-9:
        return -a
    return a * np.float32(s)


def cmul(a, angle):
    co, si = math.cos(angle), math.sin(angle)
    return (sub(scaled(a[0], co), scaled(a[1], si)), add(scaled(a[0], si), scaled(a[1], co)))


def cadd(a, b):
    return (add(a[0], b[0]), add(a[1], b[1]))


def conj(a):
    return (a[0], None if a[1] is None else -a[1])


def short_transform(values, count, rows):
    if len(values) == 1:
        return [(values[0], None)] * rows
    half = count // 2
    need = half // 2 + 1
    even = short_transform(values[0::2], half, need)
    odd = short_transform(values[1::2], half, need)

    def at(t, k):
        k %= half
        return t[k] if k < need else conj(t[half - k])

    return [cadd(at(even, k), cmul(at(odd, k), -2 * math.pi * k / count)) for k in range(rows)]


def conv_kernel(*refs):
    drives, filters, (table, table_t) = refs[:4], refs[4:8], refs[8:10]
    outs, (data, filt, first, sums) = refs[10:14], refs[14:]
    _, x, z, _ = place()
    for r, block in enumerate(drives):
        base = 2 * around(z, -r)
        filt[base + x] = filters[r][0]
        filt[base + 1 - x] = filters[r][1]
        data[base + x] = block[pl.ds(0, 128), :]
        data[base + 1 - x] = block[pl.ds(128, 128), :]
    for i in range(8):
        rows = pl.ds(16 * i, 16)
        values = [data[a, rows, :].astype(F32) for a in range(8)]
        spectrum = short_transform(values, 16, 9)
        for k in range(9):
            re, im = spectrum[k]
            if im is None:
                im = jnp.zeros_like(re)
            first[k, rows, 0:128] = re.astype(BF16)
            first[k, rows, 128:256] = im.astype(BF16)
            if 0 < k < 8:
                first[16 - k, rows, 0:128] = re.astype(BF16)
                first[16 - k, rows, 128:256] = (-im).astype(BF16)
    low = low_lanes((128, 128))

    def back(k):
        four = dot(table[k], first[k])
        re = four[:128, :128] + four[128:, 128:]
        im = four[:128, 128:] - four[128:, :128]
        pair = [filt[k // 2, part].astype(F32) for part in range(2)]
        if k % 2 == 0:
            fr, fi = [jnp.where(low, f, half_turn(f)) for f in pair]
        else:
            fr, fi = [jnp.where(low, half_turn(f), f) for f in pair]
        product = jnp.concatenate([re * fr - im * fi, re * fi + im * fr], axis=1).astype(BF16)
        four = dot(table_t[k], product)
        return four[:128, :128] - four[128:, 128:], four[128:, :128] + four[:128, 128:]

    sums[0, pl.ds(0, 128)] = back(0)[0]
    sums[8, pl.ds(0, 128)] = back(8)[0]
    for k in range(1, 8):
        one, two = back(k), back(16 - k)
        sums[k, pl.ds(0, 128)] = one[0] + two[0]
        sums[k, pl.ds(128, 128)] = one[1] - two[1]
    for i in range(16):
        rows, below = pl.ds(8 * i, 8), pl.ds(128 + 8 * i, 8)
        scale = 1.0 / 2048
        re = [sums[k, rows, :] * scale for k in range(9)]
        im = [None] + [sums[k, below, :] * scale for k in range(1, 8)] + [None]
        for a in range(5):
            groups = [None] * 4
            for k in range(9):
                ang = 2 * math.pi * (k * a % 16) / 16
                groups[k % 2] = add(groups[k % 2], scaled(re[k], math.cos(ang)))
                groups[2 + k % 2] = sub(groups[2 + k % 2], scaled(im[k], math.sin(ang)))
            ec, oc, es, os = groups
            data[a, rows, :] = add(add(ec, oc), add(es, os)).astype(BF16)
            if 0 < a < 4:
                data[8 - a, rows, :] = sub(sub(add(ec, os), oc), es).astype(BF16)
    for r, out in enumerate(outs):
        base = 2 * around(z, r)
        out[pl.ds(0, 128), :] = data[base + x]
        out[pl.ds(128, 128), :] = data[base + 1 - x]


def gate_kernel(e0, e1, e2, e3, direct, g0, g1, g2, g3, gated, conv):
    _, _, z, _ = place()
    for r, block in enumerate((e0, e1, e2, e3)):
        conv[around(z, -r)] = block[...]
    low = low_lanes((256, 128))
    for j in range(2):
        lanes = pl.ds(j * 128, 128)
        even, odd = conv[2 * j].astype(F32), conv[2 * j + 1].astype(F32)
        parts = (jnp.where(low, even, half_turn(odd)), jnp.where(low, half_turn(even), odd))
        for p, gate in enumerate((g0, g1, g2, g3)):
            rows = pl.ds(p * 128, 128)
            own = parts[p // 2][(p % 2) * 128 : (p % 2) * 128 + 128]
            y, x, _, _ = place()
            base = y * 512 + x * 256 if p == 0 else 256
            query = gate[:, pl.ds(pl.multiple_of(base + j * 128, 128), 128)].astype(F32)
            gated[rows, lanes] = (query * (own + direct[rows, lanes])).astype(BF16)


def sort_weight(*refs):
    pieces, keep, give = refs[:7], refs[7], refs[8]
    _, x, z, c = place()
    for r in range(4):
        owner = around(z, -r)
        for k in range(2):
            to = 2 * lax.rem(owner, 2) + (1 - x if k else x)

            @pl.when(owner // 2 == c)
            def _():
                keep[to] = (pieces[2 * r + k][...] if r < 3 else pieces[6][k])

            @pl.when(owner // 2 != c)
            def _():
                give[to] = (pieces[2 * r + k][...] if r < 3 else pieces[6][k])


def out_kernel(blocks, gated, other, keep, theirs, *outs):
    for p, out in zip(blocks, outs):
        rows = pl.ds(p * 128, 128)
        for i in range(4):
            total = dot_t(gated[rows, :], keep[i]) + dot_t(other[rows, :], theirs[i])
            out[:, pl.ds(i * 256, 256)] = total.astype(out.dtype)


def tables():
    k = np.arange(16)[:, None, None] + 16 * np.arange(128)[None, :, None]
    phase = 2 * np.pi / 2048 * (k * np.arange(128)[None, None, :] % 2048)
    co, si = np.cos(phase), np.sin(phase)
    back = np.concatenate([co.transpose(0, 2, 1), si.transpose(0, 2, 1)], 1)
    return np.concatenate([co, si], 1).astype(jnp.bfloat16), back.astype(jnp.bfloat16)


def planes(tokens, gate_q, gate_k, w_value, skip, filter_spectrum, w_out):
    seq, deep = 8, 4

    def permute(values, move):
        pairs = []
        for g in range(2):
            for i in range(seq):
                for k in range(2):
                    g2, z2, x2, k2 = move(g, i // 2, i % 2, k)
                    pairs.append(((g * seq + i) * 2 + k, (g2 * seq + z2 * 2 + x2) * 2 + k2))
        return lax.ppermute(values, AXES, pairs)

    def to_x(values):
        return permute(values, lambda g, z, x, k: (g, z, 1 - x, k))

    def to_core(values):
        return permute(values, lambda g, z, x, k: (g, z, x, 1 - k))

    def to_z(values, r):
        ring = (0, 1, 3, 2)
        at = [ring.index(z) for z in range(deep)]
        return permute(values, lambda g, z, x, k: (g, ring[(at[z] + r) % deep], x, k))

    def onward(values):
        return to_z(values, 1)

    def to_peer(values, p):
        return permute(values, lambda g, z, x, k: (g ^ (p // 2), z, x ^ (p % 2), k))

    def after(values, *done):
        return lax.optimization_barrier((values,) + done)[0]

    shape = jax.ShapeDtypeStruct
    block, square = shape((256, 128), BF16), shape((256, 256), BF16)
    own_v = lax.dynamic_slice_in_dim(w_value, lax.axis_index("grp") * 512, 512, axis=1)
    laid = [shape((128, 1024), BF16)] * 3 + [square] * 2 + [shape((2, 2, 128, 256), BF16)]
    *messages, own_o, away_o, away_f = copy_kernel(cut_messages, laid)(
        tokens, gate_k, gate_q, w_out, filter_spectrum, own_v
    )
    near = to_x(away_f)
    received = [to_peer(messages[p - 1], p) for p in (1, 2, 3)]
    filters = in_vmem(
        pack_filter,
        [shape((2, 2, 128, 128), BF16)] * 4,
        [pltpu.VMEM((4, 2, 2, 128, 128), BF16)],
        moved=1 << 20,
    )(filter_spectrum, near)
    filters = [filters[0]] + [to_z(filters[r], r) for r in (1, 2, 3)]
    v1 = onward(own_v)
    q1 = onward(own_o)
    v2 = onward(v1)
    q2 = onward(after(q1, v1))
    mine = in_vmem(join_tokens, shape((512, 512), BF16), moved=1 << 20)(tokens, after(received[0], q2), *received[1:])
    v3 = onward(v2)
    other = to_core(mine)
    got_o = to_x(after(away_o, v1))
    r1 = onward(after(got_o, v2))
    keep, give = in_vmem(
        value_kernel,
        [shape((512, 256), F32), shape((512, 256), BF16)],
        [pltpu.VMEM((512, 512), F32)],
        flops=1 << 29,
        moved=2 << 20,
    )(after(mine, r1, filters[0]), other, own_v, v1, v2, v3)
    r2 = onward(after(r1, keep))
    drive, *sends = in_vmem(
        drive_kernel,
        [shape((512, 256), F32)] + [block] * 4,
        [pltpu.VMEM((512, 256), BF16), pltpu.VMEM((4, 256, 128), BF16)],
        moved=2 << 20,
    )(keep, to_x(give), gate_k, *received, skip[None, :])
    columns = [sends[0]] + [to_z(sends[r], r) for r in (1, 2, 3)]
    last = onward(after(jnp.stack([q2, r2]), filters[3], *columns[1:]))
    table, table_t = tables()
    sends = in_vmem(
        conv_kernel,
        [block] * 4,
        [
            pltpu.VMEM((8, 128, 128), BF16),
            pltpu.VMEM((8, 2, 128, 128), BF16),
            pltpu.VMEM((16, 128, 256), BF16),
            pltpu.VMEM((9, 256, 128), F32),
        ],
        flops=1 << 30,
        moved=5 << 20,
    )(*columns, *filters, table, table_t)
    rows = [sends[0]] + [to_z(sends[r], r) for r in (1, 2, 3)]

    hops = [own_o, got_o, q1, r1, q2, r2, after(last, *rows[1:])]
    quad = shape((4, 256, 256), BF16)
    keep, give = in_vmem(sort_weight, [quad] * 2, moved=2 << 20)(*hops)
    theirs = to_core(give)
    gated = in_vmem(
        gate_kernel, shape((512, 256), BF16), [pltpu.VMEM((4, 256, 128), BF16)], moved=1 << 20
    )(*rows, drive, gate_q, *received)
    gated_other = to_core(gated)
    summed = (gated, gated_other, keep, theirs)
    send = shape((128, 1024), BF16)
    far = in_vmem(functools.partial(out_kernel, (3, 1)), [send] * 2, flops=1 << 29, moved=2 << 20)
    close = in_vmem(
        functools.partial(out_kernel, (2, 0)),
        [send, shape((128, 1024), F32)],
        flops=1 << 29,
        moved=2 << 20,
    )
    to_xy, to_row = far(*summed)
    parts = [to_peer(to_xy, 3), to_peer(to_row, 1)]
    to_column, total = close(*summed)
    parts.append(to_peer(to_column, 2))
    for part in parts:
        total = total + part.astype(F32)
    return total.astype(BF16)


def shards(tokens, gate_q, gate_k, w_value, skip, filter_spectrum, w_out):
    seq_count = lax.axis_size("seq")
    position = lax.axis_index("seq")
    length_b = tokens.shape[0]
    columns_each = length_b // seq_count
    freq_rows = 2 * seq_count
    freqs_each = freq_rows // seq_count
    fft_length = freq_rows * length_b
    features = lax.all_gather(tokens, "ch", axis=1, tiled=True)
    value_weight, out_weight = (
        lax.all_gather(w_value, "seq", axis=0, tiled=True),
        lax.all_gather(w_out, "seq", axis=0, tiled=True),
    )
    value = jnp.dot(features, value_weight, preferred_element_type=jnp.float32)
    value = value.astype(jnp.bfloat16)
    drive = (gate_k.astype(jnp.float32) * widened(value)).astype(jnp.bfloat16)
    channels = drive.shape[1]
    columns = lax.all_to_all(drive[None], "seq", split_axis=1, concat_axis=0, tiled=True)
    index_rows = jnp.arange(freq_rows, dtype=jnp.int32)
    index_seq = jnp.arange(seq_count, dtype=jnp.int32)
    index_b = jnp.arange(length_b, dtype=jnp.int32)
    cos_first, sin_first = angles(freq_rows, index_rows, index_seq)
    cos_first = cos_first.astype(jnp.bfloat16)
    sin_first = sin_first.astype(jnp.bfloat16)
    flattened = columns.reshape(seq_count, columns_each * channels)
    real_part = jnp.dot(cos_first, flattened, preferred_element_type=jnp.float32)
    imag_part = jnp.dot(-sin_first, flattened, preferred_element_type=jnp.float32)
    real_part = real_part.reshape(freq_rows, columns_each, channels)
    imag_part = imag_part.reshape(freq_rows, columns_each, channels)
    mine_b = position * columns_each + jnp.arange(columns_each, dtype=jnp.int32)
    twist_cos, twist_sin = angles(fft_length, index_rows, mine_b)
    twist_cos = twist_cos[:, :, None]
    twist_sin = twist_sin[:, :, None]
    section = jnp.stack(
        [
            real_part * twist_cos + imag_part * twist_sin,
            imag_part * twist_cos - real_part * twist_sin,
        ]
    ).astype(jnp.bfloat16)
    spectral = lax.all_to_all(section, "seq", split_axis=1, concat_axis=2, tiled=True)
    cos_seq, sin_seq = angles(length_b, index_b, index_b)
    cos_seq = cos_seq.astype(jnp.bfloat16)
    sin_seq = sin_seq.astype(jnp.bfloat16)
    spectrum_real = jnp.einsum(
        "qb,kbc->kqc", cos_seq, spectral[0], preferred_element_type=jnp.float32
    ) + jnp.einsum("qb,kbc->kqc", sin_seq, spectral[1], preferred_element_type=jnp.float32)
    spectrum_imag = jnp.einsum(
        "qb,kbc->kqc", cos_seq, spectral[1], preferred_element_type=jnp.float32
    ) - jnp.einsum("qb,kbc->kqc", sin_seq, spectral[0], preferred_element_type=jnp.float32)
    filter_real = filter_spectrum[0].astype(jnp.float32)
    filter_imag = filter_spectrum[1].astype(jnp.float32)
    product = jnp.stack(
        [
            spectrum_real * filter_real - spectrum_imag * filter_imag,
            spectrum_real * filter_imag + spectrum_imag * filter_real,
        ]
    ).astype(jnp.bfloat16)
    inverse_real = jnp.einsum(
        "qb,kqc->kbc", cos_seq, product[0], preferred_element_type=jnp.float32
    ) - jnp.einsum("qb,kqc->kbc", sin_seq, product[1], preferred_element_type=jnp.float32)
    inverse_imag = jnp.einsum(
        "qb,kqc->kbc", sin_seq, product[0], preferred_element_type=jnp.float32
    ) + jnp.einsum("qb,kqc->kbc", cos_seq, product[1], preferred_element_type=jnp.float32)
    mine_k = position * freqs_each + jnp.arange(freqs_each, dtype=jnp.int32)
    back_cos, back_sin = angles(fft_length, mine_k, index_b)
    back_cos = back_cos[:, :, None]
    back_sin = back_sin[:, :, None]
    back = jnp.stack(
        [
            inverse_real * back_cos - inverse_imag * back_sin,
            inverse_real * back_sin + inverse_imag * back_cos,
        ]
    ).astype(jnp.bfloat16)
    returned = lax.all_to_all(back, "seq", split_axis=2, concat_axis=1, tiled=True)
    flat_real = returned[0].reshape(freq_rows, columns_each * channels)
    flat_imag = returned[1].reshape(freq_rows, columns_each * channels)
    conv = jnp.dot(cos_first.T, flat_real, preferred_element_type=jnp.float32) - jnp.dot(
        sin_first.T, flat_imag, preferred_element_type=jnp.float32
    )
    conv = (
        (conv * (1.0 / fft_length)).reshape(seq_count, columns_each, channels).astype(jnp.bfloat16)
    )
    conv_rows = lax.all_to_all(conv, "seq", split_axis=0, concat_axis=1, tiled=True)[0]
    gated = (
        gate_q.astype(jnp.float32) * (widened(conv_rows) + skip[None, :] * widened(drive))
    ).astype(jnp.bfloat16)
    partial_value = lax.dot_general(
        gated, out_weight, (((1,), (1,)), ((), ())), preferred_element_type=jnp.float32
    )
    return lax.psum_scatter(
        partial_value.astype(jnp.bfloat16), "ch", scatter_dimension=1, tiled=True
    )


def solution(mesh):
    placed = (
        P(("grp", "seq"), "ch"),
        P(("grp", "seq"), "ch"),
        P(("grp", "seq"), "ch"),
        P("seq", "ch"),
        P("ch"),
        P(None, "seq", None, "ch"),
        P("seq", "ch"),
    )
    sizes = mesh.shape
    body = planes if (sizes["grp"], sizes["seq"], sizes["ch"]) == (2, 8, 2) else shards
    return jax.shard_map(
        body, mesh=mesh, in_specs=placed, out_specs=P(("grp", "seq"), "ch"), check_vma=False
    )
```

```python
import functools
import math

import jax
import jax.numpy as jnp
import numpy as np
from jax import lax
from jax.experimental import pallas as pl
from jax.experimental.pallas import tpu as pltpu
from jax.sharding import PartitionSpec as P

AXES = ("grp", "seq", "ch")
BF16 = jnp.bfloat16
F32 = jnp.float32


def angles(count, first, second):
    phase = 2.0 * math.pi / count * (first[:, None] * second[None, :] % count).astype(jnp.float32)
    return (jnp.cos(phase), jnp.sin(phase))


def widened(values):
    return lax.optimization_barrier(values).astype(jnp.float32)


def dot(a, b):
    return jnp.dot(a, b, preferred_element_type=F32)


def dot_t(a, b):
    return lax.dot_general(a, b, (((1,), (1,)), ((), ())), preferred_element_type=F32)


def in_vmem(kernel, out_shape, scratch=(), flops=0, moved=0):
    def call(*operands):
        specs = [pl.BlockSpec(memory_space=pltpu.VMEM)] * len(operands)
        return pl.pallas_call(
            kernel,
            out_shape=out_shape,
            in_specs=specs,
            out_specs=jax.tree.map(lambda _: pl.BlockSpec(memory_space=pltpu.VMEM), out_shape),
            scratch_shapes=list(scratch),
            compiler_params=pltpu.CompilerParams(vmem_limit_bytes=20 * 1024 * 1024),
            cost_estimate=pl.CostEstimate(flops=flops, bytes_accessed=moved, transcendentals=0),
        )(*operands)

    return call


def place():
    y, s, c = (lax.axis_index(a) for a in AXES)
    return y, lax.rem(s, 2), lax.div(s, 2), c


def around(z, r):
    at = lax.rem((z ^ lax.div(z, 2)) + r + 4, 4)
    return at ^ lax.div(at, 2)


def low_lanes(shape):
    return lax.broadcasted_iota(jnp.int32, shape, len(shape) - 1) < 64


def half_turn(values):
    return pltpu.roll(values, 64, values.ndim - 1)


def both(first, second, low):
    return (
        jnp.where(low, first, half_turn(second)).astype(BF16),
        jnp.where(low, half_turn(first), second).astype(BF16),
    )


def quarter(p):
    y, x, _, _ = place()
    row = 1 - y if p // 2 else y
    column = 1 - x if p % 2 else x
    return pl.ds(pl.multiple_of(row * 512 + column * 256, 256), 256)


def copied(moves, sem):
    copies = [pltpu.make_async_copy(a, b, sem.at[i]) for i, (a, b) in enumerate(moves)]
    for copy in copies:
        copy.start()
    for copy in copies:
        copy.wait()


def cut_messages(tokens, key, query, out, filt, after, m1, m2, m3, own_o, away_o, away_f, sem):
    _, x, _, _ = place()
    moves = [(filt.at[:, :, :, quarter(1)], away_f)]
    for p, message in enumerate((m1, m2, m3), 1):
        column = 1 - x if p % 2 else x
        for i in range(2):
            lanes = pl.ds(pl.multiple_of(i * 512 + column * 256, 256), 256)
            moves.append((tokens.at[:, lanes], message.at[:, pl.ds(512 + i * 256, 256)]))
        moves.append((key.at[:, quarter(p)], message.at[:, pl.ds(0, 256)]))
        moves.append((query.at[:, quarter(p)], message.at[:, pl.ds(256, 256)]))
    moves += [(out.at[:, quarter(0)], own_o), (out.at[:, quarter(1)], away_o)]
    copied(moves, sem)


def copy_kernel(kernel, out_shape):
    def call(*operands):
        return pl.pallas_call(
            kernel,
            out_shape=out_shape,
            in_specs=[pl.BlockSpec(memory_space=pltpu.MemorySpace.HBM)] * len(operands),
            out_specs=[pl.BlockSpec(memory_space=pltpu.VMEM)] * len(out_shape),
            scratch_shapes=[pltpu.SemaphoreType.DMA((19,))],
            compiler_params=pltpu.CompilerParams(vmem_limit_bytes=61 * 1024 * 1024),
        )(*operands)

    return call


def pack_filter(filt, near, *refs):
    y, x, z, _ = place()
    packed, outs = refs[4], refs[:4]
    low = low_lanes((128, 128))
    for k in range(2):
        for j in range(2):
            base = pl.multiple_of(y * 512 + x * 256 + j * 128, 128)
            for part in range(2):
                if k:
                    pair = [near[part, i, :, pl.ds(j * 128, 128)].astype(F32) for i in range(2)]
                else:
                    pair = [filt[part, i, :, pl.ds(base, 128)].astype(F32) for i in range(2)]
                one, two = both(*pair, low)
                packed[2 * j, k, part] = one
                packed[2 * j + 1, k, part] = two
    for r in range(4):
        outs[r][...] = packed[around(z, r)]


def join_tokens(*refs):
    _, x, _, _ = place()
    for i in range(2):
        lanes = pl.ds(pl.multiple_of(i * 512 + x * 256, 256), 256)
        refs[4][pl.ds(0, 128), pl.ds(i * 256, 256)] = refs[0][:, lanes]
    for p in (1, 2, 3):
        refs[4][pl.ds(p * 128, 128), :] = refs[p][:, pl.ds(512, 512)]


def value_kernel(mine, other, w0, w1, w2, w3, keep, give, acc):
    _, x, z, c = place()
    for r, piece in enumerate((w0, w1, w2, w3)):
        owner = around(z, -r)
        lanes = pl.ds(pl.multiple_of(lax.rem(owner, 2) * 256, 256), 256)

        @pl.when(lax.div(owner, 2) == c)
        def _():
            term = dot(mine[:, lanes], piece[...])
            acc[...] = acc[...] + term if r else term

        @pl.when(lax.div(owner, 2) != c)
        def _():
            term = dot(other[:, lanes], piece[...])
            acc[...] = acc[...] + term if r else term

    keep[...] = acc[:, pl.ds(pl.multiple_of(x * 256, 256), 256)]
    away = pl.ds(pl.multiple_of(256 - x * 256, 256), 256)
    for p in range(4):
        give[pl.ds(p * 128, 128), :] = acc[pl.ds((p ^ 1) * 128, 128), away].astype(BF16)


def drive_kernel(keep, taken, g0, g1, g2, g3, skip, direct, o0, o1, o2, o3, drive, packed):
    _, _, z, _ = place()
    for p, gate in enumerate((g0, g1, g2, g3)):
        rows = pl.ds(p * 128, 128)
        value = (keep[rows, :] + taken[rows, :].astype(F32)).astype(BF16).astype(F32)
        held = ((gate[:, 0:256] if p else gate[:, quarter(0)]).astype(F32) * value).astype(BF16)
        drive[rows, :] = held
        direct[rows, :] = skip[:, quarter(0)] * held.astype(F32)
    low = low_lanes((256, 128))
    for j in range(2):
        lanes = pl.ds(j * 128, 128)
        first = drive[pl.ds(0, 256), lanes].astype(F32)
        second = drive[pl.ds(256, 256), lanes].astype(F32)
        packed[2 * j], packed[2 * j + 1] = both(first, second, low)
    for r, out in enumerate((o0, o1, o2, o3)):
        out[...] = packed[around(z, r)]


def add(a, b):
    return b if a is None else a if b is None else a + b


def sub(a, b):
    return a if b is None else -b if a is None else a - b


def scaled(a, s):
    if a is None or abs(s) < 1e-9:
        return None
    if abs(s - 1) < 1e-9:
        return a
    if abs(s + 1) < 1e-9:
        return -a
    return a * np.float32(s)


def cmul(a, angle):
    co, si = math.cos(angle), math.sin(angle)
    return (sub(scaled(a[0], co), scaled(a[1], si)), add(scaled(a[0], si), scaled(a[1], co)))


def cadd(a, b):
    return (add(a[0], b[0]), add(a[1], b[1]))


def conj(a):
    return (a[0], None if a[1] is None else -a[1])


def short_transform(values, count, rows):
    if len(values) == 1:
        return [(values[0], None)] * rows
    half = count // 2
    need = half // 2 + 1
    even = short_transform(values[0::2], half, need)
    odd = short_transform(values[1::2], half, need)

    def at(t, k):
        k %= half
        return t[k] if k < need else conj(t[half - k])

    return [cadd(at(even, k), cmul(at(odd, k), -2 * math.pi * k / count)) for k in range(rows)]


def conv_kernel(*refs):
    drives, filters, (table, table_t) = refs[:4], refs[4:8], refs[8:10]
    outs, (data, filt, first, sums) = refs[10:14], refs[14:]
    _, x, z, _ = place()
    for r, block in enumerate(drives):
        base = 2 * around(z, -r)
        filt[base + x] = filters[r][0]
        filt[base + 1 - x] = filters[r][1]
        data[base + x] = block[pl.ds(0, 128), :]
        data[base + 1 - x] = block[pl.ds(128, 128), :]
    for i in range(8):
        rows = pl.ds(16 * i, 16)
        values = [data[a, rows, :].astype(F32) for a in range(8)]
        spectrum = short_transform(values, 16, 9)
        for k in range(9):
            re, im = spectrum[k]
            if im is None:
                im = jnp.zeros_like(re)
            first[k, rows, 0:128] = re.astype(BF16)
            first[k, rows, 128:256] = im.astype(BF16)
            if 0 < k < 8:
                first[16 - k, rows, 0:128] = re.astype(BF16)
                first[16 - k, rows, 128:256] = (-im).astype(BF16)
    low = low_lanes((128, 128))

    def back(k):
        four = dot(table[k], first[k])
        re = four[:128, :128] + four[128:, 128:]
        im = four[:128, 128:] - four[128:, :128]
        pair = [filt[k // 2, part].astype(F32) for part in range(2)]
        if k % 2 == 0:
            fr, fi = [jnp.where(low, f, half_turn(f)) for f in pair]
        else:
            fr, fi = [jnp.where(low, half_turn(f), f) for f in pair]
        product = jnp.concatenate([re * fr - im * fi, re * fi + im * fr], axis=1).astype(BF16)
        four = dot(table_t[k], product)
        return four[:128, :128] - four[128:, 128:], four[128:, :128] + four[:128, 128:]

    sums[0, pl.ds(0, 128)] = back(0)[0]
    sums[8, pl.ds(0, 128)] = back(8)[0]
    for k in range(1, 8):
        one, two = back(k), back(16 - k)
        sums[k, pl.ds(0, 128)] = one[0] + two[0]
        sums[k, pl.ds(128, 128)] = one[1] - two[1]
    for i in range(8):
        rows, below = pl.ds(16 * i, 16), pl.ds(128 + 16 * i, 16)
        scale = 1.0 / 2048
        re = [sums[k, rows, :] * scale for k in range(9)]
        im = [None] + [sums[k, below, :] * scale for k in range(1, 8)] + [None]
        for a in range(5):
            groups = [None] * 4
            for k in range(9):
                ang = 2 * math.pi * (k * a % 16) / 16
                groups[k % 2] = add(groups[k % 2], scaled(re[k], math.cos(ang)))
                groups[2 + k % 2] = sub(groups[2 + k % 2], scaled(im[k], math.sin(ang)))
            ec, oc, es, os = groups
            data[a, rows, :] = add(add(ec, oc), add(es, os)).astype(BF16)
            if 0 < a < 4:
                data[8 - a, rows, :] = sub(sub(add(ec, os), oc), es).astype(BF16)
    for r, out in enumerate(outs):
        base = 2 * around(z, r)
        out[pl.ds(0, 128), :] = data[base + x]
        out[pl.ds(128, 128), :] = data[base + 1 - x]


def gate_kernel(e0, e1, e2, e3, direct, g0, g1, g2, g3, gated, conv):
    _, _, z, _ = place()
    for r, block in enumerate((e0, e1, e2, e3)):
        conv[around(z, -r)] = block[...]
    low = low_lanes((256, 128))
    for j in range(2):
        lanes = pl.ds(j * 128, 128)
        even, odd = conv[2 * j].astype(F32), conv[2 * j + 1].astype(F32)
        parts = (jnp.where(low, even, half_turn(odd)), jnp.where(low, half_turn(even), odd))
        for p, gate in enumerate((g0, g1, g2, g3)):
            rows = pl.ds(p * 128, 128)
            own = parts[p // 2][(p % 2) * 128 : (p % 2) * 128 + 128]
            y, x, _, _ = place()
            base = y * 512 + x * 256 if p == 0 else 256
            query = gate[:, pl.ds(pl.multiple_of(base + j * 128, 128), 128)].astype(F32)
            gated[rows, lanes] = (query * (own + direct[rows, lanes])).astype(BF16)


def sort_weight(*refs):
    pieces, keep, give = refs[:7], refs[7], refs[8]
    _, x, z, c = place()
    for r in range(4):
        owner = around(z, -r)
        for k in range(2):
            to = 2 * lax.rem(owner, 2) + (1 - x if k else x)

            @pl.when(owner // 2 == c)
            def _():
                keep[to] = (pieces[2 * r + k][...] if r < 3 else pieces[6][k])

            @pl.when(owner // 2 != c)
            def _():
                give[to] = (pieces[2 * r + k][...] if r < 3 else pieces[6][k])


def out_kernel(blocks, gated, other, keep, theirs, *outs):
    for p, out in zip(blocks, outs):
        rows = pl.ds(p * 128, 128)
        for i in range(4):
            total = dot_t(gated[rows, :], keep[i]) + dot_t(other[rows, :], theirs[i])
            out[:, pl.ds(i * 256, 256)] = total.astype(out.dtype)


def tables():
    k = np.arange(16)[:, None, None] + 16 * np.arange(128)[None, :, None]
    phase = 2 * np.pi / 2048 * (k * np.arange(128)[None, None, :] % 2048)
    co, si = np.cos(phase), np.sin(phase)
    back = np.concatenate([co.transpose(0, 2, 1), si.transpose(0, 2, 1)], 1)
    return np.concatenate([co, si], 1).astype(jnp.bfloat16), back.astype(jnp.bfloat16)


def planes(tokens, gate_q, gate_k, w_value, skip, filter_spectrum, w_out):
    seq, deep = 8, 4

    def permute(values, move):
        pairs = []
        for g in range(2):
            for i in range(seq):
                for k in range(2):
                    g2, z2, x2, k2 = move(g, i // 2, i % 2, k)
                    pairs.append(((g * seq + i) * 2 + k, (g2 * seq + z2 * 2 + x2) * 2 + k2))
        return lax.ppermute(values, AXES, pairs)

    def to_x(values):
        return permute(values, lambda g, z, x, k: (g, z, 1 - x, k))

    def to_core(values):
        return permute(values, lambda g, z, x, k: (g, z, x, 1 - k))

    def to_z(values, r):
        ring = (0, 1, 3, 2)
        at = [ring.index(z) for z in range(deep)]
        return permute(values, lambda g, z, x, k: (g, ring[(at[z] + r) % deep], x, k))

    def onward(values):
        return to_z(values, 1)

    def to_peer(values, p):
        return permute(values, lambda g, z, x, k: (g ^ (p // 2), z, x ^ (p % 2), k))

    def after(values, *done):
        return lax.optimization_barrier((values,) + done)[0]

    shape = jax.ShapeDtypeStruct
    block, square = shape((256, 128), BF16), shape((256, 256), BF16)
    own_v = lax.dynamic_slice_in_dim(w_value, lax.axis_index("grp") * 512, 512, axis=1)
    laid = [shape((128, 1024), BF16)] * 3 + [square] * 2 + [shape((2, 2, 128, 256), BF16)]
    *messages, own_o, away_o, away_f = copy_kernel(cut_messages, laid)(
        tokens, gate_k, gate_q, w_out, filter_spectrum, own_v
    )
    near = to_x(away_f)
    received = [to_peer(messages[p - 1], p) for p in (1, 2, 3)]
    filters = in_vmem(
        pack_filter,
        [shape((2, 2, 128, 128), BF16)] * 4,
        [pltpu.VMEM((4, 2, 2, 128, 128), BF16)],
        moved=1 << 20,
    )(filter_spectrum, near)
    filters = [filters[0]] + [to_z(filters[r], r) for r in (1, 2, 3)]
    v1 = onward(own_v)
    q1 = onward(own_o)
    v2 = onward(v1)
    q2 = onward(after(q1, v1))
    mine = in_vmem(join_tokens, shape((512, 512), BF16), moved=1 << 20)(tokens, after(received[0], q2), *received[1:])
    v3 = onward(v2)
    other = to_core(mine)
    got_o = to_x(after(away_o, v1))
    r1 = onward(after(got_o, v2))
    keep, give = in_vmem(
        value_kernel,
        [shape((512, 256), F32), shape((512, 256), BF16)],
        [pltpu.VMEM((512, 512), F32)],
        flops=1 << 29,
        moved=2 << 20,
    )(after(mine, r1, filters[0]), other, own_v, v1, v2, v3)
    r2 = onward(after(r1, keep))
    drive, *sends = in_vmem(
        drive_kernel,
        [shape((512, 256), F32)] + [block] * 4,
        [pltpu.VMEM((512, 256), BF16), pltpu.VMEM((4, 256, 128), BF16)],
        moved=2 << 20,
    )(keep, to_x(give), gate_k, *received, skip[None, :])
    columns = [sends[0]] + [to_z(sends[r], r) for r in (1, 2, 3)]
    last = onward(after(jnp.stack([q2, r2]), filters[3], *columns[1:]))
    table, table_t = tables()
    sends = in_vmem(
        conv_kernel,
        [block] * 4,
        [
            pltpu.VMEM((8, 128, 128), BF16),
            pltpu.VMEM((8, 2, 128, 128), BF16),
            pltpu.VMEM((16, 128, 256), BF16),
            pltpu.VMEM((9, 256, 128), F32),
        ],
        flops=1 << 30,
        moved=5 << 20,
    )(*columns, *filters, table, table_t)
    rows = [sends[0]] + [to_z(sends[r], r) for r in (1, 2, 3)]

    hops = [own_o, got_o, q1, r1, q2, r2, after(last, *rows[1:])]
    quad = shape((4, 256, 256), BF16)
    keep, give = in_vmem(sort_weight, [quad] * 2, moved=2 << 20)(*hops)
    theirs = to_core(give)
    gated = in_vmem(
        gate_kernel, shape((512, 256), BF16), [pltpu.VMEM((4, 256, 128), BF16)], moved=1 << 20
    )(*rows, drive, gate_q, *received)
    gated_other = to_core(gated)
    summed = (gated, gated_other, keep, theirs)
    send = shape((128, 1024), BF16)
    far = in_vmem(functools.partial(out_kernel, (3, 1)), [send] * 2, flops=1 << 29, moved=2 << 20)
    close = in_vmem(
        functools.partial(out_kernel, (2, 0)),
        [send, shape((128, 1024), F32)],
        flops=1 << 29,
        moved=2 << 20,
    )
    to_xy, to_row = far(*summed)
    parts = [to_peer(to_xy, 3), to_peer(to_row, 1)]
    to_column, total = close(*summed)
    parts.append(to_peer(to_column, 2))
    for part in parts:
        total = total + part.astype(F32)
    return total.astype(BF16)


def shards(tokens, gate_q, gate_k, w_value, skip, filter_spectrum, w_out):
    seq_count = lax.axis_size("seq")
    position = lax.axis_index("seq")
    length_b = tokens.shape[0]
    columns_each = length_b // seq_count
    freq_rows = 2 * seq_count
    freqs_each = freq_rows // seq_count
    fft_length = freq_rows * length_b
    features = lax.all_gather(tokens, "ch", axis=1, tiled=True)
    value_weight, out_weight = (
        lax.all_gather(w_value, "seq", axis=0, tiled=True),
        lax.all_gather(w_out, "seq", axis=0, tiled=True),
    )
    value = jnp.dot(features, value_weight, preferred_element_type=jnp.float32)
    value = value.astype(jnp.bfloat16)
    drive = (gate_k.astype(jnp.float32) * widened(value)).astype(jnp.bfloat16)
    channels = drive.shape[1]
    columns = lax.all_to_all(drive[None], "seq", split_axis=1, concat_axis=0, tiled=True)
    index_rows = jnp.arange(freq_rows, dtype=jnp.int32)
    index_seq = jnp.arange(seq_count, dtype=jnp.int32)
    index_b = jnp.arange(length_b, dtype=jnp.int32)
    cos_first, sin_first = angles(freq_rows, index_rows, index_seq)
    cos_first = cos_first.astype(jnp.bfloat16)
    sin_first = sin_first.astype(jnp.bfloat16)
    flattened = columns.reshape(seq_count, columns_each * channels)
    real_part = jnp.dot(cos_first, flattened, preferred_element_type=jnp.float32)
    imag_part = jnp.dot(-sin_first, flattened, preferred_element_type=jnp.float32)
    real_part = real_part.reshape(freq_rows, columns_each, channels)
    imag_part = imag_part.reshape(freq_rows, columns_each, channels)
    mine_b = position * columns_each + jnp.arange(columns_each, dtype=jnp.int32)
    twist_cos, twist_sin = angles(fft_length, index_rows, mine_b)
    twist_cos = twist_cos[:, :, None]
    twist_sin = twist_sin[:, :, None]
    section = jnp.stack(
        [
            real_part * twist_cos + imag_part * twist_sin,
            imag_part * twist_cos - real_part * twist_sin,
        ]
    ).astype(jnp.bfloat16)
    spectral = lax.all_to_all(section, "seq", split_axis=1, concat_axis=2, tiled=True)
    cos_seq, sin_seq = angles(length_b, index_b, index_b)
    cos_seq = cos_seq.astype(jnp.bfloat16)
    sin_seq = sin_seq.astype(jnp.bfloat16)
    spectrum_real = jnp.einsum(
        "qb,kbc->kqc", cos_seq, spectral[0], preferred_element_type=jnp.float32
    ) + jnp.einsum("qb,kbc->kqc", sin_seq, spectral[1], preferred_element_type=jnp.float32)
    spectrum_imag = jnp.einsum(
        "qb,kbc->kqc", cos_seq, spectral[1], preferred_element_type=jnp.float32
    ) - jnp.einsum("qb,kbc->kqc", sin_seq, spectral[0], preferred_element_type=jnp.float32)
    filter_real = filter_spectrum[0].astype(jnp.float32)
    filter_imag = filter_spectrum[1].astype(jnp.float32)
    product = jnp.stack(
        [
            spectrum_real * filter_real - spectrum_imag * filter_imag,
            spectrum_real * filter_imag + spectrum_imag * filter_real,
        ]
    ).astype(jnp.bfloat16)
    inverse_real = jnp.einsum(
        "qb,kqc->kbc", cos_seq, product[0], preferred_element_type=jnp.float32
    ) - jnp.einsum("qb,kqc->kbc", sin_seq, product[1], preferred_element_type=jnp.float32)
    inverse_imag = jnp.einsum(
        "qb,kqc->kbc", sin_seq, product[0], preferred_element_type=jnp.float32
    ) + jnp.einsum("qb,kqc->kbc", cos_seq, product[1], preferred_element_type=jnp.float32)
    mine_k = position * freqs_each + jnp.arange(freqs_each, dtype=jnp.int32)
    back_cos, back_sin = angles(fft_length, mine_k, index_b)
    back_cos = back_cos[:, :, None]
    back_sin = back_sin[:, :, None]
    back = jnp.stack(
        [
            inverse_real * back_cos - inverse_imag * back_sin,
            inverse_real * back_sin + inverse_imag * back_cos,
        ]
    ).astype(jnp.bfloat16)
    returned = lax.all_to_all(back, "seq", split_axis=2, concat_axis=1, tiled=True)
    flat_real = returned[0].reshape(freq_rows, columns_each * channels)
    flat_imag = returned[1].reshape(freq_rows, columns_each * channels)
    conv = jnp.dot(cos_first.T, flat_real, preferred_element_type=jnp.float32) - jnp.dot(
        sin_first.T, flat_imag, preferred_element_type=jnp.float32
    )
    conv = (
        (conv * (1.0 / fft_length)).reshape(seq_count, columns_each, channels).astype(jnp.bfloat16)
    )
    conv_rows = lax.all_to_all(conv, "seq", split_axis=0, concat_axis=1, tiled=True)[0]
    gated = (
        gate_q.astype(jnp.float32) * (widened(conv_rows) + skip[None, :] * widened(drive))
    ).astype(jnp.bfloat16)
    partial_value = lax.dot_general(
        gated, out_weight, (((1,), (1,)), ((), ())), preferred_element_type=jnp.float32
    )
    return lax.psum_scatter(
        partial_value.astype(jnp.bfloat16), "ch", scatter_dimension=1, tiled=True
    )


def solution(mesh):
    placed = (
        P(("grp", "seq"), "ch"),
        P(("grp", "seq"), "ch"),
        P(("grp", "seq"), "ch"),
        P("seq", "ch"),
        P("ch"),
        P(None, "seq", None, "ch"),
        P("seq", "ch"),
    )
    sizes = mesh.shape
    body = planes if (sizes["grp"], sizes["seq"], sizes["ch"]) == (2, 8, 2) else shards
    return jax.shard_map(
        body, mesh=mesh, in_specs=placed, out_specs=P(("grp", "seq"), "ch"), check_vma=False
    )
```

```python
import functools
import math

import jax
import jax.numpy as jnp
import numpy as np
from jax import lax
from jax.experimental import pallas as pl
from jax.experimental.pallas import tpu as pltpu
from jax.sharding import PartitionSpec as P

AXES = ("grp", "seq", "ch")
BF16 = jnp.bfloat16
F32 = jnp.float32


def angles(count, first, second):
    phase = 2.0 * math.pi / count * (first[:, None] * second[None, :] % count).astype(jnp.float32)
    return (jnp.cos(phase), jnp.sin(phase))


def widened(values):
    return lax.optimization_barrier(values).astype(jnp.float32)


def dot(a, b):
    return jnp.dot(a, b, preferred_element_type=F32)


def dot_t(a, b):
    return lax.dot_general(a, b, (((1,), (1,)), ((), ())), preferred_element_type=F32)


def in_vmem(kernel, out_shape, scratch=(), flops=0, moved=0):
    def call(*operands):
        specs = [pl.BlockSpec(memory_space=pltpu.VMEM)] * len(operands)
        return pl.pallas_call(
            kernel,
            out_shape=out_shape,
            in_specs=specs,
            out_specs=jax.tree.map(lambda _: pl.BlockSpec(memory_space=pltpu.VMEM), out_shape),
            scratch_shapes=list(scratch),
            compiler_params=pltpu.CompilerParams(vmem_limit_bytes=20 * 1024 * 1024),
            cost_estimate=pl.CostEstimate(flops=flops, bytes_accessed=moved, transcendentals=0),
        )(*operands)

    return call


def place():
    y, s, c = (lax.axis_index(a) for a in AXES)
    return y, lax.rem(s, 2), lax.div(s, 2), c


def around(z, r):
    at = lax.rem((z ^ lax.div(z, 2)) + r + 4, 4)
    return at ^ lax.div(at, 2)


def low_lanes(shape):
    return lax.broadcasted_iota(jnp.int32, shape, len(shape) - 1) < 64


def half_turn(values):
    return pltpu.roll(values, 64, values.ndim - 1)


def both(first, second, low):
    return (
        jnp.where(low, first, half_turn(second)).astype(BF16),
        jnp.where(low, half_turn(first), second).astype(BF16),
    )


def quarter(p):
    y, x, _, _ = place()
    row = 1 - y if p // 2 else y
    column = 1 - x if p % 2 else x
    return pl.ds(pl.multiple_of(row * 512 + column * 256, 256), 256)


def copied(moves, sem):
    copies = [pltpu.make_async_copy(a, b, sem.at[i]) for i, (a, b) in enumerate(moves)]
    for copy in copies:
        copy.start()
    for copy in copies:
        copy.wait()


def cut_messages(tokens, key, query, out, filt, after, m1, m2, m3, own_o, away_o, away_f, sem):
    _, x, _, _ = place()
    moves = [(filt.at[:, :, :, quarter(1)], away_f)]
    for p, message in enumerate((m1, m2, m3), 1):
        column = 1 - x if p % 2 else x
        for i in range(2):
            lanes = pl.ds(pl.multiple_of(i * 512 + column * 256, 256), 256)
            moves.append((tokens.at[:, lanes], message.at[:, pl.ds(512 + i * 256, 256)]))
        moves.append((key.at[:, quarter(p)], message.at[:, pl.ds(0, 256)]))
        moves.append((query.at[:, quarter(p)], message.at[:, pl.ds(256, 256)]))
    moves += [(out.at[:, quarter(0)], own_o), (out.at[:, quarter(1)], away_o)]
    copied(moves, sem)


def copy_kernel(kernel, out_shape):
    def call(*operands):
        return pl.pallas_call(
            kernel,
            out_shape=out_shape,
            in_specs=[pl.BlockSpec(memory_space=pltpu.MemorySpace.HBM)] * len(operands),
            out_specs=[pl.BlockSpec(memory_space=pltpu.VMEM)] * len(out_shape),
            scratch_shapes=[pltpu.SemaphoreType.DMA((19,))],
            compiler_params=pltpu.CompilerParams(vmem_limit_bytes=61 * 1024 * 1024),
        )(*operands)

    return call


def pack_filter(filt, near, *refs):
    y, x, z, _ = place()
    packed, outs = refs[4], refs[:4]
    low = low_lanes((128, 128))
    for k in range(2):
        for j in range(2):
            base = pl.multiple_of(y * 512 + x * 256 + j * 128, 128)
            for part in range(2):
                if k:
                    pair = [near[part, i, :, pl.ds(j * 128, 128)].astype(F32) for i in range(2)]
                else:
                    pair = [filt[part, i, :, pl.ds(base, 128)].astype(F32) for i in range(2)]
                one, two = both(*pair, low)
                packed[2 * j, k, part] = one
                packed[2 * j + 1, k, part] = two
    for r in range(4):
        outs[r][...] = packed[around(z, r)]


def join_tokens(*refs):
    _, x, _, _ = place()
    for i in range(2):
        lanes = pl.ds(pl.multiple_of(i * 512 + x * 256, 256), 256)
        refs[4][pl.ds(0, 128), pl.ds(i * 256, 256)] = refs[0][:, lanes]
    for p in (1, 2, 3):
        refs[4][pl.ds(p * 128, 128), :] = refs[p][:, pl.ds(512, 512)]


def value_kernel(mine, other, w0, w1, w2, w3, keep, give, acc):
    _, x, z, c = place()
    for r, piece in enumerate((w0, w1, w2, w3)):
        owner = around(z, -r)
        lanes = pl.ds(pl.multiple_of(lax.rem(owner, 2) * 256, 256), 256)

        @pl.when(lax.div(owner, 2) == c)
        def _():
            term = dot(mine[:, lanes], piece[...])
            acc[...] = acc[...] + term if r else term

        @pl.when(lax.div(owner, 2) != c)
        def _():
            term = dot(other[:, lanes], piece[...])
            acc[...] = acc[...] + term if r else term

    keep[...] = acc[:, pl.ds(pl.multiple_of(x * 256, 256), 256)]
    away = pl.ds(pl.multiple_of(256 - x * 256, 256), 256)
    for p in range(4):
        give[pl.ds(p * 128, 128), :] = acc[pl.ds((p ^ 1) * 128, 128), away].astype(BF16)


def drive_kernel(keep, taken, g0, g1, g2, g3, skip, direct, o0, o1, o2, o3, drive, packed):
    _, _, z, _ = place()
    for p, gate in enumerate((g0, g1, g2, g3)):
        rows = pl.ds(p * 128, 128)
        value = (keep[rows, :] + taken[rows, :].astype(F32)).astype(BF16).astype(F32)
        held = ((gate[:, 0:256] if p else gate[:, quarter(0)]).astype(F32) * value).astype(BF16)
        drive[rows, :] = held
        direct[rows, :] = skip[:, quarter(0)] * held.astype(F32)
    low = low_lanes((256, 128))
    for j in range(2):
        lanes = pl.ds(j * 128, 128)
        first = drive[pl.ds(0, 256), lanes].astype(F32)
        second = drive[pl.ds(256, 256), lanes].astype(F32)
        packed[2 * j], packed[2 * j + 1] = both(first, second, low)
    for r, out in enumerate((o0, o1, o2, o3)):
        out[...] = packed[around(z, r)]


def add(a, b):
    return b if a is None else a if b is None else a + b


def sub(a, b):
    return a if b is None else -b if a is None else a - b


def scaled(a, s):
    if a is None or abs(s) < 1e-9:
        return None
    if abs(s - 1) < 1e-9:
        return a
    if abs(s + 1) < 1e-9:
        return -a
    return a * np.float32(s)


def cmul(a, angle):
    co, si = math.cos(angle), math.sin(angle)
    return (sub(scaled(a[0], co), scaled(a[1], si)), add(scaled(a[0], si), scaled(a[1], co)))


def cadd(a, b):
    return (add(a[0], b[0]), add(a[1], b[1]))


def conj(a):
    return (a[0], None if a[1] is None else -a[1])


def short_transform(values, count, rows):
    if len(values) == 1:
        return [(values[0], None)] * rows
    half = count // 2
    need = half // 2 + 1
    even = short_transform(values[0::2], half, need)
    odd = short_transform(values[1::2], half, need)

    def at(t, k):
        k %= half
        return t[k] if k < need else conj(t[half - k])

    return [cadd(at(even, k), cmul(at(odd, k), -2 * math.pi * k / count)) for k in range(rows)]


def conv_kernel(*refs):
    drives, filters, (table, table_t) = refs[:4], refs[4:8], refs[8:10]
    outs, (data, filt, first, sums) = refs[10:14], refs[14:]
    _, x, z, _ = place()
    for r, block in enumerate(drives):
        base = 2 * around(z, -r)
        filt[base + x] = filters[r][0]
        filt[base + 1 - x] = filters[r][1]
        data[base + x] = block[pl.ds(0, 128), :]
        data[base + 1 - x] = block[pl.ds(128, 128), :]
    for i in range(8):
        rows = pl.ds(16 * i, 16)
        values = [data[a, rows, :].astype(F32) for a in range(8)]
        spectrum = short_transform(values, 16, 9)
        for k in range(9):
            re, im = spectrum[k]
            if im is None:
                im = jnp.zeros_like(re)
            first[k, rows, 0:128] = re.astype(BF16)
            first[k, rows, 128:256] = im.astype(BF16)
            if 0 < k < 8:
                first[16 - k, rows, 0:128] = re.astype(BF16)
                first[16 - k, rows, 128:256] = (-im).astype(BF16)
    low = low_lanes((128, 128))

    def back(k):
        four = dot(table[k], first[k])
        re = four[:128, :128] + four[128:, 128:]
        im = four[:128, 128:] - four[128:, :128]
        pair = [filt[k // 2, part].astype(F32) for part in range(2)]
        if k % 2 == 0:
            fr, fi = [jnp.where(low, f, half_turn(f)) for f in pair]
        else:
            fr, fi = [jnp.where(low, half_turn(f), f) for f in pair]
        product = jnp.concatenate([re * fr - im * fi, re * fi + im * fr], axis=1).astype(BF16)
        four = dot(table_t[k], product)
        return four[:128, :128] - four[128:, 128:], four[128:, :128] + four[:128, 128:]

    sums[0, pl.ds(0, 128)] = back(0)[0]
    sums[8, pl.ds(0, 128)] = back(8)[0]
    for k in range(1, 8):
        one, two = back(k), back(16 - k)
        sums[k, pl.ds(0, 128)] = one[0] + two[0]
        sums[k, pl.ds(128, 128)] = one[1] - two[1]
    for i in range(16):
        rows, below = pl.ds(8 * i, 8), pl.ds(128 + 8 * i, 8)
        scale = 1.0 / 2048
        re = [sums[k, rows, :] * scale for k in range(9)]
        im = [None] + [sums[k, below, :] * scale for k in range(1, 8)] + [None]
        for a in range(5):
            groups = [None] * 4
            for k in range(9):
                ang = 2 * math.pi * (k * a % 16) / 16
                groups[k % 2] = add(groups[k % 2], scaled(re[k], math.cos(ang)))
                groups[2 + k % 2] = sub(groups[2 + k % 2], scaled(im[k], math.sin(ang)))
            ec, oc, es, os = groups
            data[a, rows, :] = add(add(ec, oc), add(es, os)).astype(BF16)
            if 0 < a < 4:
                data[8 - a, rows, :] = sub(sub(add(ec, os), oc), es).astype(BF16)
    for r, out in enumerate(outs):
        base = 2 * around(z, r)
        out[pl.ds(0, 128), :] = data[base + x]
        out[pl.ds(128, 128), :] = data[base + 1 - x]


def gate_kernel(e0, e1, e2, e3, direct, g0, g1, g2, g3, gated, conv):
    _, _, z, _ = place()
    for r, block in enumerate((e0, e1, e2, e3)):
        conv[around(z, -r)] = block[...]
    low = low_lanes((256, 128))
    for j in range(2):
        lanes = pl.ds(j * 128, 128)
        even, odd = conv[2 * j].astype(F32), conv[2 * j + 1].astype(F32)
        parts = (jnp.where(low, even, half_turn(odd)), jnp.where(low, half_turn(even), odd))
        for p, gate in enumerate((g0, g1, g2, g3)):
            rows = pl.ds(p * 128, 128)
            own = parts[p // 2][(p % 2) * 128 : (p % 2) * 128 + 128]
            y, x, _, _ = place()
            base = y * 512 + x * 256 if p == 0 else 256
            query = gate[:, pl.ds(pl.multiple_of(base + j * 128, 128), 128)].astype(F32)
            gated[rows, lanes] = (query * (own + direct[rows, lanes])).astype(BF16)


def sort_weight(*refs):
    pieces, keep, give = refs[:7], refs[7], refs[8]
    _, x, z, c = place()
    for r in range(4):
        owner = around(z, -r)
        for k in range(2):
            to = 2 * lax.rem(owner, 2) + (1 - x if k else x)

            @pl.when(owner // 2 == c)
            def _():
                keep[to] = (pieces[2 * r + k][...] if r < 3 else pieces[6][k])

            @pl.when(owner // 2 != c)
            def _():
                give[to] = (pieces[2 * r + k][...] if r < 3 else pieces[6][k])


def out_kernel(blocks, gated, other, keep, theirs, *outs):
    for p, out in zip(blocks, outs):
        rows = pl.ds(p * 128, 128)
        for i in range(4):
            total = dot_t(gated[rows, :], keep[i]) + dot_t(other[rows, :], theirs[i])
            out[:, pl.ds(i * 256, 256)] = total.astype(out.dtype)


def tables():
    k = np.arange(16)[:, None, None] + 16 * np.arange(128)[None, :, None]
    phase = 2 * np.pi / 2048 * (k * np.arange(128)[None, None, :] % 2048)
    co, si = np.cos(phase), np.sin(phase)
    back = np.concatenate([co.transpose(0, 2, 1), si.transpose(0, 2, 1)], 1)
    return np.concatenate([co, si], 1).astype(jnp.bfloat16), back.astype(jnp.bfloat16)


def planes(tokens, gate_q, gate_k, w_value, skip, filter_spectrum, w_out):
    seq, deep = 8, 4

    def permute(values, move):
        pairs = []
        for g in range(2):
            for i in range(seq):
                for k in range(2):
                    g2, z2, x2, k2 = move(g, i // 2, i % 2, k)
                    pairs.append(((g * seq + i) * 2 + k, (g2 * seq + z2 * 2 + x2) * 2 + k2))
        return lax.ppermute(values, AXES, pairs)

    def to_x(values):
        return permute(values, lambda g, z, x, k: (g, z, 1 - x, k))

    def to_core(values):
        return permute(values, lambda g, z, x, k: (g, z, x, 1 - k))

    def to_z(values, r):
        ring = (0, 1, 3, 2)
        at = [ring.index(z) for z in range(deep)]
        return permute(values, lambda g, z, x, k: (g, ring[(at[z] + r) % deep], x, k))

    def onward(values):
        return to_z(values, 1)

    def to_peer(values, p):
        return permute(values, lambda g, z, x, k: (g ^ (p // 2), z, x ^ (p % 2), k))

    def after(values, *done):
        return lax.optimization_barrier((values,) + done)[0]

    shape = jax.ShapeDtypeStruct
    block, square = shape((256, 128), BF16), shape((256, 256), BF16)
    own_v = lax.dynamic_slice_in_dim(w_value, lax.axis_index("grp") * 512, 512, axis=1)
    laid = [shape((128, 1024), BF16)] * 3 + [square] * 2 + [shape((2, 2, 128, 256), BF16)]
    *messages, own_o, away_o, away_f = copy_kernel(cut_messages, laid)(
        tokens, gate_k, gate_q, w_out, filter_spectrum, own_v
    )
    near = to_x(away_f)
    received = [to_peer(messages[p - 1], p) for p in (1, 2, 3)]
    filters = in_vmem(
        pack_filter,
        [shape((2, 2, 128, 128), BF16)] * 4,
        [pltpu.VMEM((4, 2, 2, 128, 128), BF16)],
        moved=1 << 20,
    )(filter_spectrum, near)
    filters = [filters[0]] + [to_z(filters[r], r) for r in (1, 2, 3)]
    v1 = onward(own_v)
    q1 = onward(own_o)
    v2 = onward(v1)
    q2 = onward(after(q1, v1))
    mine = in_vmem(join_tokens, shape((512, 512), BF16), moved=1 << 20)(tokens, after(received[0], q2), *received[1:])
    v3 = onward(v2)
    other = to_core(mine)
    got_o = to_x(after(away_o, v1))
    r1 = onward(after(got_o, v2))
    keep, give = in_vmem(
        value_kernel,
        [shape((512, 256), F32), shape((512, 256), BF16)],
        [pltpu.VMEM((512, 512), F32)],
        flops=1 << 29,
        moved=2 << 20,
    )(after(mine, filters[0], got_o), other, own_v, v1, v2, v3)
    r2 = onward(after(r1, keep))
    drive, *sends = in_vmem(
        drive_kernel,
        [shape((512, 256), F32)] + [block] * 4,
        [pltpu.VMEM((512, 256), BF16), pltpu.VMEM((4, 256, 128), BF16)],
        moved=2 << 20,
    )(keep, to_x(give), gate_k, *received, skip[None, :])
    columns = [sends[0]] + [to_z(sends[r], r) for r in (1, 2, 3)]
    last = onward(after(jnp.stack([q2, r2]), filters[3], *columns[1:]))
    table, table_t = tables()
    sends = in_vmem(
        conv_kernel,
        [block] * 4,
        [
            pltpu.VMEM((8, 128, 128), BF16),
            pltpu.VMEM((8, 2, 128, 128), BF16),
            pltpu.VMEM((16, 128, 256), BF16),
            pltpu.VMEM((9, 256, 128), F32),
        ],
        flops=1 << 30,
        moved=5 << 20,
    )(*columns, *filters, table, table_t)
    rows = [sends[0]] + [to_z(sends[r], r) for r in (1, 2, 3)]

    hops = [own_o, got_o, q1, r1, q2, r2, after(last, *rows[1:])]
    quad = shape((4, 256, 256), BF16)
    keep, give = in_vmem(sort_weight, [quad] * 2, moved=2 << 20)(*hops)
    theirs = to_core(give)
    gated = in_vmem(
        gate_kernel, shape((512, 256), BF16), [pltpu.VMEM((4, 256, 128), BF16)], moved=1 << 20
    )(*rows, drive, gate_q, *received)
    gated_other = to_core(gated)
    summed = (gated, gated_other, keep, theirs)
    send = shape((128, 1024), BF16)
    far = in_vmem(functools.partial(out_kernel, (3, 1)), [send] * 2, flops=1 << 29, moved=2 << 20)
    close = in_vmem(
        functools.partial(out_kernel, (2, 0)),
        [send, shape((128, 1024), F32)],
        flops=1 << 29,
        moved=2 << 20,
    )
    to_xy, to_row = far(*summed)
    parts = [to_peer(to_xy, 3), to_peer(to_row, 1)]
    to_column, total = close(*summed)
    parts.append(to_peer(to_column, 2))
    for part in parts:
        total = total + part.astype(F32)
    return total.astype(BF16)


def shards(tokens, gate_q, gate_k, w_value, skip, filter_spectrum, w_out):
    seq_count = lax.axis_size("seq")
    position = lax.axis_index("seq")
    length_b = tokens.shape[0]
    columns_each = length_b // seq_count
    freq_rows = 2 * seq_count
    freqs_each = freq_rows // seq_count
    fft_length = freq_rows * length_b
    features = lax.all_gather(tokens, "ch", axis=1, tiled=True)
    value_weight, out_weight = (
        lax.all_gather(w_value, "seq", axis=0, tiled=True),
        lax.all_gather(w_out, "seq", axis=0, tiled=True),
    )
    value = jnp.dot(features, value_weight, preferred_element_type=jnp.float32)
    value = value.astype(jnp.bfloat16)
    drive = (gate_k.astype(jnp.float32) * widened(value)).astype(jnp.bfloat16)
    channels = drive.shape[1]
    columns = lax.all_to_all(drive[None], "seq", split_axis=1, concat_axis=0, tiled=True)
    index_rows = jnp.arange(freq_rows, dtype=jnp.int32)
    index_seq = jnp.arange(seq_count, dtype=jnp.int32)
    index_b = jnp.arange(length_b, dtype=jnp.int32)
    cos_first, sin_first = angles(freq_rows, index_rows, index_seq)
    cos_first = cos_first.astype(jnp.bfloat16)
    sin_first = sin_first.astype(jnp.bfloat16)
    flattened = columns.reshape(seq_count, columns_each * channels)
    real_part = jnp.dot(cos_first, flattened, preferred_element_type=jnp.float32)
    imag_part = jnp.dot(-sin_first, flattened, preferred_element_type=jnp.float32)
    real_part = real_part.reshape(freq_rows, columns_each, channels)
    imag_part = imag_part.reshape(freq_rows, columns_each, channels)
    mine_b = position * columns_each + jnp.arange(columns_each, dtype=jnp.int32)
    twist_cos, twist_sin = angles(fft_length, index_rows, mine_b)
    twist_cos = twist_cos[:, :, None]
    twist_sin = twist_sin[:, :, None]
    section = jnp.stack(
        [
            real_part * twist_cos + imag_part * twist_sin,
            imag_part * twist_cos - real_part * twist_sin,
        ]
    ).astype(jnp.bfloat16)
    spectral = lax.all_to_all(section, "seq", split_axis=1, concat_axis=2, tiled=True)
    cos_seq, sin_seq = angles(length_b, index_b, index_b)
    cos_seq = cos_seq.astype(jnp.bfloat16)
    sin_seq = sin_seq.astype(jnp.bfloat16)
    spectrum_real = jnp.einsum(
        "qb,kbc->kqc", cos_seq, spectral[0], preferred_element_type=jnp.float32
    ) + jnp.einsum("qb,kbc->kqc", sin_seq, spectral[1], preferred_element_type=jnp.float32)
    spectrum_imag = jnp.einsum(
        "qb,kbc->kqc", cos_seq, spectral[1], preferred_element_type=jnp.float32
    ) - jnp.einsum("qb,kbc->kqc", sin_seq, spectral[0], preferred_element_type=jnp.float32)
    filter_real = filter_spectrum[0].astype(jnp.float32)
    filter_imag = filter_spectrum[1].astype(jnp.float32)
    product = jnp.stack(
        [
            spectrum_real * filter_real - spectrum_imag * filter_imag,
            spectrum_real * filter_imag + spectrum_imag * filter_real,
        ]
    ).astype(jnp.bfloat16)
    inverse_real = jnp.einsum(
        "qb,kqc->kbc", cos_seq, product[0], preferred_element_type=jnp.float32
    ) - jnp.einsum("qb,kqc->kbc", sin_seq, product[1], preferred_element_type=jnp.float32)
    inverse_imag = jnp.einsum(
        "qb,kqc->kbc", sin_seq, product[0], preferred_element_type=jnp.float32
    ) + jnp.einsum("qb,kqc->kbc", cos_seq, product[1], preferred_element_type=jnp.float32)
    mine_k = position * freqs_each + jnp.arange(freqs_each, dtype=jnp.int32)
    back_cos, back_sin = angles(fft_length, mine_k, index_b)
    back_cos = back_cos[:, :, None]
    back_sin = back_sin[:, :, None]
    back = jnp.stack(
        [
            inverse_real * back_cos - inverse_imag * back_sin,
            inverse_real * back_sin + inverse_imag * back_cos,
        ]
    ).astype(jnp.bfloat16)
    returned = lax.all_to_all(back, "seq", split_axis=2, concat_axis=1, tiled=True)
    flat_real = returned[0].reshape(freq_rows, columns_each * channels)
    flat_imag = returned[1].reshape(freq_rows, columns_each * channels)
    conv = jnp.dot(cos_first.T, flat_real, preferred_element_type=jnp.float32) - jnp.dot(
        sin_first.T, flat_imag, preferred_element_type=jnp.float32
    )
    conv = (
        (conv * (1.0 / fft_length)).reshape(seq_count, columns_each, channels).astype(jnp.bfloat16)
    )
    conv_rows = lax.all_to_all(conv, "seq", split_axis=0, concat_axis=1, tiled=True)[0]
    gated = (
        gate_q.astype(jnp.float32) * (widened(conv_rows) + skip[None, :] * widened(drive))
    ).astype(jnp.bfloat16)
    partial_value = lax.dot_general(
        gated, out_weight, (((1,), (1,)), ((), ())), preferred_element_type=jnp.float32
    )
    return lax.psum_scatter(
        partial_value.astype(jnp.bfloat16), "ch", scatter_dimension=1, tiled=True
    )


def solution(mesh):
    placed = (
        P(("grp", "seq"), "ch"),
        P(("grp", "seq"), "ch"),
        P(("grp", "seq"), "ch"),
        P("seq", "ch"),
        P("ch"),
        P(None, "seq", None, "ch"),
        P("seq", "ch"),
    )
    sizes = mesh.shape
    body = planes if (sizes["grp"], sizes["seq"], sizes["ch"]) == (2, 8, 2) else shards
    return jax.shard_map(
        body, mesh=mesh, in_specs=placed, out_specs=P(("grp", "seq"), "ch"), check_vma=False
    )
```

```python
import functools
import math

import jax
import jax.numpy as jnp
import numpy as np
from jax import lax
from jax.experimental import pallas as pl
from jax.experimental.pallas import tpu as pltpu
from jax.sharding import PartitionSpec as P

AXES = ("grp", "seq", "ch")
BF16 = jnp.bfloat16
F32 = jnp.float32


def angles(count, first, second):
    phase = 2.0 * math.pi / count * (first[:, None] * second[None, :] % count).astype(jnp.float32)
    return (jnp.cos(phase), jnp.sin(phase))


def widened(values):
    return lax.optimization_barrier(values).astype(jnp.float32)


def dot(a, b):
    return jnp.dot(a, b, preferred_element_type=F32)


def dot_t(a, b):
    return lax.dot_general(a, b, (((1,), (1,)), ((), ())), preferred_element_type=F32)


def in_vmem(kernel, out_shape, scratch=(), flops=0, moved=0):
    def call(*operands):
        specs = [pl.BlockSpec(memory_space=pltpu.VMEM)] * len(operands)
        return pl.pallas_call(
            kernel,
            out_shape=out_shape,
            in_specs=specs,
            out_specs=jax.tree.map(lambda _: pl.BlockSpec(memory_space=pltpu.VMEM), out_shape),
            scratch_shapes=list(scratch),
            compiler_params=pltpu.CompilerParams(vmem_limit_bytes=20 * 1024 * 1024),
            cost_estimate=pl.CostEstimate(flops=flops, bytes_accessed=moved, transcendentals=0),
        )(*operands)

    return call


def place():
    y, s, c = (lax.axis_index(a) for a in AXES)
    return y, lax.rem(s, 2), lax.div(s, 2), c


def around(z, r):
    at = lax.rem((z ^ lax.div(z, 2)) + r + 4, 4)
    return at ^ lax.div(at, 2)


def low_lanes(shape):
    return lax.broadcasted_iota(jnp.int32, shape, len(shape) - 1) < 64


def half_turn(values):
    return pltpu.roll(values, 64, values.ndim - 1)


def both(first, second, low):
    return (
        jnp.where(low, first, half_turn(second)).astype(BF16),
        jnp.where(low, half_turn(first), second).astype(BF16),
    )


def quarter(p):
    y, x, _, _ = place()
    row = 1 - y if p // 2 else y
    column = 1 - x if p % 2 else x
    return pl.ds(pl.multiple_of(row * 512 + column * 256, 256), 256)


def copied(moves, sem):
    copies = [pltpu.make_async_copy(a, b, sem.at[i]) for i, (a, b) in enumerate(moves)]
    for copy in copies:
        copy.start()
    for copy in copies:
        copy.wait()


def cut_messages(tokens, key, query, out, filt, after, m1, m2, m3, own_o, away_o, away_f, sem):
    _, x, _, _ = place()
    moves = [(filt.at[:, :, :, quarter(1)], away_f)]
    for p, message in enumerate((m1, m2, m3), 1):
        column = 1 - x if p % 2 else x
        for i in range(2):
            lanes = pl.ds(pl.multiple_of(i * 512 + column * 256, 256), 256)
            moves.append((tokens.at[:, lanes], message.at[:, pl.ds(512 + i * 256, 256)]))
        moves.append((key.at[:, quarter(p)], message.at[:, pl.ds(0, 256)]))
        moves.append((query.at[:, quarter(p)], message.at[:, pl.ds(256, 256)]))
    moves += [(out.at[:, quarter(0)], own_o), (out.at[:, quarter(1)], away_o)]
    copied(moves, sem)


def copy_kernel(kernel, out_shape):
    def call(*operands):
        return pl.pallas_call(
            kernel,
            out_shape=out_shape,
            in_specs=[pl.BlockSpec(memory_space=pltpu.MemorySpace.HBM)] * len(operands),
            out_specs=[pl.BlockSpec(memory_space=pltpu.VMEM)] * len(out_shape),
            scratch_shapes=[pltpu.SemaphoreType.DMA((19,))],
            compiler_params=pltpu.CompilerParams(vmem_limit_bytes=61 * 1024 * 1024),
        )(*operands)

    return call


def pack_filter(filt, near, *refs):
    y, x, z, _ = place()
    packed, outs = refs[4], refs[:4]
    low = low_lanes((128, 128))
    for k in range(2):
        for j in range(2):
            base = pl.multiple_of(y * 512 + x * 256 + j * 128, 128)
            for part in range(2):
                if k:
                    pair = [near[part, i, :, pl.ds(j * 128, 128)].astype(F32) for i in range(2)]
                else:
                    pair = [filt[part, i, :, pl.ds(base, 128)].astype(F32) for i in range(2)]
                one, two = both(*pair, low)
                packed[2 * j, k, part] = one
                packed[2 * j + 1, k, part] = two
    for r in range(4):
        outs[r][...] = packed[around(z, r)]


def join_tokens(*refs):
    _, x, _, _ = place()
    for i in range(2):
        lanes = pl.ds(pl.multiple_of(i * 512 + x * 256, 256), 256)
        refs[4][pl.ds(0, 128), pl.ds(i * 256, 256)] = refs[0][:, lanes]
    for p in (1, 2, 3):
        refs[4][pl.ds(p * 128, 128), :] = refs[p][:, pl.ds(512, 512)]


def value_kernel(mine, other, w0, w1, w2, w3, keep, give, acc):
    _, x, z, c = place()
    for r, piece in enumerate((w0, w1, w2, w3)):
        owner = around(z, -r)
        lanes = pl.ds(pl.multiple_of(lax.rem(owner, 2) * 256, 256), 256)

        @pl.when(lax.div(owner, 2) == c)
        def _():
            term = dot(mine[:, lanes], piece[...])
            acc[...] = acc[...] + term if r else term

        @pl.when(lax.div(owner, 2) != c)
        def _():
            term = dot(other[:, lanes], piece[...])
            acc[...] = acc[...] + term if r else term

    keep[...] = acc[:, pl.ds(pl.multiple_of(x * 256, 256), 256)]
    away = pl.ds(pl.multiple_of(256 - x * 256, 256), 256)
    for p in range(4):
        give[pl.ds(p * 128, 128), :] = acc[pl.ds((p ^ 1) * 128, 128), away].astype(BF16)


def drive_kernel(keep, taken, g0, g1, g2, g3, skip, direct, o0, o1, o2, o3, drive, packed):
    _, _, z, _ = place()
    for p, gate in enumerate((g0, g1, g2, g3)):
        rows = pl.ds(p * 128, 128)
        value = (keep[rows, :] + taken[rows, :].astype(F32)).astype(BF16).astype(F32)
        held = ((gate[:, 0:256] if p else gate[:, quarter(0)]).astype(F32) * value).astype(BF16)
        drive[rows, :] = held
        direct[rows, :] = skip[:, quarter(0)] * held.astype(F32)
    low = low_lanes((256, 128))
    for j in range(2):
        lanes = pl.ds(j * 128, 128)
        first = drive[pl.ds(0, 256), lanes].astype(F32)
        second = drive[pl.ds(256, 256), lanes].astype(F32)
        packed[2 * j], packed[2 * j + 1] = both(first, second, low)
    for r, out in enumerate((o0, o1, o2, o3)):
        out[...] = packed[around(z, r)]


def add(a, b):
    return b if a is None else a if b is None else a + b


def sub(a, b):
    return a if b is None else -b if a is None else a - b


def scaled(a, s):
    if a is None or abs(s) < 1e-9:
        return None
    if abs(s - 1) < 1e-9:
        return a
    if abs(s + 1) < 1e-9:
        return -a
    return a * np.float32(s)


def cmul(a, angle):
    co, si = math.cos(angle), math.sin(angle)
    return (sub(scaled(a[0], co), scaled(a[1], si)), add(scaled(a[0], si), scaled(a[1], co)))


def cadd(a, b):
    return (add(a[0], b[0]), add(a[1], b[1]))


def conj(a):
    return (a[0], None if a[1] is None else -a[1])


def short_transform(values, count, rows):
    if len(values) == 1:
        return [(values[0], None)] * rows
    half = count // 2
    need = half // 2 + 1
    even = short_transform(values[0::2], half, need)
    odd = short_transform(values[1::2], half, need)

    def at(t, k):
        k %= half
        return t[k] if k < need else conj(t[half - k])

    return [cadd(at(even, k), cmul(at(odd, k), -2 * math.pi * k / count)) for k in range(rows)]


def conv_kernel(*refs):
    drives, filters, (table, table_t) = refs[:4], refs[4:8], refs[8:10]
    outs, (data, filt, first, sums) = refs[10:14], refs[14:]
    _, x, z, _ = place()
    for r, block in enumerate(drives):
        base = 2 * around(z, -r)
        filt[base + x] = filters[r][0]
        filt[base + 1 - x] = filters[r][1]
        data[base + x] = block[pl.ds(0, 128), :]
        data[base + 1 - x] = block[pl.ds(128, 128), :]
    for i in range(8):
        rows = pl.ds(16 * i, 16)
        values = [data[a, rows, :].astype(F32) for a in range(8)]
        spectrum = short_transform(values, 16, 9)
        for k in range(9):
            re, im = spectrum[k]
            if im is None:
                im = jnp.zeros_like(re)
            first[k, rows, 0:128] = re.astype(BF16)
            first[k, rows, 128:256] = im.astype(BF16)
            if 0 < k < 8:
                first[16 - k, rows, 0:128] = re.astype(BF16)
                first[16 - k, rows, 128:256] = (-im).astype(BF16)
    low = low_lanes((128, 128))

    def back(k):
        four = dot(table[k], first[k])
        re = four[:128, :128] + four[128:, 128:]
        im = four[:128, 128:] - four[128:, :128]
        pair = [filt[k // 2, part].astype(F32) for part in range(2)]
        if k % 2 == 0:
            fr, fi = [jnp.where(low, f, half_turn(f)) for f in pair]
        else:
            fr, fi = [jnp.where(low, half_turn(f), f) for f in pair]
        product = jnp.concatenate([re * fr - im * fi, re * fi + im * fr], axis=1).astype(BF16)
        four = dot(table_t[k], product)
        return four[:128, :128] - four[128:, 128:], four[128:, :128] + four[:128, 128:]

    sums[0, pl.ds(0, 128)] = back(0)[0]
    sums[8, pl.ds(0, 128)] = back(8)[0]
    for k in range(1, 8):
        one, two = back(k), back(16 - k)
        sums[k, pl.ds(0, 128)] = one[0] + two[0]
        sums[k, pl.ds(128, 128)] = one[1] - two[1]
    for i in range(16):
        rows, below = pl.ds(8 * i, 8), pl.ds(128 + 8 * i, 8)
        scale = 1.0 / 2048
        re = [sums[k, rows, :] * scale for k in range(9)]
        im = [None] + [sums[k, below, :] * scale for k in range(1, 8)] + [None]
        for a in range(5):
            groups = [None] * 4
            for k in range(9):
                ang = 2 * math.pi * (k * a % 16) / 16
                groups[k % 2] = add(groups[k % 2], scaled(re[k], math.cos(ang)))
                groups[2 + k % 2] = sub(groups[2 + k % 2], scaled(im[k], math.sin(ang)))
            ec, oc, es, os = groups
            data[a, rows, :] = add(add(ec, oc), add(es, os)).astype(BF16)
            if 0 < a < 4:
                data[8 - a, rows, :] = sub(sub(add(ec, os), oc), es).astype(BF16)
    for r, out in enumerate(outs):
        base = 2 * around(z, r)
        out[pl.ds(0, 128), :] = data[base + x]
        out[pl.ds(128, 128), :] = data[base + 1 - x]


def gate_kernel(e0, e1, e2, e3, direct, g0, g1, g2, g3, gated, conv):
    _, _, z, _ = place()
    for r, block in enumerate((e0, e1, e2, e3)):
        conv[around(z, -r)] = block[...]
    low = low_lanes((256, 128))
    for j in range(2):
        lanes = pl.ds(j * 128, 128)
        even, odd = conv[2 * j].astype(F32), conv[2 * j + 1].astype(F32)
        parts = (jnp.where(low, even, half_turn(odd)), jnp.where(low, half_turn(even), odd))
        for p, gate in enumerate((g0, g1, g2, g3)):
            rows = pl.ds(p * 128, 128)
            own = parts[p // 2][(p % 2) * 128 : (p % 2) * 128 + 128]
            y, x, _, _ = place()
            base = y * 512 + x * 256 if p == 0 else 256
            query = gate[:, pl.ds(pl.multiple_of(base + j * 128, 128), 128)].astype(F32)
            gated[rows, lanes] = (query * (own + direct[rows, lanes])).astype(BF16)


def sort_weight(*refs):
    pieces, keep, give = refs[:7], refs[7], refs[8]
    _, x, z, c = place()
    for r in range(4):
        owner = around(z, -r)
        for k in range(2):
            to = 2 * lax.rem(owner, 2) + (1 - x if k else x)

            @pl.when(owner // 2 == c)
            def _():
                keep[to] = (pieces[2 * r + k][...] if r < 3 else pieces[6][k])

            @pl.when(owner // 2 != c)
            def _():
                give[to] = (pieces[2 * r + k][...] if r < 3 else pieces[6][k])


def out_kernel(blocks, gated, other, keep, theirs, *outs):
    for p, out in zip(blocks, outs):
        rows = pl.ds(p * 128, 128)
        for i in range(4):
            total = dot_t(gated[rows, :], keep[i]) + dot_t(other[rows, :], theirs[i])
            out[:, pl.ds(i * 256, 256)] = total.astype(out.dtype)


def tables():
    k = np.arange(16)[:, None, None] + 16 * np.arange(128)[None, :, None]
    phase = 2 * np.pi / 2048 * (k * np.arange(128)[None, None, :] % 2048)
    co, si = np.cos(phase), np.sin(phase)
    back = np.concatenate([co.transpose(0, 2, 1), si.transpose(0, 2, 1)], 1)
    return np.concatenate([co, si], 1).astype(jnp.bfloat16), back.astype(jnp.bfloat16)


def planes(tokens, gate_q, gate_k, w_value, skip, filter_spectrum, w_out):
    seq, deep = 8, 4

    def permute(values, move):
        pairs = []
        for g in range(2):
            for i in range(seq):
                for k in range(2):
                    g2, z2, x2, k2 = move(g, i // 2, i % 2, k)
                    pairs.append(((g * seq + i) * 2 + k, (g2 * seq + z2 * 2 + x2) * 2 + k2))
        return lax.ppermute(values, AXES, pairs)

    def to_x(values):
        return permute(values, lambda g, z, x, k: (g, z, 1 - x, k))

    def to_core(values):
        return permute(values, lambda g, z, x, k: (g, z, x, 1 - k))

    def to_z(values, r):
        ring = (0, 1, 3, 2)
        at = [ring.index(z) for z in range(deep)]
        return permute(values, lambda g, z, x, k: (g, ring[(at[z] + r) % deep], x, k))

    def onward(values):
        return to_z(values, 1)

    def to_peer(values, p):
        return permute(values, lambda g, z, x, k: (g ^ (p // 2), z, x ^ (p % 2), k))

    def after(values, *done):
        return lax.optimization_barrier((values,) + done)[0]

    shape = jax.ShapeDtypeStruct
    block, square = shape((256, 128), BF16), shape((256, 256), BF16)
    own_v = lax.dynamic_slice_in_dim(w_value, lax.axis_index("grp") * 512, 512, axis=1)
    laid = [shape((128, 1024), BF16)] * 3 + [square] * 2 + [shape((2, 2, 128, 256), BF16)]
    *messages, own_o, away_o, away_f = copy_kernel(cut_messages, laid)(
        tokens, gate_k, gate_q, w_out, filter_spectrum, own_v
    )
    near = to_x(away_f)
    received = [to_peer(messages[p - 1], p) for p in (1, 2, 3)]
    filters = in_vmem(
        pack_filter,
        [shape((2, 2, 128, 128), BF16)] * 4,
        [pltpu.VMEM((4, 2, 2, 128, 128), BF16)],
        moved=1 << 20,
    )(filter_spectrum, near)
    filters = [filters[0]] + [to_z(filters[r], r) for r in (1, 2, 3)]
    v1 = onward(own_v)
    q1 = onward(own_o)
    v2 = onward(v1)
    q2 = onward(after(q1, v1))
    mine = in_vmem(join_tokens, shape((512, 512), BF16), moved=1 << 20)(tokens, after(received[0], q2), *received[1:])
    v3 = onward(v2)
    other = to_core(mine)
    got_o = to_x(after(away_o, v1))
    r1 = onward(after(got_o, v2))
    keep, give = in_vmem(
        value_kernel,
        [shape((512, 256), F32), shape((512, 256), BF16)],
        [pltpu.VMEM((512, 512), F32)],
        flops=1 << 29,
        moved=2 << 20,
    )(after(mine, r1, filters[0]), other, own_v, v1, v2, v3)
    drive, *sends = in_vmem(
        drive_kernel,
        [shape((512, 256), F32)] + [block] * 4,
        [pltpu.VMEM((512, 256), BF16), pltpu.VMEM((4, 256, 128), BF16)],
        moved=2 << 20,
    )(keep, to_x(give), gate_k, *received, skip[None, :])
    r2 = onward(after(r1, drive))
    columns = [sends[0]] + [to_z(sends[r], r) for r in (1, 2, 3)]
    last = onward(after(jnp.stack([q2, r2]), filters[3], *columns[1:]))
    table, table_t = tables()
    sends = in_vmem(
        conv_kernel,
        [block] * 4,
        [
            pltpu.VMEM((8, 128, 128), BF16),
            pltpu.VMEM((8, 2, 128, 128), BF16),
            pltpu.VMEM((16, 128, 256), BF16),
            pltpu.VMEM((9, 256, 128), F32),
        ],
        flops=1 << 30,
        moved=5 << 20,
    )(*columns, *filters, table, table_t)
    rows = [sends[0]] + [to_z(sends[r], r) for r in (1, 2, 3)]

    hops = [own_o, got_o, q1, r1, q2, r2, after(last, *rows[1:])]
    quad = shape((4, 256, 256), BF16)
    keep, give = in_vmem(sort_weight, [quad] * 2, moved=2 << 20)(*hops)
    theirs = to_core(give)
    gated = in_vmem(
        gate_kernel, shape((512, 256), BF16), [pltpu.VMEM((4, 256, 128), BF16)], moved=1 << 20
    )(*rows, drive, gate_q, *received)
    gated_other = to_core(gated)
    summed = (gated, gated_other, keep, theirs)
    send = shape((128, 1024), BF16)
    far = in_vmem(functools.partial(out_kernel, (3, 1)), [send] * 2, flops=1 << 29, moved=2 << 20)
    close = in_vmem(
        functools.partial(out_kernel, (2, 0)),
        [send, shape((128, 1024), F32)],
        flops=1 << 29,
        moved=2 << 20,
    )
    to_xy, to_row = far(*summed)
    parts = [to_peer(to_xy, 3), to_peer(to_row, 1)]
    to_column, total = close(*summed)
    parts.append(to_peer(to_column, 2))
    for part in parts:
        total = total + part.astype(F32)
    return total.astype(BF16)


def shards(tokens, gate_q, gate_k, w_value, skip, filter_spectrum, w_out):
    seq_count = lax.axis_size("seq")
    position = lax.axis_index("seq")
    length_b = tokens.shape[0]
    columns_each = length_b // seq_count
    freq_rows = 2 * seq_count
    freqs_each = freq_rows // seq_count
    fft_length = freq_rows * length_b
    features = lax.all_gather(tokens, "ch", axis=1, tiled=True)
    value_weight, out_weight = (
        lax.all_gather(w_value, "seq", axis=0, tiled=True),
        lax.all_gather(w_out, "seq", axis=0, tiled=True),
    )
    value = jnp.dot(features, value_weight, preferred_element_type=jnp.float32)
    value = value.astype(jnp.bfloat16)
    drive = (gate_k.astype(jnp.float32) * widened(value)).astype(jnp.bfloat16)
    channels = drive.shape[1]
    columns = lax.all_to_all(drive[None], "seq", split_axis=1, concat_axis=0, tiled=True)
    index_rows = jnp.arange(freq_rows, dtype=jnp.int32)
    index_seq = jnp.arange(seq_count, dtype=jnp.int32)
    index_b = jnp.arange(length_b, dtype=jnp.int32)
    cos_first, sin_first = angles(freq_rows, index_rows, index_seq)
    cos_first = cos_first.astype(jnp.bfloat16)
    sin_first = sin_first.astype(jnp.bfloat16)
    flattened = columns.reshape(seq_count, columns_each * channels)
    real_part = jnp.dot(cos_first, flattened, preferred_element_type=jnp.float32)
    imag_part = jnp.dot(-sin_first, flattened, preferred_element_type=jnp.float32)
    real_part = real_part.reshape(freq_rows, columns_each, channels)
    imag_part = imag_part.reshape(freq_rows, columns_each, channels)
    mine_b = position * columns_each + jnp.arange(columns_each, dtype=jnp.int32)
    twist_cos, twist_sin = angles(fft_length, index_rows, mine_b)
    twist_cos = twist_cos[:, :, None]
    twist_sin = twist_sin[:, :, None]
    section = jnp.stack(
        [
            real_part * twist_cos + imag_part * twist_sin,
            imag_part * twist_cos - real_part * twist_sin,
        ]
    ).astype(jnp.bfloat16)
    spectral = lax.all_to_all(section, "seq", split_axis=1, concat_axis=2, tiled=True)
    cos_seq, sin_seq = angles(length_b, index_b, index_b)
    cos_seq = cos_seq.astype(jnp.bfloat16)
    sin_seq = sin_seq.astype(jnp.bfloat16)
    spectrum_real = jnp.einsum(
        "qb,kbc->kqc", cos_seq, spectral[0], preferred_element_type=jnp.float32
    ) + jnp.einsum("qb,kbc->kqc", sin_seq, spectral[1], preferred_element_type=jnp.float32)
    spectrum_imag = jnp.einsum(
        "qb,kbc->kqc", cos_seq, spectral[1], preferred_element_type=jnp.float32
    ) - jnp.einsum("qb,kbc->kqc", sin_seq, spectral[0], preferred_element_type=jnp.float32)
    filter_real = filter_spectrum[0].astype(jnp.float32)
    filter_imag = filter_spectrum[1].astype(jnp.float32)
    product = jnp.stack(
        [
            spectrum_real * filter_real - spectrum_imag * filter_imag,
            spectrum_real * filter_imag + spectrum_imag * filter_real,
        ]
    ).astype(jnp.bfloat16)
    inverse_real = jnp.einsum(
        "qb,kqc->kbc", cos_seq, product[0], preferred_element_type=jnp.float32
    ) - jnp.einsum("qb,kqc->kbc", sin_seq, product[1], preferred_element_type=jnp.float32)
    inverse_imag = jnp.einsum(
        "qb,kqc->kbc", sin_seq, product[0], preferred_element_type=jnp.float32
    ) + jnp.einsum("qb,kqc->kbc", cos_seq, product[1], preferred_element_type=jnp.float32)
    mine_k = position * freqs_each + jnp.arange(freqs_each, dtype=jnp.int32)
    back_cos, back_sin = angles(fft_length, mine_k, index_b)
    back_cos = back_cos[:, :, None]
    back_sin = back_sin[:, :, None]
    back = jnp.stack(
        [
            inverse_real * back_cos - inverse_imag * back_sin,
            inverse_real * back_sin + inverse_imag * back_cos,
        ]
    ).astype(jnp.bfloat16)
    returned = lax.all_to_all(back, "seq", split_axis=2, concat_axis=1, tiled=True)
    flat_real = returned[0].reshape(freq_rows, columns_each * channels)
    flat_imag = returned[1].reshape(freq_rows, columns_each * channels)
    conv = jnp.dot(cos_first.T, flat_real, preferred_element_type=jnp.float32) - jnp.dot(
        sin_first.T, flat_imag, preferred_element_type=jnp.float32
    )
    conv = (
        (conv * (1.0 / fft_length)).reshape(seq_count, columns_each, channels).astype(jnp.bfloat16)
    )
    conv_rows = lax.all_to_all(conv, "seq", split_axis=0, concat_axis=1, tiled=True)[0]
    gated = (
        gate_q.astype(jnp.float32) * (widened(conv_rows) + skip[None, :] * widened(drive))
    ).astype(jnp.bfloat16)
    partial_value = lax.dot_general(
        gated, out_weight, (((1,), (1,)), ((), ())), preferred_element_type=jnp.float32
    )
    return lax.psum_scatter(
        partial_value.astype(jnp.bfloat16), "ch", scatter_dimension=1, tiled=True
    )


def solution(mesh):
    placed = (
        P(("grp", "seq"), "ch"),
        P(("grp", "seq"), "ch"),
        P(("grp", "seq"), "ch"),
        P("seq", "ch"),
        P("ch"),
        P(None, "seq", None, "ch"),
        P("seq", "ch"),
    )
    sizes = mesh.shape
    body = planes if (sizes["grp"], sizes["seq"], sizes["ch"]) == (2, 8, 2) else shards
    return jax.shard_map(
        body, mesh=mesh, in_specs=placed, out_specs=P(("grp", "seq"), "ch"), check_vma=False
    )
```
